32 devices in a mesh: sec: 4 (over y, x), gx: 4 (over z), gz: 2 (over core).
Axes of the slice: x: 2, y: 2, z: 4, core: 2. Of those that a mesh axis runs over, the one named last changes fastest.
Arguments:
- fields: float32 [4, 5, 512, 256], P('sec', None, 'gx', 'gz'), may hold values from -6 to 6
- media: float32 [4, 3, 512, 256], P('sec', None, 'gx', 'gz'), may hold values from 0.5 to 2
- plane_rows: int32 [16], replicated, may hold values from 0 to 255, as said below
- box_offset: int32 [3], replicated, may hold values from 0 to 128
Outputs:
- evolved: float32 [4, 5, 512, 256], P('sec', None, 'gx', 'gz')
The draws below stay inside these ranges and needn't reach their ends.
Inputs may be any that keep to these rules, and one draw needn't show every extreme that they name: `plane_rows`: entries 8 * j to 8 * j + 7 are distinct rows of the j-th depth block of 128 rows; row 0 and row 255 are always among them.
All inputs are finite; a program needn't handle non-finite values.
Results may differ from the reference program's by a relative error of at most 0.00013.
Values sent between devices are 32-bit elements; how exact they have to be, the bound alone decides.
No kernel may reach another device: no remote copies, remote signals or barrier semaphores. Data moves between devices by JAX's collectives and lax.ppermute only.
A program may use at most 64 MiB of HBM per device.

```python
import math
import jax
import jax.numpy as jnp
from jax import lax

CZ = 128
RADIUS = 4
STEPS = 5
NPD = 8
NX = 512
NZ = 256
NP = 16
FAR = 3
N_SEC = 4
N_GZ = 2


def draw_plane_rows(key, part):
    scores = jax.random.randint(key, (N_GZ, CZ), 0, 4096)
    blocks = lax.broadcasted_iota(jnp.int32, (N_GZ, CZ), 0)
    columns = lax.broadcasted_iota(jnp.int32, (N_GZ, CZ), 1)
    pinned = (blocks == 0) & (columns == 0) | (blocks == N_GZ - 1) & (columns == CZ - 1)
    ranked = scores * CZ + columns + jnp.where(pinned, 8192 * CZ, 0)
    ranked_values, picked = lax.top_k(ranked, NPD)
    return (picked + blocks[:, :NPD] * CZ).reshape(NP).astype(jnp.int32)


def shard_levels(own_key, extent, split, least, high):
    factor_of, own = 1.0, jax.random.fold_in(own_key, 6)
    for position, shards_of in split:
        heights = jnp.exp(jax.random.uniform(jax.random.fold_in(own, position), (shards_of,), jnp.float32, least / len(split), high / len(split)))
        factor_of = factor_of * jnp.repeat(heights, extent[position] // shards_of).reshape([-1 if axis == position else 1 for axis in range(len(extent))])
    return factor_of


def noise(own_key, extent, width, reach, cuts=(), kind=jnp.bfloat16):
    factor_of = shard_levels(own_key, extent, cuts, -0.22, 0.18) if cuts else 1.0
    values = jax.random.normal(own_key, extent, jnp.float32) * width * factor_of
    return jnp.minimum(jnp.maximum(values, -reach), reach).astype(kind)


def setup_inputs(seed: int = 0) -> dict:
    arg_keys = jax.random.split(jax.random.key(seed), 5)
    return {
        "fields": noise(arg_keys[0], (N_SEC, 5, NX, NZ), 1.0, 6.0, ((0, 4), (2, 4), (3, 2)), jnp.float32),
        "media": jnp.clip(jnp.exp(math.log(2.0) - 1.3862944 * jax.random.uniform(arg_keys[1], (N_SEC, 3, NX, NZ), jnp.float32) ** shard_levels(arg_keys[1], (N_SEC, 3, NX, NZ), ((0, 4), (2, 4), (3, 2)), -0.2, 0.2)), 0.5, 2.0),
        "plane_rows": draw_plane_rows(jax.random.fold_in(arg_keys[4], 71), 0),
        "box_offset": jax.random.randint(arg_keys[3], (FAR,), 0, NZ // 2 + 1).astype(jnp.int32),
    }


STENCIL = (0.8, -0.2, 4.0 / 105.0, -1.0 / 280.0)
TIME_STEP = 0.2
COUPLING = 0.5
RELAXATION = (0.9, 0.5)
MEMORY_WEIGHT = (0.15, 0.1)


def along_x(padded, anchor, count_x, count_z):
    summed = jnp.zeros(padded.shape[:-2] + (count_x, count_z), jnp.float32)
    for offset, stencil_tap in enumerate(STENCIL, 1):
        forward = padded[..., anchor + offset:anchor + offset + count_x, anchor:anchor + count_z]
        backward = padded[..., anchor - offset:anchor - offset + count_x, anchor:anchor + count_z]
        summed = summed + stencil_tap * (forward - backward)
    return summed


def along_z(padded, anchor, count_x, count_z):
    summed = jnp.zeros(padded.shape[:-2] + (count_x, count_z), jnp.float32)
    for offset, stencil_tap in enumerate(STENCIL, 1):
        forward = padded[..., anchor:anchor + count_x, anchor + offset:anchor + offset + count_z]
        backward = padded[..., anchor:anchor + count_x, anchor - offset:anchor - offset + count_z]
        summed = summed + stencil_tap * (forward - backward)
    return summed


def velocity_elastic(velocity, stresses, buoyancy, anchor, count_x, count_z):
    updated_x = velocity[0] + TIME_STEP * buoyancy * (along_x(stresses[0], anchor, count_x, count_z) + along_z(stresses[2], anchor, count_x, count_z))
    updated_z = velocity[1] + TIME_STEP * buoyancy * (along_x(stresses[2], anchor, count_x, count_z) + along_z(stresses[1], anchor, count_x, count_z))
    return jnp.stack([updated_x, updated_z])


def velocity_acoustic(velocity, stresses, buoyancy, anchor, count_x, count_z):
    updated_x = velocity[0] - TIME_STEP * buoyancy * along_x(stresses[0], anchor, count_x, count_z)
    updated_z = velocity[1] - TIME_STEP * buoyancy * along_z(stresses[0], anchor, count_x, count_z)
    return jnp.stack([updated_x, updated_z])


def stress_elastic(stresses, velocity_pad, material, anchor, count_x, count_z):
    strain_x = along_x(velocity_pad[0], anchor, count_x, count_z)
    strain_z = along_z(velocity_pad[1], anchor, count_x, count_z)
    strain_shear = along_z(velocity_pad[0], anchor, count_x, count_z) + along_x(velocity_pad[1], anchor, count_x, count_z)
    lame_first = material[1]
    shear_modulus = material[2]
    normal_x = stresses[0] + TIME_STEP * ((lame_first + 2.0 * shear_modulus) * strain_x + lame_first * strain_z)
    normal_z = stresses[1] + TIME_STEP * (lame_first * strain_x + (lame_first + 2.0 * shear_modulus) * strain_z)
    shear_new = stresses[2] + TIME_STEP * shear_modulus * strain_shear
    return jnp.stack([normal_x, normal_z, shear_new])


def stress_acoustic(stresses, velocity_pad, material, anchor, count_x, count_z):
    divergence = along_x(velocity_pad[0], anchor, count_x, count_z) + along_z(velocity_pad[1], anchor, count_x, count_z)
    loading = material[1] * divergence
    memory_one = RELAXATION[0] * stresses[1] + (1.0 - RELAXATION[0]) * MEMORY_WEIGHT[0] * material[2] * loading
    memory_two = RELAXATION[1] * stresses[2] + (1.0 - RELAXATION[1]) * MEMORY_WEIGHT[1] * material[2] * loading
    pressure = stresses[0] - TIME_STEP * (loading - memory_one - memory_two)
    return jnp.stack([pressure, memory_one, memory_two])


def pad_cells(field):
    widths = [(0, 0)] * (field.ndim - 2) + [(RADIUS, RADIUS), (RADIUS, RADIUS)]
    return jnp.pad(field, widths)


def step_section(current, material, elastic):
    if elastic:
        velocity = velocity_elastic(current[0:2], pad_cells(current[2:5]), material[0], RADIUS, NX, NZ)
        stresses = stress_elastic(current[2:5], pad_cells(velocity), material, RADIUS, NX, NZ)
    else:
        velocity = velocity_acoustic(current[0:2], pad_cells(current[2:5]), material[0], RADIUS, NX, NZ)
        stresses = stress_acoustic(current[2:5], pad_cells(velocity), material, RADIUS, NX, NZ)
    return jnp.concatenate([velocity, stresses], axis=0)


def injection_rows(source, plane_rows):
    picked = jnp.take(source, plane_rows, axis=2)
    combined = jnp.stack([picked[0], picked[1], -0.5 * (picked[2] + picked[3])])
    return jnp.transpose(combined, (0, 2, 1))


def reference(fields, media, plane_rows, box_offset):
    source = fields[0]
    sections = [fields[index] for index in range(1, N_SEC)]
    depth_ids = jnp.arange(NZ, dtype=jnp.int32)
    for step_index in range(STEPS):
        source = step_section(source, media[0], True)
        rows = injection_rows(source, plane_rows)
        for index in range(N_SEC - 1):
            evolved_far = step_section(sections[index], media[index + 1], False)
            landing = (box_offset[index] + plane_rows // 2).astype(jnp.int32)
            chosen = (landing[:, None] == depth_ids[None, :]).astype(jnp.float32)
            injected = jnp.einsum("ckx,kz->cxz", rows, chosen, precision=lax.Precision.HIGHEST)
            sections[index] = jnp.concatenate([evolved_far[0:3] + COUPLING * injected, evolved_far[3:5]], axis=0)
    return jnp.stack([source] + sections)
```

```python
import functools

import jax
import jax.numpy as jnp
from jax import lax
from jax.experimental import pallas as pl
from jax.experimental.pallas import tpu as pltpu
from jax.sharding import PartitionSpec as P

RADIUS = 4
STEPS = 5
NPD = 8

STENCIL = (0.8, -0.2, 4.0 / 105.0, -1.0 / 280.0)
TIME_STEP = 0.2
COUPLING = 0.5
RELAXATION = (0.9, 0.5)
MEMORY_WEIGHT = (0.15, 0.1)


def padded_2(block, sides, width):
    for axis, dim in sides:
        count = lax.axis_size(axis)
        forward = [(i, i + 1) for i in range(count - 1)]
        backward = [(target, source) for source, target in forward]
        low = lax.ppermute(
            lax.slice_in_dim(block, block.shape[dim] - width, None, axis=dim), axis, forward
        )
        high = lax.ppermute(lax.slice_in_dim(block, 0, width, axis=dim), axis, backward)
        block = jnp.concatenate([low, block, high], axis=dim)
    return block


def broadcast(value, axis, source):
    kept = jnp.where(lax.axis_index(axis) == source, value, 0).astype(value.dtype)
    return lax.psum(kept, axis)


def along_x(padded, anchor, count_x, count_z):
    summed = jnp.zeros(padded.shape[:-2] + (count_x, count_z), jnp.float32)
    for offset, stencil_tap in enumerate(STENCIL, 1):
        forward = padded[
            ..., anchor + offset : anchor + offset + count_x, anchor : anchor + count_z
        ]
        backward = padded[
            ..., anchor - offset : anchor - offset + count_x, anchor : anchor + count_z
        ]
        summed = summed + stencil_tap * (forward - backward)
    return summed


def along_z(padded, anchor, count_x, count_z):
    summed = jnp.zeros(padded.shape[:-2] + (count_x, count_z), jnp.float32)
    for offset, stencil_tap in enumerate(STENCIL, 1):
        forward = padded[
            ..., anchor : anchor + count_x, anchor + offset : anchor + offset + count_z
        ]
        backward = padded[
            ..., anchor : anchor + count_x, anchor - offset : anchor - offset + count_z
        ]
        summed = summed + stencil_tap * (forward - backward)
    return summed


def velocity_elastic(velocity, stresses, buoyancy, anchor, count_x, count_z):
    updated_x = velocity[0] + TIME_STEP * buoyancy * (
        along_x(stresses[0], anchor, count_x, count_z)
        + along_z(stresses[2], anchor, count_x, count_z)
    )
    updated_z = velocity[1] + TIME_STEP * buoyancy * (
        along_x(stresses[2], anchor, count_x, count_z)
        + along_z(stresses[1], anchor, count_x, count_z)
    )
    return jnp.stack([updated_x, updated_z])


def velocity_acoustic(velocity, stresses, buoyancy, anchor, count_x, count_z):
    updated_x = velocity[0] - TIME_STEP * buoyancy * along_x(stresses[0], anchor, count_x, count_z)
    updated_z = velocity[1] - TIME_STEP * buoyancy * along_z(stresses[0], anchor, count_x, count_z)
    return jnp.stack([updated_x, updated_z])


def stress_elastic(stresses, velocity_pad, material, anchor, count_x, count_z):
    strain_x = along_x(velocity_pad[0], anchor, count_x, count_z)
    strain_z = along_z(velocity_pad[1], anchor, count_x, count_z)
    strain_shear = along_z(velocity_pad[0], anchor, count_x, count_z) + along_x(
        velocity_pad[1], anchor, count_x, count_z
    )
    lame_first = material[1]
    shear_modulus = material[2]
    normal_x = stresses[0] + TIME_STEP * (
        (lame_first + 2.0 * shear_modulus) * strain_x + lame_first * strain_z
    )
    normal_z = stresses[1] + TIME_STEP * (
        lame_first * strain_x + (lame_first + 2.0 * shear_modulus) * strain_z
    )
    shear_new = stresses[2] + TIME_STEP * shear_modulus * strain_shear
    return jnp.stack([normal_x, normal_z, shear_new])


def stress_acoustic(stresses, velocity_pad, material, anchor, count_x, count_z):
    divergence = along_x(velocity_pad[0], anchor, count_x, count_z) + along_z(
        velocity_pad[1], anchor, count_x, count_z
    )
    loading = material[1] * divergence
    memory_one = (
        RELAXATION[0] * stresses[1]
        + (1.0 - RELAXATION[0]) * MEMORY_WEIGHT[0] * material[2] * loading
    )
    memory_two = (
        RELAXATION[1] * stresses[2]
        + (1.0 - RELAXATION[1]) * MEMORY_WEIGHT[1] * material[2] * loading
    )
    pressure = stresses[0] - TIME_STEP * (loading - memory_one - memory_two)
    return jnp.stack([pressure, memory_one, memory_two])


def local_stepwise(fields, media, plane_rows, box_offset):
    current = fields[0]
    material = media[0]
    count_x = current.shape[1]
    count_z = current.shape[2]
    section = lax.axis_index("sec")
    is_source = section == 0
    block_z = lax.axis_index("gz")
    local_rows = lax.dynamic_slice_in_dim(plane_rows, block_z * NPD, NPD) - block_z * count_z
    offset = lax.dynamic_slice_in_dim(box_offset, jnp.maximum(section - 1, 0), 1)[0]
    depth_ids = block_z * count_z + jnp.arange(count_z, dtype=jnp.int32)
    landing = offset + plane_rows // 2
    chosen = (landing[:, None] == depth_ids[None, :]).astype(jnp.float32)
    for step_index in range(STEPS):
        stress_pad = padded_2(current[2:5], (("gx", 1), ("gz", 2)), RADIUS)
        velocity = lax.cond(
            is_source,
            lambda: velocity_elastic(
                current[0:2], stress_pad, material[0], RADIUS, count_x, count_z
            ),
            lambda: velocity_acoustic(
                current[0:2], stress_pad, material[0], RADIUS, count_x, count_z
            ),
        )
        velocity_pad = padded_2(velocity, (("gx", 1), ("gz", 2)), RADIUS)
        stresses = lax.cond(
            is_source,
            lambda: stress_elastic(current[2:5], velocity_pad, material, RADIUS, count_x, count_z),
            lambda: stress_acoustic(current[2:5], velocity_pad, material, RADIUS, count_x, count_z),
        )
        current = jnp.concatenate([velocity, stresses], axis=0)
        picked = jnp.take(current, local_rows, axis=2)
        block_plane = jnp.transpose(
            jnp.stack([picked[0], picked[1], -0.5 * (picked[2] + picked[3])]), (0, 2, 1)
        )
        joined = lax.all_gather(block_plane, "gz", axis=1, tiled=True)
        gathered = broadcast(joined, "sec", 0)
        injected = jnp.einsum("ckx,kz->cxz", gathered, chosen, precision=lax.Precision.HIGHEST)
        far_state = jnp.concatenate([current[0:3] + COUPLING * injected, current[3:5]], axis=0)
        current = jnp.where(is_source, current, far_state)
    return current[None]


HALO = 2 * RADIUS * STEPS
CELLS = 128
HALF = CELLS // 2
WINDOW = HALF + 2 * HALO
DEPTH = 2 * CELLS
PART = CELLS - (HALF - HALO)
NP = 2 * NPD
TRIM = (0, 0, 16, 16, 32)
FIRST_ROWS, FIRST_AT = 128, 8
SECOND_ROWS, SECOND_AT = 96, 24
ROWS = FIRST_ROWS + SECOND_ROWS
GROUPS = 8
SCALE = 840.0
TAPS = (672.0, -168.0, 32.0, -3.0)


def banded(shape, lag):
    distance = lax.broadcasted_iota(jnp.int32, shape, 0) - lax.broadcasted_iota(
        jnp.int32, shape, 1
    )
    distance = lag * distance
    values = jnp.zeros(shape, jnp.float32)
    for offset, tap in enumerate(TAPS, 1):
        values = jnp.where(distance == offset, tap, values)
        values = jnp.where(distance == -offset, -tap, values)
    return values.astype(jnp.bfloat16)


def halves(values):
    high = values.astype(jnp.bfloat16)
    low = (values - high.astype(jnp.float32)).astype(jnp.bfloat16)
    return high, low


def dot(left, right):
    return jnp.dot(left, right, preferred_element_type=jnp.float32)


def diff_x(band_x, parts):
    count = parts[0].shape[0]
    band = band_x[:count, :count]
    return dot(band, parts[0]) + dot(band, parts[1])


def diff_z(band_z, parts):
    return dot(parts[0], band_z) + dot(parts[1], band_z)


def assemble(window, fields, media, ahead, behind, other):
    core = lax.axis_index("gz")

    @pl.when(core == 0)
    def _():
        for index in range(8):
            own = fields[index] if index < 5 else media[index - 5]
            window[index, :HALO, :CELLS] = ahead[index]
            window[index, :HALO, CELLS:] = behind[index]
            window[index, HALO:, :CELLS] = own[:PART]
            window[index, HALO:, CELLS:] = other[index]

    @pl.when(core == 1)
    def _():
        for index in range(8):
            own = fields[index] if index < 5 else media[index - 5]
            window[index, :PART, CELLS:] = own[CELLS - PART :]
            window[index, :PART, :CELLS] = other[index]
            window[index, PART:, CELLS:] = ahead[index]
            window[index, PART:, :CELLS] = behind[index]


def trimmed(arrays, amount):
    if amount == 0:
        return arrays
    return [array[amount:-amount] for array in arrays]


def place(state, held, sent):
    start = HALF // 2 + HALF // 4 - HALO
    core = lax.axis_index("gz")
    state = [array[start : start + HALF] for array in state]

    @pl.when(core == 0)
    def _():
        for index in range(5):
            held[index, :HALF] = state[index][:, :CELLS]
            sent[index] = state[index][:, CELLS:]

    @pl.when(core == 1)
    def _():
        for index in range(5):
            held[index, HALF:] = state[index][:, CELLS:]
            sent[index] = state[index][:, :CELLS]


def source_kernel(
    ids, fields, media, ahead, behind, other, held, sent, rows, window
):
    @pl.when(lax.axis_index("sec") == 0)
    def _():
        assemble(window, fields, media, ahead, behind, other)
        band_x = banded((WINDOW, WINDOW), -1)
        band_z = banded((DEPTH, DEPTH), 1)
        depth = lax.broadcasted_iota(jnp.int32, (DEPTH, CELLS), 0)
        pick = jnp.where(depth == ids[0:1, :], 1.0, 0.0).astype(jnp.bfloat16)
        vx, vz, sxx, szz, sxz, light, lame, shear = [window[index] for index in range(8)]
        light = light * (TIME_STEP / SCALE)
        both = (lame + 2.0 * shear) * (TIME_STEP / SCALE)
        lame = lame * (TIME_STEP / SCALE)
        shear = shear * (TIME_STEP / SCALE)
        at = 0
        for step in range(STEPS):
            cut = TRIM[step] - at
            at = TRIM[step]
            vx, vz, sxx, szz, sxz, light, both, lame, shear = trimmed(
                [vx, vz, sxx, szz, sxz, light, both, lame, shear], cut
            )
            parts_xx, parts_zz, parts_xz = halves(sxx), halves(szz), halves(sxz)
            vx = vx + light * (diff_x(band_x, parts_xx) + diff_z(band_z, parts_xz))
            vz = vz + light * (diff_x(band_x, parts_xz) + diff_z(band_z, parts_zz))
            parts_x, parts_z = halves(vx), halves(vz)
            strain_x, strain_z = diff_x(band_x, parts_x), diff_z(band_z, parts_z)
            sxx = sxx + (both * strain_x + lame * strain_z)
            szz = szz + (lame * strain_x + both * strain_z)
            sxz = sxz + shear * (diff_z(band_z, parts_x) + diff_x(band_x, parts_z))
            for component, (parts, factor) in enumerate(
                ((parts_x, COUPLING), (parts_z, COUPLING), (halves(sxx + szz), -0.5 * COUPLING))
            ):
                picked = factor * (dot(parts[0], pick) + dot(parts[1], pick))
                group = 3 * step + component
                first = group < GROUPS
                base, count, start = (
                    (0, FIRST_ROWS, FIRST_AT) if first else (FIRST_ROWS, SECOND_ROWS, SECOND_AT)
                )
                low, high = max(start, at), min(start + count, WINDOW - at)
                picked = picked[low - at : high - at]
                place_at = pl.ds(base + low - start, high - low)
                if group % GROUPS:
                    lane = lax.broadcasted_iota(jnp.int32, picked.shape, 1) // NP
                    picked = jnp.where(lane >= group % GROUPS, picked, rows[place_at, :])
                rows[place_at, :] = picked
        place([vx, vz, sxx, szz, sxz], held, sent)


def far_kernel(
    ids, fields, media, ahead, behind, other, rows, held_in, sent_in, held, sent, window
):
    section = lax.axis_index("sec")

    @pl.when(section == 0)
    def _():
        held[...] = held_in[...]
        sent[...] = sent_in[...]

    @pl.when(section > 0)
    def _():
        assemble(window, fields, media, ahead, behind, other)
        band_x = banded((WINDOW, WINDOW), -1)
        band_z = banded((DEPTH, DEPTH), 1)
        depth = lax.broadcasted_iota(jnp.int32, (DEPTH, CELLS), 0)
        land = jnp.where(depth == ids[1:2, :], 1.0, 0.0).astype(jnp.bfloat16)
        vx, vz, pressure, one, two, light, kappa, loss = [window[index] for index in range(8)]
        light = light * (TIME_STEP / SCALE)
        kappa = kappa * (1.0 / SCALE)
        loss_one = loss * ((1.0 - RELAXATION[0]) * MEMORY_WEIGHT[0])
        loss_two = loss * ((1.0 - RELAXATION[1]) * MEMORY_WEIGHT[1])
        at = 0
        for step in range(STEPS):
            cut = TRIM[step] - at
            at = TRIM[step]
            vx, vz, pressure, one, two, light, kappa, loss_one, loss_two = trimmed(
                [vx, vz, pressure, one, two, light, kappa, loss_one, loss_two], cut
            )
            parts = halves(pressure)
            vx = vx - light * diff_x(band_x, parts)
            vz = vz - light * diff_z(band_z, parts)
            load = kappa * (diff_x(band_x, halves(vx)) + diff_z(band_z, halves(vz)))
            one = RELAXATION[0] * one + loss_one * load
            two = RELAXATION[1] * two + loss_two * load
            pressure = pressure - TIME_STEP * (load - one - two)
            injected = [vx, vz, pressure]
            for component in range(3):
                group = 3 * step + component
                first = group < GROUPS
                base, count, start = (
                    (0, FIRST_ROWS, FIRST_AT) if first else (FIRST_ROWS, SECOND_ROWS, SECOND_AT)
                )
                low, high = max(start, at), min(start + count, WINDOW - at)
                taken = rows[pl.ds(base + low - start, high - low), :]
                lane = lax.broadcasted_iota(jnp.int32, taken.shape, 1) // NP
                taken = halves(jnp.where(lane == group % GROUPS, taken, 0.0))
                added = sum(
                    lax.dot_general(
                        part, land, (((1,), (1,)), ((), ())), preferred_element_type=jnp.float32
                    )
                    for part in taken
                )
                low, high = low - at, high - at
                array = injected[component]
                pieces = [array[:low], array[low:high] + added, array[high:]]
                pieces = [piece for piece in pieces if piece.shape[0]]
                injected[component] = jnp.concatenate(pieces, axis=0)
            vx, vz, pressure = injected
        place([vx, vz, pressure, one, two], held, sent)


def call(kernel, outs, operands, flops):
    vmem = pl.BlockSpec(memory_space=pltpu.VMEM)
    return pl.pallas_call(
        kernel,
        out_shape=[jax.ShapeDtypeStruct(shape, jnp.float32) for shape in outs],
        in_specs=[vmem] * len(operands),
        out_specs=[vmem] * len(outs),
        scratch_shapes=[pltpu.VMEM((8, WINDOW, DEPTH), jnp.float32)],
        compiler_params=pltpu.CompilerParams(vmem_limit_bytes=48 * 1024 * 1024),
        cost_estimate=pl.CostEstimate(
            flops=flops, bytes_accessed=2 * 1024 * 1024, transcendentals=0
        ),
    )(*operands)


def local_window(columns, fields, media, plane_rows, box_offset):
    fields, media = fields[0], media[0]
    core = lax.axis_index("gz")
    is_first = core == 0
    both = jnp.concatenate([fields, media], axis=0)
    top, bottom = both[:, :HALO], both[:, CELLS - HALO :]
    straight, crossed = [], []
    for column in range(columns):
        if column + 1 < columns:
            straight.append((2 * column, 2 * column + 2))
            crossed.append((2 * column + 1, 2 * column + 2))
        if column:
            straight.append((2 * column + 1, 2 * column - 1))
            crossed.append((2 * column, 2 * column - 1))
    ahead = lax.ppermute(jnp.where(is_first, bottom, top), ("gx", "gz"), straight)
    behind = lax.ppermute(jnp.where(is_first, top, bottom), ("gx", "gz"), crossed)
    other = lax.ppermute(
        jnp.where(is_first, both[:, CELLS - PART :], both[:, :PART]), "gz", [(0, 1), (1, 0)]
    )
    section = lax.axis_index("sec")
    offset = lax.dynamic_slice_in_dim(box_offset, jnp.maximum(section - 1, 0), 1)
    ids = jnp.tile(jnp.stack([plane_rows, offset + plane_rows // 2]), (1, GROUPS))
    held_shape, sent_shape = (5, CELLS, CELLS), (5, HALF, CELLS)
    held, sent, rows = call(
        source_kernel,
        [held_shape, sent_shape, (ROWS, CELLS)],
        [ids, fields, media, ahead, behind, other],
        4_000_000_000,
    )
    arrived = [lax.ppermute(rows, "sec", [(0, target)]) for target in (1, 2, 3)]
    rows = arrived[0] + arrived[1] + arrived[2]
    held, sent = call(
        far_kernel,
        [held_shape, sent_shape],
        [ids, fields, media, ahead, behind, other, rows, held, sent],
        4_000_000_000,
    )
    swapped = lax.ppermute(sent, "gz", [(0, 1), (1, 0)])
    return lax.dynamic_update_slice_in_dim(held, swapped, HALF * (1 - core), axis=1)[None]


def solution(mesh):
    in_specs = (P("sec", None, "gx", "gz"), P("sec", None, "gx", "gz"), P(), P())
    out_specs = P("sec", None, "gx", "gz")
    if mesh.shape["gz"] == 2:
        local = functools.partial(local_window, mesh.shape["gx"])
    else:
        local = local_stepwise
    return jax.shard_map(local, mesh=mesh, in_specs=in_specs, out_specs=out_specs, check_vma=False)
```

```python
import functools

import jax
import jax.numpy as jnp
from jax import lax
from jax.experimental import pallas as pl
from jax.experimental.pallas import tpu as pltpu
from jax.sharding import PartitionSpec as P

RADIUS = 4
STEPS = 5
NPD = 8

STENCIL = (0.8, -0.2, 4.0 / 105.0, -1.0 / 280.0)
TIME_STEP = 0.2
COUPLING = 0.5
RELAXATION = (0.9, 0.5)
MEMORY_WEIGHT = (0.15, 0.1)


def padded_2(block, sides, width):
    for axis, dim in sides:
        count = lax.axis_size(axis)
        forward = [(i, i + 1) for i in range(count - 1)]
        backward = [(target, source) for source, target in forward]
        low = lax.ppermute(
            lax.slice_in_dim(block, block.shape[dim] - width, None, axis=dim), axis, forward
        )
        high = lax.ppermute(lax.slice_in_dim(block, 0, width, axis=dim), axis, backward)
        block = jnp.concatenate([low, block, high], axis=dim)
    return block


def broadcast(value, axis, source):
    kept = jnp.where(lax.axis_index(axis) == source, value, 0).astype(value.dtype)
    return lax.psum(kept, axis)


def along_x(padded, anchor, count_x, count_z):
    summed = jnp.zeros(padded.shape[:-2] + (count_x, count_z), jnp.float32)
    for offset, stencil_tap in enumerate(STENCIL, 1):
        forward = padded[
            ..., anchor + offset : anchor + offset + count_x, anchor : anchor + count_z
        ]
        backward = padded[
            ..., anchor - offset : anchor - offset + count_x, anchor : anchor + count_z
        ]
        summed = summed + stencil_tap * (forward - backward)
    return summed


def along_z(padded, anchor, count_x, count_z):
    summed = jnp.zeros(padded.shape[:-2] + (count_x, count_z), jnp.float32)
    for offset, stencil_tap in enumerate(STENCIL, 1):
        forward = padded[
            ..., anchor : anchor + count_x, anchor + offset : anchor + offset + count_z
        ]
        backward = padded[
            ..., anchor : anchor + count_x, anchor - offset : anchor - offset + count_z
        ]
        summed = summed + stencil_tap * (forward - backward)
    return summed


def velocity_elastic(velocity, stresses, buoyancy, anchor, count_x, count_z):
    updated_x = velocity[0] + TIME_STEP * buoyancy * (
        along_x(stresses[0], anchor, count_x, count_z)
        + along_z(stresses[2], anchor, count_x, count_z)
    )
    updated_z = velocity[1] + TIME_STEP * buoyancy * (
        along_x(stresses[2], anchor, count_x, count_z)
        + along_z(stresses[1], anchor, count_x, count_z)
    )
    return jnp.stack([updated_x, updated_z])


def velocity_acoustic(velocity, stresses, buoyancy, anchor, count_x, count_z):
    updated_x = velocity[0] - TIME_STEP * buoyancy * along_x(stresses[0], anchor, count_x, count_z)
    updated_z = velocity[1] - TIME_STEP * buoyancy * along_z(stresses[0], anchor, count_x, count_z)
    return jnp.stack([updated_x, updated_z])


def stress_elastic(stresses, velocity_pad, material, anchor, count_x, count_z):
    strain_x = along_x(velocity_pad[0], anchor, count_x, count_z)
    strain_z = along_z(velocity_pad[1], anchor, count_x, count_z)
    strain_shear = along_z(velocity_pad[0], anchor, count_x, count_z) + along_x(
        velocity_pad[1], anchor, count_x, count_z
    )
    lame_first = material[1]
    shear_modulus = material[2]
    normal_x = stresses[0] + TIME_STEP * (
        (lame_first + 2.0 * shear_modulus) * strain_x + lame_first * strain_z
    )
    normal_z = stresses[1] + TIME_STEP * (
        lame_first * strain_x + (lame_first + 2.0 * shear_modulus) * strain_z
    )
    shear_new = stresses[2] + TIME_STEP * shear_modulus * strain_shear
    return jnp.stack([normal_x, normal_z, shear_new])


def stress_acoustic(stresses, velocity_pad, material, anchor, count_x, count_z):
    divergence = along_x(velocity_pad[0], anchor, count_x, count_z) + along_z(
        velocity_pad[1], anchor, count_x, count_z
    )
    loading = material[1] * divergence
    memory_one = (
        RELAXATION[0] * stresses[1]
        + (1.0 - RELAXATION[0]) * MEMORY_WEIGHT[0] * material[2] * loading
    )
    memory_two = (
        RELAXATION[1] * stresses[2]
        + (1.0 - RELAXATION[1]) * MEMORY_WEIGHT[1] * material[2] * loading
    )
    pressure = stresses[0] - TIME_STEP * (loading - memory_one - memory_two)
    return jnp.stack([pressure, memory_one, memory_two])


def local_stepwise(fields, media, plane_rows, box_offset):
    current = fields[0]
    material = media[0]
    count_x = current.shape[1]
    count_z = current.shape[2]
    section = lax.axis_index("sec")
    is_source = section == 0
    block_z = lax.axis_index("gz")
    local_rows = lax.dynamic_slice_in_dim(plane_rows, block_z * NPD, NPD) - block_z * count_z
    offset = lax.dynamic_slice_in_dim(box_offset, jnp.maximum(section - 1, 0), 1)[0]
    depth_ids = block_z * count_z + jnp.arange(count_z, dtype=jnp.int32)
    landing = offset + plane_rows // 2
    chosen = (landing[:, None] == depth_ids[None, :]).astype(jnp.float32)
    for step_index in range(STEPS):
        stress_pad = padded_2(current[2:5], (("gx", 1), ("gz", 2)), RADIUS)
        velocity = lax.cond(
            is_source,
            lambda: velocity_elastic(
                current[0:2], stress_pad, material[0], RADIUS, count_x, count_z
            ),
            lambda: velocity_acoustic(
                current[0:2], stress_pad, material[0], RADIUS, count_x, count_z
            ),
        )
        velocity_pad = padded_2(velocity, (("gx", 1), ("gz", 2)), RADIUS)
        stresses = lax.cond(
            is_source,
            lambda: stress_elastic(current[2:5], velocity_pad, material, RADIUS, count_x, count_z),
            lambda: stress_acoustic(current[2:5], velocity_pad, material, RADIUS, count_x, count_z),
        )
        current = jnp.concatenate([velocity, stresses], axis=0)
        picked = jnp.take(current, local_rows, axis=2)
        block_plane = jnp.transpose(
            jnp.stack([picked[0], picked[1], -0.5 * (picked[2] + picked[3])]), (0, 2, 1)
        )
        joined = lax.all_gather(block_plane, "gz", axis=1, tiled=True)
        gathered = broadcast(joined, "sec", 0)
        injected = jnp.einsum("ckx,kz->cxz", gathered, chosen, precision=lax.Precision.HIGHEST)
        far_state = jnp.concatenate([current[0:3] + COUPLING * injected, current[3:5]], axis=0)
        current = jnp.where(is_source, current, far_state)
    return current[None]


HALO = 2 * RADIUS * STEPS
CELLS = 128
HALF = CELLS // 2
WINDOW = HALF + 2 * HALO
DEPTH = 2 * CELLS
PART = HALF + HALO
NP = 2 * NPD
TRIM = (0, 0, 16, 16, 32)
ROWS = 192
GROUPS = CELLS // NP
SLOT = (
    ((0, 0), (1, 0), (2, 0)),
    ((3, 0), (4, 0), (5, 0)),
    ((6, 0), (7, 0), (6, 96)),
    ((3, 112), (4, 112), (5, 112)),
    ((0, 128), (1, 128), (2, 128)),
)
SCALE = 840.0
TAPS = (672.0, -168.0, 32.0, -3.0)


def banded(shape, lag):
    distance = lax.broadcasted_iota(jnp.int32, shape, 0) - lax.broadcasted_iota(
        jnp.int32, shape, 1
    )
    distance = lag * distance
    values = jnp.zeros(shape, jnp.float32)
    for offset, tap in enumerate(TAPS, 1):
        values = jnp.where(distance == offset, tap, values)
        values = jnp.where(distance == -offset, -tap, values)
    return values.astype(jnp.bfloat16)


def one_hot(row):
    depth = lax.broadcasted_iota(jnp.int32, (DEPTH, CELLS), 0)
    return jnp.where(depth == row, 1.0, 0.0).astype(jnp.bfloat16)


def halves(values):
    high = values.astype(jnp.bfloat16)
    low = (values - high.astype(jnp.float32)).astype(jnp.bfloat16)
    return high, low


def dot(left, right):
    return jnp.dot(left, right, preferred_element_type=jnp.float32)


def diff_x(band_x, parts):
    count = parts[0].shape[0]
    band = band_x[:count, :count]
    return dot(band, parts[0]) + dot(band, parts[1])


def diff_z(band_z, parts):
    return dot(parts[0], band_z) + dot(parts[1], band_z)


def trimmed(arrays, amount):
    if amount == 0:
        return arrays
    return [array[amount:-amount] for array in arrays]


def lanes_of(shape):
    return lax.broadcasted_iota(jnp.int32, shape, 1) // NP


def assemble(window, fields, media, edge, other):
    core = lax.axis_index("gz")

    @pl.when(core == 0)
    def _():
        for index in range(8):
            own = fields[index] if index < 5 else media[index - 5]
            window[index, :HALO, :CELLS] = edge[1, index]
            window[index, :HALO, CELLS:] = edge[0, index]
            window[index, HALO:, :CELLS] = own[:PART]
            window[index, HALO:, CELLS:] = other[index]

    @pl.when(core == 1)
    def _():
        for index in range(8):
            own = fields[index] if index < 5 else media[index - 5]
            window[index, :PART, CELLS:] = own[CELLS - PART :]
            window[index, :PART, :CELLS] = other[index]
            window[index, PART:, CELLS:] = edge[1, index]
            window[index, PART:, :CELLS] = edge[0, index]


def place(state, held, sent):
    start = HALO - TRIM[-1]
    core = lax.axis_index("gz")
    state = [array[start : start + HALF] for array in state]

    @pl.when(core == 0)
    def _():
        for index in range(5):
            held[index, :HALF] = state[index][:, :CELLS]
            sent[index] = state[index][:, CELLS:]

    @pl.when(core == 1)
    def _():
        for index in range(5):
            held[index, HALF:] = state[index][:, CELLS:]
            sent[index] = state[index][:, :CELLS]


def acoustic(state, bands):
    vx, vz, pressure, one, two, light, kappa, loss_one, loss_two = state
    band_x, band_z = bands
    parts = halves(pressure)
    vx = vx - light * diff_x(band_x, parts)
    vz = vz - light * diff_z(band_z, parts)
    load = kappa * (diff_x(band_x, halves(vx)) + diff_z(band_z, halves(vz)))
    one = RELAXATION[0] * one + loss_one * load
    two = RELAXATION[1] * two + loss_two * load
    pressure = pressure - TIME_STEP * (load - one - two)
    return [vx, vz, pressure, one, two, light, kappa, loss_one, loss_two]


def pack_kernel(fields, media, swap):
    core = lax.axis_index("gz")

    @pl.when(core == 0)
    def _():
        swap[:5] = fields[:, CELLS - PART :]
        swap[5:] = media[:, CELLS - PART :]

    @pl.when(core == 1)
    def _():
        swap[:5] = fields[:, :PART]
        swap[5:] = media[:, :PART]


def first_kernel(ids, fields, media, edge, other, held, sent, rows, carry):
    assemble(carry, fields, media, edge, other)
    bands = band_x, band_z = banded((WINDOW, WINDOW), -1), banded((DEPTH, DEPTH), 1)
    section = lax.axis_index("sec")

    @pl.when(section == 0)
    def _():
        pick = one_hot(ids[0:1, :])
        vx, vz, sxx, szz, sxz, light, lame, shear = [carry[index] for index in range(8)]
        light = light * (TIME_STEP / SCALE)
        both = (lame + 2.0 * shear) * (TIME_STEP / SCALE)
        lame = lame * (TIME_STEP / SCALE)
        shear = shear * (TIME_STEP / SCALE)
        at = 0
        for step in range(STEPS):
            cut = TRIM[step] - at
            at = TRIM[step]
            vx, vz, sxx, szz, sxz, light, both, lame, shear = trimmed(
                [vx, vz, sxx, szz, sxz, light, both, lame, shear], cut
            )
            parts_xx, parts_zz, parts_xz = halves(sxx), halves(szz), halves(sxz)
            vx = vx + light * (diff_x(band_x, parts_xx) + diff_z(band_z, parts_xz))
            vz = vz + light * (diff_x(band_x, parts_xz) + diff_z(band_z, parts_zz))
            parts_x, parts_z = halves(vx), halves(vz)
            strain_x, strain_z = diff_x(band_x, parts_x), diff_z(band_z, parts_z)
            sxx = sxx + (both * strain_x + lame * strain_z)
            szz = szz + (lame * strain_x + both * strain_z)
            sxz = sxz + shear * (diff_z(band_z, parts_x) + diff_x(band_x, parts_z))
            low = 2 * RADIUS * (step + 1) - at
            for component, (parts, factor) in enumerate(
                ((parts_x, COUPLING), (parts_z, COUPLING), (halves(sxx + szz), -0.5 * COUPLING))
            ):
                picked = factor * (dot(parts[0], pick) + dot(parts[1], pick))
                picked = picked[low : picked.shape[0] - low]
                group, base = SLOT[step][component]
                spot = pl.ds(base, picked.shape[0])
                rows[spot] = jnp.where(lanes_of(picked.shape) == group, picked, rows[spot])
        place([vx, vz, sxx, szz, sxz], held, sent)

    @pl.when(section > 0)
    def _():
        vx, vz, pressure, one, two, light, kappa, loss = [carry[index] for index in range(8)]
        light = light * (TIME_STEP / SCALE)
        kappa = kappa * (1.0 / SCALE)
        loss_one = loss * ((1.0 - RELAXATION[0]) * MEMORY_WEIGHT[0])
        loss_two = loss * ((1.0 - RELAXATION[1]) * MEMORY_WEIGHT[1])
        state = [vx, vz, pressure, one, two, light, kappa, loss_one, loss_two]
        for index, array in enumerate(acoustic(state, bands)):
            carry[index] = array


def second_kernel(ids, carry, rows, held_in, sent_in, held, sent):
    section = lax.axis_index("sec")

    @pl.when(section == 0)
    def _():
        held[...] = held_in[...]
        sent[...] = sent_in[...]

    @pl.when(section > 0)
    def _():
        bands = banded((WINDOW, WINDOW), -1), banded((DEPTH, DEPTH), 1)
        land = one_hot(ids[1:2, :])
        state = [carry[index] for index in range(9)]
        at = 0
        for step in range(STEPS):
            if step:
                state = trimmed(state, TRIM[step] - at)
                at = TRIM[step]
                state = acoustic(state, bands)
            low = 2 * RADIUS * (step + 1) - at
            high = WINDOW - 2 * at - low
            for component in range(3):
                group, base = SLOT[step][component]
                taken = rows[pl.ds(base, high - low)]
                taken = halves(jnp.where(lanes_of(taken.shape) == group, taken, 0.0))
                added = sum(
                    lax.dot_general(
                        part, land, (((1,), (1,)), ((), ())), preferred_element_type=jnp.float32
                    )
                    for part in taken
                )
                array = state[component]
                state[component] = jnp.concatenate(
                    [array[:low], array[low:high] + added, array[high:]], axis=0
                )
        place(state[:5], held, sent)


def call(kernel, outs, operands, flops):
    vmem = pl.BlockSpec(memory_space=pltpu.VMEM)
    return pl.pallas_call(
        kernel,
        out_shape=[jax.ShapeDtypeStruct(shape, jnp.float32) for shape in outs],
        in_specs=[vmem] * len(operands),
        out_specs=[vmem] * len(outs),
        compiler_params=pltpu.CompilerParams(vmem_limit_bytes=48 * 1024 * 1024),
        cost_estimate=pl.CostEstimate(
            flops=flops, bytes_accessed=2 * 1024 * 1024, transcendentals=0
        ),
    )(*operands)


def local_window(columns, fields, media, plane_rows, box_offset):
    fields, media = fields[0], media[0]
    core = lax.axis_index("gz")
    is_first = core == 0
    turn = [(0, 1), (1, 0)]
    (swap,) = call(pack_kernel, [(8, PART, CELLS)], [fields, media], 1000)
    other = lax.ppermute(swap, "gz", turn)
    own = jnp.concatenate([fields, media], axis=0)
    edge = jnp.where(
        is_first,
        jnp.stack([own[:, :HALO], other[:, :HALO]]),
        jnp.stack([own[:, CELLS - HALO :], other[:, PART - HALO :]]),
    )
    pairs = [(2 * column + 1, 2 * column + 2) for column in range(columns - 1)]
    pairs += [(target, source) for source, target in pairs]
    edge = lax.ppermute(edge, ("gx", "gz"), pairs)
    section = lax.axis_index("sec")
    offset = lax.dynamic_slice_in_dim(box_offset, jnp.maximum(section - 1, 0), 1)
    ids = jnp.tile(jnp.stack([plane_rows, offset + plane_rows // 2]), (1, GROUPS))
    held_shape, sent_shape = (5, CELLS, CELLS), (5, HALF, CELLS)
    held, sent, rows, carry = call(
        first_kernel,
        [held_shape, sent_shape, (ROWS, CELLS), (9, WINDOW, DEPTH)],
        [ids, fields, media, edge, other],
        4_000_000_000,
    )
    arrived = [lax.ppermute(rows, "sec", [(0, target)]) for target in (1, 2, 3)]
    rows = arrived[0] + arrived[1] + arrived[2]
    held, sent = call(
        second_kernel,
        [held_shape, sent_shape],
        [ids, carry, rows, held, sent],
        4_000_000_000,
    )
    swapped = lax.ppermute(sent, "gz", turn)
    return lax.dynamic_update_slice_in_dim(held, swapped, HALF * (1 - core), axis=1)[None]


def solution(mesh):
    in_specs = (P("sec", None, "gx", "gz"), P("sec", None, "gx", "gz"), P(), P())
    out_specs = P("sec", None, "gx", "gz")
    if mesh.shape["gz"] == 2:
        local = functools.partial(local_window, mesh.shape["gx"])
    else:
        local = local_stepwise
    return jax.shard_map(local, mesh=mesh, in_specs=in_specs, out_specs=out_specs, check_vma=False)
```

```python
import functools

import jax
import jax.numpy as jnp
from jax import lax
from jax.experimental import pallas as pl
from jax.experimental.pallas import tpu as pltpu
from jax.sharding import PartitionSpec as P

RADIUS = 4
STEPS = 5
NPD = 8

STENCIL = (0.8, -0.2, 4.0 / 105.0, -1.0 / 280.0)
TIME_STEP = 0.2
COUPLING = 0.5
RELAXATION = (0.9, 0.5)
MEMORY_WEIGHT = (0.15, 0.1)


def padded_2(block, sides, width):
    for axis, dim in sides:
        count = lax.axis_size(axis)
        forward = [(i, i + 1) for i in range(count - 1)]
        backward = [(target, source) for source, target in forward]
        low = lax.ppermute(
            lax.slice_in_dim(block, block.shape[dim] - width, None, axis=dim), axis, forward
        )
        high = lax.ppermute(lax.slice_in_dim(block, 0, width, axis=dim), axis, backward)
        block = jnp.concatenate([low, block, high], axis=dim)
    return block


def broadcast(value, axis, source):
    kept = jnp.where(lax.axis_index(axis) == source, value, 0).astype(value.dtype)
    return lax.psum(kept, axis)


def along_x(padded, anchor, count_x, count_z):
    summed = jnp.zeros(padded.shape[:-2] + (count_x, count_z), jnp.float32)
    for offset, stencil_tap in enumerate(STENCIL, 1):
        forward = padded[
            ..., anchor + offset : anchor + offset + count_x, anchor : anchor + count_z
        ]
        backward = padded[
            ..., anchor - offset : anchor - offset + count_x, anchor : anchor + count_z
        ]
        summed = summed + stencil_tap * (forward - backward)
    return summed


def along_z(padded, anchor, count_x, count_z):
    summed = jnp.zeros(padded.shape[:-2] + (count_x, count_z), jnp.float32)
    for offset, stencil_tap in enumerate(STENCIL, 1):
        forward = padded[
            ..., anchor : anchor + count_x, anchor + offset : anchor + offset + count_z
        ]
        backward = padded[
            ..., anchor : anchor + count_x, anchor - offset : anchor - offset + count_z
        ]
        summed = summed + stencil_tap * (forward - backward)
    return summed


def velocity_elastic(velocity, stresses, buoyancy, anchor, count_x, count_z):
    updated_x = velocity[0] + TIME_STEP * buoyancy * (
        along_x(stresses[0], anchor, count_x, count_z)
        + along_z(stresses[2], anchor, count_x, count_z)
    )
    updated_z = velocity[1] + TIME_STEP * buoyancy * (
        along_x(stresses[2], anchor, count_x, count_z)
        + along_z(stresses[1], anchor, count_x, count_z)
    )
    return jnp.stack([updated_x, updated_z])


def velocity_acoustic(velocity, stresses, buoyancy, anchor, count_x, count_z):
    updated_x = velocity[0] - TIME_STEP * buoyancy * along_x(stresses[0], anchor, count_x, count_z)
    updated_z = velocity[1] - TIME_STEP * buoyancy * along_z(stresses[0], anchor, count_x, count_z)
    return jnp.stack([updated_x, updated_z])


def stress_elastic(stresses, velocity_pad, material, anchor, count_x, count_z):
    strain_x = along_x(velocity_pad[0], anchor, count_x, count_z)
    strain_z = along_z(velocity_pad[1], anchor, count_x, count_z)
    strain_shear = along_z(velocity_pad[0], anchor, count_x, count_z) + along_x(
        velocity_pad[1], anchor, count_x, count_z
    )
    lame_first = material[1]
    shear_modulus = material[2]
    normal_x = stresses[0] + TIME_STEP * (
        (lame_first + 2.0 * shear_modulus) * strain_x + lame_first * strain_z
    )
    normal_z = stresses[1] + TIME_STEP * (
        lame_first * strain_x + (lame_first + 2.0 * shear_modulus) * strain_z
    )
    shear_new = stresses[2] + TIME_STEP * shear_modulus * strain_shear
    return jnp.stack([normal_x, normal_z, shear_new])


def stress_acoustic(stresses, velocity_pad, material, anchor, count_x, count_z):
    divergence = along_x(velocity_pad[0], anchor, count_x, count_z) + along_z(
        velocity_pad[1], anchor, count_x, count_z
    )
    loading = material[1] * divergence
    memory_one = (
        RELAXATION[0] * stresses[1]
        + (1.0 - RELAXATION[0]) * MEMORY_WEIGHT[0] * material[2] * loading
    )
    memory_two = (
        RELAXATION[1] * stresses[2]
        + (1.0 - RELAXATION[1]) * MEMORY_WEIGHT[1] * material[2] * loading
    )
    pressure = stresses[0] - TIME_STEP * (loading - memory_one - memory_two)
    return jnp.stack([pressure, memory_one, memory_two])


def local_stepwise(fields, media, plane_rows, box_offset):
    current = fields[0]
    material = media[0]
    count_x = current.shape[1]
    count_z = current.shape[2]
    section = lax.axis_index("sec")
    is_source = section == 0
    block_z = lax.axis_index("gz")
    local_rows = lax.dynamic_slice_in_dim(plane_rows, block_z * NPD, NPD) - block_z * count_z
    offset = lax.dynamic_slice_in_dim(box_offset, jnp.maximum(section - 1, 0), 1)[0]
    depth_ids = block_z * count_z + jnp.arange(count_z, dtype=jnp.int32)
    landing = offset + plane_rows // 2
    chosen = (landing[:, None] == depth_ids[None, :]).astype(jnp.float32)
    for step_index in range(STEPS):
        stress_pad = padded_2(current[2:5], (("gx", 1), ("gz", 2)), RADIUS)
        velocity = lax.cond(
            is_source,
            lambda: velocity_elastic(
                current[0:2], stress_pad, material[0], RADIUS, count_x, count_z
            ),
            lambda: velocity_acoustic(
                current[0:2], stress_pad, material[0], RADIUS, count_x, count_z
            ),
        )
        velocity_pad = padded_2(velocity, (("gx", 1), ("gz", 2)), RADIUS)
        stresses = lax.cond(
            is_source,
            lambda: stress_elastic(current[2:5], velocity_pad, material, RADIUS, count_x, count_z),
            lambda: stress_acoustic(current[2:5], velocity_pad, material, RADIUS, count_x, count_z),
        )
        current = jnp.concatenate([velocity, stresses], axis=0)
        picked = jnp.take(current, local_rows, axis=2)
        block_plane = jnp.transpose(
            jnp.stack([picked[0], picked[1], -0.5 * (picked[2] + picked[3])]), (0, 2, 1)
        )
        joined = lax.all_gather(block_plane, "gz", axis=1, tiled=True)
        gathered = broadcast(joined, "sec", 0)
        injected = jnp.einsum("ckx,kz->cxz", gathered, chosen, precision=lax.Precision.HIGHEST)
        far_state = jnp.concatenate([current[0:3] + COUPLING * injected, current[3:5]], axis=0)
        current = jnp.where(is_source, current, far_state)
    return current[None]


HALO = 2 * RADIUS * STEPS
CELLS = 128
HALF = CELLS // 2
WINDOW = HALF + 2 * HALO
DEPTH = 2 * CELLS
PART = HALF + HALO
NP = 2 * NPD
TRIM = (0, 0, 16, 16, 32)
ROWS = 192
GROUPS = CELLS // NP
SLOT = (
    ((0, 0), (1, 0), (2, 0)),
    ((3, 0), (4, 0), (5, 0)),
    ((6, 0), (7, 0), (6, 96)),
    ((3, 112), (4, 112), (5, 112)),
    ((0, 128), (1, 128), (2, 128)),
)
SCALE = 840.0
TAPS = (672.0, -168.0, 32.0, -3.0)


def banded(shape, lag):
    distance = lax.broadcasted_iota(jnp.int32, shape, 0) - lax.broadcasted_iota(
        jnp.int32, shape, 1
    )
    distance = lag * distance
    values = jnp.zeros(shape, jnp.float32)
    for offset, tap in enumerate(TAPS, 1):
        values = jnp.where(distance == offset, tap, values)
        values = jnp.where(distance == -offset, -tap, values)
    return values.astype(jnp.bfloat16)


def one_hot(row):
    depth = lax.broadcasted_iota(jnp.int32, (DEPTH, CELLS), 0)
    return jnp.where(depth == row, 1.0, 0.0).astype(jnp.bfloat16)


def halves(values):
    high = values.astype(jnp.bfloat16)
    low = (values - high.astype(jnp.float32)).astype(jnp.bfloat16)
    return high, low


def dot(left, right):
    return jnp.dot(left, right, preferred_element_type=jnp.float32)


def diff_x(band_x, parts):
    count = parts[0].shape[0]
    band = band_x[:count, :count]
    return dot(band, parts[0]) + dot(band, parts[1])


def diff_z(band_z, parts):
    return dot(parts[0], band_z) + dot(parts[1], band_z)


def trimmed(arrays, amount):
    if amount == 0:
        return arrays
    return [array[amount:-amount] for array in arrays]


def lanes_of(shape):
    return lax.broadcasted_iota(jnp.int32, shape, 1) // NP


def assemble(window, fields, media, ahead, behind, other):
    core = lax.axis_index("gz")

    @pl.when(core == 0)
    def _():
        for index in range(8):
            own = fields[index] if index < 5 else media[index - 5]
            window[index, :HALO, :CELLS] = ahead[index]
            window[index, :HALO, CELLS:] = behind[index]
            window[index, HALO:, :CELLS] = own[:PART]
            window[index, HALO:, CELLS:] = other[index]

    @pl.when(core == 1)
    def _():
        for index in range(8):
            own = fields[index] if index < 5 else media[index - 5]
            window[index, :PART, CELLS:] = own[CELLS - PART :]
            window[index, :PART, :CELLS] = other[index]
            window[index, PART:, CELLS:] = ahead[index]
            window[index, PART:, :CELLS] = behind[index]


def place(state, held, sent):
    start = HALO - TRIM[-1]
    core = lax.axis_index("gz")
    state = [array[start : start + HALF] for array in state]

    @pl.when(core == 0)
    def _():
        for index in range(5):
            held[index, :HALF] = state[index][:, :CELLS]
            sent[index] = state[index][:, CELLS:]

    @pl.when(core == 1)
    def _():
        for index in range(5):
            held[index, HALF:] = state[index][:, CELLS:]
            sent[index] = state[index][:, :CELLS]


def acoustic(state, bands):
    vx, vz, pressure, one, two, light, kappa, loss_one, loss_two = state
    band_x, band_z = bands
    parts = halves(pressure)
    vx = vx - light * diff_x(band_x, parts)
    vz = vz - light * diff_z(band_z, parts)
    load = kappa * (diff_x(band_x, halves(vx)) + diff_z(band_z, halves(vz)))
    one = RELAXATION[0] * one + loss_one * load
    two = RELAXATION[1] * two + loss_two * load
    pressure = pressure - TIME_STEP * (load - one - two)
    return [vx, vz, pressure, one, two, light, kappa, loss_one, loss_two]


def pack_kernel(fields, media, straight, crossed, swap, sems):
    core = lax.axis_index("gz")
    bottom = CELLS - HALO
    copies = []
    for target, start, count in (
        (straight, bottom * (1 - core), HALO),
        (crossed, bottom * core, HALO),
        (swap, (CELLS - PART) * (1 - core), PART),
    ):
        span = pl.ds(pl.multiple_of(start, 8), count)
        for source, low, high in ((fields, 0, 5), (media, 5, 8)):
            copies.append(
                pltpu.make_async_copy(
                    source.at[:, span], target.at[low:high], sems.at[len(copies)]
                )
            )
    for copy in copies:
        copy.start()
    for copy in copies:
        copy.wait()


def first_kernel(ids, fields, media, ahead, behind, other, held, sent, rows, carry):
    assemble(carry, fields, media, ahead, behind, other)
    bands = band_x, band_z = banded((WINDOW, WINDOW), -1), banded((DEPTH, DEPTH), 1)
    section = lax.axis_index("sec")

    @pl.when(section == 0)
    def _():
        pick = one_hot(ids[0:1, :])
        vx, vz, sxx, szz, sxz, light, lame, shear = [carry[index] for index in range(8)]
        light = light * (TIME_STEP / SCALE)
        both = (lame + 2.0 * shear) * (TIME_STEP / SCALE)
        lame = lame * (TIME_STEP / SCALE)
        shear = shear * (TIME_STEP / SCALE)
        at = 0
        for step in range(STEPS):
            cut = TRIM[step] - at
            at = TRIM[step]
            vx, vz, sxx, szz, sxz, light, both, lame, shear = trimmed(
                [vx, vz, sxx, szz, sxz, light, both, lame, shear], cut
            )
            parts_xx, parts_zz, parts_xz = halves(sxx), halves(szz), halves(sxz)
            vx = vx + light * (diff_x(band_x, parts_xx) + diff_z(band_z, parts_xz))
            vz = vz + light * (diff_x(band_x, parts_xz) + diff_z(band_z, parts_zz))
            parts_x, parts_z = halves(vx), halves(vz)
            strain_x, strain_z = diff_x(band_x, parts_x), diff_z(band_z, parts_z)
            sxx = sxx + (both * strain_x + lame * strain_z)
            szz = szz + (lame * strain_x + both * strain_z)
            sxz = sxz + shear * (diff_z(band_z, parts_x) + diff_x(band_x, parts_z))
            low = 2 * RADIUS * (step + 1) - at
            for component, (parts, factor) in enumerate(
                ((parts_x, COUPLING), (parts_z, COUPLING), (halves(sxx + szz), -0.5 * COUPLING))
            ):
                picked = factor * (dot(parts[0], pick) + dot(parts[1], pick))
                picked = picked[low : picked.shape[0] - low]
                group, base = SLOT[step][component]
                spot = pl.ds(base, picked.shape[0])
                kept = rows[0, spot]
                rows[0, spot] = jnp.where(lanes_of(picked.shape) == group, picked, kept)
        for target in range(1, 4):
            rows[target] = rows[0]
        place([vx, vz, sxx, szz, sxz], held, sent)

    @pl.when(section > 0)
    def _():
        vx, vz, pressure, one, two, light, kappa, loss = [carry[index] for index in range(8)]
        light = light * (TIME_STEP / SCALE)
        kappa = kappa * (1.0 / SCALE)
        loss_one = loss * ((1.0 - RELAXATION[0]) * MEMORY_WEIGHT[0])
        loss_two = loss * ((1.0 - RELAXATION[1]) * MEMORY_WEIGHT[1])
        state = [vx, vz, pressure, one, two, light, kappa, loss_one, loss_two]
        for index, array in enumerate(acoustic(state, bands)):
            carry[index] = array


def second_kernel(ids, carry, rows, held_in, sent_in, held, sent):
    section = lax.axis_index("sec")

    @pl.when(section == 0)
    def _():
        held[...] = held_in[...]
        sent[...] = sent_in[...]

    @pl.when(section > 0)
    def _():
        bands = banded((WINDOW, WINDOW), -1), banded((DEPTH, DEPTH), 1)
        land = one_hot(ids[1:2, :])
        state = [carry[index] for index in range(9)]
        at = 0
        for step in range(STEPS):
            if step:
                state = trimmed(state, TRIM[step] - at)
                at = TRIM[step]
                state = acoustic(state, bands)
            low = 2 * RADIUS * (step + 1) - at
            high = WINDOW - 2 * at - low
            for component in range(3):
                group, base = SLOT[step][component]
                taken = rows[0, pl.ds(base, high - low)]
                taken = halves(jnp.where(lanes_of(taken.shape) == group, taken, 0.0))
                added = sum(
                    lax.dot_general(
                        part, land, (((1,), (1,)), ((), ())), preferred_element_type=jnp.float32
                    )
                    for part in taken
                )
                array = state[component]
                state[component] = jnp.concatenate(
                    [array[:low], array[low:high] + added, array[high:]], axis=0
                )
        place(state[:5], held, sent)


def call(kernel, outs, operands, flops, place_in=pltpu.VMEM, scratch=()):
    return pl.pallas_call(
        kernel,
        out_shape=[jax.ShapeDtypeStruct(shape, jnp.float32) for shape in outs],
        in_specs=[pl.BlockSpec(memory_space=place_in)] * len(operands),
        out_specs=[pl.BlockSpec(memory_space=pltpu.VMEM)] * len(outs),
        scratch_shapes=scratch,
        compiler_params=pltpu.CompilerParams(vmem_limit_bytes=48 * 1024 * 1024),
        cost_estimate=pl.CostEstimate(
            flops=flops, bytes_accessed=2 * 1024 * 1024, transcendentals=0
        ),
    )(*operands)


def local_window(columns, fields, media, plane_rows, box_offset):
    fields, media = fields[0], media[0]
    core = lax.axis_index("gz")
    straight, crossed, swap = call(
        pack_kernel,
        [(8, HALO, CELLS), (8, HALO, CELLS), (8, PART, CELLS)],
        [fields, media],
        1000,
        pltpu.HBM,
        [pltpu.SemaphoreType.DMA((6,))],
    )
    straight_pairs, crossed_pairs = [], []
    for column in range(columns):
        if column + 1 < columns:
            straight_pairs.append((2 * column, 2 * column + 2))
            crossed_pairs.append((2 * column + 1, 2 * column + 2))
        if column:
            straight_pairs.append((2 * column + 1, 2 * column - 1))
            crossed_pairs.append((2 * column, 2 * column - 1))
    turn = [(0, 1), (1, 0)]
    ahead = lax.ppermute(straight, ("gx", "gz"), straight_pairs)
    behind = lax.ppermute(crossed, ("gx", "gz"), crossed_pairs)
    other = lax.ppermute(swap, "gz", turn)
    section = lax.axis_index("sec")
    offset = jnp.where(section < 2, box_offset[0], box_offset[1])
    offset = jnp.where(section < 3, offset, box_offset[2])
    ids = jnp.tile(jnp.stack([plane_rows, offset + plane_rows // 2]), (1, GROUPS))
    held_shape, sent_shape = (5, CELLS, CELLS), (5, HALF, CELLS)
    held, sent, rows, carry = call(
        first_kernel,
        [held_shape, sent_shape, (4, ROWS, CELLS), (9, WINDOW, DEPTH)],
        [ids, fields, media, ahead, behind, other],
        4_000_000_000,
    )
    rows = lax.all_to_all(rows, "sec", 0, 0)
    held, sent = call(
        second_kernel,
        [held_shape, sent_shape],
        [ids, carry, rows, held, sent],
        4_000_000_000,
    )
    swapped = lax.ppermute(sent, "gz", turn)
    return lax.dynamic_update_slice_in_dim(held, swapped, HALF * (1 - core), axis=1)[None]


def solution(mesh):
    in_specs = (P("sec", None, "gx", "gz"), P("sec", None, "gx", "gz"), P(), P())
    out_specs = P("sec", None, "gx", "gz")
    if mesh.shape["gz"] == 2:
        local = functools.partial(local_window, mesh.shape["gx"])
    else:
        local = local_stepwise
    return jax.shard_map(local, mesh=mesh, in_specs=in_specs, out_specs=out_specs, check_vma=False)
```

```python
import functools

import jax
import jax.numpy as jnp
from jax import lax
from jax.experimental import pallas as pl
from jax.experimental.pallas import tpu as pltpu
from jax.sharding import PartitionSpec as P

RADIUS = 4
STEPS = 5
NPD = 8

STENCIL = (0.8, -0.2, 4.0 / 105.0, -1.0 / 280.0)
TIME_STEP = 0.2
COUPLING = 0.5
RELAXATION = (0.9, 0.5)
MEMORY_WEIGHT = (0.15, 0.1)


def padded_2(block, sides, width):
    for axis, dim in sides:
        count = lax.axis_size(axis)
        forward = [(i, i + 1) for i in range(count - 1)]
        backward = [(target, source) for source, target in forward]
        low = lax.ppermute(
            lax.slice_in_dim(block, block.shape[dim] - width, None, axis=dim), axis, forward
        )
        high = lax.ppermute(lax.slice_in_dim(block, 0, width, axis=dim), axis, backward)
        block = jnp.concatenate([low, block, high], axis=dim)
    return block


def broadcast(value, axis, source):
    kept = jnp.where(lax.axis_index(axis) == source, value, 0).astype(value.dtype)
    return lax.psum(kept, axis)


def along_x(padded, anchor, count_x, count_z):
    summed = jnp.zeros(padded.shape[:-2] + (count_x, count_z), jnp.float32)
    for offset, stencil_tap in enumerate(STENCIL, 1):
        forward = padded[
            ..., anchor + offset : anchor + offset + count_x, anchor : anchor + count_z
        ]
        backward = padded[
            ..., anchor - offset : anchor - offset + count_x, anchor : anchor + count_z
        ]
        summed = summed + stencil_tap * (forward - backward)
    return summed


def along_z(padded, anchor, count_x, count_z):
    summed = jnp.zeros(padded.shape[:-2] + (count_x, count_z), jnp.float32)
    for offset, stencil_tap in enumerate(STENCIL, 1):
        forward = padded[
            ..., anchor : anchor + count_x, anchor + offset : anchor + offset + count_z
        ]
        backward = padded[
            ..., anchor : anchor + count_x, anchor - offset : anchor - offset + count_z
        ]
        summed = summed + stencil_tap * (forward - backward)
    return summed


def velocity_elastic(velocity, stresses, buoyancy, anchor, count_x, count_z):
    updated_x = velocity[0] + TIME_STEP * buoyancy * (
        along_x(stresses[0], anchor, count_x, count_z)
        + along_z(stresses[2], anchor, count_x, count_z)
    )
    updated_z = velocity[1] + TIME_STEP * buoyancy * (
        along_x(stresses[2], anchor, count_x, count_z)
        + along_z(stresses[1], anchor, count_x, count_z)
    )
    return jnp.stack([updated_x, updated_z])


def velocity_acoustic(velocity, stresses, buoyancy, anchor, count_x, count_z):
    updated_x = velocity[0] - TIME_STEP * buoyancy * along_x(stresses[0], anchor, count_x, count_z)
    updated_z = velocity[1] - TIME_STEP * buoyancy * along_z(stresses[0], anchor, count_x, count_z)
    return jnp.stack([updated_x, updated_z])


def stress_elastic(stresses, velocity_pad, material, anchor, count_x, count_z):
    strain_x = along_x(velocity_pad[0], anchor, count_x, count_z)
    strain_z = along_z(velocity_pad[1], anchor, count_x, count_z)
    strain_shear = along_z(velocity_pad[0], anchor, count_x, count_z) + along_x(
        velocity_pad[1], anchor, count_x, count_z
    )
    lame_first = material[1]
    shear_modulus = material[2]
    normal_x = stresses[0] + TIME_STEP * (
        (lame_first + 2.0 * shear_modulus) * strain_x + lame_first * strain_z
    )
    normal_z = stresses[1] + TIME_STEP * (
        lame_first * strain_x + (lame_first + 2.0 * shear_modulus) * strain_z
    )
    shear_new = stresses[2] + TIME_STEP * shear_modulus * strain_shear
    return jnp.stack([normal_x, normal_z, shear_new])


def stress_acoustic(stresses, velocity_pad, material, anchor, count_x, count_z):
    divergence = along_x(velocity_pad[0], anchor, count_x, count_z) + along_z(
        velocity_pad[1], anchor, count_x, count_z
    )
    loading = material[1] * divergence
    memory_one = (
        RELAXATION[0] * stresses[1]
        + (1.0 - RELAXATION[0]) * MEMORY_WEIGHT[0] * material[2] * loading
    )
    memory_two = (
        RELAXATION[1] * stresses[2]
        + (1.0 - RELAXATION[1]) * MEMORY_WEIGHT[1] * material[2] * loading
    )
    pressure = stresses[0] - TIME_STEP * (loading - memory_one - memory_two)
    return jnp.stack([pressure, memory_one, memory_two])


def local_stepwise(fields, media, plane_rows, box_offset):
    current = fields[0]
    material = media[0]
    count_x = current.shape[1]
    count_z = current.shape[2]
    section = lax.axis_index("sec")
    is_source = section == 0
    block_z = lax.axis_index("gz")
    local_rows = lax.dynamic_slice_in_dim(plane_rows, block_z * NPD, NPD) - block_z * count_z
    offset = lax.dynamic_slice_in_dim(box_offset, jnp.maximum(section - 1, 0), 1)[0]
    depth_ids = block_z * count_z + jnp.arange(count_z, dtype=jnp.int32)
    landing = offset + plane_rows // 2
    chosen = (landing[:, None] == depth_ids[None, :]).astype(jnp.float32)
    for step_index in range(STEPS):
        stress_pad = padded_2(current[2:5], (("gx", 1), ("gz", 2)), RADIUS)
        velocity = lax.cond(
            is_source,
            lambda: velocity_elastic(
                current[0:2], stress_pad, material[0], RADIUS, count_x, count_z
            ),
            lambda: velocity_acoustic(
                current[0:2], stress_pad, material[0], RADIUS, count_x, count_z
            ),
        )
        velocity_pad = padded_2(velocity, (("gx", 1), ("gz", 2)), RADIUS)
        stresses = lax.cond(
            is_source,
            lambda: stress_elastic(current[2:5], velocity_pad, material, RADIUS, count_x, count_z),
            lambda: stress_acoustic(current[2:5], velocity_pad, material, RADIUS, count_x, count_z),
        )
        current = jnp.concatenate([velocity, stresses], axis=0)
        picked = jnp.take(current, local_rows, axis=2)
        block_plane = jnp.transpose(
            jnp.stack([picked[0], picked[1], -0.5 * (picked[2] + picked[3])]), (0, 2, 1)
        )
        joined = lax.all_gather(block_plane, "gz", axis=1, tiled=True)
        gathered = broadcast(joined, "sec", 0)
        injected = jnp.einsum("ckx,kz->cxz", gathered, chosen, precision=lax.Precision.HIGHEST)
        far_state = jnp.concatenate([current[0:3] + COUPLING * injected, current[3:5]], axis=0)
        current = jnp.where(is_source, current, far_state)
    return current[None]


HALO = 2 * RADIUS * STEPS
CELLS = 128
HALF = CELLS // 2
WINDOW = HALF + 2 * HALO
DEPTH = 2 * CELLS
PART = HALF + HALO
NP = 2 * NPD
TRIM = (0, 0, 16, 16, 32)
ROWS = 192
GROUPS = CELLS // NP
SLOT = (
    ((0, 0), (1, 0), (2, 0)),
    ((3, 0), (4, 0), (5, 0)),
    ((6, 0), (7, 0), (6, 96)),
    ((3, 112), (4, 112), (5, 112)),
    ((0, 128), (1, 128), (2, 128)),
)
SCALE = 840.0
TAPS = (672.0, -168.0, 32.0, -3.0)


def banded(shape, lag):
    distance = lax.broadcasted_iota(jnp.int32, shape, 0) - lax.broadcasted_iota(
        jnp.int32, shape, 1
    )
    distance = lag * distance
    values = jnp.zeros(shape, jnp.float32)
    for offset, tap in enumerate(TAPS, 1):
        values = jnp.where(distance == offset, tap, values)
        values = jnp.where(distance == -offset, -tap, values)
    return values.astype(jnp.bfloat16)


def halves(values):
    high = values.astype(jnp.bfloat16)
    low = (values - high.astype(jnp.float32)).astype(jnp.bfloat16)
    return high, low


def dot(left, right):
    return jnp.dot(left, right, preferred_element_type=jnp.float32)


def diff_x(band_x, parts):
    count = parts[0].shape[0]
    band = band_x[:count, :count]
    return dot(band, parts[0]) + dot(band, parts[1])


def diff_z(band_z, parts):
    return dot(parts[0], band_z[...]) + dot(parts[1], band_z[...])


def trimmed(arrays, amount):
    if amount == 0:
        return arrays
    return [array[amount:-amount] for array in arrays]


def lanes_of(shape):
    return lax.broadcasted_iota(jnp.int32, shape, 1) // NP


def assemble(window, fields, media, ahead, behind, other):
    core = lax.axis_index("gz")

    @pl.when(core == 0)
    def _():
        for index in range(8):
            own = fields[index] if index < 5 else media[index - 5]
            window[index, :HALO, :CELLS] = ahead[index]
            window[index, :HALO, CELLS:] = behind[index]
            window[index, HALO:, :CELLS] = own[:PART]
            window[index, HALO:, CELLS:] = other[index]

    @pl.when(core == 1)
    def _():
        for index in range(8):
            own = fields[index] if index < 5 else media[index - 5]
            window[index, :PART, CELLS:] = own[CELLS - PART :]
            window[index, :PART, :CELLS] = other[index]
            window[index, PART:, CELLS:] = ahead[index]
            window[index, PART:, :CELLS] = behind[index]


def place(state, held, sent):
    start = HALO - TRIM[-1]
    core = lax.axis_index("gz")
    state = [array[start : start + HALF] for array in state]

    @pl.when(core == 0)
    def _():
        for index in range(5):
            held[index] = state[index][:, :CELLS]
            sent[index] = state[index][:, CELLS:]

    @pl.when(core == 1)
    def _():
        for index in range(5):
            held[index] = state[index][:, CELLS:]
            sent[index] = state[index][:, :CELLS]


def acoustic(state, bands):
    vx, vz, pressure, one, two, light, kappa, loss_one, loss_two = state
    band_x, band_z = bands
    parts = halves(pressure)
    vx = vx - light * diff_x(band_x, parts)
    vz = vz - light * diff_z(band_z, parts)
    load = kappa * (diff_x(band_x, halves(vx)) + diff_z(band_z, halves(vz)))
    one = RELAXATION[0] * one + loss_one * load
    two = RELAXATION[1] * two + loss_two * load
    pressure = pressure - TIME_STEP * (load - one - two)
    return [vx, vz, pressure, one, two, light, kappa, loss_one, loss_two]


def constants_kernel(plane_rows, box_offset, band_x, band_z, pick, land):
    band_x[...] = banded((WINDOW, WINDOW), -1)
    band_z[...] = banded((DEPTH, DEPTH), 1)
    row = plane_rows[...]
    lane = lax.broadcasted_iota(jnp.int32, box_offset.shape, 1)
    offset = jnp.where(lane == lax.axis_index("sec") - 1, box_offset[...], 0)
    landing = row // 2 + jnp.sum(offset, axis=1, keepdims=True)
    depth = lax.broadcasted_iota(jnp.int32, (DEPTH, NP), 0)
    spread = lax.broadcasted_iota(jnp.int32, (NP, CELLS), 1) % NP
    spread = spread == lax.broadcasted_iota(jnp.int32, (NP, CELLS), 0)
    spread = jnp.where(spread, 1.0, 0.0).astype(jnp.bfloat16)
    for target, where in ((pick, row), (land, landing)):
        hot = jnp.where(depth == where, 1.0, 0.0).astype(jnp.bfloat16)
        target[...] = dot(hot, spread).astype(jnp.bfloat16)


def first_kernel(
    band_x, band_z, pick, fields, media, ahead, behind, other, held, sent, rows, carry
):
    assemble(carry, fields, media, ahead, behind, other)
    section = lax.axis_index("sec")

    @pl.when(section == 0)
    def _():
        vx, vz, sxx, szz, sxz, light, lame, shear = [carry[index] for index in range(8)]
        light = light * (TIME_STEP / SCALE)
        both = (lame + 2.0 * shear) * (TIME_STEP / SCALE)
        lame = lame * (TIME_STEP / SCALE)
        shear = shear * (TIME_STEP / SCALE)
        at = 0
        for step in range(STEPS):
            cut = TRIM[step] - at
            at = TRIM[step]
            vx, vz, sxx, szz, sxz, light, both, lame, shear = trimmed(
                [vx, vz, sxx, szz, sxz, light, both, lame, shear], cut
            )
            parts_xx, parts_zz, parts_xz = halves(sxx), halves(szz), halves(sxz)
            vx = vx + light * (diff_x(band_x, parts_xx) + diff_z(band_z, parts_xz))
            vz = vz + light * (diff_x(band_x, parts_xz) + diff_z(band_z, parts_zz))
            parts_x, parts_z = halves(vx), halves(vz)
            strain_x, strain_z = diff_x(band_x, parts_x), diff_z(band_z, parts_z)
            sxx = sxx + (both * strain_x + lame * strain_z)
            szz = szz + (lame * strain_x + both * strain_z)
            sxz = sxz + shear * (diff_z(band_z, parts_x) + diff_x(band_x, parts_z))
            low = 2 * RADIUS * (step + 1) - at
            for component, (parts, factor) in enumerate(
                ((parts_x, COUPLING), (parts_z, COUPLING), (halves(sxx + szz), -0.5 * COUPLING))
            ):
                picked = factor * (dot(parts[0], pick[...]) + dot(parts[1], pick[...]))
                picked = picked[low : picked.shape[0] - low]
                group, base = SLOT[step][component]
                spot = pl.ds(base, picked.shape[0])
                rows[spot] = jnp.where(lanes_of(picked.shape) == group, picked, rows[spot])
        place([vx, vz, sxx, szz, sxz], held, sent)

    @pl.when(section > 0)
    def _():
        vx, vz, pressure, one, two, light, kappa, loss = [carry[index] for index in range(8)]
        light = light * (TIME_STEP / SCALE)
        kappa = kappa * (1.0 / SCALE)
        loss_one = loss * ((1.0 - RELAXATION[0]) * MEMORY_WEIGHT[0])
        loss_two = loss * ((1.0 - RELAXATION[1]) * MEMORY_WEIGHT[1])
        state = [vx, vz, pressure, one, two, light, kappa, loss_one, loss_two]
        for index, array in enumerate(acoustic(state, (band_x, band_z))):
            carry[index] = array


def second_kernel(band_x, band_z, land, carry, rows, held_in, sent_in, held, sent):
    section = lax.axis_index("sec")

    @pl.when(section == 0)
    def _():
        held[...] = held_in[...]
        sent[...] = sent_in[...]

    @pl.when(section > 0)
    def _():
        state = [carry[index] for index in range(9)]
        at = 0
        for step in range(STEPS):
            if step:
                state = trimmed(state, TRIM[step] - at)
                at = TRIM[step]
                state = acoustic(state, (band_x, band_z))
            low = 2 * RADIUS * (step + 1) - at
            high = WINDOW - 2 * at - low
            for component in range(3):
                group, base = SLOT[step][component]
                taken = rows[pl.ds(base, high - low)]
                taken = halves(jnp.where(lanes_of(taken.shape) == group, taken, 0.0))
                added = sum(
                    lax.dot_general(
                        part, land[...], (((1,), (1,)), ((), ())), preferred_element_type=jnp.float32
                    )
                    for part in taken
                )
                array = state[component]
                state[component] = jnp.concatenate(
                    [array[:low], array[low:high] + added, array[high:]], axis=0
                )
        place(state[:5], held, sent)


def last_kernel(held, swapped, out, sems):
    core = lax.axis_index("gz")
    copies = [
        pltpu.make_async_copy(
            source, out.at[:, pl.ds(pl.multiple_of(HALF * half, HALF), HALF)], sems.at[index]
        )
        for index, (source, half) in enumerate(((held, core), (swapped, 1 - core)))
    ]
    for copy in copies:
        copy.start()
    for copy in copies:
        copy.wait()


def call(kernel, outs, operands, flops, place_out=pltpu.VMEM, scratch=()):
    return pl.pallas_call(
        kernel,
        out_shape=outs,
        in_specs=[pl.BlockSpec(memory_space=pltpu.VMEM)] * len(operands),
        out_specs=[pl.BlockSpec(memory_space=place_out)] * len(outs),
        scratch_shapes=scratch,
        compiler_params=pltpu.CompilerParams(vmem_limit_bytes=48 * 1024 * 1024),
        cost_estimate=pl.CostEstimate(
            flops=flops, bytes_accessed=2 * 1024 * 1024, transcendentals=0
        ),
    )(*operands)


def full(*shape):
    return jax.ShapeDtypeStruct(shape, jnp.float32)


def narrow(*shape):
    return jax.ShapeDtypeStruct(shape, jnp.bfloat16)


def local_window(columns, fields, media, plane_rows, box_offset):
    fields, media = fields[0], media[0]
    core = lax.axis_index("gz")
    is_first = core == 0
    both = jnp.concatenate([fields, media], axis=0)
    top, bottom = both[:, :HALO], both[:, CELLS - HALO :]
    straight, crossed = [], []
    for column in range(columns):
        if column + 1 < columns:
            straight.append((2 * column, 2 * column + 2))
            crossed.append((2 * column + 1, 2 * column + 2))
        if column:
            straight.append((2 * column + 1, 2 * column - 1))
            crossed.append((2 * column, 2 * column - 1))
    turn = [(0, 1), (1, 0)]
    ahead = lax.ppermute(jnp.where(is_first, bottom, top), ("gx", "gz"), straight)
    behind = lax.ppermute(jnp.where(is_first, top, bottom), ("gx", "gz"), crossed)
    other = jnp.where(is_first, both[:, CELLS - PART :], both[:, :PART])
    other = lax.ppermute(other, "gz", turn)
    band_x, band_z, pick, land = call(
        constants_kernel,
        [narrow(WINDOW, WINDOW), narrow(DEPTH, DEPTH), narrow(DEPTH, CELLS), narrow(DEPTH, CELLS)],
        [plane_rows[None], box_offset[None]],
        1_000_000_000,
    )
    held, sent, rows, carry = call(
        first_kernel,
        [
            full(5, HALF, CELLS),
            full(5, HALF, CELLS),
            full(ROWS, CELLS),
            full(9, WINDOW, DEPTH),
        ],
        [band_x, band_z, pick, fields, media, ahead, behind, other],
        4_000_000_000,
    )
    arrived = [lax.ppermute(rows, "sec", [(0, target)]) for target in (1, 2, 3)]
    rows = arrived[0] + arrived[1] + arrived[2]
    held, sent = call(
        second_kernel,
        [full(5, HALF, CELLS), full(5, HALF, CELLS)],
        [band_x, band_z, land, carry, rows, held, sent],
        4_000_000_000,
    )
    swapped = lax.ppermute(sent, "gz", turn)
    (out,) = call(
        last_kernel,
        [full(5, CELLS, CELLS)],
        [held, swapped],
        1000,
        pl.ANY,
        [pltpu.SemaphoreType.DMA((2,))],
    )
    return out[None]


def solution(mesh):
    in_specs = (P("sec", None, "gx", "gz"), P("sec", None, "gx", "gz"), P(), P())
    out_specs = P("sec", None, "gx", "gz")
    if mesh.shape["gz"] == 2:
        local = functools.partial(local_window, mesh.shape["gx"])
    else:
        local = local_stepwise
    return jax.shard_map(local, mesh=mesh, in_specs=in_specs, out_specs=out_specs, check_vma=False)
```

```python
import functools

import jax
import jax.numpy as jnp
from jax import lax
from jax.experimental import pallas as pl
from jax.experimental.pallas import tpu as pltpu
from jax.sharding import PartitionSpec as P

RADIUS = 4
STEPS = 5
NPD = 8

STENCIL = (0.8, -0.2, 4.0 / 105.0, -1.0 / 280.0)
TIME_STEP = 0.2
COUPLING = 0.5
RELAXATION = (0.9, 0.5)
MEMORY_WEIGHT = (0.15, 0.1)


def padded_2(block, sides, width):
    for axis, dim in sides:
        count = lax.axis_size(axis)
        forward = [(i, i + 1) for i in range(count - 1)]
        backward = [(target, source) for source, target in forward]
        low = lax.ppermute(
            lax.slice_in_dim(block, block.shape[dim] - width, None, axis=dim), axis, forward
        )
        high = lax.ppermute(lax.slice_in_dim(block, 0, width, axis=dim), axis, backward)
        block = jnp.concatenate([low, block, high], axis=dim)
    return block


def broadcast(value, axis, source):
    kept = jnp.where(lax.axis_index(axis) == source, value, 0).astype(value.dtype)
    return lax.psum(kept, axis)


def along_x(padded, anchor, count_x, count_z):
    summed = jnp.zeros(padded.shape[:-2] + (count_x, count_z), jnp.float32)
    for offset, stencil_tap in enumerate(STENCIL, 1):
        forward = padded[
            ..., anchor + offset : anchor + offset + count_x, anchor : anchor + count_z
        ]
        backward = padded[
            ..., anchor - offset : anchor - offset + count_x, anchor : anchor + count_z
        ]
        summed = summed + stencil_tap * (forward - backward)
    return summed


def along_z(padded, anchor, count_x, count_z):
    summed = jnp.zeros(padded.shape[:-2] + (count_x, count_z), jnp.float32)
    for offset, stencil_tap in enumerate(STENCIL, 1):
        forward = padded[
            ..., anchor : anchor + count_x, anchor + offset : anchor + offset + count_z
        ]
        backward = padded[
            ..., anchor : anchor + count_x, anchor - offset : anchor - offset + count_z
        ]
        summed = summed + stencil_tap * (forward - backward)
    return summed


def velocity_elastic(velocity, stresses, buoyancy, anchor, count_x, count_z):
    updated_x = velocity[0] + TIME_STEP * buoyancy * (
        along_x(stresses[0], anchor, count_x, count_z)
        + along_z(stresses[2], anchor, count_x, count_z)
    )
    updated_z = velocity[1] + TIME_STEP * buoyancy * (
        along_x(stresses[2], anchor, count_x, count_z)
        + along_z(stresses[1], anchor, count_x, count_z)
    )
    return jnp.stack([updated_x, updated_z])


def velocity_acoustic(velocity, stresses, buoyancy, anchor, count_x, count_z):
    updated_x = velocity[0] - TIME_STEP * buoyancy * along_x(stresses[0], anchor, count_x, count_z)
    updated_z = velocity[1] - TIME_STEP * buoyancy * along_z(stresses[0], anchor, count_x, count_z)
    return jnp.stack([updated_x, updated_z])


def stress_elastic(stresses, velocity_pad, material, anchor, count_x, count_z):
    strain_x = along_x(velocity_pad[0], anchor, count_x, count_z)
    strain_z = along_z(velocity_pad[1], anchor, count_x, count_z)
    strain_shear = along_z(velocity_pad[0], anchor, count_x, count_z) + along_x(
        velocity_pad[1], anchor, count_x, count_z
    )
    lame_first = material[1]
    shear_modulus = material[2]
    normal_x = stresses[0] + TIME_STEP * (
        (lame_first + 2.0 * shear_modulus) * strain_x + lame_first * strain_z
    )
    normal_z = stresses[1] + TIME_STEP * (
        lame_first * strain_x + (lame_first + 2.0 * shear_modulus) * strain_z
    )
    shear_new = stresses[2] + TIME_STEP * shear_modulus * strain_shear
    return jnp.stack([normal_x, normal_z, shear_new])


def stress_acoustic(stresses, velocity_pad, material, anchor, count_x, count_z):
    divergence = along_x(velocity_pad[0], anchor, count_x, count_z) + along_z(
        velocity_pad[1], anchor, count_x, count_z
    )
    loading = material[1] * divergence
    memory_one = (
        RELAXATION[0] * stresses[1]
        + (1.0 - RELAXATION[0]) * MEMORY_WEIGHT[0] * material[2] * loading
    )
    memory_two = (
        RELAXATION[1] * stresses[2]
        + (1.0 - RELAXATION[1]) * MEMORY_WEIGHT[1] * material[2] * loading
    )
    pressure = stresses[0] - TIME_STEP * (loading - memory_one - memory_two)
    return jnp.stack([pressure, memory_one, memory_two])


def local_stepwise(fields, media, plane_rows, box_offset):
    current = fields[0]
    material = media[0]
    count_x = current.shape[1]
    count_z = current.shape[2]
    section = lax.axis_index("sec")
    is_source = section == 0
    block_z = lax.axis_index("gz")
    local_rows = lax.dynamic_slice_in_dim(plane_rows, block_z * NPD, NPD) - block_z * count_z
    offset = lax.dynamic_slice_in_dim(box_offset, jnp.maximum(section - 1, 0), 1)[0]
    depth_ids = block_z * count_z + jnp.arange(count_z, dtype=jnp.int32)
    landing = offset + plane_rows // 2
    chosen = (landing[:, None] == depth_ids[None, :]).astype(jnp.float32)
    for step_index in range(STEPS):
        stress_pad = padded_2(current[2:5], (("gx", 1), ("gz", 2)), RADIUS)
        velocity = lax.cond(
            is_source,
            lambda: velocity_elastic(
                current[0:2], stress_pad, material[0], RADIUS, count_x, count_z
            ),
            lambda: velocity_acoustic(
                current[0:2], stress_pad, material[0], RADIUS, count_x, count_z
            ),
        )
        velocity_pad = padded_2(velocity, (("gx", 1), ("gz", 2)), RADIUS)
        stresses = lax.cond(
            is_source,
            lambda: stress_elastic(current[2:5], velocity_pad, material, RADIUS, count_x, count_z),
            lambda: stress_acoustic(current[2:5], velocity_pad, material, RADIUS, count_x, count_z),
        )
        current = jnp.concatenate([velocity, stresses], axis=0)
        picked = jnp.take(current, local_rows, axis=2)
        block_plane = jnp.transpose(
            jnp.stack([picked[0], picked[1], -0.5 * (picked[2] + picked[3])]), (0, 2, 1)
        )
        joined = lax.all_gather(block_plane, "gz", axis=1, tiled=True)
        gathered = broadcast(joined, "sec", 0)
        injected = jnp.einsum("ckx,kz->cxz", gathered, chosen, precision=lax.Precision.HIGHEST)
        far_state = jnp.concatenate([current[0:3] + COUPLING * injected, current[3:5]], axis=0)
        current = jnp.where(is_source, current, far_state)
    return current[None]


HALO = 2 * RADIUS * STEPS
CELLS = 128
HALF = CELLS // 2
WINDOW = HALF + 2 * HALO
DEPTH = 2 * CELLS
PART = HALF + HALO
NP = 2 * NPD
TRIM = (0, 0, 16, 16, 32)
ROWS = 192
GROUPS = CELLS // NP
SLOT = (
    ((0, 0), (1, 0), (2, 0)),
    ((3, 0), (4, 0), (5, 0)),
    ((6, 0), (7, 0), (6, 96)),
    ((3, 112), (4, 112), (5, 112)),
    ((0, 128), (1, 128), (2, 128)),
)
SCALE = 840.0
TAPS = (672.0, -168.0, 32.0, -3.0)


def banded(shape, lag):
    distance = lax.broadcasted_iota(jnp.int32, shape, 0) - lax.broadcasted_iota(
        jnp.int32, shape, 1
    )
    distance = lag * distance
    values = jnp.zeros(shape, jnp.float32)
    for offset, tap in enumerate(TAPS, 1):
        values = jnp.where(distance == offset, tap, values)
        values = jnp.where(distance == -offset, -tap, values)
    return values.astype(jnp.bfloat16)


def halves(values):
    high = values.astype(jnp.bfloat16)
    low = (values - high.astype(jnp.float32)).astype(jnp.bfloat16)
    return high, low


def dot(left, right):
    return jnp.dot(left, right, preferred_element_type=jnp.float32)


def diff_x(band_x, parts):
    count = parts[0].shape[0]
    band = band_x[:count, :count]
    return dot(band, parts[0]) + dot(band, parts[1])


def diff_z(band_z, parts):
    return dot(parts[0], band_z[...]) + dot(parts[1], band_z[...])


def trimmed(arrays, amount):
    if amount == 0:
        return arrays
    return [array[amount:-amount] for array in arrays]


def lanes_of(shape):
    return lax.broadcasted_iota(jnp.int32, shape, 1) // NP


def reach(index):
    return HALO if index < 6 else HALO - 2 * RADIUS


def starts():
    return [sum(reach(before) for before in range(index)) for index in range(9)]


PACK_VMEM = 61 * 1024 * 1024
EDGE_ROWS = 6 * HALO + 2 * (HALO - 2 * RADIUS)


def assemble(window, fields, media, ahead, behind, other):
    core = lax.axis_index("gz")
    first = starts()

    @pl.when(core == 0)
    def _():
        for index in range(8):
            own = fields[index] if index < 5 else media[index - 5]
            taken, span = slice(HALO - reach(index), HALO), slice(first[index], first[index + 1])
            window[index, taken, :CELLS] = ahead[span]
            window[index, taken, CELLS:] = behind[span]
            window[index, HALO:, :CELLS] = own[:PART]
            window[index, HALO:, CELLS:] = other[index]

    @pl.when(core == 1)
    def _():
        for index in range(8):
            own = fields[index] if index < 5 else media[index - 5]
            taken, span = slice(PART, PART + reach(index)), slice(first[index], first[index + 1])
            window[index, :PART, CELLS:] = own[CELLS - PART :]
            window[index, :PART, :CELLS] = other[index]
            window[index, taken, CELLS:] = ahead[span]
            window[index, taken, :CELLS] = behind[span]

    for index in range(8):
        spare = HALO - reach(index)
        if spare:
            at = pl.multiple_of((WINDOW - spare) * core, 8)
            window[index, pl.ds(at, spare)] = jnp.zeros((spare, DEPTH), jnp.float32)


def place(state, held, sent):
    start = HALO - TRIM[-1]
    core = lax.axis_index("gz")
    state = [array[start : start + HALF] for array in state]

    @pl.when(core == 0)
    def _():
        for index in range(5):
            held[index] = state[index][:, :CELLS]
            sent[index] = state[index][:, CELLS:]

    @pl.when(core == 1)
    def _():
        for index in range(5):
            held[index] = state[index][:, CELLS:]
            sent[index] = state[index][:, :CELLS]


def acoustic(state, bands):
    vx, vz, pressure, one, two, light, kappa, loss_one, loss_two = state
    band_x, band_z = bands
    parts = halves(pressure)
    vx = vx - light * diff_x(band_x, parts)
    vz = vz - light * diff_z(band_z, parts)
    load = kappa * (diff_x(band_x, halves(vx)) + diff_z(band_z, halves(vz)))
    one = RELAXATION[0] * one + loss_one * load
    two = RELAXATION[1] * two + loss_two * load
    pressure = pressure - TIME_STEP * (load - one - two)
    return [vx, vz, pressure, one, two, light, kappa, loss_one, loss_two]


def pack_kernel(fields, media, straight, crossed, swap, sems):
    core = lax.axis_index("gz")
    first = starts()
    copies = []

    def copy(source, target):
        copies.append(pltpu.make_async_copy(source, target, sems.at[len(copies)]))

    for target, low in ((straight, core), (crossed, 1 - core)):
        for index in range(8):
            source = fields.at[index] if index < 5 else media.at[index - 5]
            count = reach(index)
            at = pl.multiple_of((CELLS - count) * (1 - low), 8)
            copy(source.at[pl.ds(at, count)], target.at[first[index] : first[index + 1]])
    span = pl.ds(pl.multiple_of((CELLS - PART) * (1 - core), 8), PART)
    copy(fields.at[:, span], swap.at[:5])
    copy(media.at[:, span], swap.at[5:])
    for each in copies:
        each.start()
    for each in copies:
        each.wait()


def constants_kernel(plane_rows, box_offset, band_x, band_z, pick, land):
    band_x[...] = banded((WINDOW, WINDOW), -1)
    band_z[...] = banded((DEPTH, DEPTH), 1)
    row = plane_rows[...]
    lane = lax.broadcasted_iota(jnp.int32, box_offset.shape, 1)
    offset = jnp.where(lane == lax.axis_index("sec") - 1, box_offset[...], 0)
    landing = row // 2 + jnp.sum(offset, axis=1, keepdims=True)
    depth = lax.broadcasted_iota(jnp.int32, (DEPTH, NP), 0)
    spread = lax.broadcasted_iota(jnp.int32, (NP, CELLS), 1) % NP
    spread = spread == lax.broadcasted_iota(jnp.int32, (NP, CELLS), 0)
    spread = jnp.where(spread, 1.0, 0.0).astype(jnp.bfloat16)
    for target, where in ((pick, row), (land, landing)):
        hot = jnp.where(depth == where, 1.0, 0.0).astype(jnp.bfloat16)
        target[...] = dot(hot, spread).astype(jnp.bfloat16)


def first_kernel(
    band_x, band_z, pick, fields, media, ahead, behind, other, held, sent, rows, carry
):
    assemble(carry, fields, media, ahead, behind, other)
    section = lax.axis_index("sec")

    @pl.when(section == 0)
    def _():
        vx, vz, sxx, szz, sxz, light, lame, shear = [carry[index] for index in range(8)]
        light = light * (TIME_STEP / SCALE)
        both = (lame + 2.0 * shear) * (TIME_STEP / SCALE)
        lame = lame * (TIME_STEP / SCALE)
        shear = shear * (TIME_STEP / SCALE)
        at = 0
        for step in range(STEPS):
            cut = TRIM[step] - at
            at = TRIM[step]
            vx, vz, sxx, szz, sxz, light, both, lame, shear = trimmed(
                [vx, vz, sxx, szz, sxz, light, both, lame, shear], cut
            )
            parts_xx, parts_zz, parts_xz = halves(sxx), halves(szz), halves(sxz)
            vx = vx + light * (diff_x(band_x, parts_xx) + diff_z(band_z, parts_xz))
            vz = vz + light * (diff_x(band_x, parts_xz) + diff_z(band_z, parts_zz))
            parts_x, parts_z = halves(vx), halves(vz)
            strain_x, strain_z = diff_x(band_x, parts_x), diff_z(band_z, parts_z)
            sxx = sxx + (both * strain_x + lame * strain_z)
            szz = szz + (lame * strain_x + both * strain_z)
            sxz = sxz + shear * (diff_z(band_z, parts_x) + diff_x(band_x, parts_z))
            low = 2 * RADIUS * (step + 1) - at
            for component, (parts, factor) in enumerate(
                ((parts_x, COUPLING), (parts_z, COUPLING), (halves(sxx + szz), -0.5 * COUPLING))
            ):
                picked = factor * (dot(parts[0], pick[...]) + dot(parts[1], pick[...]))
                picked = picked[low : picked.shape[0] - low]
                group, base = SLOT[step][component]
                spot = pl.ds(base, picked.shape[0])
                rows[spot] = jnp.where(lanes_of(picked.shape) == group, picked, rows[spot])
        place([vx, vz, sxx, szz, sxz], held, sent)

    @pl.when(section > 0)
    def _():
        vx, vz, pressure, one, two, light, kappa, loss = [carry[index] for index in range(8)]
        light = light * (TIME_STEP / SCALE)
        kappa = kappa * (1.0 / SCALE)
        loss_one = loss * ((1.0 - RELAXATION[0]) * MEMORY_WEIGHT[0])
        loss_two = loss * ((1.0 - RELAXATION[1]) * MEMORY_WEIGHT[1])
        state = [vx, vz, pressure, one, two, light, kappa, loss_one, loss_two]
        for index, array in enumerate(acoustic(state, (band_x, band_z))):
            carry[index] = array


def second_kernel(band_x, band_z, land, carry, rows, held_in, sent_in, held, sent):
    section = lax.axis_index("sec")

    @pl.when(section == 0)
    def _():
        held[...] = held_in[...]
        sent[...] = sent_in[...]

    @pl.when(section > 0)
    def _():
        state = [carry[index] for index in range(9)]
        at = 0
        for step in range(STEPS):
            if step:
                state = trimmed(state, TRIM[step] - at)
                at = TRIM[step]
                state = acoustic(state, (band_x, band_z))
            low = 2 * RADIUS * (step + 1) - at
            high = WINDOW - 2 * at - low
            for component in range(3):
                group, base = SLOT[step][component]
                taken = rows[pl.ds(base, high - low)]
                taken = halves(jnp.where(lanes_of(taken.shape) == group, taken, 0.0))
                added = sum(
                    lax.dot_general(
                        part, land[...], (((1,), (1,)), ((), ())), preferred_element_type=jnp.float32
                    )
                    for part in taken
                )
                array = state[component]
                state[component] = jnp.concatenate(
                    [array[:low], array[low:high] + added, array[high:]], axis=0
                )
        place(state[:5], held, sent)


def last_kernel(held, swapped, out, sems):
    core = lax.axis_index("gz")
    copies = [
        pltpu.make_async_copy(
            source, out.at[:, pl.ds(pl.multiple_of(HALF * half, HALF), HALF)], sems.at[index]
        )
        for index, (source, half) in enumerate(((held, core), (swapped, 1 - core)))
    ]
    for copy in copies:
        copy.start()
    for copy in copies:
        copy.wait()


def call(
    kernel,
    outs,
    operands,
    flops,
    place_in=pltpu.VMEM,
    place_out=pltpu.VMEM,
    scratch=(),
    vmem=48 * 1024 * 1024,
):
    return pl.pallas_call(
        kernel,
        out_shape=outs,
        in_specs=[pl.BlockSpec(memory_space=place_in)] * len(operands),
        out_specs=[pl.BlockSpec(memory_space=place_out)] * len(outs),
        scratch_shapes=scratch,
        compiler_params=pltpu.CompilerParams(vmem_limit_bytes=vmem),
        cost_estimate=pl.CostEstimate(
            flops=flops, bytes_accessed=2 * 1024 * 1024, transcendentals=0
        ),
    )(*operands)


def full(*shape):
    return jax.ShapeDtypeStruct(shape, jnp.float32)


def narrow(*shape):
    return jax.ShapeDtypeStruct(shape, jnp.bfloat16)


def local_window(columns, fields, media, plane_rows, box_offset):
    fields, media = fields[0], media[0]
    straight, crossed, swap = call(
        pack_kernel,
        [full(EDGE_ROWS, CELLS), full(EDGE_ROWS, CELLS), full(8, PART, CELLS)],
        [fields, media],
        1000,
        place_in=pl.ANY,
        place_out=pl.ANY,
        scratch=[pltpu.SemaphoreType.DMA((18,))],
        vmem=PACK_VMEM,
    )
    straight_pairs, crossed_pairs = [], []
    for column in range(columns):
        if column + 1 < columns:
            straight_pairs.append((2 * column, 2 * column + 2))
            crossed_pairs.append((2 * column + 1, 2 * column + 2))
        if column:
            straight_pairs.append((2 * column + 1, 2 * column - 1))
            crossed_pairs.append((2 * column, 2 * column - 1))
    turn = [(0, 1), (1, 0)]
    ahead = lax.ppermute(straight, ("gx", "gz"), straight_pairs)
    behind = lax.ppermute(crossed, ("gx", "gz"), crossed_pairs)
    other = lax.ppermute(swap, "gz", turn)
    band_x, band_z, pick, land = call(
        constants_kernel,
        [narrow(WINDOW, WINDOW), narrow(DEPTH, DEPTH), narrow(DEPTH, CELLS), narrow(DEPTH, CELLS)],
        [plane_rows[None], box_offset[None]],
        1_000_000_000,
    )
    held, sent, rows, carry = call(
        first_kernel,
        [
            full(5, HALF, CELLS),
            full(5, HALF, CELLS),
            full(ROWS, CELLS),
            full(9, WINDOW, DEPTH),
        ],
        [band_x, band_z, pick, fields, media, ahead, behind, other],
        4_000_000_000,
    )
    arrived = [lax.ppermute(rows, "sec", [(0, target)]) for target in (1, 2, 3)]
    rows = arrived[0] + arrived[1] + arrived[2]
    held, sent = call(
        second_kernel,
        [full(5, HALF, CELLS), full(5, HALF, CELLS)],
        [band_x, band_z, land, carry, rows, held, sent],
        4_000_000_000,
    )
    swapped = lax.ppermute(sent, "gz", turn)
    (out,) = call(
        last_kernel,
        [full(5, CELLS, CELLS)],
        [held, swapped],
        1000,
        place_out=pl.ANY,
        scratch=[pltpu.SemaphoreType.DMA((2,))],
    )
    return out[None]


def solution(mesh):
    in_specs = (P("sec", None, "gx", "gz"), P("sec", None, "gx", "gz"), P(), P())
    out_specs = P("sec", None, "gx", "gz")
    if mesh.shape["gz"] == 2:
        local = functools.partial(local_window, mesh.shape["gx"])
    else:
        local = local_stepwise
    return jax.shard_map(local, mesh=mesh, in_specs=in_specs, out_specs=out_specs, check_vma=False)
```

```python
import functools

import jax
import jax.numpy as jnp
from jax import lax
from jax.experimental import pallas as pl
from jax.experimental.pallas import tpu as pltpu
from jax.sharding import PartitionSpec as P

RADIUS = 4
STEPS = 5
NPD = 8

STENCIL = (0.8, -0.2, 4.0 / 105.0, -1.0 / 280.0)
TIME_STEP = 0.2
COUPLING = 0.5
RELAXATION = (0.9, 0.5)
MEMORY_WEIGHT = (0.15, 0.1)


def padded_2(block, sides, width):
    for axis, dim in sides:
        count = lax.axis_size(axis)
        forward = [(i, i + 1) for i in range(count - 1)]
        backward = [(target, source) for source, target in forward]
        low = lax.ppermute(
            lax.slice_in_dim(block, block.shape[dim] - width, None, axis=dim), axis, forward
        )
        high = lax.ppermute(lax.slice_in_dim(block, 0, width, axis=dim), axis, backward)
        block = jnp.concatenate([low, block, high], axis=dim)
    return block


def broadcast(value, axis, source):
    kept = jnp.where(lax.axis_index(axis) == source, value, 0).astype(value.dtype)
    return lax.psum(kept, axis)


def along_x(padded, anchor, count_x, count_z):
    summed = jnp.zeros(padded.shape[:-2] + (count_x, count_z), jnp.float32)
    for offset, stencil_tap in enumerate(STENCIL, 1):
        forward = padded[
            ..., anchor + offset : anchor + offset + count_x, anchor : anchor + count_z
        ]
        backward = padded[
            ..., anchor - offset : anchor - offset + count_x, anchor : anchor + count_z
        ]
        summed = summed + stencil_tap * (forward - backward)
    return summed


def along_z(padded, anchor, count_x, count_z):
    summed = jnp.zeros(padded.shape[:-2] + (count_x, count_z), jnp.float32)
    for offset, stencil_tap in enumerate(STENCIL, 1):
        forward = padded[
            ..., anchor : anchor + count_x, anchor + offset : anchor + offset + count_z
        ]
        backward = padded[
            ..., anchor : anchor + count_x, anchor - offset : anchor - offset + count_z
        ]
        summed = summed + stencil_tap * (forward - backward)
    return summed


def velocity_elastic(velocity, stresses, buoyancy, anchor, count_x, count_z):
    updated_x = velocity[0] + TIME_STEP * buoyancy * (
        along_x(stresses[0], anchor, count_x, count_z)
        + along_z(stresses[2], anchor, count_x, count_z)
    )
    updated_z = velocity[1] + TIME_STEP * buoyancy * (
        along_x(stresses[2], anchor, count_x, count_z)
        + along_z(stresses[1], anchor, count_x, count_z)
    )
    return jnp.stack([updated_x, updated_z])


def velocity_acoustic(velocity, stresses, buoyancy, anchor, count_x, count_z):
    updated_x = velocity[0] - TIME_STEP * buoyancy * along_x(stresses[0], anchor, count_x, count_z)
    updated_z = velocity[1] - TIME_STEP * buoyancy * along_z(stresses[0], anchor, count_x, count_z)
    return jnp.stack([updated_x, updated_z])


def stress_elastic(stresses, velocity_pad, material, anchor, count_x, count_z):
    strain_x = along_x(velocity_pad[0], anchor, count_x, count_z)
    strain_z = along_z(velocity_pad[1], anchor, count_x, count_z)
    strain_shear = along_z(velocity_pad[0], anchor, count_x, count_z) + along_x(
        velocity_pad[1], anchor, count_x, count_z
    )
    lame_first = material[1]
    shear_modulus = material[2]
    normal_x = stresses[0] + TIME_STEP * (
        (lame_first + 2.0 * shear_modulus) * strain_x + lame_first * strain_z
    )
    normal_z = stresses[1] + TIME_STEP * (
        lame_first * strain_x + (lame_first + 2.0 * shear_modulus) * strain_z
    )
    shear_new = stresses[2] + TIME_STEP * shear_modulus * strain_shear
    return jnp.stack([normal_x, normal_z, shear_new])


def stress_acoustic(stresses, velocity_pad, material, anchor, count_x, count_z):
    divergence = along_x(velocity_pad[0], anchor, count_x, count_z) + along_z(
        velocity_pad[1], anchor, count_x, count_z
    )
    loading = material[1] * divergence
    memory_one = (
        RELAXATION[0] * stresses[1]
        + (1.0 - RELAXATION[0]) * MEMORY_WEIGHT[0] * material[2] * loading
    )
    memory_two = (
        RELAXATION[1] * stresses[2]
        + (1.0 - RELAXATION[1]) * MEMORY_WEIGHT[1] * material[2] * loading
    )
    pressure = stresses[0] - TIME_STEP * (loading - memory_one - memory_two)
    return jnp.stack([pressure, memory_one, memory_two])


def local_stepwise(fields, media, plane_rows, box_offset):
    current = fields[0]
    material = media[0]
    count_x = current.shape[1]
    count_z = current.shape[2]
    section = lax.axis_index("sec")
    is_source = section == 0
    block_z = lax.axis_index("gz")
    local_rows = lax.dynamic_slice_in_dim(plane_rows, block_z * NPD, NPD) - block_z * count_z
    offset = lax.dynamic_slice_in_dim(box_offset, jnp.maximum(section - 1, 0), 1)[0]
    depth_ids = block_z * count_z + jnp.arange(count_z, dtype=jnp.int32)
    landing = offset + plane_rows // 2
    chosen = (landing[:, None] == depth_ids[None, :]).astype(jnp.float32)
    for step_index in range(STEPS):
        stress_pad = padded_2(current[2:5], (("gx", 1), ("gz", 2)), RADIUS)
        velocity = lax.cond(
            is_source,
            lambda: velocity_elastic(
                current[0:2], stress_pad, material[0], RADIUS, count_x, count_z
            ),
            lambda: velocity_acoustic(
                current[0:2], stress_pad, material[0], RADIUS, count_x, count_z
            ),
        )
        velocity_pad = padded_2(velocity, (("gx", 1), ("gz", 2)), RADIUS)
        stresses = lax.cond(
            is_source,
            lambda: stress_elastic(current[2:5], velocity_pad, material, RADIUS, count_x, count_z),
            lambda: stress_acoustic(current[2:5], velocity_pad, material, RADIUS, count_x, count_z),
        )
        current = jnp.concatenate([velocity, stresses], axis=0)
        picked = jnp.take(current, local_rows, axis=2)
        block_plane = jnp.transpose(
            jnp.stack([picked[0], picked[1], -0.5 * (picked[2] + picked[3])]), (0, 2, 1)
        )
        joined = lax.all_gather(block_plane, "gz", axis=1, tiled=True)
        gathered = broadcast(joined, "sec", 0)
        injected = jnp.einsum("ckx,kz->cxz", gathered, chosen, precision=lax.Precision.HIGHEST)
        far_state = jnp.concatenate([current[0:3] + COUPLING * injected, current[3:5]], axis=0)
        current = jnp.where(is_source, current, far_state)
    return current[None]


HALO = 2 * RADIUS * STEPS
CELLS = 128
HALF = CELLS // 2
WINDOW = HALF + 2 * HALO
DEPTH = 2 * CELLS
PART = HALF + HALO
NP = 2 * NPD
TRIM = (0, 0, 16, 16, 32)
WINDOWS = [WINDOW - 2 * amount for amount in sorted(set(TRIM))]
COUNTS = len(WINDOWS)
ROWS = 192
GROUPS = CELLS // NP
SLOT = (
    ((0, 0), (1, 0), (2, 0)),
    ((3, 0), (4, 0), (5, 0)),
    ((6, 0), (7, 0), (6, 96)),
    ((3, 112), (4, 112), (5, 112)),
    ((0, 128), (1, 128), (2, 128)),
)
SCALE = 840.0
TAPS = (672.0, -168.0, 32.0, -3.0)


def banded(distance):
    values = jnp.zeros(distance.shape, jnp.float32)
    for offset, tap in enumerate(TAPS, 1):
        values = jnp.where(distance == offset, tap, values)
        values = jnp.where(distance == -offset, -tap, values)
    return values.astype(jnp.bfloat16)


def halves(values):
    high = values.astype(jnp.bfloat16)
    low = (values - high.astype(jnp.float32)).astype(jnp.bfloat16)
    return high, low


def dot(left, right):
    return jnp.dot(left, right, preferred_element_type=jnp.float32)


def diff_x(bands, parts):
    return dot(bands[parts[0].shape[0]][...], jnp.concatenate(parts, axis=0))


def along_depth(matrix, parts):
    return dot(jnp.concatenate(parts, axis=1), matrix[...])


def trimmed(arrays, amount):
    if amount == 0:
        return arrays
    return [array[amount:-amount] for array in arrays]


def lanes_of(shape):
    return lax.broadcasted_iota(jnp.int32, shape, 1) // NP


def assemble(window, block, ahead, behind, other):
    core = lax.axis_index("gz")

    @pl.when(core == 0)
    def _():
        for index in range(8):
            window[index, :HALO, :CELLS] = ahead[index]
            window[index, :HALO, CELLS:] = behind[index]
            window[index, HALO:, :CELLS] = block[index, :PART]
            window[index, HALO:, CELLS:] = other[index]

    @pl.when(core == 1)
    def _():
        for index in range(8):
            window[index, :PART, CELLS:] = block[index, CELLS - PART :]
            window[index, :PART, :CELLS] = other[index]
            window[index, PART:, CELLS:] = ahead[index]
            window[index, PART:, :CELLS] = behind[index]


def place(state, held, sent):
    start = HALO - TRIM[-1]
    core = lax.axis_index("gz")
    state = [array[start : start + HALF] for array in state]

    @pl.when(core == 0)
    def _():
        for index in range(5):
            held[index] = state[index][:, :CELLS]
            sent[index] = state[index][:, CELLS:]

    @pl.when(core == 1)
    def _():
        for index in range(5):
            held[index] = state[index][:, CELLS:]
            sent[index] = state[index][:, :CELLS]


def acoustic(state, bands):
    vx, vz, pressure, one, two, light, kappa, loss_one, loss_two = state
    band_x, band_z = bands
    parts = halves(pressure)
    vx = vx - light * diff_x(band_x, parts)
    vz = vz - light * along_depth(band_z, parts)
    load = kappa * (diff_x(band_x, halves(vx)) + along_depth(band_z, halves(vz)))
    one = RELAXATION[0] * one + loss_one * load
    two = RELAXATION[1] * two + loss_two * load
    pressure = pressure - TIME_STEP * (load - one - two)
    return [vx, vz, pressure, one, two, light, kappa, loss_one, loss_two]


def constants_kernel(plane_rows, box_offset, *targets):
    *bands_x, band_z, pick, land = targets
    for target in bands_x:
        count = target.shape[0]
        row = lax.broadcasted_iota(jnp.int32, target.shape, 0)
        column = lax.broadcasted_iota(jnp.int32, target.shape, 1)
        target[...] = banded(jnp.where(column < count, column, column - count) - row)
    shape = (DEPTH, DEPTH)
    distance = lax.broadcasted_iota(jnp.int32, shape, 0) - lax.broadcasted_iota(jnp.int32, shape, 1)
    band_z[:DEPTH] = banded(distance)
    band_z[DEPTH:] = band_z[:DEPTH]
    row = plane_rows[...]
    lane = lax.broadcasted_iota(jnp.int32, box_offset.shape, 1)
    offset = jnp.where(lane == lax.axis_index("sec") - 1, box_offset[...], 0)
    landing = row // 2 + jnp.sum(offset, axis=1, keepdims=True)
    depth = lax.broadcasted_iota(jnp.int32, (DEPTH, NP), 0)
    spread = lax.broadcasted_iota(jnp.int32, (NP, CELLS), 1) % NP
    spread = spread == lax.broadcasted_iota(jnp.int32, (NP, CELLS), 0)
    spread = jnp.where(spread, 1.0, 0.0).astype(jnp.bfloat16)
    hot = jnp.where(depth == row, 1.0, 0.0).astype(jnp.bfloat16)
    pick[:DEPTH] = dot(hot, spread).astype(jnp.bfloat16)
    pick[DEPTH:] = pick[:DEPTH]
    hot = jnp.where(depth == landing, 1.0, 0.0).astype(jnp.bfloat16)
    land[:, :CELLS] = dot(hot, spread).astype(jnp.bfloat16)
    land[:, CELLS:] = land[:, :CELLS]


def first_kernel(*refs):
    bands_x, (band_z, pick, block, ahead, behind, other) = refs[:COUNTS], refs[COUNTS:-4]
    held, sent, rows, carry = refs[-4:]
    band_x = {band.shape[0]: band for band in bands_x}
    assemble(carry, block, ahead, behind, other)
    section = lax.axis_index("sec")

    @pl.when(section == 0)
    def _():
        vx, vz, sxx, szz, sxz, light, lame, shear = [carry[index] for index in range(8)]
        light = light * (TIME_STEP / SCALE)
        both = (lame + 2.0 * shear) * (TIME_STEP / SCALE)
        lame = lame * (TIME_STEP / SCALE)
        shear = shear * (TIME_STEP / SCALE)
        at = 0
        for step in range(STEPS):
            cut = TRIM[step] - at
            at = TRIM[step]
            vx, vz, sxx, szz, sxz, light, both, lame, shear = trimmed(
                [vx, vz, sxx, szz, sxz, light, both, lame, shear], cut
            )
            parts_xx, parts_zz, parts_xz = halves(sxx), halves(szz), halves(sxz)
            vx = vx + light * (diff_x(band_x, parts_xx) + along_depth(band_z, parts_xz))
            vz = vz + light * (diff_x(band_x, parts_xz) + along_depth(band_z, parts_zz))
            parts_x, parts_z = halves(vx), halves(vz)
            strain_x, strain_z = diff_x(band_x, parts_x), along_depth(band_z, parts_z)
            sxx = sxx + (both * strain_x + lame * strain_z)
            szz = szz + (lame * strain_x + both * strain_z)
            sxz = sxz + shear * (along_depth(band_z, parts_x) + diff_x(band_x, parts_z))
            low = 2 * RADIUS * (step + 1) - at
            for component, (parts, factor) in enumerate(
                ((parts_x, COUPLING), (parts_z, COUPLING), (halves(sxx + szz), -0.5 * COUPLING))
            ):
                picked = factor * along_depth(pick, parts)
                picked = picked[low : picked.shape[0] - low]
                group, base = SLOT[step][component]
                spot = pl.ds(base, picked.shape[0])
                rows[spot] = jnp.where(lanes_of(picked.shape) == group, picked, rows[spot])
        place([vx, vz, sxx, szz, sxz], held, sent)

    @pl.when(section > 0)
    def _():
        vx, vz, pressure, one, two, light, kappa, loss = [carry[index] for index in range(8)]
        light = light * (TIME_STEP / SCALE)
        kappa = kappa * (1.0 / SCALE)
        loss_one = loss * ((1.0 - RELAXATION[0]) * MEMORY_WEIGHT[0])
        loss_two = loss * ((1.0 - RELAXATION[1]) * MEMORY_WEIGHT[1])
        state = [vx, vz, pressure, one, two, light, kappa, loss_one, loss_two]
        for index, array in enumerate(acoustic(state, (band_x, band_z))):
            carry[index] = array


def second_kernel(*refs):
    bands_x, (band_z, land, carry, rows, held_in, sent_in, held, sent) = refs[:COUNTS], refs[COUNTS:]
    band_x = {band.shape[0]: band for band in bands_x}
    section = lax.axis_index("sec")

    @pl.when(section == 0)
    def _():
        held[...] = held_in[...]
        sent[...] = sent_in[...]

    @pl.when(section > 0)
    def _():
        state = [carry[index] for index in range(9)]
        at = 0
        for step in range(STEPS):
            if step:
                state = trimmed(state, TRIM[step] - at)
                at = TRIM[step]
                state = acoustic(state, (band_x, band_z))
            low = 2 * RADIUS * (step + 1) - at
            high = WINDOW - 2 * at - low
            for component in range(3):
                group, base = SLOT[step][component]
                taken = rows[pl.ds(base, high - low)]
                taken = halves(jnp.where(lanes_of(taken.shape) == group, taken, 0.0))
                added = lax.dot_general(
                    jnp.concatenate(taken, axis=1),
                    land[...],
                    (((1,), (1,)), ((), ())),
                    preferred_element_type=jnp.float32,
                )
                array = state[component]
                state[component] = jnp.concatenate(
                    [array[:low], array[low:high] + added, array[high:]], axis=0
                )
        place(state[:5], held, sent)


def last_kernel(held, swapped, out, sems):
    core = lax.axis_index("gz")
    copies = [
        pltpu.make_async_copy(
            source, out.at[:, pl.ds(pl.multiple_of(HALF * half, HALF), HALF)], sems.at[index]
        )
        for index, (source, half) in enumerate(((held, core), (swapped, 1 - core)))
    ]
    for copy in copies:
        copy.start()
    for copy in copies:
        copy.wait()


def call(kernel, outs, operands, flops, place_out=pltpu.VMEM, scratch=()):
    return pl.pallas_call(
        kernel,
        out_shape=outs,
        in_specs=[pl.BlockSpec(memory_space=pltpu.VMEM)] * len(operands),
        out_specs=[pl.BlockSpec(memory_space=place_out)] * len(outs),
        scratch_shapes=scratch,
        compiler_params=pltpu.CompilerParams(vmem_limit_bytes=48 * 1024 * 1024),
        cost_estimate=pl.CostEstimate(
            flops=flops, bytes_accessed=2 * 1024 * 1024, transcendentals=0
        ),
    )(*operands)


def full(*shape):
    return jax.ShapeDtypeStruct(shape, jnp.float32)


def narrow(*shape):
    return jax.ShapeDtypeStruct(shape, jnp.bfloat16)


def local_window(columns, fields, media, plane_rows, box_offset):
    fields, media = fields[0], media[0]
    core = lax.axis_index("gz")
    is_first = core == 0
    block = lax.optimization_barrier(jnp.concatenate([fields, media], axis=0))
    top, bottom = block[:, :HALO], block[:, CELLS - HALO :]
    straight_pairs, crossed_pairs = [], []
    for column in range(columns):
        if column + 1 < columns:
            straight_pairs.append((2 * column, 2 * column + 2))
            crossed_pairs.append((2 * column + 1, 2 * column + 2))
        if column:
            straight_pairs.append((2 * column + 1, 2 * column - 1))
            crossed_pairs.append((2 * column, 2 * column - 1))
    turn = [(0, 1), (1, 0)]
    ahead = lax.ppermute(jnp.where(is_first, bottom, top), ("gx", "gz"), straight_pairs)
    behind = lax.ppermute(jnp.where(is_first, top, bottom), ("gx", "gz"), crossed_pairs)
    other = jnp.where(is_first, block[:, CELLS - PART :], block[:, :PART])
    other = lax.ppermute(other, "gz", turn)
    *bands, pick, land = call(
        constants_kernel,
        [narrow(count, 2 * count) for count in WINDOWS]
        + [narrow(2 * DEPTH, DEPTH), narrow(2 * DEPTH, CELLS), narrow(DEPTH, 2 * CELLS)],
        [plane_rows[None], box_offset[None]],
        1_000_000_000,
    )
    held, sent, rows, carry = call(
        first_kernel,
        [
            full(5, HALF, CELLS),
            full(5, HALF, CELLS),
            full(ROWS, CELLS),
            full(9, WINDOW, DEPTH),
        ],
        [*bands, pick, block, ahead, behind, other],
        4_000_000_000,
    )
    arrived = [lax.ppermute(rows, "sec", [(0, target)]) for target in (1, 2, 3)]
    rows = arrived[0] + arrived[1] + arrived[2]
    held, sent = call(
        second_kernel,
        [full(5, HALF, CELLS), full(5, HALF, CELLS)],
        [*bands, land, carry, rows, held, sent],
        4_000_000_000,
    )
    swapped = lax.ppermute(sent, "gz", turn)
    (out,) = call(
        last_kernel,
        [full(5, CELLS, CELLS)],
        [held, swapped],
        1000,
        pl.ANY,
        [pltpu.SemaphoreType.DMA((2,))],
    )
    return out[None]


def solution(mesh):
    in_specs = (P("sec", None, "gx", "gz"), P("sec", None, "gx", "gz"), P(), P())
    out_specs = P("sec", None, "gx", "gz")
    if mesh.shape["gz"] == 2:
        local = functools.partial(local_window, mesh.shape["gx"])
    else:
        local = local_stepwise
    return jax.shard_map(local, mesh=mesh, in_specs=in_specs, out_specs=out_specs, check_vma=False)
```

```python
import functools

import jax
import jax.numpy as jnp
from jax import lax
from jax.experimental import pallas as pl
from jax.experimental.pallas import tpu as pltpu
from jax.sharding import PartitionSpec as P

RADIUS = 4
STEPS = 5
NPD = 8

STENCIL = (0.8, -0.2, 4.0 / 105.0, -1.0 / 280.0)
TIME_STEP = 0.2
COUPLING = 0.5
RELAXATION = (0.9, 0.5)
MEMORY_WEIGHT = (0.15, 0.1)


def padded_2(block, sides, width):
    for axis, dim in sides:
        count = lax.axis_size(axis)
        forward = [(i, i + 1) for i in range(count - 1)]
        backward = [(target, source) for source, target in forward]
        low = lax.ppermute(
            lax.slice_in_dim(block, block.shape[dim] - width, None, axis=dim), axis, forward
        )
        high = lax.ppermute(lax.slice_in_dim(block, 0, width, axis=dim), axis, backward)
        block = jnp.concatenate([low, block, high], axis=dim)
    return block


def broadcast(value, axis, source):
    kept = jnp.where(lax.axis_index(axis) == source, value, 0).astype(value.dtype)
    return lax.psum(kept, axis)


def along_x(padded, anchor, count_x, count_z):
    summed = jnp.zeros(padded.shape[:-2] + (count_x, count_z), jnp.float32)
    for offset, stencil_tap in enumerate(STENCIL, 1):
        forward = padded[
            ..., anchor + offset : anchor + offset + count_x, anchor : anchor + count_z
        ]
        backward = padded[
            ..., anchor - offset : anchor - offset + count_x, anchor : anchor + count_z
        ]
        summed = summed + stencil_tap * (forward - backward)
    return summed


def along_z(padded, anchor, count_x, count_z):
    summed = jnp.zeros(padded.shape[:-2] + (count_x, count_z), jnp.float32)
    for offset, stencil_tap in enumerate(STENCIL, 1):
        forward = padded[
            ..., anchor : anchor + count_x, anchor + offset : anchor + offset + count_z
        ]
        backward = padded[
            ..., anchor : anchor + count_x, anchor - offset : anchor - offset + count_z
        ]
        summed = summed + stencil_tap * (forward - backward)
    return summed


def velocity_elastic(velocity, stresses, buoyancy, anchor, count_x, count_z):
    updated_x = velocity[0] + TIME_STEP * buoyancy * (
        along_x(stresses[0], anchor, count_x, count_z)
        + along_z(stresses[2], anchor, count_x, count_z)
    )
    updated_z = velocity[1] + TIME_STEP * buoyancy * (
        along_x(stresses[2], anchor, count_x, count_z)
        + along_z(stresses[1], anchor, count_x, count_z)
    )
    return jnp.stack([updated_x, updated_z])


def velocity_acoustic(velocity, stresses, buoyancy, anchor, count_x, count_z):
    updated_x = velocity[0] - TIME_STEP * buoyancy * along_x(stresses[0], anchor, count_x, count_z)
    updated_z = velocity[1] - TIME_STEP * buoyancy * along_z(stresses[0], anchor, count_x, count_z)
    return jnp.stack([updated_x, updated_z])


def stress_elastic(stresses, velocity_pad, material, anchor, count_x, count_z):
    strain_x = along_x(velocity_pad[0], anchor, count_x, count_z)
    strain_z = along_z(velocity_pad[1], anchor, count_x, count_z)
    strain_shear = along_z(velocity_pad[0], anchor, count_x, count_z) + along_x(
        velocity_pad[1], anchor, count_x, count_z
    )
    lame_first = material[1]
    shear_modulus = material[2]
    normal_x = stresses[0] + TIME_STEP * (
        (lame_first + 2.0 * shear_modulus) * strain_x + lame_first * strain_z
    )
    normal_z = stresses[1] + TIME_STEP * (
        lame_first * strain_x + (lame_first + 2.0 * shear_modulus) * strain_z
    )
    shear_new = stresses[2] + TIME_STEP * shear_modulus * strain_shear
    return jnp.stack([normal_x, normal_z, shear_new])


def stress_acoustic(stresses, velocity_pad, material, anchor, count_x, count_z):
    divergence = along_x(velocity_pad[0], anchor, count_x, count_z) + along_z(
        velocity_pad[1], anchor, count_x, count_z
    )
    loading = material[1] * divergence
    memory_one = (
        RELAXATION[0] * stresses[1]
        + (1.0 - RELAXATION[0]) * MEMORY_WEIGHT[0] * material[2] * loading
    )
    memory_two = (
        RELAXATION[1] * stresses[2]
        + (1.0 - RELAXATION[1]) * MEMORY_WEIGHT[1] * material[2] * loading
    )
    pressure = stresses[0] - TIME_STEP * (loading - memory_one - memory_two)
    return jnp.stack([pressure, memory_one, memory_two])


def local_stepwise(fields, media, plane_rows, box_offset):
    current = fields[0]
    material = media[0]
    count_x = current.shape[1]
    count_z = current.shape[2]
    section = lax.axis_index("sec")
    is_source = section == 0
    block_z = lax.axis_index("gz")
    local_rows = lax.dynamic_slice_in_dim(plane_rows, block_z * NPD, NPD) - block_z * count_z
    offset = lax.dynamic_slice_in_dim(box_offset, jnp.maximum(section - 1, 0), 1)[0]
    depth_ids = block_z * count_z + jnp.arange(count_z, dtype=jnp.int32)
    landing = offset + plane_rows // 2
    chosen = (landing[:, None] == depth_ids[None, :]).astype(jnp.float32)
    for step_index in range(STEPS):
        stress_pad = padded_2(current[2:5], (("gx", 1), ("gz", 2)), RADIUS)
        velocity = lax.cond(
            is_source,
            lambda: velocity_elastic(
                current[0:2], stress_pad, material[0], RADIUS, count_x, count_z
            ),
            lambda: velocity_acoustic(
                current[0:2], stress_pad, material[0], RADIUS, count_x, count_z
            ),
        )
        velocity_pad = padded_2(velocity, (("gx", 1), ("gz", 2)), RADIUS)
        stresses = lax.cond(
            is_source,
            lambda: stress_elastic(current[2:5], velocity_pad, material, RADIUS, count_x, count_z),
            lambda: stress_acoustic(current[2:5], velocity_pad, material, RADIUS, count_x, count_z),
        )
        current = jnp.concatenate([velocity, stresses], axis=0)
        picked = jnp.take(current, local_rows, axis=2)
        block_plane = jnp.transpose(
            jnp.stack([picked[0], picked[1], -0.5 * (picked[2] + picked[3])]), (0, 2, 1)
        )
        joined = lax.all_gather(block_plane, "gz", axis=1, tiled=True)
        gathered = broadcast(joined, "sec", 0)
        injected = jnp.einsum("ckx,kz->cxz", gathered, chosen, precision=lax.Precision.HIGHEST)
        far_state = jnp.concatenate([current[0:3] + COUPLING * injected, current[3:5]], axis=0)
        current = jnp.where(is_source, current, far_state)
    return current[None]


HALO = 2 * RADIUS * STEPS
CELLS = 128
HALF = CELLS // 2
WINDOW = HALF + 2 * HALO
DEPTH = 2 * CELLS
PART = HALF + HALO
NP = 2 * NPD
TRIM = (0, 0, 16, 16, 32)
WINDOWS = [WINDOW - 2 * amount for amount in sorted(set(TRIM))]
COUNTS = len(WINDOWS)
ROWS = 192
GROUPS = CELLS // NP
SLOT = (
    ((0, 0), (1, 0), (2, 0)),
    ((3, 0), (4, 0), (5, 0)),
    ((6, 0), (7, 0), (6, 96)),
    ((3, 112), (4, 112), (5, 112)),
    ((0, 128), (1, 128), (2, 128)),
)
SCALE = 840.0
TAPS = (672.0, -168.0, 32.0, -3.0)


def banded(distance):
    values = jnp.zeros(distance.shape, jnp.float32)
    for offset, tap in enumerate(TAPS, 1):
        values = jnp.where(distance == offset, tap, values)
        values = jnp.where(distance == -offset, -tap, values)
    return values.astype(jnp.bfloat16)


def halves(values):
    high = values.astype(jnp.bfloat16)
    low = (values - high.astype(jnp.float32)).astype(jnp.bfloat16)
    return high, low


def dot(left, right):
    return jnp.dot(left, right, preferred_element_type=jnp.float32)


def diff_x(bands, parts):
    return dot(bands[parts[0].shape[0]][...], jnp.concatenate(parts, axis=0))


def along_depth(matrix, parts):
    return dot(jnp.concatenate(parts, axis=1), matrix[...])


def trimmed(arrays, amount):
    if amount == 0:
        return arrays
    return [array[amount:-amount] for array in arrays]


def lanes_of(shape):
    return lax.broadcasted_iota(jnp.int32, shape, 1) // NP


def assemble(window, block, ahead, behind, other):
    core = lax.axis_index("gz")

    @pl.when(core == 0)
    def _():
        for index in range(8):
            window[index, :HALO, :CELLS] = ahead[index]
            window[index, :HALO, CELLS:] = behind[index]
            window[index, HALO:, :CELLS] = block[index, :PART]
            window[index, HALO:, CELLS:] = other[index]

    @pl.when(core == 1)
    def _():
        for index in range(8):
            window[index, :PART, CELLS:] = block[index, CELLS - PART :]
            window[index, :PART, :CELLS] = other[index]
            window[index, PART:, CELLS:] = ahead[index]
            window[index, PART:, :CELLS] = behind[index]


def place(state, held, sent):
    start = HALO - TRIM[-1]
    core = lax.axis_index("gz")
    state = [array[start : start + HALF] for array in state]

    @pl.when(core == 0)
    def _():
        for index in range(5):
            held[index] = state[index][:, :CELLS]
            sent[index] = state[index][:, CELLS:]

    @pl.when(core == 1)
    def _():
        for index in range(5):
            held[index] = state[index][:, CELLS:]
            sent[index] = state[index][:, :CELLS]


def acoustic(state, bands):
    vx, vz, pressure, one, two, light, kappa, loss_one, loss_two = state
    band_x, band_z = bands
    parts = halves(pressure)
    vx = vx - light * diff_x(band_x, parts)
    vz = vz - light * along_depth(band_z, parts)
    load = kappa * (diff_x(band_x, halves(vx)) + along_depth(band_z, halves(vz)))
    one = RELAXATION[0] * one + loss_one * load
    two = RELAXATION[1] * two + loss_two * load
    pressure = pressure - TIME_STEP * (load - one - two)
    return [vx, vz, pressure, one, two, light, kappa, loss_one, loss_two]


def constants_kernel(plane_rows, box_offset, *targets):
    *bands_x, band_z, pick, land = targets
    for target in bands_x:
        count = target.shape[0]
        row = lax.broadcasted_iota(jnp.int32, target.shape, 0)
        column = lax.broadcasted_iota(jnp.int32, target.shape, 1)
        target[...] = banded(jnp.where(column < count, column, column - count) - row)
    shape = (DEPTH, DEPTH)
    distance = lax.broadcasted_iota(jnp.int32, shape, 0) - lax.broadcasted_iota(jnp.int32, shape, 1)
    band_z[:DEPTH] = banded(distance)
    band_z[DEPTH:] = band_z[:DEPTH]
    row = plane_rows[...]
    lane = lax.broadcasted_iota(jnp.int32, box_offset.shape, 1)
    offset = jnp.where(lane == lax.axis_index("sec") - 1, box_offset[...], 0)
    landing = row // 2 + jnp.sum(offset, axis=1, keepdims=True)
    depth = lax.broadcasted_iota(jnp.int32, (DEPTH, NP), 0)
    spread = lax.broadcasted_iota(jnp.int32, (NP, CELLS), 1) % NP
    spread = spread == lax.broadcasted_iota(jnp.int32, (NP, CELLS), 0)
    spread = jnp.where(spread, 1.0, 0.0).astype(jnp.bfloat16)
    hot = jnp.where(depth == row, 1.0, 0.0).astype(jnp.bfloat16)
    pick[:DEPTH] = dot(hot, spread).astype(jnp.bfloat16)
    pick[DEPTH:] = pick[:DEPTH]
    hot = jnp.where(depth == landing, 1.0, 0.0).astype(jnp.bfloat16)
    land[:, :CELLS] = dot(hot, spread).astype(jnp.bfloat16)
    land[:, CELLS:] = land[:, :CELLS]


def first_kernel(*refs):
    bands_x, (band_z, pick, block, ahead, behind, other) = refs[:COUNTS], refs[COUNTS:-4]
    held, sent, rows, carry = refs[-4:]
    band_x = {band.shape[0]: band for band in bands_x}
    assemble(carry, block, ahead, behind, other)
    section = lax.axis_index("sec")

    @pl.when(section == 0)
    def _():
        vx, vz, sxx, szz, sxz, light, lame, shear = [carry[index] for index in range(8)]
        light = light * (TIME_STEP / SCALE)
        both = (lame + 2.0 * shear) * (TIME_STEP / SCALE)
        lame = lame * (TIME_STEP / SCALE)
        shear = shear * (TIME_STEP / SCALE)
        at = 0
        for step in range(STEPS):
            cut = TRIM[step] - at
            at = TRIM[step]
            vx, vz, sxx, szz, sxz, light, both, lame, shear = trimmed(
                [vx, vz, sxx, szz, sxz, light, both, lame, shear], cut
            )
            parts_xx, parts_zz, parts_xz = halves(sxx), halves(szz), halves(sxz)
            vx = vx + light * (diff_x(band_x, parts_xx) + along_depth(band_z, parts_xz))
            vz = vz + light * (diff_x(band_x, parts_xz) + along_depth(band_z, parts_zz))
            parts_x, parts_z = halves(vx), halves(vz)
            strain_x, strain_z = diff_x(band_x, parts_x), along_depth(band_z, parts_z)
            sxx = sxx + (both * strain_x + lame * strain_z)
            szz = szz + (lame * strain_x + both * strain_z)
            sxz = sxz + shear * (along_depth(band_z, parts_x) + diff_x(band_x, parts_z))
            low = 2 * RADIUS * (step + 1) - at
            for component, (parts, factor) in enumerate(
                ((parts_x, COUPLING), (parts_z, COUPLING), (halves(sxx + szz), -0.5 * COUPLING))
            ):
                picked = factor * along_depth(pick, parts)
                picked = picked[low : picked.shape[0] - low]
                group, base = SLOT[step][component]
                spot = pl.ds(base, picked.shape[0])
                rows[spot] = jnp.where(lanes_of(picked.shape) == group, picked, rows[spot])
        place([vx, vz, sxx, szz, sxz], held, sent)

    @pl.when(section > 0)
    def _():
        vx, vz, pressure, one, two, light, kappa, loss = [carry[index] for index in range(8)]
        light = light * (TIME_STEP / SCALE)
        kappa = kappa * (1.0 / SCALE)
        loss_one = loss * ((1.0 - RELAXATION[0]) * MEMORY_WEIGHT[0])
        loss_two = loss * ((1.0 - RELAXATION[1]) * MEMORY_WEIGHT[1])
        state = [vx, vz, pressure, one, two, light, kappa, loss_one, loss_two]
        for index, array in enumerate(acoustic(state, (band_x, band_z))):
            carry[index] = array


def second_kernel(*refs):
    bands_x, (band_z, land, carry, rows, held_in, sent_in, held, sent) = refs[:COUNTS], refs[COUNTS:]
    band_x = {band.shape[0]: band for band in bands_x}
    section = lax.axis_index("sec")

    @pl.when(section == 0)
    def _():
        held[...] = held_in[...]
        sent[...] = sent_in[...]

    @pl.when(section > 0)
    def _():
        state = [carry[index] for index in range(9)]
        at = 0
        for step in range(STEPS):
            if step:
                state = trimmed(state, TRIM[step] - at)
                at = TRIM[step]
                state = acoustic(state, (band_x, band_z))
            low = 2 * RADIUS * (step + 1) - at
            high = WINDOW - 2 * at - low
            for component in range(3):
                group, base = SLOT[step][component]
                taken = rows[pl.ds(base, high - low)]
                taken = halves(jnp.where(lanes_of(taken.shape) == group, taken, 0.0))
                added = lax.dot_general(
                    jnp.concatenate(taken, axis=1),
                    land[...],
                    (((1,), (1,)), ((), ())),
                    preferred_element_type=jnp.float32,
                )
                array = state[component]
                state[component] = jnp.concatenate(
                    [array[:low], array[low:high] + added, array[high:]], axis=0
                )
        place(state[:5], held, sent)


def last_kernel(held, swapped, out, sems):
    core = lax.axis_index("gz")
    copies = [
        pltpu.make_async_copy(
            source, out.at[:, pl.ds(pl.multiple_of(HALF * half, HALF), HALF)], sems.at[index]
        )
        for index, (source, half) in enumerate(((held, core), (swapped, 1 - core)))
    ]
    for copy in copies:
        copy.start()
    for copy in copies:
        copy.wait()


def call(kernel, outs, operands, flops, place_out=pltpu.VMEM, scratch=()):
    return pl.pallas_call(
        kernel,
        out_shape=outs,
        in_specs=[pl.BlockSpec(memory_space=pltpu.VMEM)] * len(operands),
        out_specs=[pl.BlockSpec(memory_space=place_out)] * len(outs),
        scratch_shapes=scratch,
        compiler_params=pltpu.CompilerParams(vmem_limit_bytes=48 * 1024 * 1024),
        cost_estimate=pl.CostEstimate(
            flops=flops, bytes_accessed=2 * 1024 * 1024, transcendentals=0
        ),
    )(*operands)


def full(*shape):
    return jax.ShapeDtypeStruct(shape, jnp.float32)


def narrow(*shape):
    return jax.ShapeDtypeStruct(shape, jnp.bfloat16)


def local_window(columns, fields, media, plane_rows, box_offset):
    fields, media = fields[0], media[0]
    core = lax.axis_index("gz")
    is_first = core == 0
    block = lax.optimization_barrier(jnp.concatenate([fields, media], axis=0))
    top, bottom = block[:, :HALO], block[:, CELLS - HALO :]
    straight_pairs, crossed_pairs = [], []
    for column in range(columns):
        if column + 1 < columns:
            straight_pairs.append((2 * column, 2 * column + 2))
            crossed_pairs.append((2 * column + 1, 2 * column + 2))
        if column:
            straight_pairs.append((2 * column + 1, 2 * column - 1))
            crossed_pairs.append((2 * column, 2 * column - 1))
    turn = [(0, 1), (1, 0)]
    ahead = lax.ppermute(jnp.where(is_first, bottom, top), ("gx", "gz"), straight_pairs)
    behind = lax.ppermute(jnp.where(is_first, top, bottom), ("gx", "gz"), crossed_pairs)
    other = jnp.concatenate(
        [
            jnp.where(is_first, joined[1, :, :PART], joined[0, :, CELLS - PART :])
            for joined in (lax.all_gather(fields, "gz"), lax.all_gather(media, "gz"))
        ],
        axis=0,
    )
    *bands, pick, land = call(
        constants_kernel,
        [narrow(count, 2 * count) for count in WINDOWS]
        + [narrow(2 * DEPTH, DEPTH), narrow(2 * DEPTH, CELLS), narrow(DEPTH, 2 * CELLS)],
        [plane_rows[None], box_offset[None]],
        1_000_000_000,
    )
    held, sent, rows, carry = call(
        first_kernel,
        [
            full(5, HALF, CELLS),
            full(5, HALF, CELLS),
            full(ROWS, CELLS),
            full(9, WINDOW, DEPTH),
        ],
        [*bands, pick, block, ahead, behind, other],
        4_000_000_000,
    )
    arrived = [lax.ppermute(rows, "sec", [(0, target)]) for target in (1, 2, 3)]
    rows = arrived[0] + arrived[1] + arrived[2]
    held, sent = call(
        second_kernel,
        [full(5, HALF, CELLS), full(5, HALF, CELLS)],
        [*bands, land, carry, rows, held, sent],
        4_000_000_000,
    )
    swapped = lax.ppermute(sent, "gz", turn)
    (out,) = call(
        last_kernel,
        [full(5, CELLS, CELLS)],
        [held, swapped],
        1000,
        pl.ANY,
        [pltpu.SemaphoreType.DMA((2,))],
    )
    return out[None]


def solution(mesh):
    in_specs = (P("sec", None, "gx", "gz"), P("sec", None, "gx", "gz"), P(), P())
    out_specs = P("sec", None, "gx", "gz")
    if mesh.shape["gz"] == 2:
        local = functools.partial(local_window, mesh.shape["gx"])
    else:
        local = local_stepwise
    return jax.shard_map(local, mesh=mesh, in_specs=in_specs, out_specs=out_specs, check_vma=False)
```

```python
import functools

import jax
import jax.numpy as jnp
from jax import lax
from jax.experimental import pallas as pl
from jax.experimental.pallas import tpu as pltpu
from jax.sharding import PartitionSpec as P

RADIUS = 4
STEPS = 5
NPD = 8

STENCIL = (0.8, -0.2, 4.0 / 105.0, -1.0 / 280.0)
TIME_STEP = 0.2
COUPLING = 0.5
RELAXATION = (0.9, 0.5)
MEMORY_WEIGHT = (0.15, 0.1)


def padded_2(block, sides, width):
    for axis, dim in sides:
        count = lax.axis_size(axis)
        forward = [(i, i + 1) for i in range(count - 1)]
        backward = [(target, source) for source, target in forward]
        low = lax.ppermute(
            lax.slice_in_dim(block, block.shape[dim] - width, None, axis=dim), axis, forward
        )
        high = lax.ppermute(lax.slice_in_dim(block, 0, width, axis=dim), axis, backward)
        block = jnp.concatenate([low, block, high], axis=dim)
    return block


def broadcast(value, axis, source):
    kept = jnp.where(lax.axis_index(axis) == source, value, 0).astype(value.dtype)
    return lax.psum(kept, axis)


def along_x(padded, anchor, count_x, count_z):
    summed = jnp.zeros(padded.shape[:-2] + (count_x, count_z), jnp.float32)
    for offset, stencil_tap in enumerate(STENCIL, 1):
        forward = padded[
            ..., anchor + offset : anchor + offset + count_x, anchor : anchor + count_z
        ]
        backward = padded[
            ..., anchor - offset : anchor - offset + count_x, anchor : anchor + count_z
        ]
        summed = summed + stencil_tap * (forward - backward)
    return summed


def along_z(padded, anchor, count_x, count_z):
    summed = jnp.zeros(padded.shape[:-2] + (count_x, count_z), jnp.float32)
    for offset, stencil_tap in enumerate(STENCIL, 1):
        forward = padded[
            ..., anchor : anchor + count_x, anchor + offset : anchor + offset + count_z
        ]
        backward = padded[
            ..., anchor : anchor + count_x, anchor - offset : anchor - offset + count_z
        ]
        summed = summed + stencil_tap * (forward - backward)
    return summed


def velocity_elastic(velocity, stresses, buoyancy, anchor, count_x, count_z):
    updated_x = velocity[0] + TIME_STEP * buoyancy * (
        along_x(stresses[0], anchor, count_x, count_z)
        + along_z(stresses[2], anchor, count_x, count_z)
    )
    updated_z = velocity[1] + TIME_STEP * buoyancy * (
        along_x(stresses[2], anchor, count_x, count_z)
        + along_z(stresses[1], anchor, count_x, count_z)
    )
    return jnp.stack([updated_x, updated_z])


def velocity_acoustic(velocity, stresses, buoyancy, anchor, count_x, count_z):
    updated_x = velocity[0] - TIME_STEP * buoyancy * along_x(stresses[0], anchor, count_x, count_z)
    updated_z = velocity[1] - TIME_STEP * buoyancy * along_z(stresses[0], anchor, count_x, count_z)
    return jnp.stack([updated_x, updated_z])


def stress_elastic(stresses, velocity_pad, material, anchor, count_x, count_z):
    strain_x = along_x(velocity_pad[0], anchor, count_x, count_z)
    strain_z = along_z(velocity_pad[1], anchor, count_x, count_z)
    strain_shear = along_z(velocity_pad[0], anchor, count_x, count_z) + along_x(
        velocity_pad[1], anchor, count_x, count_z
    )
    lame_first = material[1]
    shear_modulus = material[2]
    normal_x = stresses[0] + TIME_STEP * (
        (lame_first + 2.0 * shear_modulus) * strain_x + lame_first * strain_z
    )
    normal_z = stresses[1] + TIME_STEP * (
        lame_first * strain_x + (lame_first + 2.0 * shear_modulus) * strain_z
    )
    shear_new = stresses[2] + TIME_STEP * shear_modulus * strain_shear
    return jnp.stack([normal_x, normal_z, shear_new])


def stress_acoustic(stresses, velocity_pad, material, anchor, count_x, count_z):
    divergence = along_x(velocity_pad[0], anchor, count_x, count_z) + along_z(
        velocity_pad[1], anchor, count_x, count_z
    )
    loading = material[1] * divergence
    memory_one = (
        RELAXATION[0] * stresses[1]
        + (1.0 - RELAXATION[0]) * MEMORY_WEIGHT[0] * material[2] * loading
    )
    memory_two = (
        RELAXATION[1] * stresses[2]
        + (1.0 - RELAXATION[1]) * MEMORY_WEIGHT[1] * material[2] * loading
    )
    pressure = stresses[0] - TIME_STEP * (loading - memory_one - memory_two)
    return jnp.stack([pressure, memory_one, memory_two])


def local_stepwise(fields, media, plane_rows, box_offset):
    current = fields[0]
    material = media[0]
    count_x = current.shape[1]
    count_z = current.shape[2]
    section = lax.axis_index("sec")
    is_source = section == 0
    block_z = lax.axis_index("gz")
    local_rows = lax.dynamic_slice_in_dim(plane_rows, block_z * NPD, NPD) - block_z * count_z
    offset = lax.dynamic_slice_in_dim(box_offset, jnp.maximum(section - 1, 0), 1)[0]
    depth_ids = block_z * count_z + jnp.arange(count_z, dtype=jnp.int32)
    landing = offset + plane_rows // 2
    chosen = (landing[:, None] == depth_ids[None, :]).astype(jnp.float32)
    for step_index in range(STEPS):
        stress_pad = padded_2(current[2:5], (("gx", 1), ("gz", 2)), RADIUS)
        velocity = lax.cond(
            is_source,
            lambda: velocity_elastic(
                current[0:2], stress_pad, material[0], RADIUS, count_x, count_z
            ),
            lambda: velocity_acoustic(
                current[0:2], stress_pad, material[0], RADIUS, count_x, count_z
            ),
        )
        velocity_pad = padded_2(velocity, (("gx", 1), ("gz", 2)), RADIUS)
        stresses = lax.cond(
            is_source,
            lambda: stress_elastic(current[2:5], velocity_pad, material, RADIUS, count_x, count_z),
            lambda: stress_acoustic(current[2:5], velocity_pad, material, RADIUS, count_x, count_z),
        )
        current = jnp.concatenate([velocity, stresses], axis=0)
        picked = jnp.take(current, local_rows, axis=2)
        block_plane = jnp.transpose(
            jnp.stack([picked[0], picked[1], -0.5 * (picked[2] + picked[3])]), (0, 2, 1)
        )
        joined = lax.all_gather(block_plane, "gz", axis=1, tiled=True)
        gathered = broadcast(joined, "sec", 0)
        injected = jnp.einsum("ckx,kz->cxz", gathered, chosen, precision=lax.Precision.HIGHEST)
        far_state = jnp.concatenate([current[0:3] + COUPLING * injected, current[3:5]], axis=0)
        current = jnp.where(is_source, current, far_state)
    return current[None]


HALO = 2 * RADIUS * STEPS
CELLS = 128
HALF = CELLS // 2
WINDOW = HALF + 2 * HALO
DEPTH = 2 * CELLS
PART = HALF + HALO
NP = 2 * NPD
TRIM = (0, 0, 16, 16, 32)
WINDOWS = [WINDOW - 2 * amount for amount in sorted(set(TRIM))]
COUNTS = len(WINDOWS)
ROWS = 192
GROUPS = CELLS // NP
SLOT = (
    ((0, 0), (1, 0), (2, 0)),
    ((3, 0), (4, 0), (5, 0)),
    ((6, 0), (7, 0), (6, 96)),
    ((3, 112), (4, 112), (5, 112)),
    ((0, 128), (1, 128), (2, 128)),
)
SCALE = 840.0
TAPS = (672.0, -168.0, 32.0, -3.0)


def banded(distance):
    values = jnp.zeros(distance.shape, jnp.float32)
    for offset, tap in enumerate(TAPS, 1):
        values = jnp.where(distance == offset, tap, values)
        values = jnp.where(distance == -offset, -tap, values)
    return values.astype(jnp.bfloat16)


def halves(values):
    high = values.astype(jnp.bfloat16)
    low = (values - high.astype(jnp.float32)).astype(jnp.bfloat16)
    return high, low


def dot(left, right):
    return jnp.dot(left, right, preferred_element_type=jnp.float32)


def diff_x(bands, parts):
    return dot(bands[parts[0].shape[0]][...], jnp.concatenate(parts, axis=0))


def along_depth(matrix, parts):
    return dot(jnp.concatenate(parts, axis=1), matrix[...])


def trimmed(arrays, amount):
    if amount == 0:
        return arrays
    return [array[amount:-amount] for array in arrays]


def lanes_of(shape):
    return lax.broadcasted_iota(jnp.int32, shape, 1) // NP


def assemble(window, block, ahead, behind, other):
    core = lax.axis_index("gz")

    @pl.when(core == 0)
    def _():
        for index in range(8):
            window[index, :HALO, :CELLS] = ahead[index]
            window[index, :HALO, CELLS:] = behind[index]
            window[index, HALO:, :CELLS] = block[index, :PART]
            window[index, HALO:, CELLS:] = other[index]

    @pl.when(core == 1)
    def _():
        for index in range(8):
            window[index, :PART, CELLS:] = block[index, CELLS - PART :]
            window[index, :PART, :CELLS] = other[index]
            window[index, PART:, CELLS:] = ahead[index]
            window[index, PART:, :CELLS] = behind[index]


def place(state, held, sent):
    start = HALO - TRIM[-1]
    core = lax.axis_index("gz")
    state = [array[start : start + HALF] for array in state]

    @pl.when(core == 0)
    def _():
        for index in range(5):
            held[index] = state[index][:, :CELLS]
            sent[index] = state[index][:, CELLS:]

    @pl.when(core == 1)
    def _():
        for index in range(5):
            held[index] = state[index][:, CELLS:]
            sent[index] = state[index][:, :CELLS]


def acoustic(state, bands):
    vx, vz, pressure, one, two, light, kappa, loss_one, loss_two = state
    band_x, band_z = bands
    parts = halves(pressure)
    vx = vx - light * diff_x(band_x, parts)
    vz = vz - light * along_depth(band_z, parts)
    load = kappa * (diff_x(band_x, halves(vx)) + along_depth(band_z, halves(vz)))
    one = RELAXATION[0] * one + loss_one * load
    two = RELAXATION[1] * two + loss_two * load
    pressure = pressure - TIME_STEP * (load - one - two)
    return [vx, vz, pressure, one, two, light, kappa, loss_one, loss_two]


def constants_kernel(plane_rows, box_offset, *targets):
    *bands_x, band_z, pick, land = targets
    for target in bands_x:
        count = target.shape[0]
        row = lax.broadcasted_iota(jnp.int32, target.shape, 0)
        column = lax.broadcasted_iota(jnp.int32, target.shape, 1)
        target[...] = banded(jnp.where(column < count, column, column - count) - row)
    shape = (DEPTH, DEPTH)
    distance = lax.broadcasted_iota(jnp.int32, shape, 0) - lax.broadcasted_iota(jnp.int32, shape, 1)
    band_z[:DEPTH] = banded(distance)
    band_z[DEPTH:] = band_z[:DEPTH]
    row = plane_rows[...]
    lane = lax.broadcasted_iota(jnp.int32, box_offset.shape, 1)
    offset = jnp.where(lane == lax.axis_index("sec") - 1, box_offset[...], 0)
    landing = row // 2 + jnp.sum(offset, axis=1, keepdims=True)
    depth = lax.broadcasted_iota(jnp.int32, (DEPTH, NP), 0)
    spread = lax.broadcasted_iota(jnp.int32, (NP, CELLS), 1) % NP
    spread = spread == lax.broadcasted_iota(jnp.int32, (NP, CELLS), 0)
    spread = jnp.where(spread, 1.0, 0.0).astype(jnp.bfloat16)
    hot = jnp.where(depth == row, 1.0, 0.0).astype(jnp.bfloat16)
    pick[:DEPTH] = dot(hot, spread).astype(jnp.bfloat16)
    pick[DEPTH:] = pick[:DEPTH]
    hot = jnp.where(depth == landing, 1.0, 0.0).astype(jnp.bfloat16)
    land[:, :CELLS] = dot(hot, spread).astype(jnp.bfloat16)
    land[:, CELLS:] = land[:, :CELLS]


def first_kernel(*refs):
    bands_x, (band_z, pick, block, ahead, behind, other) = refs[:COUNTS], refs[COUNTS:-4]
    held, sent, rows, carry = refs[-4:]
    band_x = {band.shape[0]: band for band in bands_x}
    assemble(carry, block, ahead, behind, other)
    section = lax.axis_index("sec")

    @pl.when(section == 0)
    def _():
        vx, vz, sxx, szz, sxz, light, lame, shear = [carry[index] for index in range(8)]
        light = light * (TIME_STEP / SCALE)
        both = (lame + 2.0 * shear) * (TIME_STEP / SCALE)
        lame = lame * (TIME_STEP / SCALE)
        shear = shear * (TIME_STEP / SCALE)
        at = 0
        for step in range(STEPS):
            cut = TRIM[step] - at
            at = TRIM[step]
            vx, vz, sxx, szz, sxz, light, both, lame, shear = trimmed(
                [vx, vz, sxx, szz, sxz, light, both, lame, shear], cut
            )
            parts_xx, parts_zz, parts_xz = halves(sxx), halves(szz), halves(sxz)
            vx = vx + light * (diff_x(band_x, parts_xx) + along_depth(band_z, parts_xz))
            vz = vz + light * (diff_x(band_x, parts_xz) + along_depth(band_z, parts_zz))
            parts_x, parts_z = halves(vx), halves(vz)
            strain_x, strain_z = diff_x(band_x, parts_x), along_depth(band_z, parts_z)
            sxx = sxx + (both * strain_x + lame * strain_z)
            szz = szz + (lame * strain_x + both * strain_z)
            sxz = sxz + shear * (along_depth(band_z, parts_x) + diff_x(band_x, parts_z))
            low = 2 * RADIUS * (step + 1) - at
            for component, (parts, factor) in enumerate(
                ((parts_x, COUPLING), (parts_z, COUPLING), (halves(sxx + szz), -0.5 * COUPLING))
            ):
                picked = factor * along_depth(pick, parts)
                picked = picked[low : picked.shape[0] - low]
                group, base = SLOT[step][component]
                spot = pl.ds(base, picked.shape[0])
                rows[spot] = jnp.where(lanes_of(picked.shape) == group, picked, rows[spot])
        place([vx, vz, sxx, szz, sxz], held, sent)

    @pl.when(section > 0)
    def _():
        vx, vz, pressure, one, two, light, kappa, loss = [carry[index] for index in range(8)]
        light = light * (TIME_STEP / SCALE)
        kappa = kappa * (1.0 / SCALE)
        loss_one = loss * ((1.0 - RELAXATION[0]) * MEMORY_WEIGHT[0])
        loss_two = loss * ((1.0 - RELAXATION[1]) * MEMORY_WEIGHT[1])
        state = [vx, vz, pressure, one, two, light, kappa, loss_one, loss_two]
        for index, array in enumerate(acoustic(state, (band_x, band_z))):
            carry[index] = array


def second_kernel(*refs):
    bands_x, (band_z, land, carry, rows, held_in, sent_in, held, sent) = refs[:COUNTS], refs[COUNTS:]
    band_x = {band.shape[0]: band for band in bands_x}
    section = lax.axis_index("sec")

    @pl.when(section == 0)
    def _():
        held[...] = held_in[...]
        sent[...] = sent_in[...]

    @pl.when(section > 0)
    def _():
        state = [carry[index] for index in range(9)]
        at = 0
        for step in range(STEPS):
            if step:
                state = trimmed(state, TRIM[step] - at)
                at = TRIM[step]
                state = acoustic(state, (band_x, band_z))
            low = 2 * RADIUS * (step + 1) - at
            high = WINDOW - 2 * at - low
            for component in range(3):
                group, base = SLOT[step][component]
                taken = rows[pl.ds(base, high - low)]
                taken = halves(jnp.where(lanes_of(taken.shape) == group, taken, 0.0))
                added = lax.dot_general(
                    jnp.concatenate(taken, axis=1),
                    land[...],
                    (((1,), (1,)), ((), ())),
                    preferred_element_type=jnp.float32,
                )
                array = state[component]
                state[component] = jnp.concatenate(
                    [array[:low], array[low:high] + added, array[high:]], axis=0
                )
        place(state[:5], held, sent)


def last_kernel(held, swapped, out, sems):
    core = lax.axis_index("gz")
    copies = [
        pltpu.make_async_copy(
            source, out.at[:, pl.ds(pl.multiple_of(HALF * half, HALF), HALF)], sems.at[index]
        )
        for index, (source, half) in enumerate(((held, core), (swapped, 1 - core)))
    ]
    for copy in copies:
        copy.start()
    for copy in copies:
        copy.wait()


def call(kernel, outs, operands, flops, place_out=pltpu.VMEM, scratch=()):
    return pl.pallas_call(
        kernel,
        out_shape=outs,
        in_specs=[pl.BlockSpec(memory_space=pltpu.VMEM)] * len(operands),
        out_specs=[pl.BlockSpec(memory_space=place_out)] * len(outs),
        scratch_shapes=scratch,
        compiler_params=pltpu.CompilerParams(vmem_limit_bytes=48 * 1024 * 1024),
        cost_estimate=pl.CostEstimate(
            flops=flops, bytes_accessed=2 * 1024 * 1024, transcendentals=0
        ),
    )(*operands)


def full(*shape):
    return jax.ShapeDtypeStruct(shape, jnp.float32)


def narrow(*shape):
    return jax.ShapeDtypeStruct(shape, jnp.bfloat16)


def local_window(columns, fields, media, plane_rows, box_offset):
    fields, media = fields[0], media[0]
    core = lax.axis_index("gz")
    is_first = core == 0
    block = lax.optimization_barrier(jnp.concatenate([fields, media], axis=0))
    top, bottom = block[:, :HALO], block[:, CELLS - HALO :]
    straight_pairs, crossed_pairs = [], []
    for column in range(columns):
        if column + 1 < columns:
            straight_pairs.append((2 * column, 2 * column + 2))
            crossed_pairs.append((2 * column + 1, 2 * column + 2))
        if column:
            straight_pairs.append((2 * column + 1, 2 * column - 1))
            crossed_pairs.append((2 * column, 2 * column - 1))
    turn = [(0, 1), (1, 0)]
    ahead = lax.ppermute(jnp.where(is_first, bottom, top), ("gx", "gz"), straight_pairs)
    behind = lax.ppermute(jnp.where(is_first, top, bottom), ("gx", "gz"), crossed_pairs)
    other = lax.all_gather(block, "gz")
    other = jnp.where(is_first, other[1, :, :PART], other[0, :, CELLS - PART :])
    *bands, pick, land = call(
        constants_kernel,
        [narrow(count, 2 * count) for count in WINDOWS]
        + [narrow(2 * DEPTH, DEPTH), narrow(2 * DEPTH, CELLS), narrow(DEPTH, 2 * CELLS)],
        [plane_rows[None], box_offset[None]],
        1_000_000_000,
    )
    held, sent, rows, carry = call(
        first_kernel,
        [
            full(5, HALF, CELLS),
            full(5, HALF, CELLS),
            full(ROWS, CELLS),
            full(9, WINDOW, DEPTH),
        ],
        [*bands, pick, block, ahead, behind, other],
        4_000_000_000,
    )
    arrived = [lax.ppermute(rows, "sec", [(0, target)]) for target in (1, 2, 3)]
    rows = arrived[0] + arrived[1] + arrived[2]
    held, sent = call(
        second_kernel,
        [full(5, HALF, CELLS), full(5, HALF, CELLS)],
        [*bands, land, carry, rows, held, sent],
        4_000_000_000,
    )
    swapped = lax.ppermute(sent, "gz", turn)
    (out,) = call(
        last_kernel,
        [full(5, CELLS, CELLS)],
        [held, swapped],
        1000,
        pl.ANY,
        [pltpu.SemaphoreType.DMA((2,))],
    )
    return out[None]


def solution(mesh):
    in_specs = (P("sec", None, "gx", "gz"), P("sec", None, "gx", "gz"), P(), P())
    out_specs = P("sec", None, "gx", "gz")
    if mesh.shape["gz"] == 2:
        local = functools.partial(local_window, mesh.shape["gx"])
    else:
        local = local_stepwise
    return jax.shard_map(local, mesh=mesh, in_specs=in_specs, out_specs=out_specs, check_vma=False)
```

```python
import functools

import jax
import jax.numpy as jnp
from jax import lax
from jax.experimental import pallas as pl
from jax.experimental.pallas import tpu as pltpu
from jax.sharding import PartitionSpec as P

RADIUS = 4
STEPS = 5
NPD = 8

STENCIL = (0.8, -0.2, 4.0 / 105.0, -1.0 / 280.0)
TIME_STEP = 0.2
COUPLING = 0.5
RELAXATION = (0.9, 0.5)
MEMORY_WEIGHT = (0.15, 0.1)


def padded_2(block, sides, width):
    for axis, dim in sides:
        count = lax.axis_size(axis)
        forward = [(i, i + 1) for i in range(count - 1)]
        backward = [(target, source) for source, target in forward]
        low = lax.ppermute(
            lax.slice_in_dim(block, block.shape[dim] - width, None, axis=dim), axis, forward
        )
        high = lax.ppermute(lax.slice_in_dim(block, 0, width, axis=dim), axis, backward)
        block = jnp.concatenate([low, block, high], axis=dim)
    return block


def broadcast(value, axis, source):
    kept = jnp.where(lax.axis_index(axis) == source, value, 0).astype(value.dtype)
    return lax.psum(kept, axis)


def along_x(padded, anchor, count_x, count_z):
    summed = jnp.zeros(padded.shape[:-2] + (count_x, count_z), jnp.float32)
    for offset, stencil_tap in enumerate(STENCIL, 1):
        forward = padded[
            ..., anchor + offset : anchor + offset + count_x, anchor : anchor + count_z
        ]
        backward = padded[
            ..., anchor - offset : anchor - offset + count_x, anchor : anchor + count_z
        ]
        summed = summed + stencil_tap * (forward - backward)
    return summed


def along_z(padded, anchor, count_x, count_z):
    summed = jnp.zeros(padded.shape[:-2] + (count_x, count_z), jnp.float32)
    for offset, stencil_tap in enumerate(STENCIL, 1):
        forward = padded[
            ..., anchor : anchor + count_x, anchor + offset : anchor + offset + count_z
        ]
        backward = padded[
            ..., anchor : anchor + count_x, anchor - offset : anchor - offset + count_z
        ]
        summed = summed + stencil_tap * (forward - backward)
    return summed


def velocity_elastic(velocity, stresses, buoyancy, anchor, count_x, count_z):
    updated_x = velocity[0] + TIME_STEP * buoyancy * (
        along_x(stresses[0], anchor, count_x, count_z)
        + along_z(stresses[2], anchor, count_x, count_z)
    )
    updated_z = velocity[1] + TIME_STEP * buoyancy * (
        along_x(stresses[2], anchor, count_x, count_z)
        + along_z(stresses[1], anchor, count_x, count_z)
    )
    return jnp.stack([updated_x, updated_z])


def velocity_acoustic(velocity, stresses, buoyancy, anchor, count_x, count_z):
    updated_x = velocity[0] - TIME_STEP * buoyancy * along_x(stresses[0], anchor, count_x, count_z)
    updated_z = velocity[1] - TIME_STEP * buoyancy * along_z(stresses[0], anchor, count_x, count_z)
    return jnp.stack([updated_x, updated_z])


def stress_elastic(stresses, velocity_pad, material, anchor, count_x, count_z):
    strain_x = along_x(velocity_pad[0], anchor, count_x, count_z)
    strain_z = along_z(velocity_pad[1], anchor, count_x, count_z)
    strain_shear = along_z(velocity_pad[0], anchor, count_x, count_z) + along_x(
        velocity_pad[1], anchor, count_x, count_z
    )
    lame_first = material[1]
    shear_modulus = material[2]
    normal_x = stresses[0] + TIME_STEP * (
        (lame_first + 2.0 * shear_modulus) * strain_x + lame_first * strain_z
    )
    normal_z = stresses[1] + TIME_STEP * (
        lame_first * strain_x + (lame_first + 2.0 * shear_modulus) * strain_z
    )
    shear_new = stresses[2] + TIME_STEP * shear_modulus * strain_shear
    return jnp.stack([normal_x, normal_z, shear_new])


def stress_acoustic(stresses, velocity_pad, material, anchor, count_x, count_z):
    divergence = along_x(velocity_pad[0], anchor, count_x, count_z) + along_z(
        velocity_pad[1], anchor, count_x, count_z
    )
    loading = material[1] * divergence
    memory_one = (
        RELAXATION[0] * stresses[1]
        + (1.0 - RELAXATION[0]) * MEMORY_WEIGHT[0] * material[2] * loading
    )
    memory_two = (
        RELAXATION[1] * stresses[2]
        + (1.0 - RELAXATION[1]) * MEMORY_WEIGHT[1] * material[2] * loading
    )
    pressure = stresses[0] - TIME_STEP * (loading - memory_one - memory_two)
    return jnp.stack([pressure, memory_one, memory_two])


def local_stepwise(fields, media, plane_rows, box_offset):
    current = fields[0]
    material = media[0]
    count_x = current.shape[1]
    count_z = current.shape[2]
    section = lax.axis_index("sec")
    is_source = section == 0
    block_z = lax.axis_index("gz")
    local_rows = lax.dynamic_slice_in_dim(plane_rows, block_z * NPD, NPD) - block_z * count_z
    offset = lax.dynamic_slice_in_dim(box_offset, jnp.maximum(section - 1, 0), 1)[0]
    depth_ids = block_z * count_z + jnp.arange(count_z, dtype=jnp.int32)
    landing = offset + plane_rows // 2
    chosen = (landing[:, None] == depth_ids[None, :]).astype(jnp.float32)
    for step_index in range(STEPS):
        stress_pad = padded_2(current[2:5], (("gx", 1), ("gz", 2)), RADIUS)
        velocity = lax.cond(
            is_source,
            lambda: velocity_elastic(
                current[0:2], stress_pad, material[0], RADIUS, count_x, count_z
            ),
            lambda: velocity_acoustic(
                current[0:2], stress_pad, material[0], RADIUS, count_x, count_z
            ),
        )
        velocity_pad = padded_2(velocity, (("gx", 1), ("gz", 2)), RADIUS)
        stresses = lax.cond(
            is_source,
            lambda: stress_elastic(current[2:5], velocity_pad, material, RADIUS, count_x, count_z),
            lambda: stress_acoustic(current[2:5], velocity_pad, material, RADIUS, count_x, count_z),
        )
        current = jnp.concatenate([velocity, stresses], axis=0)
        picked = jnp.take(current, local_rows, axis=2)
        block_plane = jnp.transpose(
            jnp.stack([picked[0], picked[1], -0.5 * (picked[2] + picked[3])]), (0, 2, 1)
        )
        joined = lax.all_gather(block_plane, "gz", axis=1, tiled=True)
        gathered = broadcast(joined, "sec", 0)
        injected = jnp.einsum("ckx,kz->cxz", gathered, chosen, precision=lax.Precision.HIGHEST)
        far_state = jnp.concatenate([current[0:3] + COUPLING * injected, current[3:5]], axis=0)
        current = jnp.where(is_source, current, far_state)
    return current[None]


HALO = 2 * RADIUS * STEPS
CELLS = 128
HALF = CELLS // 2
WINDOW = HALF + 2 * HALO
DEPTH = 2 * CELLS
PART = HALF + HALO
NP = 2 * NPD
TRIM = (0, 0, 16, 16, 32)
WINDOWS = [WINDOW - 2 * amount for amount in sorted(set(TRIM))]
COUNTS = len(WINDOWS)
ROWS = 192
GROUPS = CELLS // NP
SLOT = (
    ((0, 0), (1, 0), (2, 0)),
    ((3, 0), (4, 0), (5, 0)),
    ((6, 0), (7, 0), (6, 96)),
    ((3, 112), (4, 112), (5, 112)),
    ((0, 128), (1, 128), (2, 128)),
)
SCALE = 840.0
TAPS = (672.0, -168.0, 32.0, -3.0)


def banded(distance):
    values = jnp.zeros(distance.shape, jnp.float32)
    for offset, tap in enumerate(TAPS, 1):
        values = jnp.where(distance == offset, tap, values)
        values = jnp.where(distance == -offset, -tap, values)
    return values.astype(jnp.bfloat16)


def halves(values):
    high = values.astype(jnp.bfloat16)
    low = (values - high.astype(jnp.float32)).astype(jnp.bfloat16)
    return high, low


def dot(left, right):
    return jnp.dot(left, right, preferred_element_type=jnp.float32)


def diff_x(bands, parts):
    return dot(bands[parts[0].shape[0]][...], jnp.concatenate(parts, axis=0))


def along_depth(matrix, parts):
    return dot(jnp.concatenate(parts, axis=1), matrix[...])


def trimmed(arrays, amount):
    if amount == 0:
        return arrays
    return [array[amount:-amount] for array in arrays]


def lanes_of(shape):
    return lax.broadcasted_iota(jnp.int32, shape, 1) // NP


def assemble(window, block, ahead, behind, other):
    core = lax.axis_index("gz")

    @pl.when(core == 0)
    def _():
        for index in range(8):
            window[index, :HALO, :CELLS] = ahead[index]
            window[index, :HALO, CELLS:] = behind[index]
            window[index, HALO:, :CELLS] = block[index, :PART]
            window[index, HALO:, CELLS:] = other[index]

    @pl.when(core == 1)
    def _():
        for index in range(8):
            window[index, :PART, CELLS:] = block[index, CELLS - PART :]
            window[index, :PART, :CELLS] = other[index]
            window[index, PART:, CELLS:] = ahead[index]
            window[index, PART:, :CELLS] = behind[index]


def place(state, held, sent):
    start = HALO - TRIM[-1]
    core = lax.axis_index("gz")
    state = [array[start : start + HALF] for array in state]

    @pl.when(core == 0)
    def _():
        for index in range(5):
            held[index] = state[index][:, :CELLS]
            sent[index] = state[index][:, CELLS:]

    @pl.when(core == 1)
    def _():
        for index in range(5):
            held[index] = state[index][:, CELLS:]
            sent[index] = state[index][:, :CELLS]


def acoustic(state, bands):
    vx, vz, pressure, one, two, light, kappa, loss_one, loss_two = state
    band_x, band_z = bands
    parts = halves(pressure)
    vx = vx - light * diff_x(band_x, parts)
    vz = vz - light * along_depth(band_z, parts)
    load = kappa * (diff_x(band_x, halves(vx)) + along_depth(band_z, halves(vz)))
    one = RELAXATION[0] * one + loss_one * load
    two = RELAXATION[1] * two + loss_two * load
    pressure = pressure - TIME_STEP * (load - one - two)
    return [vx, vz, pressure, one, two, light, kappa, loss_one, loss_two]


def constants_kernel(plane_rows, box_offset, *targets):
    *bands_x, band_z, pick, land = targets
    for target in bands_x:
        count = target.shape[0]
        row = lax.broadcasted_iota(jnp.int32, target.shape, 0)
        column = lax.broadcasted_iota(jnp.int32, target.shape, 1)
        target[...] = banded(jnp.where(column < count, column, column - count) - row)
    shape = (DEPTH, DEPTH)
    distance = lax.broadcasted_iota(jnp.int32, shape, 0) - lax.broadcasted_iota(jnp.int32, shape, 1)
    band_z[:DEPTH] = banded(distance)
    band_z[DEPTH:] = band_z[:DEPTH]
    row = plane_rows[...]
    lane = lax.broadcasted_iota(jnp.int32, box_offset.shape, 1)
    offset = jnp.where(lane == lax.axis_index("sec") - 1, box_offset[...], 0)
    landing = row // 2 + jnp.sum(offset, axis=1, keepdims=True)
    depth = lax.broadcasted_iota(jnp.int32, (DEPTH, NP), 0)
    spread = lax.broadcasted_iota(jnp.int32, (NP, CELLS), 1) % NP
    spread = spread == lax.broadcasted_iota(jnp.int32, (NP, CELLS), 0)
    spread = jnp.where(spread, 1.0, 0.0).astype(jnp.bfloat16)
    hot = jnp.where(depth == row, 1.0, 0.0).astype(jnp.bfloat16)
    pick[:DEPTH] = dot(hot, spread).astype(jnp.bfloat16)
    pick[DEPTH:] = pick[:DEPTH]
    hot = jnp.where(depth == landing, 1.0, 0.0).astype(jnp.bfloat16)
    land[:, :CELLS] = dot(hot, spread).astype(jnp.bfloat16)
    land[:, CELLS:] = land[:, :CELLS]


def first_kernel(*refs):
    bands_x, (band_z, pick, block, ahead, behind, other) = refs[:COUNTS], refs[COUNTS:-4]
    held, sent, rows, carry = refs[-4:]
    band_x = {band.shape[0]: band for band in bands_x}
    assemble(carry, block, ahead, behind, other)
    section = lax.axis_index("sec")

    @pl.when(section == 0)
    def _():
        vx, vz, sxx, szz, sxz, light, lame, shear = [carry[index] for index in range(8)]
        light = light * (TIME_STEP / SCALE)
        both = (lame + 2.0 * shear) * (TIME_STEP / SCALE)
        lame = lame * (TIME_STEP / SCALE)
        shear = shear * (TIME_STEP / SCALE)
        at = 0
        for step in range(STEPS):
            cut = TRIM[step] - at
            at = TRIM[step]
            vx, vz, sxx, szz, sxz, light, both, lame, shear = trimmed(
                [vx, vz, sxx, szz, sxz, light, both, lame, shear], cut
            )
            parts_xx, parts_zz, parts_xz = halves(sxx), halves(szz), halves(sxz)
            vx = vx + light * (diff_x(band_x, parts_xx) + along_depth(band_z, parts_xz))
            vz = vz + light * (diff_x(band_x, parts_xz) + along_depth(band_z, parts_zz))
            parts_x, parts_z = halves(vx), halves(vz)
            strain_x, strain_z = diff_x(band_x, parts_x), along_depth(band_z, parts_z)
            sxx = sxx + (both * strain_x + lame * strain_z)
            szz = szz + (lame * strain_x + both * strain_z)
            sxz = sxz + shear * (along_depth(band_z, parts_x) + diff_x(band_x, parts_z))
            low = 2 * RADIUS * (step + 1) - at
            for component, (parts, factor) in enumerate(
                ((parts_x, COUPLING), (parts_z, COUPLING), (halves(sxx + szz), -0.5 * COUPLING))
            ):
                picked = factor * along_depth(pick, parts)
                picked = picked[low : picked.shape[0] - low]
                group, base = SLOT[step][component]
                spot = pl.ds(base, picked.shape[0])
                rows[spot] = jnp.where(lanes_of(picked.shape) == group, picked, rows[spot])
        place([vx, vz, sxx, szz, sxz], held, sent)

    @pl.when(section > 0)
    def _():
        vx, vz, pressure, one, two, light, kappa, loss = [carry[index] for index in range(8)]
        light = light * (TIME_STEP / SCALE)
        kappa = kappa * (1.0 / SCALE)
        loss_one = loss * ((1.0 - RELAXATION[0]) * MEMORY_WEIGHT[0])
        loss_two = loss * ((1.0 - RELAXATION[1]) * MEMORY_WEIGHT[1])
        state = [vx, vz, pressure, one, two, light, kappa, loss_one, loss_two]
        for index, array in enumerate(acoustic(state, (band_x, band_z))):
            carry[index] = array


def second_kernel(*refs):
    bands_x, (band_z, land, carry, rows, held_in, sent_in, held, sent) = refs[:COUNTS], refs[COUNTS:]
    band_x = {band.shape[0]: band for band in bands_x}
    section = lax.axis_index("sec")

    @pl.when(section == 0)
    def _():
        held[...] = held_in[...]
        sent[...] = sent_in[...]

    @pl.when(section > 0)
    def _():
        state = [carry[index] for index in range(9)]
        at = 0
        for step in range(STEPS):
            if step:
                state = trimmed(state, TRIM[step] - at)
                at = TRIM[step]
                state = acoustic(state, (band_x, band_z))
            low = 2 * RADIUS * (step + 1) - at
            high = WINDOW - 2 * at - low
            for component in range(3):
                group, base = SLOT[step][component]
                taken = rows[pl.ds(base, high - low)]
                taken = halves(jnp.where(lanes_of(taken.shape) == group, taken, 0.0))
                added = lax.dot_general(
                    jnp.concatenate(taken, axis=1),
                    land[...],
                    (((1,), (1,)), ((), ())),
                    preferred_element_type=jnp.float32,
                )
                array = state[component]
                state[component] = jnp.concatenate(
                    [array[:low], array[low:high] + added, array[high:]], axis=0
                )
        place(state[:5], held, sent)


def last_kernel(held, swapped, out, sems):
    core = lax.axis_index("gz")
    copies = [
        pltpu.make_async_copy(
            source, out.at[:, pl.ds(pl.multiple_of(HALF * half, HALF), HALF)], sems.at[index]
        )
        for index, (source, half) in enumerate(((held, core), (swapped, 1 - core)))
    ]
    for copy in copies:
        copy.start()
    for copy in copies:
        copy.wait()


def call(kernel, outs, operands, flops, place_out=pltpu.VMEM, scratch=()):
    return pl.pallas_call(
        kernel,
        out_shape=outs,
        in_specs=[pl.BlockSpec(memory_space=pltpu.VMEM)] * len(operands),
        out_specs=[pl.BlockSpec(memory_space=place_out)] * len(outs),
        scratch_shapes=scratch,
        compiler_params=pltpu.CompilerParams(vmem_limit_bytes=48 * 1024 * 1024),
        cost_estimate=pl.CostEstimate(
            flops=flops, bytes_accessed=2 * 1024 * 1024, transcendentals=0
        ),
    )(*operands)


def full(*shape):
    return jax.ShapeDtypeStruct(shape, jnp.float32)


def narrow(*shape):
    return jax.ShapeDtypeStruct(shape, jnp.bfloat16)


def local_window(columns, fields, media, plane_rows, box_offset):
    fields, media = fields[0], media[0]
    core = lax.axis_index("gz")
    is_first = core == 0
    block = lax.optimization_barrier(jnp.concatenate([fields, media], axis=0))
    top, bottom = block[:, :HALO], block[:, CELLS - HALO :]
    straight_pairs, crossed_pairs = [], []
    for column in range(columns):
        if column + 1 < columns:
            straight_pairs.append((2 * column, 2 * column + 2))
            crossed_pairs.append((2 * column + 1, 2 * column + 2))
        if column:
            straight_pairs.append((2 * column + 1, 2 * column - 1))
            crossed_pairs.append((2 * column, 2 * column - 1))
    turn = [(0, 1), (1, 0)]
    ahead = lax.ppermute(jnp.where(is_first, bottom, top), ("gx", "gz"), straight_pairs)
    behind = lax.ppermute(jnp.where(is_first, top, bottom), ("gx", "gz"), crossed_pairs)
    other = jnp.where(is_first, block[:, CELLS - PART :], block[:, :PART])
    joined = lax.all_gather(other, "gz")
    other = jnp.where(is_first, joined[1], joined[0])
    *bands, pick, land = call(
        constants_kernel,
        [narrow(count, 2 * count) for count in WINDOWS]
        + [narrow(2 * DEPTH, DEPTH), narrow(2 * DEPTH, CELLS), narrow(DEPTH, 2 * CELLS)],
        [plane_rows[None], box_offset[None]],
        1_000_000_000,
    )
    held, sent, rows, carry = call(
        first_kernel,
        [
            full(5, HALF, CELLS),
            full(5, HALF, CELLS),
            full(ROWS, CELLS),
            full(9, WINDOW, DEPTH),
        ],
        [*bands, pick, block, ahead, behind, other],
        4_000_000_000,
    )
    arrived = [lax.ppermute(rows, "sec", [(0, target)]) for target in (1, 2, 3)]
    rows = arrived[0] + arrived[1] + arrived[2]
    held, sent = call(
        second_kernel,
        [full(5, HALF, CELLS), full(5, HALF, CELLS)],
        [*bands, land, carry, rows, held, sent],
        4_000_000_000,
    )
    swapped = lax.ppermute(sent, "gz", turn)
    (out,) = call(
        last_kernel,
        [full(5, CELLS, CELLS)],
        [held, swapped],
        1000,
        pl.ANY,
        [pltpu.SemaphoreType.DMA((2,))],
    )
    return out[None]


def solution(mesh):
    in_specs = (P("sec", None, "gx", "gz"), P("sec", None, "gx", "gz"), P(), P())
    out_specs = P("sec", None, "gx", "gz")
    if mesh.shape["gz"] == 2:
        local = functools.partial(local_window, mesh.shape["gx"])
    else:
        local = local_stepwise
    return jax.shard_map(local, mesh=mesh, in_specs=in_specs, out_specs=out_specs, check_vma=False)
```

```python
import functools

import jax
import jax.numpy as jnp
from jax import lax
from jax.experimental import pallas as pl
from jax.experimental.pallas import tpu as pltpu
from jax.sharding import PartitionSpec as P

RADIUS = 4
STEPS = 5
NPD = 8

STENCIL = (0.8, -0.2, 4.0 / 105.0, -1.0 / 280.0)
TIME_STEP = 0.2
COUPLING = 0.5
RELAXATION = (0.9, 0.5)
MEMORY_WEIGHT = (0.15, 0.1)


def padded_2(block, sides, width):
    for axis, dim in sides:
        count = lax.axis_size(axis)
        forward = [(i, i + 1) for i in range(count - 1)]
        backward = [(target, source) for source, target in forward]
        low = lax.ppermute(
            lax.slice_in_dim(block, block.shape[dim] - width, None, axis=dim), axis, forward
        )
        high = lax.ppermute(lax.slice_in_dim(block, 0, width, axis=dim), axis, backward)
        block = jnp.concatenate([low, block, high], axis=dim)
    return block


def broadcast(value, axis, source):
    kept = jnp.where(lax.axis_index(axis) == source, value, 0).astype(value.dtype)
    return lax.psum(kept, axis)


def along_x(padded, anchor, count_x, count_z):
    summed = jnp.zeros(padded.shape[:-2] + (count_x, count_z), jnp.float32)
    for offset, stencil_tap in enumerate(STENCIL, 1):
        forward = padded[
            ..., anchor + offset : anchor + offset + count_x, anchor : anchor + count_z
        ]
        backward = padded[
            ..., anchor - offset : anchor - offset + count_x, anchor : anchor + count_z
        ]
        summed = summed + stencil_tap * (forward - backward)
    return summed


def along_z(padded, anchor, count_x, count_z):
    summed = jnp.zeros(padded.shape[:-2] + (count_x, count_z), jnp.float32)
    for offset, stencil_tap in enumerate(STENCIL, 1):
        forward = padded[
            ..., anchor : anchor + count_x, anchor + offset : anchor + offset + count_z
        ]
        backward = padded[
            ..., anchor : anchor + count_x, anchor - offset : anchor - offset + count_z
        ]
        summed = summed + stencil_tap * (forward - backward)
    return summed


def velocity_elastic(velocity, stresses, buoyancy, anchor, count_x, count_z):
    updated_x = velocity[0] + TIME_STEP * buoyancy * (
        along_x(stresses[0], anchor, count_x, count_z)
        + along_z(stresses[2], anchor, count_x, count_z)
    )
    updated_z = velocity[1] + TIME_STEP * buoyancy * (
        along_x(stresses[2], anchor, count_x, count_z)
        + along_z(stresses[1], anchor, count_x, count_z)
    )
    return jnp.stack([updated_x, updated_z])


def velocity_acoustic(velocity, stresses, buoyancy, anchor, count_x, count_z):
    updated_x = velocity[0] - TIME_STEP * buoyancy * along_x(stresses[0], anchor, count_x, count_z)
    updated_z = velocity[1] - TIME_STEP * buoyancy * along_z(stresses[0], anchor, count_x, count_z)
    return jnp.stack([updated_x, updated_z])


def stress_elastic(stresses, velocity_pad, material, anchor, count_x, count_z):
    strain_x = along_x(velocity_pad[0], anchor, count_x, count_z)
    strain_z = along_z(velocity_pad[1], anchor, count_x, count_z)
    strain_shear = along_z(velocity_pad[0], anchor, count_x, count_z) + along_x(
        velocity_pad[1], anchor, count_x, count_z
    )
    lame_first = material[1]
    shear_modulus = material[2]
    normal_x = stresses[0] + TIME_STEP * (
        (lame_first + 2.0 * shear_modulus) * strain_x + lame_first * strain_z
    )
    normal_z = stresses[1] + TIME_STEP * (
        lame_first * strain_x + (lame_first + 2.0 * shear_modulus) * strain_z
    )
    shear_new = stresses[2] + TIME_STEP * shear_modulus * strain_shear
    return jnp.stack([normal_x, normal_z, shear_new])


def stress_acoustic(stresses, velocity_pad, material, anchor, count_x, count_z):
    divergence = along_x(velocity_pad[0], anchor, count_x, count_z) + along_z(
        velocity_pad[1], anchor, count_x, count_z
    )
    loading = material[1] * divergence
    memory_one = (
        RELAXATION[0] * stresses[1]
        + (1.0 - RELAXATION[0]) * MEMORY_WEIGHT[0] * material[2] * loading
    )
    memory_two = (
        RELAXATION[1] * stresses[2]
        + (1.0 - RELAXATION[1]) * MEMORY_WEIGHT[1] * material[2] * loading
    )
    pressure = stresses[0] - TIME_STEP * (loading - memory_one - memory_two)
    return jnp.stack([pressure, memory_one, memory_two])


def local_stepwise(fields, media, plane_rows, box_offset):
    current = fields[0]
    material = media[0]
    count_x = current.shape[1]
    count_z = current.shape[2]
    section = lax.axis_index("sec")
    is_source = section == 0
    block_z = lax.axis_index("gz")
    local_rows = lax.dynamic_slice_in_dim(plane_rows, block_z * NPD, NPD) - block_z * count_z
    offset = lax.dynamic_slice_in_dim(box_offset, jnp.maximum(section - 1, 0), 1)[0]
    depth_ids = block_z * count_z + jnp.arange(count_z, dtype=jnp.int32)
    landing = offset + plane_rows // 2
    chosen = (landing[:, None] == depth_ids[None, :]).astype(jnp.float32)
    for step_index in range(STEPS):
        stress_pad = padded_2(current[2:5], (("gx", 1), ("gz", 2)), RADIUS)
        velocity = lax.cond(
            is_source,
            lambda: velocity_elastic(
                current[0:2], stress_pad, material[0], RADIUS, count_x, count_z
            ),
            lambda: velocity_acoustic(
                current[0:2], stress_pad, material[0], RADIUS, count_x, count_z
            ),
        )
        velocity_pad = padded_2(velocity, (("gx", 1), ("gz", 2)), RADIUS)
        stresses = lax.cond(
            is_source,
            lambda: stress_elastic(current[2:5], velocity_pad, material, RADIUS, count_x, count_z),
            lambda: stress_acoustic(current[2:5], velocity_pad, material, RADIUS, count_x, count_z),
        )
        current = jnp.concatenate([velocity, stresses], axis=0)
        picked = jnp.take(current, local_rows, axis=2)
        block_plane = jnp.transpose(
            jnp.stack([picked[0], picked[1], -0.5 * (picked[2] + picked[3])]), (0, 2, 1)
        )
        joined = lax.all_gather(block_plane, "gz", axis=1, tiled=True)
        gathered = broadcast(joined, "sec", 0)
        injected = jnp.einsum("ckx,kz->cxz", gathered, chosen, precision=lax.Precision.HIGHEST)
        far_state = jnp.concatenate([current[0:3] + COUPLING * injected, current[3:5]], axis=0)
        current = jnp.where(is_source, current, far_state)
    return current[None]


HALO = 2 * RADIUS * STEPS
CELLS = 128
HALF = CELLS // 2
WINDOW = HALF + 2 * HALO
DEPTH = 2 * CELLS
PART = HALF + HALO
NP = 2 * NPD
TRIM = (0, 0, 16, 16, 32)
WINDOWS = [WINDOW - 2 * amount for amount in sorted(set(TRIM))]
COUNTS = len(WINDOWS)
ROWS = 192
GROUPS = CELLS // NP
SLOT = (
    ((0, 0), (1, 0), (2, 0)),
    ((3, 0), (4, 0), (5, 0)),
    ((6, 0), (7, 0), (6, 96)),
    ((3, 112), (4, 112), (5, 112)),
    ((0, 128), (1, 128), (2, 128)),
)
SCALE = 840.0
TAPS = (672.0, -168.0, 32.0, -3.0)


def banded(distance):
    values = jnp.zeros(distance.shape, jnp.float32)
    for offset, tap in enumerate(TAPS, 1):
        values = jnp.where(distance == offset, tap, values)
        values = jnp.where(distance == -offset, -tap, values)
    return values.astype(jnp.bfloat16)


def halves(values):
    high = values.astype(jnp.bfloat16)
    low = (values - high.astype(jnp.float32)).astype(jnp.bfloat16)
    return high, low


def dot(left, right):
    return jnp.dot(left, right, preferred_element_type=jnp.float32)


def diff_x(bands, parts):
    return dot(bands[parts[0].shape[0]][...], jnp.concatenate(parts, axis=0))


def along_depth(matrix, parts):
    return dot(jnp.concatenate(parts, axis=1), matrix[...])


def trimmed(arrays, amount):
    if amount == 0:
        return arrays
    return [array[amount:-amount] for array in arrays]


def lanes_of(shape):
    return lax.broadcasted_iota(jnp.int32, shape, 1) // NP


def assemble(window, block, ahead, behind, other):
    core = lax.axis_index("gz")

    @pl.when(core == 0)
    def _():
        for index in range(8):
            window[index, :HALO, :CELLS] = ahead[index]
            window[index, :HALO, CELLS:] = behind[index]
            window[index, HALO:, :CELLS] = block[index, :PART]
            window[index, HALO:, CELLS:] = other[index]

    @pl.when(core == 1)
    def _():
        for index in range(8):
            window[index, :PART, CELLS:] = block[index, CELLS - PART :]
            window[index, :PART, :CELLS] = other[index]
            window[index, PART:, CELLS:] = ahead[index]
            window[index, PART:, :CELLS] = behind[index]


def place(state, held, sent):
    start = HALO - TRIM[-1]
    core = lax.axis_index("gz")
    state = [array[start : start + HALF] for array in state]

    @pl.when(core == 0)
    def _():
        for index in range(5):
            held[index] = state[index][:, :CELLS]
            sent[index] = state[index][:, CELLS:]

    @pl.when(core == 1)
    def _():
        for index in range(5):
            held[index] = state[index][:, CELLS:]
            sent[index] = state[index][:, :CELLS]


def acoustic(state, bands):
    vx, vz, pressure, one, two, light, kappa, loss_one, loss_two = state
    band_x, band_z = bands
    parts = halves(pressure)
    vx = vx - light * diff_x(band_x, parts)
    vz = vz - light * along_depth(band_z, parts)
    load = kappa * (diff_x(band_x, halves(vx)) + along_depth(band_z, halves(vz)))
    one = RELAXATION[0] * one + loss_one * load
    two = RELAXATION[1] * two + loss_two * load
    pressure = pressure - TIME_STEP * (load - one - two)
    return [vx, vz, pressure, one, two, light, kappa, loss_one, loss_two]


def constants_kernel(plane_rows, box_offset, *targets):
    *bands_x, band_z, pick, land = targets
    for target in bands_x:
        count = target.shape[0]
        row = lax.broadcasted_iota(jnp.int32, target.shape, 0)
        column = lax.broadcasted_iota(jnp.int32, target.shape, 1)
        target[...] = banded(jnp.where(column < count, column, column - count) - row)
    shape = (DEPTH, DEPTH)
    distance = lax.broadcasted_iota(jnp.int32, shape, 0) - lax.broadcasted_iota(jnp.int32, shape, 1)
    band_z[:DEPTH] = banded(distance)
    band_z[DEPTH:] = band_z[:DEPTH]
    row = plane_rows[...]
    lane = lax.broadcasted_iota(jnp.int32, box_offset.shape, 1)
    offset = jnp.where(lane == lax.axis_index("sec") - 1, box_offset[...], 0)
    landing = row // 2 + jnp.sum(offset, axis=1, keepdims=True)
    depth = lax.broadcasted_iota(jnp.int32, (DEPTH, NP), 0)
    spread = lax.broadcasted_iota(jnp.int32, (NP, CELLS), 1) % NP
    spread = spread == lax.broadcasted_iota(jnp.int32, (NP, CELLS), 0)
    spread = jnp.where(spread, 1.0, 0.0).astype(jnp.bfloat16)
    hot = jnp.where(depth == row, 1.0, 0.0).astype(jnp.bfloat16)
    pick[:DEPTH] = dot(hot, spread).astype(jnp.bfloat16)
    pick[DEPTH:] = pick[:DEPTH]
    hot = jnp.where(depth == landing, 1.0, 0.0).astype(jnp.bfloat16)
    land[:, :CELLS] = dot(hot, spread).astype(jnp.bfloat16)
    land[:, CELLS:] = land[:, :CELLS]


def first_kernel(*refs):
    bands_x, (band_z, pick, block, ahead, behind, other) = refs[:COUNTS], refs[COUNTS:-4]
    held, sent, rows, carry = refs[-4:]
    band_x = {band.shape[0]: band for band in bands_x}
    assemble(carry, block, ahead, behind, other)
    section = lax.axis_index("sec")

    @pl.when(section == 0)
    def _():
        vx, vz, sxx, szz, sxz, light, lame, shear = [carry[index] for index in range(8)]
        light = light * (TIME_STEP / SCALE)
        both = (lame + 2.0 * shear) * (TIME_STEP / SCALE)
        lame = lame * (TIME_STEP / SCALE)
        shear = shear * (TIME_STEP / SCALE)
        at = 0
        for step in range(STEPS):
            cut = TRIM[step] - at
            at = TRIM[step]
            vx, vz, sxx, szz, sxz, light, both, lame, shear = trimmed(
                [vx, vz, sxx, szz, sxz, light, both, lame, shear], cut
            )
            parts_xx, parts_zz, parts_xz = halves(sxx), halves(szz), halves(sxz)
            vx = vx + light * (diff_x(band_x, parts_xx) + along_depth(band_z, parts_xz))
            vz = vz + light * (diff_x(band_x, parts_xz) + along_depth(band_z, parts_zz))
            parts_x, parts_z = halves(vx), halves(vz)
            strain_x, strain_z = diff_x(band_x, parts_x), along_depth(band_z, parts_z)
            sxx = sxx + (both * strain_x + lame * strain_z)
            szz = szz + (lame * strain_x + both * strain_z)
            sxz = sxz + shear * (along_depth(band_z, parts_x) + diff_x(band_x, parts_z))
            low = 2 * RADIUS * (step + 1) - at
            for component, (parts, factor) in enumerate(
                ((parts_x, COUPLING), (parts_z, COUPLING), (halves(sxx + szz), -0.5 * COUPLING))
            ):
                picked = factor * along_depth(pick, parts)
                picked = picked[low : picked.shape[0] - low]
                group, base = SLOT[step][component]
                spot = pl.ds(base, picked.shape[0])
                rows[spot] = jnp.where(lanes_of(picked.shape) == group, picked, rows[spot])
        place([vx, vz, sxx, szz, sxz], held, sent)

    @pl.when(section > 0)
    def _():
        vx, vz, pressure, one, two, light, kappa, loss = [carry[index] for index in range(8)]
        light = light * (TIME_STEP / SCALE)
        kappa = kappa * (1.0 / SCALE)
        loss_one = loss * ((1.0 - RELAXATION[0]) * MEMORY_WEIGHT[0])
        loss_two = loss * ((1.0 - RELAXATION[1]) * MEMORY_WEIGHT[1])
        state = [vx, vz, pressure, one, two, light, kappa, loss_one, loss_two]
        for index, array in enumerate(acoustic(state, (band_x, band_z))):
            carry[index] = array


def second_kernel(*refs):
    bands_x, (band_z, land, carry, rows, held_in, sent_in, held, sent) = refs[:COUNTS], refs[COUNTS:]
    band_x = {band.shape[0]: band for band in bands_x}
    section = lax.axis_index("sec")

    @pl.when(section == 0)
    def _():
        held[...] = held_in[...]
        sent[...] = sent_in[...]

    @pl.when(section > 0)
    def _():
        state = [carry[index] for index in range(9)]
        at = 0
        for step in range(STEPS):
            if step:
                state = trimmed(state, TRIM[step] - at)
                at = TRIM[step]
                state = acoustic(state, (band_x, band_z))
            low = 2 * RADIUS * (step + 1) - at
            high = WINDOW - 2 * at - low
            for component in range(3):
                group, base = SLOT[step][component]
                taken = rows[pl.ds(base, high - low)]
                taken = halves(jnp.where(lanes_of(taken.shape) == group, taken, 0.0))
                added = lax.dot_general(
                    jnp.concatenate(taken, axis=1),
                    land[...],
                    (((1,), (1,)), ((), ())),
                    preferred_element_type=jnp.float32,
                )
                array = state[component]
                state[component] = jnp.concatenate(
                    [array[:low], array[low:high] + added, array[high:]], axis=0
                )
        place(state[:5], held, sent)


def last_kernel(held, swapped, out, sems):
    core = lax.axis_index("gz")
    copies = [
        pltpu.make_async_copy(
            source, out.at[:, pl.ds(pl.multiple_of(HALF * half, HALF), HALF)], sems.at[index]
        )
        for index, (source, half) in enumerate(((held, core), (swapped, 1 - core)))
    ]
    for copy in copies:
        copy.start()
    for copy in copies:
        copy.wait()


def call(kernel, outs, operands, flops, place_out=pltpu.VMEM, scratch=()):
    return pl.pallas_call(
        kernel,
        out_shape=outs,
        in_specs=[pl.BlockSpec(memory_space=pltpu.VMEM)] * len(operands),
        out_specs=[pl.BlockSpec(memory_space=place_out)] * len(outs),
        scratch_shapes=scratch,
        compiler_params=pltpu.CompilerParams(vmem_limit_bytes=48 * 1024 * 1024),
        cost_estimate=pl.CostEstimate(
            flops=flops, bytes_accessed=2 * 1024 * 1024, transcendentals=0
        ),
    )(*operands)


def full(*shape):
    return jax.ShapeDtypeStruct(shape, jnp.float32)


def narrow(*shape):
    return jax.ShapeDtypeStruct(shape, jnp.bfloat16)


def local_window(columns, fields, media, plane_rows, box_offset):
    fields, media = fields[0], media[0]
    core = lax.axis_index("gz")
    is_first = core == 0
    block = lax.optimization_barrier(jnp.concatenate([fields, media], axis=0))
    top, bottom = block[:, :HALO], block[:, CELLS - HALO :]
    straight_pairs, crossed_pairs = [], []
    for column in range(columns):
        if column + 1 < columns:
            straight_pairs.append((2 * column, 2 * column + 2))
            crossed_pairs.append((2 * column + 1, 2 * column + 2))
        if column:
            straight_pairs.append((2 * column + 1, 2 * column - 1))
            crossed_pairs.append((2 * column, 2 * column - 1))
    turn = [(0, 1), (1, 0)]
    ahead = lax.ppermute(jnp.where(is_first, bottom, top), ("gx", "gz"), straight_pairs)
    behind = lax.ppermute(jnp.where(is_first, top, bottom), ("gx", "gz"), crossed_pairs)
    other = jnp.where(is_first, block[:, CELLS - PART :], block[:, :PART])
    joined = lax.all_gather(other, "gz")
    other = jnp.where(is_first, joined[1], joined[0])
    *bands, pick, land = call(
        constants_kernel,
        [narrow(count, 2 * count) for count in WINDOWS]
        + [narrow(2 * DEPTH, DEPTH), narrow(2 * DEPTH, CELLS), narrow(DEPTH, 2 * CELLS)],
        [plane_rows[None], box_offset[None]],
        1_000_000_000,
    )
    held, sent, rows, carry = call(
        first_kernel,
        [
            full(5, HALF, CELLS),
            full(5, HALF, CELLS),
            full(ROWS, CELLS),
            full(9, WINDOW, DEPTH),
        ],
        [*bands, pick, block, ahead, behind, other],
        4_000_000_000,
    )
    rows = lax.all_gather(rows, "sec")[0]
    held, sent = call(
        second_kernel,
        [full(5, HALF, CELLS), full(5, HALF, CELLS)],
        [*bands, land, carry, rows, held, sent],
        4_000_000_000,
    )
    swapped = lax.ppermute(sent, "gz", turn)
    (out,) = call(
        last_kernel,
        [full(5, CELLS, CELLS)],
        [held, swapped],
        1000,
        pl.ANY,
        [pltpu.SemaphoreType.DMA((2,))],
    )
    return out[None]


def solution(mesh):
    in_specs = (P("sec", None, "gx", "gz"), P("sec", None, "gx", "gz"), P(), P())
    out_specs = P("sec", None, "gx", "gz")
    if mesh.shape["gz"] == 2:
        local = functools.partial(local_window, mesh.shape["gx"])
    else:
        local = local_stepwise
    return jax.shard_map(local, mesh=mesh, in_specs=in_specs, out_specs=out_specs, check_vma=False)
```

```python
import functools

import jax
import jax.numpy as jnp
from jax import lax
from jax.experimental import pallas as pl
from jax.experimental.pallas import tpu as pltpu
from jax.sharding import PartitionSpec as P

RADIUS = 4
STEPS = 5
NPD = 8

STENCIL = (0.8, -0.2, 4.0 / 105.0, -1.0 / 280.0)
TIME_STEP = 0.2
COUPLING = 0.5
RELAXATION = (0.9, 0.5)
MEMORY_WEIGHT = (0.15, 0.1)


def padded_2(block, sides, width):
    for axis, dim in sides:
        count = lax.axis_size(axis)
        forward = [(i, i + 1) for i in range(count - 1)]
        backward = [(target, source) for source, target in forward]
        low = lax.ppermute(
            lax.slice_in_dim(block, block.shape[dim] - width, None, axis=dim), axis, forward
        )
        high = lax.ppermute(lax.slice_in_dim(block, 0, width, axis=dim), axis, backward)
        block = jnp.concatenate([low, block, high], axis=dim)
    return block


def broadcast(value, axis, source):
    kept = jnp.where(lax.axis_index(axis) == source, value, 0).astype(value.dtype)
    return lax.psum(kept, axis)


def along_x(padded, anchor, count_x, count_z):
    summed = jnp.zeros(padded.shape[:-2] + (count_x, count_z), jnp.float32)
    for offset, stencil_tap in enumerate(STENCIL, 1):
        forward = padded[
            ..., anchor + offset : anchor + offset + count_x, anchor : anchor + count_z
        ]
        backward = padded[
            ..., anchor - offset : anchor - offset + count_x, anchor : anchor + count_z
        ]
        summed = summed + stencil_tap * (forward - backward)
    return summed


def along_z(padded, anchor, count_x, count_z):
    summed = jnp.zeros(padded.shape[:-2] + (count_x, count_z), jnp.float32)
    for offset, stencil_tap in enumerate(STENCIL, 1):
        forward = padded[
            ..., anchor : anchor + count_x, anchor + offset : anchor + offset + count_z
        ]
        backward = padded[
            ..., anchor : anchor + count_x, anchor - offset : anchor - offset + count_z
        ]
        summed = summed + stencil_tap * (forward - backward)
    return summed


def velocity_elastic(velocity, stresses, buoyancy, anchor, count_x, count_z):
    updated_x = velocity[0] + TIME_STEP * buoyancy * (
        along_x(stresses[0], anchor, count_x, count_z)
        + along_z(stresses[2], anchor, count_x, count_z)
    )
    updated_z = velocity[1] + TIME_STEP * buoyancy * (
        along_x(stresses[2], anchor, count_x, count_z)
        + along_z(stresses[1], anchor, count_x, count_z)
    )
    return jnp.stack([updated_x, updated_z])


def velocity_acoustic(velocity, stresses, buoyancy, anchor, count_x, count_z):
    updated_x = velocity[0] - TIME_STEP * buoyancy * along_x(stresses[0], anchor, count_x, count_z)
    updated_z = velocity[1] - TIME_STEP * buoyancy * along_z(stresses[0], anchor, count_x, count_z)
    return jnp.stack([updated_x, updated_z])


def stress_elastic(stresses, velocity_pad, material, anchor, count_x, count_z):
    strain_x = along_x(velocity_pad[0], anchor, count_x, count_z)
    strain_z = along_z(velocity_pad[1], anchor, count_x, count_z)
    strain_shear = along_z(velocity_pad[0], anchor, count_x, count_z) + along_x(
        velocity_pad[1], anchor, count_x, count_z
    )
    lame_first = material[1]
    shear_modulus = material[2]
    normal_x = stresses[0] + TIME_STEP * (
        (lame_first + 2.0 * shear_modulus) * strain_x + lame_first * strain_z
    )
    normal_z = stresses[1] + TIME_STEP * (
        lame_first * strain_x + (lame_first + 2.0 * shear_modulus) * strain_z
    )
    shear_new = stresses[2] + TIME_STEP * shear_modulus * strain_shear
    return jnp.stack([normal_x, normal_z, shear_new])


def stress_acoustic(stresses, velocity_pad, material, anchor, count_x, count_z):
    divergence = along_x(velocity_pad[0], anchor, count_x, count_z) + along_z(
        velocity_pad[1], anchor, count_x, count_z
    )
    loading = material[1] * divergence
    memory_one = (
        RELAXATION[0] * stresses[1]
        + (1.0 - RELAXATION[0]) * MEMORY_WEIGHT[0] * material[2] * loading
    )
    memory_two = (
        RELAXATION[1] * stresses[2]
        + (1.0 - RELAXATION[1]) * MEMORY_WEIGHT[1] * material[2] * loading
    )
    pressure = stresses[0] - TIME_STEP * (loading - memory_one - memory_two)
    return jnp.stack([pressure, memory_one, memory_two])


def local_stepwise(fields, media, plane_rows, box_offset):
    current = fields[0]
    material = media[0]
    count_x = current.shape[1]
    count_z = current.shape[2]
    section = lax.axis_index("sec")
    is_source = section == 0
    block_z = lax.axis_index("gz")
    local_rows = lax.dynamic_slice_in_dim(plane_rows, block_z * NPD, NPD) - block_z * count_z
    offset = lax.dynamic_slice_in_dim(box_offset, jnp.maximum(section - 1, 0), 1)[0]
    depth_ids = block_z * count_z + jnp.arange(count_z, dtype=jnp.int32)
    landing = offset + plane_rows // 2
    chosen = (landing[:, None] == depth_ids[None, :]).astype(jnp.float32)
    for step_index in range(STEPS):
        stress_pad = padded_2(current[2:5], (("gx", 1), ("gz", 2)), RADIUS)
        velocity = lax.cond(
            is_source,
            lambda: velocity_elastic(
                current[0:2], stress_pad, material[0], RADIUS, count_x, count_z
            ),
            lambda: velocity_acoustic(
                current[0:2], stress_pad, material[0], RADIUS, count_x, count_z
            ),
        )
        velocity_pad = padded_2(velocity, (("gx", 1), ("gz", 2)), RADIUS)
        stresses = lax.cond(
            is_source,
            lambda: stress_elastic(current[2:5], velocity_pad, material, RADIUS, count_x, count_z),
            lambda: stress_acoustic(current[2:5], velocity_pad, material, RADIUS, count_x, count_z),
        )
        current = jnp.concatenate([velocity, stresses], axis=0)
        picked = jnp.take(current, local_rows, axis=2)
        block_plane = jnp.transpose(
            jnp.stack([picked[0], picked[1], -0.5 * (picked[2] + picked[3])]), (0, 2, 1)
        )
        joined = lax.all_gather(block_plane, "gz", axis=1, tiled=True)
        gathered = broadcast(joined, "sec", 0)
        injected = jnp.einsum("ckx,kz->cxz", gathered, chosen, precision=lax.Precision.HIGHEST)
        far_state = jnp.concatenate([current[0:3] + COUPLING * injected, current[3:5]], axis=0)
        current = jnp.where(is_source, current, far_state)
    return current[None]


HALO = 2 * RADIUS * STEPS
CELLS = 128
HALF = CELLS // 2
WINDOW = HALF + 2 * HALO
DEPTH = 2 * CELLS
PART = HALF + HALO
NP = 2 * NPD
TRIM = (0, 8, 16, 24, 32)
WINDOWS = [WINDOW - 2 * amount for amount in TRIM]
COUNTS = len(WINDOWS)
ROWS = 192
GROUPS = CELLS // NP
SLOT = (
    ((0, 0), (1, 0), (2, 0)),
    ((3, 0), (4, 0), (5, 0)),
    ((6, 0), (7, 0), (6, 96)),
    ((3, 112), (4, 112), (5, 112)),
    ((0, 128), (1, 128), (2, 128)),
)
SCALE = 840.0
TAPS = (672.0, -168.0, 32.0, -3.0)


def banded(distance):
    values = jnp.zeros(distance.shape, jnp.float32)
    for offset, tap in enumerate(TAPS, 1):
        values = jnp.where(distance == offset, tap, values)
        values = jnp.where(distance == -offset, -tap, values)
    return values.astype(jnp.bfloat16)


def halves(values):
    high = values.astype(jnp.bfloat16)
    low = (values - high.astype(jnp.float32)).astype(jnp.bfloat16)
    return high, low


def dot(left, right):
    return jnp.dot(left, right, preferred_element_type=jnp.float32)


def diff_x(bands, parts):
    return dot(bands[parts[0].shape[0]][...], jnp.concatenate(parts, axis=0))


def along_depth(matrix, parts):
    return dot(jnp.concatenate(parts, axis=1), matrix[...])


def trimmed(arrays, amount):
    if amount == 0:
        return arrays
    return [array[amount:-amount] for array in arrays]


def lanes_of(shape):
    return lax.broadcasted_iota(jnp.int32, shape, 1) // NP


BODY = HALO - 8
WHOLE = (2, 4)
PAIRED = ((0, 1), (3, 5))
EDGE_ROWS = 8 * BODY + 8 * len(WHOLE) + 8 * len(PAIRED)


def pack_edge(block, target, at_end):
    body, rest = (CELLS - BODY, CELLS - HALO) if at_end else (0, BODY)
    near = lax.broadcasted_iota(jnp.int32, (8, CELLS), 0) // 4 == int(at_end)
    for index in range(8):
        target[BODY * index : BODY * (index + 1)] = block[index, body : body + BODY]
    row = 8 * BODY
    for index in WHOLE:
        target[row : row + 8] = block[index, rest : rest + 8]
        row += 8
    for one, two in PAIRED:
        turned = pltpu.roll(block[two, rest : rest + 8], 4, 0)
        target[row : row + 8] = jnp.where(near, block[one, rest : rest + 8], turned)
        row += 8


def unpack_edge(edge, window, lanes, before):
    body, rest = (8, 0) if before else (PART, WINDOW - 8)
    near = lax.broadcasted_iota(jnp.int32, (8, CELLS), 0) // 4 == int(before)
    for index in range(8):
        window[index, body : body + BODY, lanes] = edge[BODY * index : BODY * (index + 1)]
    row = 8 * BODY
    for index in WHOLE:
        window[index, rest : rest + 8, lanes] = edge[row : row + 8]
        row += 8
    for one, two in PAIRED:
        tile = edge[row : row + 8]
        window[one, rest : rest + 8, lanes] = jnp.where(near, tile, 0.0)
        window[two, rest : rest + 8, lanes] = jnp.where(near, pltpu.roll(tile, 4, 0), 0.0)
        row += 8
    for index in (6, 7):
        window[index, rest : rest + 8, lanes] = jnp.zeros((8, CELLS), jnp.float32)


def pack_kernel(block, straight, crossed, swap):
    core = lax.axis_index("gz")

    @pl.when(core == 0)
    def _():
        pack_edge(block, straight, True)
        pack_edge(block, crossed, False)
        swap[...] = block[:, CELLS - PART :]

    @pl.when(core == 1)
    def _():
        pack_edge(block, straight, False)
        pack_edge(block, crossed, True)
        swap[...] = block[:, :PART]


def assemble(window, block, ahead, behind, other):
    core = lax.axis_index("gz")
    low, high = slice(0, CELLS), slice(CELLS, DEPTH)

    @pl.when(core == 0)
    def _():
        unpack_edge(ahead, window, low, True)
        unpack_edge(behind, window, high, True)
        window[:8, HALO:, low] = block[:, :PART]
        window[:8, HALO:, high] = other[...]

    @pl.when(core == 1)
    def _():
        window[:8, :PART, high] = block[:, CELLS - PART :]
        window[:8, :PART, low] = other[...]
        unpack_edge(ahead, window, high, False)
        unpack_edge(behind, window, low, False)


def place(state, held, sent):
    start = HALO - TRIM[-1]
    core = lax.axis_index("gz")
    state = [array[start : start + HALF] for array in state]

    @pl.when(core == 0)
    def _():
        for index in range(5):
            held[index] = state[index][:, :CELLS]
            sent[index] = state[index][:, CELLS:]

    @pl.when(core == 1)
    def _():
        for index in range(5):
            held[index] = state[index][:, CELLS:]
            sent[index] = state[index][:, :CELLS]


def acoustic(state, bands):
    vx, vz, pressure, one, two, light, kappa, loss_one, loss_two = state
    band_x, band_z = bands
    parts = halves(pressure)
    vx = vx - light * diff_x(band_x, parts)
    vz = vz - light * along_depth(band_z, parts)
    load = kappa * (diff_x(band_x, halves(vx)) + along_depth(band_z, halves(vz)))
    one = RELAXATION[0] * one + loss_one * load
    two = RELAXATION[1] * two + loss_two * load
    pressure = pressure - TIME_STEP * (load - one - two)
    return [vx, vz, pressure, one, two, light, kappa, loss_one, loss_two]


def constants_kernel(plane_rows, box_offset, *targets):
    *bands_x, band_z, pick, land = targets
    for target in bands_x:
        count = target.shape[0]
        row = lax.broadcasted_iota(jnp.int32, target.shape, 0)
        column = lax.broadcasted_iota(jnp.int32, target.shape, 1)
        target[...] = banded(jnp.where(column < count, column, column - count) - row)
    shape = (DEPTH, DEPTH)
    distance = lax.broadcasted_iota(jnp.int32, shape, 0) - lax.broadcasted_iota(jnp.int32, shape, 1)
    band_z[:DEPTH] = banded(distance)
    band_z[DEPTH:] = band_z[:DEPTH]
    row = plane_rows[...]
    lane = lax.broadcasted_iota(jnp.int32, box_offset.shape, 1)
    offset = jnp.where(lane == lax.axis_index("sec") - 1, box_offset[...], 0)
    landing = row // 2 + jnp.sum(offset, axis=1, keepdims=True)
    depth = lax.broadcasted_iota(jnp.int32, (DEPTH, NP), 0)
    spread = lax.broadcasted_iota(jnp.int32, (NP, CELLS), 1) % NP
    spread = spread == lax.broadcasted_iota(jnp.int32, (NP, CELLS), 0)
    spread = jnp.where(spread, 1.0, 0.0).astype(jnp.bfloat16)
    hot = jnp.where(depth == row, 1.0, 0.0).astype(jnp.bfloat16)
    pick[:DEPTH] = dot(hot, spread).astype(jnp.bfloat16)
    pick[DEPTH:] = pick[:DEPTH]
    hot = jnp.where(depth == landing, 1.0, 0.0).astype(jnp.bfloat16)
    land[:, :CELLS] = dot(hot, spread).astype(jnp.bfloat16)
    land[:, CELLS:] = land[:, :CELLS]


def first_kernel(*refs):
    bands_x, (band_z, pick, block, ahead, behind, other) = refs[:COUNTS], refs[COUNTS:-4]
    held, sent, rows, carry = refs[-4:]
    band_x = {band.shape[0]: band for band in bands_x}
    assemble(carry, block, ahead, behind, other)
    section = lax.axis_index("sec")

    @pl.when(section == 0)
    def _():
        vx, vz, sxx, szz, sxz, light, lame, shear = [carry[index] for index in range(8)]
        light = light * (TIME_STEP / SCALE)
        both = (lame + 2.0 * shear) * (TIME_STEP / SCALE)
        lame = lame * (TIME_STEP / SCALE)
        shear = shear * (TIME_STEP / SCALE)
        at = 0
        for step in range(STEPS):
            cut = TRIM[step] - at
            at = TRIM[step]
            vx, vz, sxx, szz, sxz, light, both, lame, shear = trimmed(
                [vx, vz, sxx, szz, sxz, light, both, lame, shear], cut
            )
            parts_xx, parts_zz, parts_xz = halves(sxx), halves(szz), halves(sxz)
            vx = vx + light * (diff_x(band_x, parts_xx) + along_depth(band_z, parts_xz))
            vz = vz + light * (diff_x(band_x, parts_xz) + along_depth(band_z, parts_zz))
            parts_x, parts_z = halves(vx), halves(vz)
            strain_x, strain_z = diff_x(band_x, parts_x), along_depth(band_z, parts_z)
            sxx = sxx + (both * strain_x + lame * strain_z)
            szz = szz + (lame * strain_x + both * strain_z)
            sxz = sxz + shear * (along_depth(band_z, parts_x) + diff_x(band_x, parts_z))
            low = 2 * RADIUS * (step + 1) - at
            for component, (parts, factor) in enumerate(
                ((parts_x, COUPLING), (parts_z, COUPLING), (halves(sxx + szz), -0.5 * COUPLING))
            ):
                picked = factor * along_depth(pick, parts)
                picked = picked[low : picked.shape[0] - low]
                group, base = SLOT[step][component]
                spot = pl.ds(base, picked.shape[0])
                rows[spot] = jnp.where(lanes_of(picked.shape) == group, picked, rows[spot])
        place([vx, vz, sxx, szz, sxz], held, sent)

    @pl.when(section > 0)
    def _():
        vx, vz, pressure, one, two, light, kappa, loss = [carry[index] for index in range(8)]
        light = light * (TIME_STEP / SCALE)
        kappa = kappa * (1.0 / SCALE)
        loss_one = loss * ((1.0 - RELAXATION[0]) * MEMORY_WEIGHT[0])
        loss_two = loss * ((1.0 - RELAXATION[1]) * MEMORY_WEIGHT[1])
        state = [vx, vz, pressure, one, two, light, kappa, loss_one, loss_two]
        for index, array in enumerate(acoustic(state, (band_x, band_z))):
            carry[index] = array


def second_kernel(*refs):
    bands_x, (band_z, land, carry, rows, held_in, sent_in, held, sent) = refs[:COUNTS], refs[COUNTS:]
    band_x = {band.shape[0]: band for band in bands_x}
    section = lax.axis_index("sec")

    @pl.when(section == 0)
    def _():
        held[...] = held_in[...]
        sent[...] = sent_in[...]

    @pl.when(section > 0)
    def _():
        state = [carry[index] for index in range(9)]
        at = 0
        for step in range(STEPS):
            if step:
                state = trimmed(state, TRIM[step] - at)
                at = TRIM[step]
                state = acoustic(state, (band_x, band_z))
            low = 2 * RADIUS * (step + 1) - at
            high = WINDOW - 2 * at - low
            for component in range(3):
                group, base = SLOT[step][component]
                taken = rows[pl.ds(base, high - low)]
                taken = halves(jnp.where(lanes_of(taken.shape) == group, taken, 0.0))
                added = lax.dot_general(
                    jnp.concatenate(taken, axis=1),
                    land[...],
                    (((1,), (1,)), ((), ())),
                    preferred_element_type=jnp.float32,
                )
                array = state[component]
                state[component] = jnp.concatenate(
                    [array[:low], array[low:high] + added, array[high:]], axis=0
                )
        place(state[:5], held, sent)


def last_kernel(held, swapped, out, sems):
    core = lax.axis_index("gz")
    copies = [
        pltpu.make_async_copy(
            source, out.at[:, pl.ds(pl.multiple_of(HALF * half, HALF), HALF)], sems.at[index]
        )
        for index, (source, half) in enumerate(((held, core), (swapped, 1 - core)))
    ]
    for copy in copies:
        copy.start()
    for copy in copies:
        copy.wait()


def call(kernel, outs, operands, flops, place_out=pltpu.VMEM, scratch=()):
    return pl.pallas_call(
        kernel,
        out_shape=outs,
        in_specs=[pl.BlockSpec(memory_space=pltpu.VMEM)] * len(operands),
        out_specs=[pl.BlockSpec(memory_space=place_out)] * len(outs),
        scratch_shapes=scratch,
        compiler_params=pltpu.CompilerParams(vmem_limit_bytes=48 * 1024 * 1024),
        cost_estimate=pl.CostEstimate(
            flops=flops, bytes_accessed=2 * 1024 * 1024, transcendentals=0
        ),
    )(*operands)


def full(*shape):
    return jax.ShapeDtypeStruct(shape, jnp.float32)


def narrow(*shape):
    return jax.ShapeDtypeStruct(shape, jnp.bfloat16)


def local_window(columns, fields, media, plane_rows, box_offset):
    fields, media = fields[0], media[0]
    core = lax.axis_index("gz")
    is_first = core == 0
    block = lax.optimization_barrier(jnp.concatenate([fields, media], axis=0))
    straight, crossed, swap = call(
        pack_kernel,
        [full(EDGE_ROWS, CELLS), full(EDGE_ROWS, CELLS), full(8, PART, CELLS)],
        [block],
        1000,
    )
    straight_pairs, crossed_pairs = [], []
    for column in range(columns):
        if column + 1 < columns:
            straight_pairs.append((2 * column, 2 * column + 2))
            crossed_pairs.append((2 * column + 1, 2 * column + 2))
        if column:
            straight_pairs.append((2 * column + 1, 2 * column - 1))
            crossed_pairs.append((2 * column, 2 * column - 1))
    turn = [(0, 1), (1, 0)]
    ahead = lax.ppermute(straight, ("gx", "gz"), straight_pairs)
    behind = lax.ppermute(crossed, ("gx", "gz"), crossed_pairs)
    joined = lax.all_gather(swap, "gz")
    other = jnp.where(is_first, joined[1], joined[0])
    *bands, pick, land = call(
        constants_kernel,
        [narrow(count, 2 * count) for count in WINDOWS]
        + [narrow(2 * DEPTH, DEPTH), narrow(2 * DEPTH, CELLS), narrow(DEPTH, 2 * CELLS)],
        [plane_rows[None], box_offset[None]],
        1_000_000_000,
    )
    held, sent, rows, carry = call(
        first_kernel,
        [
            full(5, HALF, CELLS),
            full(5, HALF, CELLS),
            full(ROWS, CELLS),
            full(9, WINDOW, DEPTH),
        ],
        [*bands, pick, block, ahead, behind, other],
        4_000_000_000,
    )
    arrived = [lax.ppermute(rows, "sec", [(0, target)]) for target in (1, 2, 3)]
    rows = arrived[0] + arrived[1] + arrived[2]
    held, sent = call(
        second_kernel,
        [full(5, HALF, CELLS), full(5, HALF, CELLS)],
        [*bands, land, carry, rows, held, sent],
        4_000_000_000,
    )
    swapped = lax.ppermute(sent, "gz", turn)
    (out,) = call(
        last_kernel,
        [full(5, CELLS, CELLS)],
        [held, swapped],
        1000,
        pl.ANY,
        [pltpu.SemaphoreType.DMA((2,))],
    )
    return out[None]


def solution(mesh):
    in_specs = (P("sec", None, "gx", "gz"), P("sec", None, "gx", "gz"), P(), P())
    out_specs = P("sec", None, "gx", "gz")
    if mesh.shape["gz"] == 2:
        local = functools.partial(local_window, mesh.shape["gx"])
    else:
        local = local_stepwise
    return jax.shard_map(local, mesh=mesh, in_specs=in_specs, out_specs=out_specs, check_vma=False)
```

```python
import functools

import jax
import jax.numpy as jnp
from jax import lax
from jax.experimental import pallas as pl
from jax.experimental.pallas import tpu as pltpu
from jax.sharding import PartitionSpec as P

RADIUS = 4
STEPS = 5
NPD = 8

STENCIL = (0.8, -0.2, 4.0 / 105.0, -1.0 / 280.0)
TIME_STEP = 0.2
COUPLING = 0.5
RELAXATION = (0.9, 0.5)
MEMORY_WEIGHT = (0.15, 0.1)


def padded_2(block, sides, width):
    for axis, dim in sides:
        count = lax.axis_size(axis)
        forward = [(i, i + 1) for i in range(count - 1)]
        backward = [(target, source) for source, target in forward]
        low = lax.ppermute(
            lax.slice_in_dim(block, block.shape[dim] - width, None, axis=dim), axis, forward
        )
        high = lax.ppermute(lax.slice_in_dim(block, 0, width, axis=dim), axis, backward)
        block = jnp.concatenate([low, block, high], axis=dim)
    return block


def broadcast(value, axis, source):
    kept = jnp.where(lax.axis_index(axis) == source, value, 0).astype(value.dtype)
    return lax.psum(kept, axis)


def along_x(padded, anchor, count_x, count_z):
    summed = jnp.zeros(padded.shape[:-2] + (count_x, count_z), jnp.float32)
    for offset, stencil_tap in enumerate(STENCIL, 1):
        forward = padded[
            ..., anchor + offset : anchor + offset + count_x, anchor : anchor + count_z
        ]
        backward = padded[
            ..., anchor - offset : anchor - offset + count_x, anchor : anchor + count_z
        ]
        summed = summed + stencil_tap * (forward - backward)
    return summed


def along_z(padded, anchor, count_x, count_z):
    summed = jnp.zeros(padded.shape[:-2] + (count_x, count_z), jnp.float32)
    for offset, stencil_tap in enumerate(STENCIL, 1):
        forward = padded[
            ..., anchor : anchor + count_x, anchor + offset : anchor + offset + count_z
        ]
        backward = padded[
            ..., anchor : anchor + count_x, anchor - offset : anchor - offset + count_z
        ]
        summed = summed + stencil_tap * (forward - backward)
    return summed


def velocity_elastic(velocity, stresses, buoyancy, anchor, count_x, count_z):
    updated_x = velocity[0] + TIME_STEP * buoyancy * (
        along_x(stresses[0], anchor, count_x, count_z)
        + along_z(stresses[2], anchor, count_x, count_z)
    )
    updated_z = velocity[1] + TIME_STEP * buoyancy * (
        along_x(stresses[2], anchor, count_x, count_z)
        + along_z(stresses[1], anchor, count_x, count_z)
    )
    return jnp.stack([updated_x, updated_z])


def velocity_acoustic(velocity, stresses, buoyancy, anchor, count_x, count_z):
    updated_x = velocity[0] - TIME_STEP * buoyancy * along_x(stresses[0], anchor, count_x, count_z)
    updated_z = velocity[1] - TIME_STEP * buoyancy * along_z(stresses[0], anchor, count_x, count_z)
    return jnp.stack([updated_x, updated_z])


def stress_elastic(stresses, velocity_pad, material, anchor, count_x, count_z):
    strain_x = along_x(velocity_pad[0], anchor, count_x, count_z)
    strain_z = along_z(velocity_pad[1], anchor, count_x, count_z)
    strain_shear = along_z(velocity_pad[0], anchor, count_x, count_z) + along_x(
        velocity_pad[1], anchor, count_x, count_z
    )
    lame_first = material[1]
    shear_modulus = material[2]
    normal_x = stresses[0] + TIME_STEP * (
        (lame_first + 2.0 * shear_modulus) * strain_x + lame_first * strain_z
    )
    normal_z = stresses[1] + TIME_STEP * (
        lame_first * strain_x + (lame_first + 2.0 * shear_modulus) * strain_z
    )
    shear_new = stresses[2] + TIME_STEP * shear_modulus * strain_shear
    return jnp.stack([normal_x, normal_z, shear_new])


def stress_acoustic(stresses, velocity_pad, material, anchor, count_x, count_z):
    divergence = along_x(velocity_pad[0], anchor, count_x, count_z) + along_z(
        velocity_pad[1], anchor, count_x, count_z
    )
    loading = material[1] * divergence
    memory_one = (
        RELAXATION[0] * stresses[1]
        + (1.0 - RELAXATION[0]) * MEMORY_WEIGHT[0] * material[2] * loading
    )
    memory_two = (
        RELAXATION[1] * stresses[2]
        + (1.0 - RELAXATION[1]) * MEMORY_WEIGHT[1] * material[2] * loading
    )
    pressure = stresses[0] - TIME_STEP * (loading - memory_one - memory_two)
    return jnp.stack([pressure, memory_one, memory_two])


def local_stepwise(fields, media, plane_rows, box_offset):
    current = fields[0]
    material = media[0]
    count_x = current.shape[1]
    count_z = current.shape[2]
    section = lax.axis_index("sec")
    is_source = section == 0
    block_z = lax.axis_index("gz")
    local_rows = lax.dynamic_slice_in_dim(plane_rows, block_z * NPD, NPD) - block_z * count_z
    offset = lax.dynamic_slice_in_dim(box_offset, jnp.maximum(section - 1, 0), 1)[0]
    depth_ids = block_z * count_z + jnp.arange(count_z, dtype=jnp.int32)
    landing = offset + plane_rows // 2
    chosen = (landing[:, None] == depth_ids[None, :]).astype(jnp.float32)
    for step_index in range(STEPS):
        stress_pad = padded_2(current[2:5], (("gx", 1), ("gz", 2)), RADIUS)
        velocity = lax.cond(
            is_source,
            lambda: velocity_elastic(
                current[0:2], stress_pad, material[0], RADIUS, count_x, count_z
            ),
            lambda: velocity_acoustic(
                current[0:2], stress_pad, material[0], RADIUS, count_x, count_z
            ),
        )
        velocity_pad = padded_2(velocity, (("gx", 1), ("gz", 2)), RADIUS)
        stresses = lax.cond(
            is_source,
            lambda: stress_elastic(current[2:5], velocity_pad, material, RADIUS, count_x, count_z),
            lambda: stress_acoustic(current[2:5], velocity_pad, material, RADIUS, count_x, count_z),
        )
        current = jnp.concatenate([velocity, stresses], axis=0)
        picked = jnp.take(current, local_rows, axis=2)
        block_plane = jnp.transpose(
            jnp.stack([picked[0], picked[1], -0.5 * (picked[2] + picked[3])]), (0, 2, 1)
        )
        joined = lax.all_gather(block_plane, "gz", axis=1, tiled=True)
        gathered = broadcast(joined, "sec", 0)
        injected = jnp.einsum("ckx,kz->cxz", gathered, chosen, precision=lax.Precision.HIGHEST)
        far_state = jnp.concatenate([current[0:3] + COUPLING * injected, current[3:5]], axis=0)
        current = jnp.where(is_source, current, far_state)
    return current[None]


HALO = 2 * RADIUS * STEPS
CELLS = 128
HALF = CELLS // 2
WINDOW = HALF + 2 * HALO
DEPTH = 2 * CELLS
PART = HALF + HALO
NP = 2 * NPD
TRIM = (0, 8, 16, 24, 32)
WINDOWS = [WINDOW - 2 * amount for amount in TRIM]
COUNTS = len(WINDOWS)
ROWS = 192
GROUPS = CELLS // NP
SLOT = (
    ((0, 0), (1, 0), (2, 0)),
    ((3, 0), (4, 0), (5, 0)),
    ((6, 0), (7, 0), (6, 96)),
    ((3, 112), (4, 112), (5, 112)),
    ((0, 128), (1, 128), (2, 128)),
)
SCALE = 840.0
TAPS = (672.0, -168.0, 32.0, -3.0)


def banded(distance):
    values = jnp.zeros(distance.shape, jnp.float32)
    for offset, tap in enumerate(TAPS, 1):
        values = jnp.where(distance == offset, tap, values)
        values = jnp.where(distance == -offset, -tap, values)
    return values.astype(jnp.bfloat16)


def halves(values):
    high = values.astype(jnp.bfloat16)
    low = (values - high.astype(jnp.float32)).astype(jnp.bfloat16)
    return high, low


def dot(left, right):
    return jnp.dot(left, right, preferred_element_type=jnp.float32)


def diff_x(bands, parts):
    return dot(bands[parts[0].shape[0]][...], jnp.concatenate(parts, axis=0))


def along_depth(matrix, parts):
    return dot(jnp.concatenate(parts, axis=1), matrix[...])


def trimmed(arrays, amount):
    if amount == 0:
        return arrays
    return [array[amount:-amount] for array in arrays]


def lanes_of(shape):
    return lax.broadcasted_iota(jnp.int32, shape, 1) // NP


BODY = HALO - 8
WHOLE = (2, 4)
PAIRED = ((0, 1), (3, 5))
EDGE_ROWS = 8 * BODY + 8 * len(WHOLE) + 8 * len(PAIRED)


def pack_edge(block, target, at_end):
    body, rest = (CELLS - BODY, CELLS - HALO) if at_end else (0, BODY)
    near = lax.broadcasted_iota(jnp.int32, (8, CELLS), 0) // 4 == int(at_end)
    for index in range(8):
        target[BODY * index : BODY * (index + 1)] = block[index, body : body + BODY]
    row = 8 * BODY
    for index in WHOLE:
        target[row : row + 8] = block[index, rest : rest + 8]
        row += 8
    for one, two in PAIRED:
        turned = pltpu.roll(block[two, rest : rest + 8], 4, 0)
        target[row : row + 8] = jnp.where(near, block[one, rest : rest + 8], turned)
        row += 8


def unpack_edge(edge, window, lanes, before):
    body, rest = (8, 0) if before else (PART, WINDOW - 8)
    near = lax.broadcasted_iota(jnp.int32, (8, CELLS), 0) // 4 == int(before)
    for index in range(8):
        window[index, body : body + BODY, lanes] = edge[BODY * index : BODY * (index + 1)]
    row = 8 * BODY
    for index in WHOLE:
        window[index, rest : rest + 8, lanes] = edge[row : row + 8]
        row += 8
    for one, two in PAIRED:
        tile = edge[row : row + 8]
        window[one, rest : rest + 8, lanes] = jnp.where(near, tile, 0.0)
        window[two, rest : rest + 8, lanes] = jnp.where(near, pltpu.roll(tile, 4, 0), 0.0)
        row += 8
    for index in (6, 7):
        window[index, rest : rest + 8, lanes] = jnp.zeros((8, CELLS), jnp.float32)


def pack_kernel(block, straight, crossed, swap):
    core = lax.axis_index("gz")

    @pl.when(core == 0)
    def _():
        pack_edge(block, straight, True)
        pack_edge(block, crossed, False)
        swap[...] = block[:, CELLS - PART :]

    @pl.when(core == 1)
    def _():
        pack_edge(block, straight, False)
        pack_edge(block, crossed, True)
        swap[...] = block[:, :PART]


def assemble(window, block, ahead, behind, other):
    core = lax.axis_index("gz")
    low, high = slice(0, CELLS), slice(CELLS, DEPTH)

    @pl.when(core == 0)
    def _():
        unpack_edge(ahead, window, low, True)
        unpack_edge(behind, window, high, True)
        window[:8, HALO:, low] = block[:, :PART]
        window[:8, HALO:, high] = other[...]

    @pl.when(core == 1)
    def _():
        window[:8, :PART, high] = block[:, CELLS - PART :]
        window[:8, :PART, low] = other[...]
        unpack_edge(ahead, window, high, False)
        unpack_edge(behind, window, low, False)


def place(state, held, sent):
    start = HALO - TRIM[-1]
    core = lax.axis_index("gz")
    state = [array[start : start + HALF] for array in state]

    @pl.when(core == 0)
    def _():
        for index in range(5):
            held[index] = state[index][:, :CELLS]
            sent[index] = state[index][:, CELLS:]

    @pl.when(core == 1)
    def _():
        for index in range(5):
            held[index] = state[index][:, CELLS:]
            sent[index] = state[index][:, :CELLS]


def acoustic(state, bands):
    vx, vz, pressure, one, two, light, kappa, loss_one, loss_two = state
    band_x, band_z = bands
    parts = halves(pressure)
    vx = vx - light * diff_x(band_x, parts)
    vz = vz - light * along_depth(band_z, parts)
    load = kappa * (diff_x(band_x, halves(vx)) + along_depth(band_z, halves(vz)))
    one = RELAXATION[0] * one + loss_one * load
    two = RELAXATION[1] * two + loss_two * load
    pressure = pressure - TIME_STEP * (load - one - two)
    return [vx, vz, pressure, one, two, light, kappa, loss_one, loss_two]


def constants_kernel(plane_rows, box_offset, *targets):
    *bands_x, band_z, pick, land = targets
    for target in bands_x:
        count = target.shape[0]
        row = lax.broadcasted_iota(jnp.int32, target.shape, 0)
        column = lax.broadcasted_iota(jnp.int32, target.shape, 1)
        target[...] = banded(jnp.where(column < count, column, column - count) - row)
    shape = (DEPTH, DEPTH)
    distance = lax.broadcasted_iota(jnp.int32, shape, 0) - lax.broadcasted_iota(jnp.int32, shape, 1)
    band_z[:DEPTH] = banded(distance)
    band_z[DEPTH:] = band_z[:DEPTH]
    row = plane_rows[...]
    lane = lax.broadcasted_iota(jnp.int32, box_offset.shape, 1)
    offset = jnp.where(lane == lax.axis_index("sec") - 1, box_offset[...], 0)
    landing = row // 2 + jnp.sum(offset, axis=1, keepdims=True)
    depth = lax.broadcasted_iota(jnp.int32, (DEPTH, NP), 0)
    spread = lax.broadcasted_iota(jnp.int32, (NP, CELLS), 1) % NP
    spread = spread == lax.broadcasted_iota(jnp.int32, (NP, CELLS), 0)
    spread = jnp.where(spread, 1.0, 0.0).astype(jnp.bfloat16)
    hot = jnp.where(depth == row, 1.0, 0.0).astype(jnp.bfloat16)
    pick[:DEPTH] = dot(hot, spread).astype(jnp.bfloat16)
    pick[DEPTH:] = pick[:DEPTH]
    hot = jnp.where(depth == landing, 1.0, 0.0).astype(jnp.bfloat16)
    land[:, :CELLS] = dot(hot, spread).astype(jnp.bfloat16)
    land[:, CELLS:] = land[:, :CELLS]


def first_kernel(*refs):
    bands_x, (band_z, pick, block, behind, ahead, other) = refs[:COUNTS], refs[COUNTS:-4]
    held, sent, rows, carry = refs[-4:]
    band_x = {band.shape[0]: band for band in bands_x}
    assemble(carry, block, ahead, behind, other)
    section = lax.axis_index("sec")

    @pl.when(section == 0)
    def _():
        vx, vz, sxx, szz, sxz, light, lame, shear = [carry[index] for index in range(8)]
        light = light * (TIME_STEP / SCALE)
        both = (lame + 2.0 * shear) * (TIME_STEP / SCALE)
        lame = lame * (TIME_STEP / SCALE)
        shear = shear * (TIME_STEP / SCALE)
        at = 0
        for step in range(STEPS):
            cut = TRIM[step] - at
            at = TRIM[step]
            vx, vz, sxx, szz, sxz, light, both, lame, shear = trimmed(
                [vx, vz, sxx, szz, sxz, light, both, lame, shear], cut
            )
            parts_xx, parts_zz, parts_xz = halves(sxx), halves(szz), halves(sxz)
            vx = vx + light * (diff_x(band_x, parts_xx) + along_depth(band_z, parts_xz))
            vz = vz + light * (diff_x(band_x, parts_xz) + along_depth(band_z, parts_zz))
            parts_x, parts_z = halves(vx), halves(vz)
            strain_x, strain_z = diff_x(band_x, parts_x), along_depth(band_z, parts_z)
            sxx = sxx + (both * strain_x + lame * strain_z)
            szz = szz + (lame * strain_x + both * strain_z)
            sxz = sxz + shear * (along_depth(band_z, parts_x) + diff_x(band_x, parts_z))
            low = 2 * RADIUS * (step + 1) - at
            for component, (parts, factor) in enumerate(
                ((parts_x, COUPLING), (parts_z, COUPLING), (halves(sxx + szz), -0.5 * COUPLING))
            ):
                picked = factor * along_depth(pick, parts)
                picked = picked[low : picked.shape[0] - low]
                group, base = SLOT[step][component]
                spot = pl.ds(base, picked.shape[0])
                rows[spot] = jnp.where(lanes_of(picked.shape) == group, picked, rows[spot])
        place([vx, vz, sxx, szz, sxz], held, sent)

    @pl.when(section > 0)
    def _():
        vx, vz, pressure, one, two, light, kappa, loss = [carry[index] for index in range(8)]
        light = light * (TIME_STEP / SCALE)
        kappa = kappa * (1.0 / SCALE)
        loss_one = loss * ((1.0 - RELAXATION[0]) * MEMORY_WEIGHT[0])
        loss_two = loss * ((1.0 - RELAXATION[1]) * MEMORY_WEIGHT[1])
        state = [vx, vz, pressure, one, two, light, kappa, loss_one, loss_two]
        for index, array in enumerate(acoustic(state, (band_x, band_z))):
            carry[index] = array


def second_kernel(*refs):
    bands_x, (band_z, land, carry, rows, held_in, sent_in, held, sent) = refs[:COUNTS], refs[COUNTS:]
    band_x = {band.shape[0]: band for band in bands_x}
    section = lax.axis_index("sec")

    @pl.when(section == 0)
    def _():
        held[...] = held_in[...]
        sent[...] = sent_in[...]

    @pl.when(section > 0)
    def _():
        state = [carry[index] for index in range(9)]
        at = 0
        for step in range(STEPS):
            if step:
                state = trimmed(state, TRIM[step] - at)
                at = TRIM[step]
                state = acoustic(state, (band_x, band_z))
            low = 2 * RADIUS * (step + 1) - at
            high = WINDOW - 2 * at - low
            for component in range(3):
                group, base = SLOT[step][component]
                taken = rows[pl.ds(base, high - low)]
                taken = halves(jnp.where(lanes_of(taken.shape) == group, taken, 0.0))
                added = lax.dot_general(
                    jnp.concatenate(taken, axis=1),
                    land[...],
                    (((1,), (1,)), ((), ())),
                    preferred_element_type=jnp.float32,
                )
                array = state[component]
                state[component] = jnp.concatenate(
                    [array[:low], array[low:high] + added, array[high:]], axis=0
                )
        place(state[:5], held, sent)


def last_kernel(held, swapped, out, sems):
    core = lax.axis_index("gz")
    copies = [
        pltpu.make_async_copy(
            source, out.at[:, pl.ds(pl.multiple_of(HALF * half, HALF), HALF)], sems.at[index]
        )
        for index, (source, half) in enumerate(((held, core), (swapped, 1 - core)))
    ]
    for copy in copies:
        copy.start()
    for copy in copies:
        copy.wait()


def call(kernel, outs, operands, flops, place_out=pltpu.VMEM, scratch=()):
    return pl.pallas_call(
        kernel,
        out_shape=outs,
        in_specs=[pl.BlockSpec(memory_space=pltpu.VMEM)] * len(operands),
        out_specs=[pl.BlockSpec(memory_space=place_out)] * len(outs),
        scratch_shapes=scratch,
        compiler_params=pltpu.CompilerParams(vmem_limit_bytes=48 * 1024 * 1024),
        cost_estimate=pl.CostEstimate(
            flops=flops, bytes_accessed=2 * 1024 * 1024, transcendentals=0
        ),
    )(*operands)


def full(*shape):
    return jax.ShapeDtypeStruct(shape, jnp.float32)


def narrow(*shape):
    return jax.ShapeDtypeStruct(shape, jnp.bfloat16)


def local_window(columns, fields, media, plane_rows, box_offset):
    fields, media = fields[0], media[0]
    core = lax.axis_index("gz")
    is_first = core == 0
    block = lax.optimization_barrier(jnp.concatenate([fields, media], axis=0))
    straight, crossed, swap = call(
        pack_kernel,
        [full(EDGE_ROWS, CELLS), full(EDGE_ROWS, CELLS), full(8, PART, CELLS)],
        [block],
        1000,
    )
    straight_pairs, crossed_pairs = [], []
    for column in range(columns):
        if column + 1 < columns:
            straight_pairs.append((2 * column, 2 * column + 2))
            crossed_pairs.append((2 * column + 1, 2 * column + 2))
        if column:
            straight_pairs.append((2 * column + 1, 2 * column - 1))
            crossed_pairs.append((2 * column, 2 * column - 1))
    turn = [(0, 1), (1, 0)]
    behind = lax.ppermute(crossed, ("gx", "gz"), crossed_pairs)
    ahead = lax.ppermute(straight, ("gx", "gz"), straight_pairs)
    joined = lax.all_gather(swap, "gz")
    other = jnp.where(is_first, joined[1], joined[0])
    *bands, pick, land = call(
        constants_kernel,
        [narrow(count, 2 * count) for count in WINDOWS]
        + [narrow(2 * DEPTH, DEPTH), narrow(2 * DEPTH, CELLS), narrow(DEPTH, 2 * CELLS)],
        [plane_rows[None], box_offset[None]],
        1_000_000_000,
    )
    held, sent, rows, carry = call(
        first_kernel,
        [
            full(5, HALF, CELLS),
            full(5, HALF, CELLS),
            full(ROWS, CELLS),
            full(9, WINDOW, DEPTH),
        ],
        [*bands, pick, block, behind, ahead, other],
        4_000_000_000,
    )
    arrived = [lax.ppermute(rows, "sec", [(0, target)]) for target in (1, 2, 3)]
    rows = arrived[0] + arrived[1] + arrived[2]
    held, sent = call(
        second_kernel,
        [full(5, HALF, CELLS), full(5, HALF, CELLS)],
        [*bands, land, carry, rows, held, sent],
        4_000_000_000,
    )
    swapped = lax.ppermute(sent, "gz", turn)
    (out,) = call(
        last_kernel,
        [full(5, CELLS, CELLS)],
        [held, swapped],
        1000,
        pl.ANY,
        [pltpu.SemaphoreType.DMA((2,))],
    )
    return out[None]


def solution(mesh):
    in_specs = (P("sec", None, "gx", "gz"), P("sec", None, "gx", "gz"), P(), P())
    out_specs = P("sec", None, "gx", "gz")
    if mesh.shape["gz"] == 2:
        local = functools.partial(local_window, mesh.shape["gx"])
    else:
        local = local_stepwise
    return jax.shard_map(local, mesh=mesh, in_specs=in_specs, out_specs=out_specs, check_vma=False)
```

```python
import functools

import jax
import jax.numpy as jnp
from jax import lax
from jax.experimental import pallas as pl
from jax.experimental.pallas import tpu as pltpu
from jax.sharding import PartitionSpec as P

RADIUS = 4
STEPS = 5
NPD = 8

STENCIL = (0.8, -0.2, 4.0 / 105.0, -1.0 / 280.0)
TIME_STEP = 0.2
COUPLING = 0.5
RELAXATION = (0.9, 0.5)
MEMORY_WEIGHT = (0.15, 0.1)


def padded_2(block, sides, width):
    for axis, dim in sides:
        count = lax.axis_size(axis)
        forward = [(i, i + 1) for i in range(count - 1)]
        backward = [(target, source) for source, target in forward]
        low = lax.ppermute(
            lax.slice_in_dim(block, block.shape[dim] - width, None, axis=dim), axis, forward
        )
        high = lax.ppermute(lax.slice_in_dim(block, 0, width, axis=dim), axis, backward)
        block = jnp.concatenate([low, block, high], axis=dim)
    return block


def broadcast(value, axis, source):
    kept = jnp.where(lax.axis_index(axis) == source, value, 0).astype(value.dtype)
    return lax.psum(kept, axis)


def along_x(padded, anchor, count_x, count_z):
    summed = jnp.zeros(padded.shape[:-2] + (count_x, count_z), jnp.float32)
    for offset, stencil_tap in enumerate(STENCIL, 1):
        forward = padded[
            ..., anchor + offset : anchor + offset + count_x, anchor : anchor + count_z
        ]
        backward = padded[
            ..., anchor - offset : anchor - offset + count_x, anchor : anchor + count_z
        ]
        summed = summed + stencil_tap * (forward - backward)
    return summed


def along_z(padded, anchor, count_x, count_z):
    summed = jnp.zeros(padded.shape[:-2] + (count_x, count_z), jnp.float32)
    for offset, stencil_tap in enumerate(STENCIL, 1):
        forward = padded[
            ..., anchor : anchor + count_x, anchor + offset : anchor + offset + count_z
        ]
        backward = padded[
            ..., anchor : anchor + count_x, anchor - offset : anchor - offset + count_z
        ]
        summed = summed + stencil_tap * (forward - backward)
    return summed


def velocity_elastic(velocity, stresses, buoyancy, anchor, count_x, count_z):
    updated_x = velocity[0] + TIME_STEP * buoyancy * (
        along_x(stresses[0], anchor, count_x, count_z)
        + along_z(stresses[2], anchor, count_x, count_z)
    )
    updated_z = velocity[1] + TIME_STEP * buoyancy * (
        along_x(stresses[2], anchor, count_x, count_z)
        + along_z(stresses[1], anchor, count_x, count_z)
    )
    return jnp.stack([updated_x, updated_z])


def velocity_acoustic(velocity, stresses, buoyancy, anchor, count_x, count_z):
    updated_x = velocity[0] - TIME_STEP * buoyancy * along_x(stresses[0], anchor, count_x, count_z)
    updated_z = velocity[1] - TIME_STEP * buoyancy * along_z(stresses[0], anchor, count_x, count_z)
    return jnp.stack([updated_x, updated_z])


def stress_elastic(stresses, velocity_pad, material, anchor, count_x, count_z):
    strain_x = along_x(velocity_pad[0], anchor, count_x, count_z)
    strain_z = along_z(velocity_pad[1], anchor, count_x, count_z)
    strain_shear = along_z(velocity_pad[0], anchor, count_x, count_z) + along_x(
        velocity_pad[1], anchor, count_x, count_z
    )
    lame_first = material[1]
    shear_modulus = material[2]
    normal_x = stresses[0] + TIME_STEP * (
        (lame_first + 2.0 * shear_modulus) * strain_x + lame_first * strain_z
    )
    normal_z = stresses[1] + TIME_STEP * (
        lame_first * strain_x + (lame_first + 2.0 * shear_modulus) * strain_z
    )
    shear_new = stresses[2] + TIME_STEP * shear_modulus * strain_shear
    return jnp.stack([normal_x, normal_z, shear_new])


def stress_acoustic(stresses, velocity_pad, material, anchor, count_x, count_z):
    divergence = along_x(velocity_pad[0], anchor, count_x, count_z) + along_z(
        velocity_pad[1], anchor, count_x, count_z
    )
    loading = material[1] * divergence
    memory_one = (
        RELAXATION[0] * stresses[1]
        + (1.0 - RELAXATION[0]) * MEMORY_WEIGHT[0] * material[2] * loading
    )
    memory_two = (
        RELAXATION[1] * stresses[2]
        + (1.0 - RELAXATION[1]) * MEMORY_WEIGHT[1] * material[2] * loading
    )
    pressure = stresses[0] - TIME_STEP * (loading - memory_one - memory_two)
    return jnp.stack([pressure, memory_one, memory_two])


def local_stepwise(fields, media, plane_rows, box_offset):
    current = fields[0]
    material = media[0]
    count_x = current.shape[1]
    count_z = current.shape[2]
    section = lax.axis_index("sec")
    is_source = section == 0
    block_z = lax.axis_index("gz")
    local_rows = lax.dynamic_slice_in_dim(plane_rows, block_z * NPD, NPD) - block_z * count_z
    offset = lax.dynamic_slice_in_dim(box_offset, jnp.maximum(section - 1, 0), 1)[0]
    depth_ids = block_z * count_z + jnp.arange(count_z, dtype=jnp.int32)
    landing = offset + plane_rows // 2
    chosen = (landing[:, None] == depth_ids[None, :]).astype(jnp.float32)
    for step_index in range(STEPS):
        stress_pad = padded_2(current[2:5], (("gx", 1), ("gz", 2)), RADIUS)
        velocity = lax.cond(
            is_source,
            lambda: velocity_elastic(
                current[0:2], stress_pad, material[0], RADIUS, count_x, count_z
            ),
            lambda: velocity_acoustic(
                current[0:2], stress_pad, material[0], RADIUS, count_x, count_z
            ),
        )
        velocity_pad = padded_2(velocity, (("gx", 1), ("gz", 2)), RADIUS)
        stresses = lax.cond(
            is_source,
            lambda: stress_elastic(current[2:5], velocity_pad, material, RADIUS, count_x, count_z),
            lambda: stress_acoustic(current[2:5], velocity_pad, material, RADIUS, count_x, count_z),
        )
        current = jnp.concatenate([velocity, stresses], axis=0)
        picked = jnp.take(current, local_rows, axis=2)
        block_plane = jnp.transpose(
            jnp.stack([picked[0], picked[1], -0.5 * (picked[2] + picked[3])]), (0, 2, 1)
        )
        joined = lax.all_gather(block_plane, "gz", axis=1, tiled=True)
        gathered = broadcast(joined, "sec", 0)
        injected = jnp.einsum("ckx,kz->cxz", gathered, chosen, precision=lax.Precision.HIGHEST)
        far_state = jnp.concatenate([current[0:3] + COUPLING * injected, current[3:5]], axis=0)
        current = jnp.where(is_source, current, far_state)
    return current[None]


HALO = 2 * RADIUS * STEPS
CELLS = 128
HALF = CELLS // 2
WINDOW = HALF + 2 * HALO
DEPTH = 2 * CELLS
PART = HALF + HALO
NP = 2 * NPD
TRIM = (0, 8, 16, 24, 32)
WINDOWS = [WINDOW - 2 * amount for amount in TRIM]
COUNTS = len(WINDOWS)
ROWS = 192
GROUPS = CELLS // NP
SLOT = (
    ((0, 0), (1, 0), (2, 0)),
    ((3, 0), (4, 0), (5, 0)),
    ((6, 0), (7, 0), (6, 96)),
    ((3, 112), (4, 112), (5, 112)),
    ((0, 128), (1, 128), (2, 128)),
)
SCALE = 840.0
TAPS = (672.0, -168.0, 32.0, -3.0)


def banded(distance):
    values = jnp.zeros(distance.shape, jnp.float32)
    for offset, tap in enumerate(TAPS, 1):
        values = jnp.where(distance == offset, tap, values)
        values = jnp.where(distance == -offset, -tap, values)
    return values.astype(jnp.bfloat16)


def halves(values):
    high = values.astype(jnp.bfloat16)
    low = (values - high.astype(jnp.float32)).astype(jnp.bfloat16)
    return high, low


def dot(left, right):
    return jnp.dot(left, right, preferred_element_type=jnp.float32)


def diff_x(bands, parts):
    return dot(bands[parts[0].shape[0]][...], jnp.concatenate(parts, axis=0))


def along_depth(matrix, parts):
    return dot(jnp.concatenate(parts, axis=1), matrix[...])


def trimmed(arrays, amount):
    if amount == 0:
        return arrays
    return [array[amount:-amount] for array in arrays]


def lanes_of(shape):
    return lax.broadcasted_iota(jnp.int32, shape, 1) // NP


BODY = HALO - 8
WHOLE = (2, 4)
PAIRED = ((0, 1), (3, 5))
EDGE_ROWS = 8 * BODY + 8 * len(WHOLE) + 8 * len(PAIRED)


def pack_edge(block, first, target, at_end):
    body, rest = (CELLS - BODY, CELLS - HALO) if at_end else (0, BODY)
    body, rest = body - first, rest - first
    near = lax.broadcasted_iota(jnp.int32, (8, CELLS), 0) // 4 == int(at_end)
    for index in range(8):
        target[BODY * index : BODY * (index + 1)] = block[index, body : body + BODY]
    row = 8 * BODY
    for index in WHOLE:
        target[row : row + 8] = block[index, rest : rest + 8]
        row += 8
    for one, two in PAIRED:
        turned = pltpu.roll(block[two, rest : rest + 8], 4, 0)
        target[row : row + 8] = jnp.where(near, block[one, rest : rest + 8], turned)
        row += 8


def unpack_edge(edge, window, lanes, before, inside):
    body, rest = (8, 0) if before else (PART, WINDOW - 8)
    near = lax.broadcasted_iota(jnp.int32, (8, CELLS), 0) // 4 == int(before)
    near = near & inside
    for index in range(8):
        taken = edge[BODY * index : BODY * (index + 1)]
        window[index, body : body + BODY, lanes] = jnp.where(inside, taken, 0.0)
    row = 8 * BODY
    for index in WHOLE:
        window[index, rest : rest + 8, lanes] = jnp.where(inside, edge[row : row + 8], 0.0)
        row += 8
    for one, two in PAIRED:
        tile = edge[row : row + 8]
        window[one, rest : rest + 8, lanes] = jnp.where(near, tile, 0.0)
        window[two, rest : rest + 8, lanes] = jnp.where(near, pltpu.roll(tile, 4, 0), 0.0)
        row += 8
    for index in (6, 7):
        window[index, rest : rest + 8, lanes] = jnp.zeros((8, CELLS), jnp.float32)


def pack_kernel(block, joined, edge):
    core = lax.axis_index("gz")

    @pl.when(core == 0)
    def _():
        pack_edge(block, 0, edge.at[0], False)
        pack_edge(joined.at[1], 0, edge.at[1], False)

    @pl.when(core == 1)
    def _():
        pack_edge(joined.at[0], CELLS - PART, edge.at[0], True)
        pack_edge(block, 0, edge.at[1], True)


def assemble(window, block, joined, edges):
    core, column = lax.axis_index("gz"), lax.axis_index("gx")
    low, high = slice(0, CELLS), slice(CELLS, DEPTH)

    @pl.when(core == 0)
    def _():
        inside = column > 0
        unpack_edge(edges.at[0, 0], window, low, True, inside)
        unpack_edge(edges.at[0, 1], window, high, True, inside)
        window[:8, HALO:, low] = block[:, :PART]
        window[:8, HALO:, high] = joined[1]

    @pl.when(core == 1)
    def _():
        inside = column < lax.axis_size("gx") - 1
        window[:8, :PART, high] = block[:, CELLS - PART :]
        window[:8, :PART, low] = joined[0]
        unpack_edge(edges.at[1, 0], window, low, False, inside)
        unpack_edge(edges.at[1, 1], window, high, False, inside)


def place(state, held, sent):
    start = HALO - TRIM[-1]
    core = lax.axis_index("gz")
    state = [array[start : start + HALF] for array in state]

    @pl.when(core == 0)
    def _():
        for index in range(5):
            held[index] = state[index][:, :CELLS]
            sent[index] = state[index][:, CELLS:]

    @pl.when(core == 1)
    def _():
        for index in range(5):
            held[index] = state[index][:, CELLS:]
            sent[index] = state[index][:, :CELLS]


def acoustic(state, bands):
    vx, vz, pressure, one, two, light, kappa, loss_one, loss_two = state
    band_x, band_z = bands
    parts = halves(pressure)
    vx = vx - light * diff_x(band_x, parts)
    vz = vz - light * along_depth(band_z, parts)
    load = kappa * (diff_x(band_x, halves(vx)) + along_depth(band_z, halves(vz)))
    one = RELAXATION[0] * one + loss_one * load
    two = RELAXATION[1] * two + loss_two * load
    pressure = pressure - TIME_STEP * (load - one - two)
    return [vx, vz, pressure, one, two, light, kappa, loss_one, loss_two]


def constants_kernel(plane_rows, box_offset, *targets):
    *bands_x, band_z, pick, land = targets
    for target in bands_x:
        count = target.shape[0]
        row = lax.broadcasted_iota(jnp.int32, target.shape, 0)
        column = lax.broadcasted_iota(jnp.int32, target.shape, 1)
        target[...] = banded(jnp.where(column < count, column, column - count) - row)
    shape = (DEPTH, DEPTH)
    distance = lax.broadcasted_iota(jnp.int32, shape, 0) - lax.broadcasted_iota(jnp.int32, shape, 1)
    band_z[:DEPTH] = banded(distance)
    band_z[DEPTH:] = band_z[:DEPTH]
    row = plane_rows[...]
    lane = lax.broadcasted_iota(jnp.int32, box_offset.shape, 1)
    offset = jnp.where(lane == lax.axis_index("sec") - 1, box_offset[...], 0)
    landing = row // 2 + jnp.sum(offset, axis=1, keepdims=True)
    depth = lax.broadcasted_iota(jnp.int32, (DEPTH, NP), 0)
    spread = lax.broadcasted_iota(jnp.int32, (NP, CELLS), 1) % NP
    spread = spread == lax.broadcasted_iota(jnp.int32, (NP, CELLS), 0)
    spread = jnp.where(spread, 1.0, 0.0).astype(jnp.bfloat16)
    hot = jnp.where(depth == row, 1.0, 0.0).astype(jnp.bfloat16)
    pick[:DEPTH] = dot(hot, spread).astype(jnp.bfloat16)
    pick[DEPTH:] = pick[:DEPTH]
    hot = jnp.where(depth == landing, 1.0, 0.0).astype(jnp.bfloat16)
    land[:, :CELLS] = dot(hot, spread).astype(jnp.bfloat16)
    land[:, CELLS:] = land[:, :CELLS]


def first_kernel(*refs):
    bands_x, (band_z, pick, block, joined, edges) = refs[:COUNTS], refs[COUNTS:-4]
    held, sent, rows, carry = refs[-4:]
    band_x = {band.shape[0]: band for band in bands_x}
    assemble(carry, block, joined, edges)
    section = lax.axis_index("sec")

    @pl.when(section == 0)
    def _():
        vx, vz, sxx, szz, sxz, light, lame, shear = [carry[index] for index in range(8)]
        light = light * (TIME_STEP / SCALE)
        both = (lame + 2.0 * shear) * (TIME_STEP / SCALE)
        lame = lame * (TIME_STEP / SCALE)
        shear = shear * (TIME_STEP / SCALE)
        at = 0
        for step in range(STEPS):
            cut = TRIM[step] - at
            at = TRIM[step]
            vx, vz, sxx, szz, sxz, light, both, lame, shear = trimmed(
                [vx, vz, sxx, szz, sxz, light, both, lame, shear], cut
            )
            parts_xx, parts_zz, parts_xz = halves(sxx), halves(szz), halves(sxz)
            vx = vx + light * (diff_x(band_x, parts_xx) + along_depth(band_z, parts_xz))
            vz = vz + light * (diff_x(band_x, parts_xz) + along_depth(band_z, parts_zz))
            parts_x, parts_z = halves(vx), halves(vz)
            strain_x, strain_z = diff_x(band_x, parts_x), along_depth(band_z, parts_z)
            sxx = sxx + (both * strain_x + lame * strain_z)
            szz = szz + (lame * strain_x + both * strain_z)
            sxz = sxz + shear * (along_depth(band_z, parts_x) + diff_x(band_x, parts_z))
            low = 2 * RADIUS * (step + 1) - at
            for component, (parts, factor) in enumerate(
                ((parts_x, COUPLING), (parts_z, COUPLING), (halves(sxx + szz), -0.5 * COUPLING))
            ):
                picked = factor * along_depth(pick, parts)
                picked = picked[low : picked.shape[0] - low]
                group, base = SLOT[step][component]
                spot = pl.ds(base, picked.shape[0])
                rows[spot] = jnp.where(lanes_of(picked.shape) == group, picked, rows[spot])
        place([vx, vz, sxx, szz, sxz], held, sent)

    @pl.when(section > 0)
    def _():
        vx, vz, pressure, one, two, light, kappa, loss = [carry[index] for index in range(8)]
        light = light * (TIME_STEP / SCALE)
        kappa = kappa * (1.0 / SCALE)
        loss_one = loss * ((1.0 - RELAXATION[0]) * MEMORY_WEIGHT[0])
        loss_two = loss * ((1.0 - RELAXATION[1]) * MEMORY_WEIGHT[1])
        state = [vx, vz, pressure, one, two, light, kappa, loss_one, loss_two]
        for index, array in enumerate(acoustic(state, (band_x, band_z))):
            carry[index] = array


def second_kernel(*refs):
    bands_x, (band_z, land, carry, rows, held_in, sent_in, held, sent) = refs[:COUNTS], refs[COUNTS:]
    band_x = {band.shape[0]: band for band in bands_x}
    section = lax.axis_index("sec")

    @pl.when(section == 0)
    def _():
        held[...] = held_in[...]
        sent[...] = sent_in[...]

    @pl.when(section > 0)
    def _():
        state = [carry[index] for index in range(9)]
        at = 0
        for step in range(STEPS):
            if step:
                state = trimmed(state, TRIM[step] - at)
                at = TRIM[step]
                state = acoustic(state, (band_x, band_z))
            low = 2 * RADIUS * (step + 1) - at
            high = WINDOW - 2 * at - low
            for component in range(3):
                group, base = SLOT[step][component]
                taken = rows[pl.ds(base, high - low)]
                taken = halves(jnp.where(lanes_of(taken.shape) == group, taken, 0.0))
                added = lax.dot_general(
                    jnp.concatenate(taken, axis=1),
                    land[...],
                    (((1,), (1,)), ((), ())),
                    preferred_element_type=jnp.float32,
                )
                array = state[component]
                state[component] = jnp.concatenate(
                    [array[:low], array[low:high] + added, array[high:]], axis=0
                )
        place(state[:5], held, sent)


def last_kernel(held, swapped, out, sems):
    core = lax.axis_index("gz")
    copies = [
        pltpu.make_async_copy(
            source, out.at[:, pl.ds(pl.multiple_of(HALF * half, HALF), HALF)], sems.at[index]
        )
        for index, (source, half) in enumerate(((held, core), (swapped, 1 - core)))
    ]
    for copy in copies:
        copy.start()
    for copy in copies:
        copy.wait()


def call(kernel, outs, operands, flops, place_out=pltpu.VMEM, scratch=()):
    return pl.pallas_call(
        kernel,
        out_shape=outs,
        in_specs=[pl.BlockSpec(memory_space=pltpu.VMEM)] * len(operands),
        out_specs=[pl.BlockSpec(memory_space=place_out)] * len(outs),
        scratch_shapes=scratch,
        compiler_params=pltpu.CompilerParams(vmem_limit_bytes=48 * 1024 * 1024),
        cost_estimate=pl.CostEstimate(
            flops=flops, bytes_accessed=2 * 1024 * 1024, transcendentals=0
        ),
    )(*operands)


def full(*shape):
    return jax.ShapeDtypeStruct(shape, jnp.float32)


def narrow(*shape):
    return jax.ShapeDtypeStruct(shape, jnp.bfloat16)


def pairs(columns):
    def device(section, column, core):
        return (section * columns + column) * 2 + core

    groups = [
        [device(section, column, 1), device(section, column + 1, 0)]
        for section in range(4)
        for column in range(columns - 1)
    ]
    for section in (0, 2):
        for column, core in ((0, 0), (columns - 1, 1)):
            groups.append([device(section, column, core), device(section + 1, column, core)])
    return groups


def local_window(columns, fields, media, plane_rows, box_offset):
    fields, media = fields[0], media[0]
    core = lax.axis_index("gz")
    is_first = core == 0
    block = lax.optimization_barrier(jnp.concatenate([fields, media], axis=0))
    swap = jnp.where(is_first, block[:, CELLS - PART :], block[:, :PART])
    joined = lax.all_gather(swap, "gz")
    (edge,) = call(pack_kernel, [full(2, EDGE_ROWS, CELLS)], [block, joined], 1000)
    edges = lax.all_gather(edge, ("sec", "gx", "gz"), axis_index_groups=pairs(columns))
    turn = [(0, 1), (1, 0)]
    *bands, pick, land = call(
        constants_kernel,
        [narrow(count, 2 * count) for count in WINDOWS]
        + [narrow(2 * DEPTH, DEPTH), narrow(2 * DEPTH, CELLS), narrow(DEPTH, 2 * CELLS)],
        [plane_rows[None], box_offset[None]],
        1_000_000_000,
    )
    held, sent, rows, carry = call(
        first_kernel,
        [
            full(5, HALF, CELLS),
            full(5, HALF, CELLS),
            full(ROWS, CELLS),
            full(9, WINDOW, DEPTH),
        ],
        [*bands, pick, block, joined, edges],
        4_000_000_000,
    )
    arrived = [lax.ppermute(rows, "sec", [(0, target)]) for target in (1, 2, 3)]
    rows = arrived[0] + arrived[1] + arrived[2]
    held, sent = call(
        second_kernel,
        [full(5, HALF, CELLS), full(5, HALF, CELLS)],
        [*bands, land, carry, rows, held, sent],
        4_000_000_000,
    )
    swapped = lax.ppermute(sent, "gz", turn)
    (out,) = call(
        last_kernel,
        [full(5, CELLS, CELLS)],
        [held, swapped],
        1000,
        pl.ANY,
        [pltpu.SemaphoreType.DMA((2,))],
    )
    return out[None]


def solution(mesh):
    in_specs = (P("sec", None, "gx", "gz"), P("sec", None, "gx", "gz"), P(), P())
    out_specs = P("sec", None, "gx", "gz")
    if mesh.shape["gz"] == 2:
        local = functools.partial(local_window, mesh.shape["gx"])
    else:
        local = local_stepwise
    return jax.shard_map(local, mesh=mesh, in_specs=in_specs, out_specs=out_specs, check_vma=False)
```

```python
import functools

import jax
import jax.numpy as jnp
from jax import lax
from jax.experimental import pallas as pl
from jax.experimental.pallas import tpu as pltpu
from jax.sharding import PartitionSpec as P

RADIUS = 4
STEPS = 5
NPD = 8

STENCIL = (0.8, -0.2, 4.0 / 105.0, -1.0 / 280.0)
TIME_STEP = 0.2
COUPLING = 0.5
RELAXATION = (0.9, 0.5)
MEMORY_WEIGHT = (0.15, 0.1)


def padded_2(block, sides, width):
    for axis, dim in sides:
        count = lax.axis_size(axis)
        forward = [(i, i + 1) for i in range(count - 1)]
        backward = [(target, source) for source, target in forward]
        low = lax.ppermute(
            lax.slice_in_dim(block, block.shape[dim] - width, None, axis=dim), axis, forward
        )
        high = lax.ppermute(lax.slice_in_dim(block, 0, width, axis=dim), axis, backward)
        block = jnp.concatenate([low, block, high], axis=dim)
    return block


def broadcast(value, axis, source):
    kept = jnp.where(lax.axis_index(axis) == source, value, 0).astype(value.dtype)
    return lax.psum(kept, axis)


def along_x(padded, anchor, count_x, count_z):
    summed = jnp.zeros(padded.shape[:-2] + (count_x, count_z), jnp.float32)
    for offset, stencil_tap in enumerate(STENCIL, 1):
        forward = padded[
            ..., anchor + offset : anchor + offset + count_x, anchor : anchor + count_z
        ]
        backward = padded[
            ..., anchor - offset : anchor - offset + count_x, anchor : anchor + count_z
        ]
        summed = summed + stencil_tap * (forward - backward)
    return summed


def along_z(padded, anchor, count_x, count_z):
    summed = jnp.zeros(padded.shape[:-2] + (count_x, count_z), jnp.float32)
    for offset, stencil_tap in enumerate(STENCIL, 1):
        forward = padded[
            ..., anchor : anchor + count_x, anchor + offset : anchor + offset + count_z
        ]
        backward = padded[
            ..., anchor : anchor + count_x, anchor - offset : anchor - offset + count_z
        ]
        summed = summed + stencil_tap * (forward - backward)
    return summed


def velocity_elastic(velocity, stresses, buoyancy, anchor, count_x, count_z):
    updated_x = velocity[0] + TIME_STEP * buoyancy * (
        along_x(stresses[0], anchor, count_x, count_z)
        + along_z(stresses[2], anchor, count_x, count_z)
    )
    updated_z = velocity[1] + TIME_STEP * buoyancy * (
        along_x(stresses[2], anchor, count_x, count_z)
        + along_z(stresses[1], anchor, count_x, count_z)
    )
    return jnp.stack([updated_x, updated_z])


def velocity_acoustic(velocity, stresses, buoyancy, anchor, count_x, count_z):
    updated_x = velocity[0] - TIME_STEP * buoyancy * along_x(stresses[0], anchor, count_x, count_z)
    updated_z = velocity[1] - TIME_STEP * buoyancy * along_z(stresses[0], anchor, count_x, count_z)
    return jnp.stack([updated_x, updated_z])


def stress_elastic(stresses, velocity_pad, material, anchor, count_x, count_z):
    strain_x = along_x(velocity_pad[0], anchor, count_x, count_z)
    strain_z = along_z(velocity_pad[1], anchor, count_x, count_z)
    strain_shear = along_z(velocity_pad[0], anchor, count_x, count_z) + along_x(
        velocity_pad[1], anchor, count_x, count_z
    )
    lame_first = material[1]
    shear_modulus = material[2]
    normal_x = stresses[0] + TIME_STEP * (
        (lame_first + 2.0 * shear_modulus) * strain_x + lame_first * strain_z
    )
    normal_z = stresses[1] + TIME_STEP * (
        lame_first * strain_x + (lame_first + 2.0 * shear_modulus) * strain_z
    )
    shear_new = stresses[2] + TIME_STEP * shear_modulus * strain_shear
    return jnp.stack([normal_x, normal_z, shear_new])


def stress_acoustic(stresses, velocity_pad, material, anchor, count_x, count_z):
    divergence = along_x(velocity_pad[0], anchor, count_x, count_z) + along_z(
        velocity_pad[1], anchor, count_x, count_z
    )
    loading = material[1] * divergence
    memory_one = (
        RELAXATION[0] * stresses[1]
        + (1.0 - RELAXATION[0]) * MEMORY_WEIGHT[0] * material[2] * loading
    )
    memory_two = (
        RELAXATION[1] * stresses[2]
        + (1.0 - RELAXATION[1]) * MEMORY_WEIGHT[1] * material[2] * loading
    )
    pressure = stresses[0] - TIME_STEP * (loading - memory_one - memory_two)
    return jnp.stack([pressure, memory_one, memory_two])


def local_stepwise(fields, media, plane_rows, box_offset):
    current = fields[0]
    material = media[0]
    count_x = current.shape[1]
    count_z = current.shape[2]
    section = lax.axis_index("sec")
    is_source = section == 0
    block_z = lax.axis_index("gz")
    local_rows = lax.dynamic_slice_in_dim(plane_rows, block_z * NPD, NPD) - block_z * count_z
    offset = lax.dynamic_slice_in_dim(box_offset, jnp.maximum(section - 1, 0), 1)[0]
    depth_ids = block_z * count_z + jnp.arange(count_z, dtype=jnp.int32)
    landing = offset + plane_rows // 2
    chosen = (landing[:, None] == depth_ids[None, :]).astype(jnp.float32)
    for step_index in range(STEPS):
        stress_pad = padded_2(current[2:5], (("gx", 1), ("gz", 2)), RADIUS)
        velocity = lax.cond(
            is_source,
            lambda: velocity_elastic(
                current[0:2], stress_pad, material[0], RADIUS, count_x, count_z
            ),
            lambda: velocity_acoustic(
                current[0:2], stress_pad, material[0], RADIUS, count_x, count_z
            ),
        )
        velocity_pad = padded_2(velocity, (("gx", 1), ("gz", 2)), RADIUS)
        stresses = lax.cond(
            is_source,
            lambda: stress_elastic(current[2:5], velocity_pad, material, RADIUS, count_x, count_z),
            lambda: stress_acoustic(current[2:5], velocity_pad, material, RADIUS, count_x, count_z),
        )
        current = jnp.concatenate([velocity, stresses], axis=0)
        picked = jnp.take(current, local_rows, axis=2)
        block_plane = jnp.transpose(
            jnp.stack([picked[0], picked[1], -0.5 * (picked[2] + picked[3])]), (0, 2, 1)
        )
        joined = lax.all_gather(block_plane, "gz", axis=1, tiled=True)
        gathered = broadcast(joined, "sec", 0)
        injected = jnp.einsum("ckx,kz->cxz", gathered, chosen, precision=lax.Precision.HIGHEST)
        far_state = jnp.concatenate([current[0:3] + COUPLING * injected, current[3:5]], axis=0)
        current = jnp.where(is_source, current, far_state)
    return current[None]


HALO = 2 * RADIUS * STEPS
CELLS = 128
HALF = CELLS // 2
WINDOW = HALF + 2 * HALO
DEPTH = 2 * CELLS
PART = HALF + HALO
NP = 2 * NPD
TRIM = (0, 8, 16, 24, 32)
WINDOWS = [WINDOW - 2 * amount for amount in TRIM]
COUNTS = len(WINDOWS)
ROWS = 192
GROUPS = CELLS // NP
SLOT = (
    ((0, 0), (1, 0), (2, 0)),
    ((3, 0), (4, 0), (5, 0)),
    ((6, 0), (7, 0), (6, 96)),
    ((3, 112), (4, 112), (5, 112)),
    ((0, 128), (1, 128), (2, 128)),
)
SCALE = 840.0
TAPS = (672.0, -168.0, 32.0, -3.0)


def banded(distance):
    values = jnp.zeros(distance.shape, jnp.float32)
    for offset, tap in enumerate(TAPS, 1):
        values = jnp.where(distance == offset, tap, values)
        values = jnp.where(distance == -offset, -tap, values)
    return values.astype(jnp.bfloat16)


def halves(values):
    high = values.astype(jnp.bfloat16)
    low = (values - high.astype(jnp.float32)).astype(jnp.bfloat16)
    return high, low


def dot(left, right):
    return jnp.dot(left, right, preferred_element_type=jnp.float32)


def diff_x(bands, parts):
    return dot(bands[parts[0].shape[0]][...], jnp.concatenate(parts, axis=0))


def along_depth(matrix, parts):
    return dot(jnp.concatenate(parts, axis=1), matrix[...])


def trimmed(arrays, amount):
    if amount == 0:
        return arrays
    return [array[amount:-amount] for array in arrays]


def lanes_of(shape):
    return lax.broadcasted_iota(jnp.int32, shape, 1) // NP


BODY = HALO - 8
WHOLE = (2, 4)
PAIRED = ((0, 1), (3, 5))
EDGE_ROWS = 8 * BODY + 8 * len(WHOLE) + 8 * len(PAIRED)


def pack_edge(block, target, at_end):
    body, rest = (CELLS - BODY, CELLS - HALO) if at_end else (0, BODY)
    near = lax.broadcasted_iota(jnp.int32, (8, CELLS), 0) // 4 == int(at_end)
    for index in range(8):
        target[BODY * index : BODY * (index + 1)] = block[index, body : body + BODY]
    row = 8 * BODY
    for index in WHOLE:
        target[row : row + 8] = block[index, rest : rest + 8]
        row += 8
    for one, two in PAIRED:
        turned = pltpu.roll(block[two, rest : rest + 8], 4, 0)
        target[row : row + 8] = jnp.where(near, block[one, rest : rest + 8], turned)
        row += 8


def unpack_edge(edge, window, lanes, before):
    body, rest = (8, 0) if before else (PART, WINDOW - 8)
    near = lax.broadcasted_iota(jnp.int32, (8, CELLS), 0) // 4 == int(before)
    for index in range(8):
        window[index, body : body + BODY, lanes] = edge[BODY * index : BODY * (index + 1)]
    row = 8 * BODY
    for index in WHOLE:
        window[index, rest : rest + 8, lanes] = edge[row : row + 8]
        row += 8
    for one, two in PAIRED:
        tile = edge[row : row + 8]
        window[one, rest : rest + 8, lanes] = jnp.where(near, tile, 0.0)
        window[two, rest : rest + 8, lanes] = jnp.where(near, pltpu.roll(tile, 4, 0), 0.0)
        row += 8
    for index in (6, 7):
        window[index, rest : rest + 8, lanes] = jnp.zeros((8, CELLS), jnp.float32)


def pack_kernel(block, straight, crossed, swap):
    core = lax.axis_index("gz")

    @pl.when(core == 0)
    def _():
        pack_edge(block, straight, True)
        pack_edge(block, crossed, False)
        swap[...] = block[:, CELLS - PART :]

    @pl.when(core == 1)
    def _():
        pack_edge(block, straight, False)
        pack_edge(block, crossed, True)
        swap[...] = block[:, :PART]


def assemble(window, block, ahead, behind, other):
    core = lax.axis_index("gz")
    low, high = slice(0, CELLS), slice(CELLS, DEPTH)

    @pl.when(core == 0)
    def _():
        unpack_edge(ahead, window, low, True)
        unpack_edge(behind, window, high, True)
        window[:8, HALO:, low] = block[:, :PART]
        window[:8, HALO:, high] = other[...]

    @pl.when(core == 1)
    def _():
        window[:8, :PART, high] = block[:, CELLS - PART :]
        window[:8, :PART, low] = other[...]
        unpack_edge(ahead, window, high, False)
        unpack_edge(behind, window, low, False)


def place(state, held, sent):
    start = HALO - TRIM[-1]
    core = lax.axis_index("gz")
    state = [array[start : start + HALF] for array in state]

    @pl.when(core == 0)
    def _():
        for index in range(5):
            held[index] = state[index][:, :CELLS]
            sent[index] = state[index][:, CELLS:]

    @pl.when(core == 1)
    def _():
        for index in range(5):
            held[index] = state[index][:, CELLS:]
            sent[index] = state[index][:, :CELLS]


def acoustic(state, bands):
    vx, vz, pressure, one, two, light, kappa, loss_one, loss_two = state
    band_x, band_z = bands
    parts = halves(pressure)
    vx = vx - light * diff_x(band_x, parts)
    vz = vz - light * along_depth(band_z, parts)
    load = kappa * (diff_x(band_x, halves(vx)) + along_depth(band_z, halves(vz)))
    one = RELAXATION[0] * one + loss_one * load
    two = RELAXATION[1] * two + loss_two * load
    pressure = pressure - TIME_STEP * (load - one - two)
    return [vx, vz, pressure, one, two, light, kappa, loss_one, loss_two]


def constants_kernel(plane_rows, box_offset, *targets):
    *bands_x, band_z, pick, land = targets
    for target in bands_x:
        count = target.shape[0]
        row = lax.broadcasted_iota(jnp.int32, target.shape, 0)
        column = lax.broadcasted_iota(jnp.int32, target.shape, 1)
        target[...] = banded(jnp.where(column < count, column, column - count) - row)
    shape = (DEPTH, DEPTH)
    distance = lax.broadcasted_iota(jnp.int32, shape, 0) - lax.broadcasted_iota(jnp.int32, shape, 1)
    band_z[:DEPTH] = banded(distance)
    band_z[DEPTH:] = band_z[:DEPTH]
    row = plane_rows[...]
    lane = lax.broadcasted_iota(jnp.int32, box_offset.shape, 1)
    offset = jnp.where(lane == lax.axis_index("sec") - 1, box_offset[...], 0)
    landing = row // 2 + jnp.sum(offset, axis=1, keepdims=True)
    depth = lax.broadcasted_iota(jnp.int32, (DEPTH, NP), 0)
    spread = lax.broadcasted_iota(jnp.int32, (NP, CELLS), 1) % NP
    spread = spread == lax.broadcasted_iota(jnp.int32, (NP, CELLS), 0)
    spread = jnp.where(spread, 1.0, 0.0).astype(jnp.bfloat16)
    hot = jnp.where(depth == row, 1.0, 0.0).astype(jnp.bfloat16)
    pick[:DEPTH] = dot(hot, spread).astype(jnp.bfloat16)
    pick[DEPTH:] = pick[:DEPTH]
    hot = jnp.where(depth == landing, 1.0, 0.0).astype(jnp.bfloat16)
    land[:, :CELLS] = dot(hot, spread).astype(jnp.bfloat16)
    land[:, CELLS:] = land[:, :CELLS]


def first_kernel(*refs):
    bands_x, (band_z, pick, block, behind, ahead, other) = refs[:COUNTS], refs[COUNTS:-4]
    held, sent, rows, carry = refs[-4:]
    band_x = {band.shape[0]: band for band in bands_x}
    assemble(carry, block, ahead, behind, other)
    section = lax.axis_index("sec")

    @pl.when(section == 0)
    def _():
        vx, vz, sxx, szz, sxz, light, lame, shear = [carry[index] for index in range(8)]
        light = light * (TIME_STEP / SCALE)
        both = (lame + 2.0 * shear) * (TIME_STEP / SCALE)
        lame = lame * (TIME_STEP / SCALE)
        shear = shear * (TIME_STEP / SCALE)
        at = 0
        for step in range(STEPS):
            cut = TRIM[step] - at
            at = TRIM[step]
            vx, vz, sxx, szz, sxz, light, both, lame, shear = trimmed(
                [vx, vz, sxx, szz, sxz, light, both, lame, shear], cut
            )
            parts_xx, parts_zz, parts_xz = halves(sxx), halves(szz), halves(sxz)
            vx = vx + light * (diff_x(band_x, parts_xx) + along_depth(band_z, parts_xz))
            vz = vz + light * (diff_x(band_x, parts_xz) + along_depth(band_z, parts_zz))
            parts_x, parts_z = halves(vx), halves(vz)
            strain_x, strain_z = diff_x(band_x, parts_x), along_depth(band_z, parts_z)
            sxx = sxx + (both * strain_x + lame * strain_z)
            szz = szz + (lame * strain_x + both * strain_z)
            sxz = sxz + shear * (along_depth(band_z, parts_x) + diff_x(band_x, parts_z))
            low = 2 * RADIUS * (step + 1) - at
            for component, (parts, factor) in enumerate(
                ((parts_x, COUPLING), (parts_z, COUPLING), (halves(sxx + szz), -0.5 * COUPLING))
            ):
                picked = factor * along_depth(pick, parts)
                picked = picked[low : picked.shape[0] - low]
                group, base = SLOT[step][component]
                spot = pl.ds(base, picked.shape[0])
                rows[spot] = jnp.where(lanes_of(picked.shape) == group, picked, rows[spot])
        place([vx, vz, sxx, szz, sxz], held, sent)

    @pl.when(section > 0)
    def _():
        vx, vz, pressure, one, two, light, kappa, loss = [carry[index] for index in range(8)]
        light = light * (TIME_STEP / SCALE)
        kappa = kappa * (1.0 / SCALE)
        loss_one = loss * ((1.0 - RELAXATION[0]) * MEMORY_WEIGHT[0])
        loss_two = loss * ((1.0 - RELAXATION[1]) * MEMORY_WEIGHT[1])
        state = [vx, vz, pressure, one, two, light, kappa, loss_one, loss_two]
        for index, array in enumerate(acoustic(state, (band_x, band_z))):
            carry[index] = array


def second_kernel(*refs):
    bands_x, (band_z, land, carry, rows, held_in, sent_in, held, sent) = refs[:COUNTS], refs[COUNTS:]
    band_x = {band.shape[0]: band for band in bands_x}
    section = lax.axis_index("sec")

    @pl.when(section == 0)
    def _():
        held[...] = held_in[...]
        sent[...] = sent_in[...]

    @pl.when(section > 0)
    def _():
        state = [carry[index] for index in range(9)]
        at = 0
        for step in range(STEPS):
            if step:
                state = trimmed(state, TRIM[step] - at)
                at = TRIM[step]
                state = acoustic(state, (band_x, band_z))
            low = 2 * RADIUS * (step + 1) - at
            high = WINDOW - 2 * at - low
            for component in range(3):
                group, base = SLOT[step][component]
                taken = rows[pl.ds(base, high - low)]
                taken = halves(jnp.where(lanes_of(taken.shape) == group, taken, 0.0))
                added = lax.dot_general(
                    jnp.concatenate(taken, axis=1),
                    land[...],
                    (((1,), (1,)), ((), ())),
                    preferred_element_type=jnp.float32,
                )
                array = state[component]
                state[component] = jnp.concatenate(
                    [array[:low], array[low:high] + added, array[high:]], axis=0
                )
        place(state[:5], held, sent)


def last_kernel(held, swapped, out, sems):
    core = lax.axis_index("gz")
    copies = [
        pltpu.make_async_copy(
            source, out.at[:, pl.ds(pl.multiple_of(HALF * half, HALF), HALF)], sems.at[index]
        )
        for index, (source, half) in enumerate(((held, core), (swapped, 1 - core)))
    ]
    for copy in copies:
        copy.start()
    for copy in copies:
        copy.wait()


def call(kernel, outs, operands, flops, place_out=pltpu.VMEM, scratch=()):
    return pl.pallas_call(
        kernel,
        out_shape=outs,
        in_specs=[pl.BlockSpec(memory_space=pltpu.VMEM)] * len(operands),
        out_specs=[pl.BlockSpec(memory_space=place_out)] * len(outs),
        scratch_shapes=scratch,
        compiler_params=pltpu.CompilerParams(vmem_limit_bytes=48 * 1024 * 1024),
        cost_estimate=pl.CostEstimate(
            flops=flops, bytes_accessed=2 * 1024 * 1024, transcendentals=0
        ),
    )(*operands)


def full(*shape):
    return jax.ShapeDtypeStruct(shape, jnp.float32)


def narrow(*shape):
    return jax.ShapeDtypeStruct(shape, jnp.bfloat16)


def local_window(columns, fields, media, plane_rows, box_offset):
    fields, media = fields[0], media[0]
    core = lax.axis_index("gz")
    is_first = core == 0
    block = lax.optimization_barrier(jnp.concatenate([fields, media], axis=0))
    straight, crossed, swap = call(
        pack_kernel,
        [full(EDGE_ROWS, CELLS), full(EDGE_ROWS, CELLS), full(8, PART, CELLS)],
        [block],
        1000,
    )
    straight_pairs, crossed_pairs = [], []
    for column in range(columns):
        if column + 1 < columns:
            straight_pairs.append((2 * column, 2 * column + 2))
            crossed_pairs.append((2 * column + 1, 2 * column + 2))
        if column:
            straight_pairs.append((2 * column + 1, 2 * column - 1))
            crossed_pairs.append((2 * column, 2 * column - 1))
    turn = [(0, 1), (1, 0)]
    behind = lax.ppermute(crossed, ("gx", "gz"), crossed_pairs)
    ahead = lax.ppermute(straight, ("gx", "gz"), straight_pairs)
    joined = lax.all_gather(swap, "gz")
    other = jnp.where(is_first, joined[1], joined[0])
    *bands, pick, land = call(
        constants_kernel,
        [narrow(count, 2 * count) for count in WINDOWS]
        + [narrow(2 * DEPTH, DEPTH), narrow(2 * DEPTH, CELLS), narrow(DEPTH, 2 * CELLS)],
        [plane_rows[None], box_offset[None]],
        1_000_000_000,
    )
    held, sent, rows, carry = call(
        first_kernel,
        [
            full(5, HALF, CELLS),
            full(5, HALF, CELLS),
            full(ROWS, CELLS),
            full(9, WINDOW, DEPTH),
        ],
        [*bands, pick, block, behind, ahead, other],
        4_000_000_000,
    )
    for groups in ([[0, 1], [2, 3]], [[0, 2], [1, 3]]):
        rows = lax.all_gather(rows, "sec", axis_index_groups=groups)[0]
    held, sent = call(
        second_kernel,
        [full(5, HALF, CELLS), full(5, HALF, CELLS)],
        [*bands, land, carry, rows, held, sent],
        4_000_000_000,
    )
    swapped = lax.ppermute(sent, "gz", turn)
    (out,) = call(
        last_kernel,
        [full(5, CELLS, CELLS)],
        [held, swapped],
        1000,
        pl.ANY,
        [pltpu.SemaphoreType.DMA((2,))],
    )
    return out[None]


def solution(mesh):
    in_specs = (P("sec", None, "gx", "gz"), P("sec", None, "gx", "gz"), P(), P())
    out_specs = P("sec", None, "gx", "gz")
    if mesh.shape["gz"] == 2:
        local = functools.partial(local_window, mesh.shape["gx"])
    else:
        local = local_stepwise
    return jax.shard_map(local, mesh=mesh, in_specs=in_specs, out_specs=out_specs, check_vma=False)
```

```python
import functools

import jax
import jax.numpy as jnp
from jax import lax
from jax.experimental import pallas as pl
from jax.experimental.pallas import tpu as pltpu
from jax.sharding import PartitionSpec as P

RADIUS = 4
STEPS = 5
NPD = 8

STENCIL = (0.8, -0.2, 4.0 / 105.0, -1.0 / 280.0)
TIME_STEP = 0.2
COUPLING = 0.5
RELAXATION = (0.9, 0.5)
MEMORY_WEIGHT = (0.15, 0.1)


def padded_2(block, sides, width):
    for axis, dim in sides:
        count = lax.axis_size(axis)
        forward = [(i, i + 1) for i in range(count - 1)]
        backward = [(target, source) for source, target in forward]
        low = lax.ppermute(
            lax.slice_in_dim(block, block.shape[dim] - width, None, axis=dim), axis, forward
        )
        high = lax.ppermute(lax.slice_in_dim(block, 0, width, axis=dim), axis, backward)
        block = jnp.concatenate([low, block, high], axis=dim)
    return block


def broadcast(value, axis, source):
    kept = jnp.where(lax.axis_index(axis) == source, value, 0).astype(value.dtype)
    return lax.psum(kept, axis)


def along_x(padded, anchor, count_x, count_z):
    summed = jnp.zeros(padded.shape[:-2] + (count_x, count_z), jnp.float32)
    for offset, stencil_tap in enumerate(STENCIL, 1):
        forward = padded[
            ..., anchor + offset : anchor + offset + count_x, anchor : anchor + count_z
        ]
        backward = padded[
            ..., anchor - offset : anchor - offset + count_x, anchor : anchor + count_z
        ]
        summed = summed + stencil_tap * (forward - backward)
    return summed


def along_z(padded, anchor, count_x, count_z):
    summed = jnp.zeros(padded.shape[:-2] + (count_x, count_z), jnp.float32)
    for offset, stencil_tap in enumerate(STENCIL, 1):
        forward = padded[
            ..., anchor : anchor + count_x, anchor + offset : anchor + offset + count_z
        ]
        backward = padded[
            ..., anchor : anchor + count_x, anchor - offset : anchor - offset + count_z
        ]
        summed = summed + stencil_tap * (forward - backward)
    return summed


def velocity_elastic(velocity, stresses, buoyancy, anchor, count_x, count_z):
    updated_x = velocity[0] + TIME_STEP * buoyancy * (
        along_x(stresses[0], anchor, count_x, count_z)
        + along_z(stresses[2], anchor, count_x, count_z)
    )
    updated_z = velocity[1] + TIME_STEP * buoyancy * (
        along_x(stresses[2], anchor, count_x, count_z)
        + along_z(stresses[1], anchor, count_x, count_z)
    )
    return jnp.stack([updated_x, updated_z])


def velocity_acoustic(velocity, stresses, buoyancy, anchor, count_x, count_z):
    updated_x = velocity[0] - TIME_STEP * buoyancy * along_x(stresses[0], anchor, count_x, count_z)
    updated_z = velocity[1] - TIME_STEP * buoyancy * along_z(stresses[0], anchor, count_x, count_z)
    return jnp.stack([updated_x, updated_z])


def stress_elastic(stresses, velocity_pad, material, anchor, count_x, count_z):
    strain_x = along_x(velocity_pad[0], anchor, count_x, count_z)
    strain_z = along_z(velocity_pad[1], anchor, count_x, count_z)
    strain_shear = along_z(velocity_pad[0], anchor, count_x, count_z) + along_x(
        velocity_pad[1], anchor, count_x, count_z
    )
    lame_first = material[1]
    shear_modulus = material[2]
    normal_x = stresses[0] + TIME_STEP * (
        (lame_first + 2.0 * shear_modulus) * strain_x + lame_first * strain_z
    )
    normal_z = stresses[1] + TIME_STEP * (
        lame_first * strain_x + (lame_first + 2.0 * shear_modulus) * strain_z
    )
    shear_new = stresses[2] + TIME_STEP * shear_modulus * strain_shear
    return jnp.stack([normal_x, normal_z, shear_new])


def stress_acoustic(stresses, velocity_pad, material, anchor, count_x, count_z):
    divergence = along_x(velocity_pad[0], anchor, count_x, count_z) + along_z(
        velocity_pad[1], anchor, count_x, count_z
    )
    loading = material[1] * divergence
    memory_one = (
        RELAXATION[0] * stresses[1]
        + (1.0 - RELAXATION[0]) * MEMORY_WEIGHT[0] * material[2] * loading
    )
    memory_two = (
        RELAXATION[1] * stresses[2]
        + (1.0 - RELAXATION[1]) * MEMORY_WEIGHT[1] * material[2] * loading
    )
    pressure = stresses[0] - TIME_STEP * (loading - memory_one - memory_two)
    return jnp.stack([pressure, memory_one, memory_two])


def local_stepwise(fields, media, plane_rows, box_offset):
    current = fields[0]
    material = media[0]
    count_x = current.shape[1]
    count_z = current.shape[2]
    section = lax.axis_index("sec")
    is_source = section == 0
    block_z = lax.axis_index("gz")
    local_rows = lax.dynamic_slice_in_dim(plane_rows, block_z * NPD, NPD) - block_z * count_z
    offset = lax.dynamic_slice_in_dim(box_offset, jnp.maximum(section - 1, 0), 1)[0]
    depth_ids = block_z * count_z + jnp.arange(count_z, dtype=jnp.int32)
    landing = offset + plane_rows // 2
    chosen = (landing[:, None] == depth_ids[None, :]).astype(jnp.float32)
    for step_index in range(STEPS):
        stress_pad = padded_2(current[2:5], (("gx", 1), ("gz", 2)), RADIUS)
        velocity = lax.cond(
            is_source,
            lambda: velocity_elastic(
                current[0:2], stress_pad, material[0], RADIUS, count_x, count_z
            ),
            lambda: velocity_acoustic(
                current[0:2], stress_pad, material[0], RADIUS, count_x, count_z
            ),
        )
        velocity_pad = padded_2(velocity, (("gx", 1), ("gz", 2)), RADIUS)
        stresses = lax.cond(
            is_source,
            lambda: stress_elastic(current[2:5], velocity_pad, material, RADIUS, count_x, count_z),
            lambda: stress_acoustic(current[2:5], velocity_pad, material, RADIUS, count_x, count_z),
        )
        current = jnp.concatenate([velocity, stresses], axis=0)
        picked = jnp.take(current, local_rows, axis=2)
        block_plane = jnp.transpose(
            jnp.stack([picked[0], picked[1], -0.5 * (picked[2] + picked[3])]), (0, 2, 1)
        )
        joined = lax.all_gather(block_plane, "gz", axis=1, tiled=True)
        gathered = broadcast(joined, "sec", 0)
        injected = jnp.einsum("ckx,kz->cxz", gathered, chosen, precision=lax.Precision.HIGHEST)
        far_state = jnp.concatenate([current[0:3] + COUPLING * injected, current[3:5]], axis=0)
        current = jnp.where(is_source, current, far_state)
    return current[None]


HALO = 2 * RADIUS * STEPS
CELLS = 128
HALF = CELLS // 2
WINDOW = HALF + 2 * HALO
DEPTH = 2 * CELLS
PART = HALF + HALO
NP = 2 * NPD
TRIM = (0, 8, 16, 24, 32)
WINDOWS = [WINDOW - 2 * amount for amount in TRIM]
COUNTS = len(WINDOWS)
ROWS = 192
GROUPS = CELLS // NP
SLOT = (
    ((0, 0), (1, 0), (2, 0)),
    ((3, 0), (4, 0), (5, 0)),
    ((6, 0), (7, 0), (6, 96)),
    ((3, 112), (4, 112), (5, 112)),
    ((0, 128), (1, 128), (2, 128)),
)
SCALE = 840.0
TAPS = (672.0, -168.0, 32.0, -3.0)


def banded(distance):
    values = jnp.zeros(distance.shape, jnp.float32)
    for offset, tap in enumerate(TAPS, 1):
        values = jnp.where(distance == offset, tap, values)
        values = jnp.where(distance == -offset, -tap, values)
    return values.astype(jnp.bfloat16)


def halves(values):
    high = values.astype(jnp.bfloat16)
    low = (values - high.astype(jnp.float32)).astype(jnp.bfloat16)
    return high, low


def dot(left, right):
    return jnp.dot(left, right, preferred_element_type=jnp.float32)


def diff_x(bands, parts):
    return dot(bands[parts[0].shape[0]][...], jnp.concatenate(parts, axis=0))


def along_depth(matrix, parts):
    return dot(jnp.concatenate(parts, axis=1), matrix[...])


def pair_along_depth(matrix, one, two):
    fields = [jnp.concatenate(parts, axis=1) for parts in (one, two)]
    both = dot(jnp.concatenate(fields, axis=0), matrix[...])
    count = one[0].shape[0]
    return both[:count], both[count:]


def trimmed(arrays, amount):
    if amount == 0:
        return arrays
    return [array[amount:-amount] for array in arrays]


def lanes_of(shape):
    return lax.broadcasted_iota(jnp.int32, shape, 1) // NP


BODY = HALO - 8
WHOLE = (2, 4)
PAIRED = ((0, 1), (3, 5))
EDGE_ROWS = 8 * BODY + 8 * len(WHOLE) + 8 * len(PAIRED)


def pack_edge(block, target, at_end):
    body, rest = (CELLS - BODY, CELLS - HALO) if at_end else (0, BODY)
    near = lax.broadcasted_iota(jnp.int32, (8, CELLS), 0) // 4 == int(at_end)
    for index in range(8):
        target[BODY * index : BODY * (index + 1)] = block[index, body : body + BODY]
    row = 8 * BODY
    for index in WHOLE:
        target[row : row + 8] = block[index, rest : rest + 8]
        row += 8
    for one, two in PAIRED:
        turned = pltpu.roll(block[two, rest : rest + 8], 4, 0)
        target[row : row + 8] = jnp.where(near, block[one, rest : rest + 8], turned)
        row += 8


def unpack_edge(edge, window, lanes, before):
    body, rest = (8, 0) if before else (PART, WINDOW - 8)
    near = lax.broadcasted_iota(jnp.int32, (8, CELLS), 0) // 4 == int(before)
    for index in range(8):
        window[index, body : body + BODY, lanes] = edge[BODY * index : BODY * (index + 1)]
    row = 8 * BODY
    for index in WHOLE:
        window[index, rest : rest + 8, lanes] = edge[row : row + 8]
        row += 8
    for one, two in PAIRED:
        tile = edge[row : row + 8]
        window[one, rest : rest + 8, lanes] = jnp.where(near, tile, 0.0)
        window[two, rest : rest + 8, lanes] = jnp.where(near, pltpu.roll(tile, 4, 0), 0.0)
        row += 8
    for index in (6, 7):
        window[index, rest : rest + 8, lanes] = jnp.zeros((8, CELLS), jnp.float32)


def pack_kernel(fields, media, block, straight, crossed, swap, sems):
    core = lax.axis_index("gz")
    copies = [
        pltpu.make_async_copy(fields, block.at[:5], sems.at[0]),
        pltpu.make_async_copy(media, block.at[5:], sems.at[1]),
    ]
    for copy in copies:
        copy.start()
    for copy in copies:
        copy.wait()

    @pl.when(core == 0)
    def _():
        pack_edge(block, straight, True)
        pack_edge(block, crossed, False)
        swap[...] = block[:, CELLS - PART :]

    @pl.when(core == 1)
    def _():
        pack_edge(block, straight, False)
        pack_edge(block, crossed, True)
        swap[...] = block[:, :PART]


def assemble(window, block, ahead, behind, other):
    core = lax.axis_index("gz")
    low, high = slice(0, CELLS), slice(CELLS, DEPTH)

    @pl.when(core == 0)
    def _():
        unpack_edge(ahead, window, low, True)
        unpack_edge(behind, window, high, True)
        window[:8, HALO:, low] = block[:, :PART]
        window[:8, HALO:, high] = other[...]

    @pl.when(core == 1)
    def _():
        window[:8, :PART, high] = block[:, CELLS - PART :]
        window[:8, :PART, low] = other[...]
        unpack_edge(ahead, window, high, False)
        unpack_edge(behind, window, low, False)


def place(state, held, sent):
    start = HALO - TRIM[-1]
    core = lax.axis_index("gz")
    state = [array[start : start + HALF] for array in state]

    @pl.when(core == 0)
    def _():
        for index in range(5):
            held[index] = state[index][:, :CELLS]
            sent[index] = state[index][:, CELLS:]

    @pl.when(core == 1)
    def _():
        for index in range(5):
            held[index] = state[index][:, CELLS:]
            sent[index] = state[index][:, :CELLS]


def acoustic(state, bands):
    vx, vz, pressure, one, two, light, kappa, loss_one, loss_two = state
    band_x, band_z = bands
    parts = halves(pressure)
    vx = vx - light * diff_x(band_x, parts)
    vz = vz - light * along_depth(band_z, parts)
    load = kappa * (diff_x(band_x, halves(vx)) + along_depth(band_z, halves(vz)))
    one = RELAXATION[0] * one + loss_one * load
    two = RELAXATION[1] * two + loss_two * load
    pressure = pressure - TIME_STEP * (load - one - two)
    return [vx, vz, pressure, one, two, light, kappa, loss_one, loss_two]


def constants_kernel(plane_rows, box_offset, *targets):
    *bands_x, band_z, pick, land = targets
    for target in bands_x:
        count = target.shape[0]
        row = lax.broadcasted_iota(jnp.int32, target.shape, 0)
        column = lax.broadcasted_iota(jnp.int32, target.shape, 1)
        target[...] = banded(jnp.where(column < count, column, column - count) - row)
    shape = (DEPTH, DEPTH)
    distance = lax.broadcasted_iota(jnp.int32, shape, 0) - lax.broadcasted_iota(jnp.int32, shape, 1)
    band_z[:DEPTH] = banded(distance)
    band_z[DEPTH:] = band_z[:DEPTH]
    row = plane_rows[...]
    lane = lax.broadcasted_iota(jnp.int32, box_offset.shape, 1)
    offset = jnp.where(lane == lax.axis_index("sec") - 1, box_offset[...], 0)
    landing = row // 2 + jnp.sum(offset, axis=1, keepdims=True)
    depth = lax.broadcasted_iota(jnp.int32, (DEPTH, NP), 0)
    spread = lax.broadcasted_iota(jnp.int32, (NP, CELLS), 1) % NP
    spread = spread == lax.broadcasted_iota(jnp.int32, (NP, CELLS), 0)
    spread = jnp.where(spread, 1.0, 0.0).astype(jnp.bfloat16)
    hot = jnp.where(depth == row, 1.0, 0.0).astype(jnp.bfloat16)
    pick[:DEPTH] = dot(hot, spread).astype(jnp.bfloat16)
    pick[DEPTH:] = pick[:DEPTH]
    hot = jnp.where(depth == landing, 1.0, 0.0).astype(jnp.bfloat16)
    land[:, :CELLS] = dot(hot, spread).astype(jnp.bfloat16)
    land[:, CELLS:] = land[:, :CELLS]


def first_kernel(*refs):
    bands_x, (band_z, pick, block, behind, ahead, other) = refs[:COUNTS], refs[COUNTS:-4]
    held, sent, rows, carry = refs[-4:]
    band_x = {band.shape[0]: band for band in bands_x}
    assemble(carry, block, ahead, behind, other)
    section = lax.axis_index("sec")

    @pl.when(section == 0)
    def _():
        vx, vz, sxx, szz, sxz, light, lame, shear = [carry[index] for index in range(8)]
        light = light * (TIME_STEP / SCALE)
        both = (lame + 2.0 * shear) * (TIME_STEP / SCALE)
        lame = lame * (TIME_STEP / SCALE)
        shear = shear * (TIME_STEP / SCALE)
        at = 0
        for step in range(STEPS):
            cut = TRIM[step] - at
            at = TRIM[step]
            vx, vz, sxx, szz, sxz, light, both, lame, shear = trimmed(
                [vx, vz, sxx, szz, sxz, light, both, lame, shear], cut
            )
            parts_xx, parts_zz, parts_xz = halves(sxx), halves(szz), halves(sxz)
            slope_xz, slope_zz = pair_along_depth(band_z, parts_xz, parts_zz)
            vx = vx + light * (diff_x(band_x, parts_xx) + slope_xz)
            vz = vz + light * (diff_x(band_x, parts_xz) + slope_zz)
            parts_x, parts_z = halves(vx), halves(vz)
            slope_x, strain_z = pair_along_depth(band_z, parts_x, parts_z)
            strain_x = diff_x(band_x, parts_x)
            sxx = sxx + (both * strain_x + lame * strain_z)
            szz = szz + (lame * strain_x + both * strain_z)
            sxz = sxz + shear * (slope_x + diff_x(band_x, parts_z))
            rows_x, rows_z = pair_along_depth(pick, parts_x, parts_z)
            stress = along_depth(pick, halves(sxx + szz))
            low = 2 * RADIUS * (step + 1) - at
            for component, (picked, factor) in enumerate(
                ((rows_x, COUPLING), (rows_z, COUPLING), (stress, -0.5 * COUPLING))
            ):
                picked = factor * picked
                picked = picked[low : picked.shape[0] - low]
                group, base = SLOT[step][component]
                spot = pl.ds(base, picked.shape[0])
                rows[spot] = jnp.where(lanes_of(picked.shape) == group, picked, rows[spot])
        place([vx, vz, sxx, szz, sxz], held, sent)

    @pl.when(section > 0)
    def _():
        vx, vz, pressure, one, two, light, kappa, loss = [carry[index] for index in range(8)]
        light = light * (TIME_STEP / SCALE)
        kappa = kappa * (1.0 / SCALE)
        loss_one = loss * ((1.0 - RELAXATION[0]) * MEMORY_WEIGHT[0])
        loss_two = loss * ((1.0 - RELAXATION[1]) * MEMORY_WEIGHT[1])
        state = [vx, vz, pressure, one, two, light, kappa, loss_one, loss_two]
        for index, array in enumerate(acoustic(state, (band_x, band_z))):
            carry[index] = array


def second_kernel(*refs):
    bands_x, (band_z, land, carry, rows, held_in, sent_in, held, sent) = refs[:COUNTS], refs[COUNTS:]
    band_x = {band.shape[0]: band for band in bands_x}
    section = lax.axis_index("sec")

    @pl.when(section == 0)
    def _():
        held[...] = held_in[...]
        sent[...] = sent_in[...]

    @pl.when(section > 0)
    def _():
        state = [carry[index] for index in range(9)]
        at = 0
        for step in range(STEPS):
            if step:
                state = trimmed(state, TRIM[step] - at)
                at = TRIM[step]
                state = acoustic(state, (band_x, band_z))
            low = 2 * RADIUS * (step + 1) - at
            high = WINDOW - 2 * at - low
            for component in range(3):
                group, base = SLOT[step][component]
                taken = rows[pl.ds(base, high - low)]
                taken = halves(jnp.where(lanes_of(taken.shape) == group, taken, 0.0))
                added = lax.dot_general(
                    jnp.concatenate(taken, axis=1),
                    land[...],
                    (((1,), (1,)), ((), ())),
                    preferred_element_type=jnp.float32,
                )
                array = state[component]
                state[component] = jnp.concatenate(
                    [array[:low], array[low:high] + added, array[high:]], axis=0
                )
        place(state[:5], held, sent)


def last_kernel(held, swapped, out, sems):
    core = lax.axis_index("gz")
    copies = [
        pltpu.make_async_copy(
            source, out.at[:, pl.ds(pl.multiple_of(HALF * half, HALF), HALF)], sems.at[index]
        )
        for index, (source, half) in enumerate(((held, core), (swapped, 1 - core)))
    ]
    for copy in copies:
        copy.start()
    for copy in copies:
        copy.wait()


def call(
    kernel,
    outs,
    operands,
    flops,
    place_in=pltpu.VMEM,
    place_out=pltpu.VMEM,
    scratch=(),
):
    return pl.pallas_call(
        kernel,
        out_shape=outs,
        in_specs=[pl.BlockSpec(memory_space=place_in)] * len(operands),
        out_specs=[pl.BlockSpec(memory_space=place_out)] * len(outs),
        scratch_shapes=scratch,
        compiler_params=pltpu.CompilerParams(vmem_limit_bytes=48 * 1024 * 1024),
        cost_estimate=pl.CostEstimate(
            flops=flops, bytes_accessed=2 * 1024 * 1024, transcendentals=0
        ),
    )(*operands)


def full(*shape):
    return jax.ShapeDtypeStruct(shape, jnp.float32)


def narrow(*shape):
    return jax.ShapeDtypeStruct(shape, jnp.bfloat16)


def local_window(columns, fields, media, plane_rows, box_offset):
    fields, media = fields[0], media[0]
    core = lax.axis_index("gz")
    is_first = core == 0
    block, straight, crossed, swap = call(
        pack_kernel,
        [
            full(8, CELLS, CELLS),
            full(EDGE_ROWS, CELLS),
            full(EDGE_ROWS, CELLS),
            full(8, PART, CELLS),
        ],
        [pltpu.with_memory_space_constraint(array, pltpu.HBM) for array in (fields, media)],
        1000,
        place_in=pltpu.HBM,
        scratch=[pltpu.SemaphoreType.DMA((2,))],
    )
    straight_pairs, crossed_pairs = [], []
    for column in range(columns):
        if column + 1 < columns:
            straight_pairs.append((2 * column, 2 * column + 2))
            crossed_pairs.append((2 * column + 1, 2 * column + 2))
        if column:
            straight_pairs.append((2 * column + 1, 2 * column - 1))
            crossed_pairs.append((2 * column, 2 * column - 1))
    turn = [(0, 1), (1, 0)]
    behind = lax.ppermute(crossed, ("gx", "gz"), crossed_pairs)
    ahead = lax.ppermute(straight, ("gx", "gz"), straight_pairs)
    joined = lax.all_gather(swap, "gz")
    other = jnp.where(is_first, joined[1], joined[0])
    *bands, pick, land = call(
        constants_kernel,
        [narrow(count, 2 * count) for count in WINDOWS]
        + [narrow(2 * DEPTH, DEPTH), narrow(2 * DEPTH, CELLS), narrow(DEPTH, 2 * CELLS)],
        [plane_rows[None], box_offset[None]],
        1_000_000_000,
    )
    held, sent, rows, carry = call(
        first_kernel,
        [
            full(5, HALF, CELLS),
            full(5, HALF, CELLS),
            full(ROWS, CELLS),
            full(9, WINDOW, DEPTH),
        ],
        [*bands, pick, block, behind, ahead, other],
        4_000_000_000,
    )
    arrived = [lax.ppermute(rows, "sec", [(0, target)]) for target in (1, 2, 3)]
    rows = arrived[0] + arrived[1] + arrived[2]
    held, sent = call(
        second_kernel,
        [full(5, HALF, CELLS), full(5, HALF, CELLS)],
        [*bands, land, carry, rows, held, sent],
        4_000_000_000,
    )
    swapped = lax.ppermute(sent, "gz", turn)
    (out,) = call(
        last_kernel,
        [full(5, CELLS, CELLS)],
        [held, swapped],
        1000,
        place_out=pl.ANY,
        scratch=[pltpu.SemaphoreType.DMA((2,))],
    )
    return out[None]


def solution(mesh):
    in_specs = (P("sec", None, "gx", "gz"), P("sec", None, "gx", "gz"), P(), P())
    out_specs = P("sec", None, "gx", "gz")
    if mesh.shape["gz"] == 2:
        local = functools.partial(local_window, mesh.shape["gx"])
    else:
        local = local_stepwise
    return jax.shard_map(local, mesh=mesh, in_specs=in_specs, out_specs=out_specs, check_vma=False)
```

```python
import functools

import jax
import jax.numpy as jnp
from jax import lax
from jax.experimental import pallas as pl
from jax.experimental.pallas import tpu as pltpu
from jax.sharding import PartitionSpec as P

RADIUS = 4
STEPS = 5
NPD = 8

STENCIL = (0.8, -0.2, 4.0 / 105.0, -1.0 / 280.0)
TIME_STEP = 0.2
COUPLING = 0.5
RELAXATION = (0.9, 0.5)
MEMORY_WEIGHT = (0.15, 0.1)


def padded_2(block, sides, width):
    for axis, dim in sides:
        count = lax.axis_size(axis)
        forward = [(i, i + 1) for i in range(count - 1)]
        backward = [(target, source) for source, target in forward]
        low = lax.ppermute(
            lax.slice_in_dim(block, block.shape[dim] - width, None, axis=dim), axis, forward
        )
        high = lax.ppermute(lax.slice_in_dim(block, 0, width, axis=dim), axis, backward)
        block = jnp.concatenate([low, block, high], axis=dim)
    return block


def broadcast(value, axis, source):
    kept = jnp.where(lax.axis_index(axis) == source, value, 0).astype(value.dtype)
    return lax.psum(kept, axis)


def along_x(padded, anchor, count_x, count_z):
    summed = jnp.zeros(padded.shape[:-2] + (count_x, count_z), jnp.float32)
    for offset, stencil_tap in enumerate(STENCIL, 1):
        forward = padded[
            ..., anchor + offset : anchor + offset + count_x, anchor : anchor + count_z
        ]
        backward = padded[
            ..., anchor - offset : anchor - offset + count_x, anchor : anchor + count_z
        ]
        summed = summed + stencil_tap * (forward - backward)
    return summed


def along_z(padded, anchor, count_x, count_z):
    summed = jnp.zeros(padded.shape[:-2] + (count_x, count_z), jnp.float32)
    for offset, stencil_tap in enumerate(STENCIL, 1):
        forward = padded[
            ..., anchor : anchor + count_x, anchor + offset : anchor + offset + count_z
        ]
        backward = padded[
            ..., anchor : anchor + count_x, anchor - offset : anchor - offset + count_z
        ]
        summed = summed + stencil_tap * (forward - backward)
    return summed


def velocity_elastic(velocity, stresses, buoyancy, anchor, count_x, count_z):
    updated_x = velocity[0] + TIME_STEP * buoyancy * (
        along_x(stresses[0], anchor, count_x, count_z)
        + along_z(stresses[2], anchor, count_x, count_z)
    )
    updated_z = velocity[1] + TIME_STEP * buoyancy * (
        along_x(stresses[2], anchor, count_x, count_z)
        + along_z(stresses[1], anchor, count_x, count_z)
    )
    return jnp.stack([updated_x, updated_z])


def velocity_acoustic(velocity, stresses, buoyancy, anchor, count_x, count_z):
    updated_x = velocity[0] - TIME_STEP * buoyancy * along_x(stresses[0], anchor, count_x, count_z)
    updated_z = velocity[1] - TIME_STEP * buoyancy * along_z(stresses[0], anchor, count_x, count_z)
    return jnp.stack([updated_x, updated_z])


def stress_elastic(stresses, velocity_pad, material, anchor, count_x, count_z):
    strain_x = along_x(velocity_pad[0], anchor, count_x, count_z)
    strain_z = along_z(velocity_pad[1], anchor, count_x, count_z)
    strain_shear = along_z(velocity_pad[0], anchor, count_x, count_z) + along_x(
        velocity_pad[1], anchor, count_x, count_z
    )
    lame_first = material[1]
    shear_modulus = material[2]
    normal_x = stresses[0] + TIME_STEP * (
        (lame_first + 2.0 * shear_modulus) * strain_x + lame_first * strain_z
    )
    normal_z = stresses[1] + TIME_STEP * (
        lame_first * strain_x + (lame_first + 2.0 * shear_modulus) * strain_z
    )
    shear_new = stresses[2] + TIME_STEP * shear_modulus * strain_shear
    return jnp.stack([normal_x, normal_z, shear_new])


def stress_acoustic(stresses, velocity_pad, material, anchor, count_x, count_z):
    divergence = along_x(velocity_pad[0], anchor, count_x, count_z) + along_z(
        velocity_pad[1], anchor, count_x, count_z
    )
    loading = material[1] * divergence
    memory_one = (
        RELAXATION[0] * stresses[1]
        + (1.0 - RELAXATION[0]) * MEMORY_WEIGHT[0] * material[2] * loading
    )
    memory_two = (
        RELAXATION[1] * stresses[2]
        + (1.0 - RELAXATION[1]) * MEMORY_WEIGHT[1] * material[2] * loading
    )
    pressure = stresses[0] - TIME_STEP * (loading - memory_one - memory_two)
    return jnp.stack([pressure, memory_one, memory_two])


def local_stepwise(fields, media, plane_rows, box_offset):
    current = fields[0]
    material = media[0]
    count_x = current.shape[1]
    count_z = current.shape[2]
    section = lax.axis_index("sec")
    is_source = section == 0
    block_z = lax.axis_index("gz")
    local_rows = lax.dynamic_slice_in_dim(plane_rows, block_z * NPD, NPD) - block_z * count_z
    offset = lax.dynamic_slice_in_dim(box_offset, jnp.maximum(section - 1, 0), 1)[0]
    depth_ids = block_z * count_z + jnp.arange(count_z, dtype=jnp.int32)
    landing = offset + plane_rows // 2
    chosen = (landing[:, None] == depth_ids[None, :]).astype(jnp.float32)
    for step_index in range(STEPS):
        stress_pad = padded_2(current[2:5], (("gx", 1), ("gz", 2)), RADIUS)
        velocity = lax.cond(
            is_source,
            lambda: velocity_elastic(
                current[0:2], stress_pad, material[0], RADIUS, count_x, count_z
            ),
            lambda: velocity_acoustic(
                current[0:2], stress_pad, material[0], RADIUS, count_x, count_z
            ),
        )
        velocity_pad = padded_2(velocity, (("gx", 1), ("gz", 2)), RADIUS)
        stresses = lax.cond(
            is_source,
            lambda: stress_elastic(current[2:5], velocity_pad, material, RADIUS, count_x, count_z),
            lambda: stress_acoustic(current[2:5], velocity_pad, material, RADIUS, count_x, count_z),
        )
        current = jnp.concatenate([velocity, stresses], axis=0)
        picked = jnp.take(current, local_rows, axis=2)
        block_plane = jnp.transpose(
            jnp.stack([picked[0], picked[1], -0.5 * (picked[2] + picked[3])]), (0, 2, 1)
        )
        joined = lax.all_gather(block_plane, "gz", axis=1, tiled=True)
        gathered = broadcast(joined, "sec", 0)
        injected = jnp.einsum("ckx,kz->cxz", gathered, chosen, precision=lax.Precision.HIGHEST)
        far_state = jnp.concatenate([current[0:3] + COUPLING * injected, current[3:5]], axis=0)
        current = jnp.where(is_source, current, far_state)
    return current[None]


HALO = 2 * RADIUS * STEPS
CELLS = 128
HALF = CELLS // 2
WINDOW = HALF + 2 * HALO
DEPTH = 2 * CELLS
PART = HALF + HALO
NP = 2 * NPD
ROWS = 192
GROUPS = CELLS // NP
SLOT = (
    ((0, 0), (1, 0), (2, 0)),
    ((3, 0), (4, 0), (5, 0)),
    ((6, 0), (7, 0), (6, 96)),
    ((3, 112), (4, 112), (5, 112)),
    ((0, 128), (1, 128), (2, 128)),
)
SCALE = 840.0
TAPS = (672.0, -168.0, 32.0, -3.0)


def banded(distance):
    values = jnp.zeros(distance.shape, jnp.float32)
    for offset, tap in enumerate(TAPS, 1):
        values = jnp.where(distance == offset, tap, values)
        values = jnp.where(distance == -offset, -tap, values)
    return values.astype(jnp.bfloat16)


def halves(values):
    high = values.astype(jnp.bfloat16)
    low = (values - high.astype(jnp.float32)).astype(jnp.bfloat16)
    return high, low


def dot(left, right):
    return jnp.dot(left, right, preferred_element_type=jnp.float32)


def diff_x(bands, parts):
    return dot(bands[...], jnp.concatenate(parts, axis=0))


def along_depth(matrix, parts):
    return dot(jnp.concatenate(parts, axis=1), matrix[...])


def lanes_of(shape):
    return lax.broadcasted_iota(jnp.int32, shape, 1) // NP


BODY = HALO - 8
WHOLE = (2, 4)
PAIRED = ((0, 1), (3, 5))
EDGE_ROWS = 8 * BODY + 8 * len(WHOLE) + 8 * len(PAIRED)


def pack_edge(block, target, at_end):
    body, rest = (CELLS - BODY, CELLS - HALO) if at_end else (0, BODY)
    near = lax.broadcasted_iota(jnp.int32, (8, CELLS), 0) // 4 == int(at_end)
    for index in range(8):
        target[BODY * index : BODY * (index + 1)] = block[index, body : body + BODY]
    row = 8 * BODY
    for index in WHOLE:
        target[row : row + 8] = block[index, rest : rest + 8]
        row += 8
    for one, two in PAIRED:
        turned = pltpu.roll(block[two, rest : rest + 8], 4, 0)
        target[row : row + 8] = jnp.where(near, block[one, rest : rest + 8], turned)
        row += 8


def unpack_edge(edge, window, lanes, before):
    body, rest = (8, 0) if before else (PART, WINDOW - 8)
    near = lax.broadcasted_iota(jnp.int32, (8, CELLS), 0) // 4 == int(before)
    for index in range(8):
        window[index, body : body + BODY, lanes] = edge[BODY * index : BODY * (index + 1)]
    row = 8 * BODY
    for index in WHOLE:
        window[index, rest : rest + 8, lanes] = edge[row : row + 8]
        row += 8
    for one, two in PAIRED:
        tile = edge[row : row + 8]
        window[one, rest : rest + 8, lanes] = jnp.where(near, tile, 0.0)
        window[two, rest : rest + 8, lanes] = jnp.where(near, pltpu.roll(tile, 4, 0), 0.0)
        row += 8
    for index in (6, 7):
        window[index, rest : rest + 8, lanes] = jnp.zeros((8, CELLS), jnp.float32)


def pack_kernel(fields, media, block, straight, crossed, swap, sems):
    core = lax.axis_index("gz")
    copies = [
        pltpu.make_async_copy(fields, block.at[:5], sems.at[0]),
        pltpu.make_async_copy(media, block.at[5:], sems.at[1]),
    ]
    for copy in copies:
        copy.start()
    for copy in copies:
        copy.wait()

    @pl.when(core == 0)
    def _():
        pack_edge(block, straight, True)
        pack_edge(block, crossed, False)
        swap[...] = block[:, CELLS - PART :]

    @pl.when(core == 1)
    def _():
        pack_edge(block, straight, False)
        pack_edge(block, crossed, True)
        swap[...] = block[:, :PART]


def assemble(window, block, ahead, behind, other):
    core = lax.axis_index("gz")
    low, high = slice(0, CELLS), slice(CELLS, DEPTH)

    @pl.when(core == 0)
    def _():
        unpack_edge(ahead, window, low, True)
        unpack_edge(behind, window, high, True)
        window[:8, HALO:, low] = block[:, :PART]
        window[:8, HALO:, high] = other[...]

    @pl.when(core == 1)
    def _():
        window[:8, :PART, high] = block[:, CELLS - PART :]
        window[:8, :PART, low] = other[...]
        unpack_edge(ahead, window, high, False)
        unpack_edge(behind, window, low, False)


def span(step):
    gone = 2 * RADIUS * (step + 1)
    return pl.ds(gone, WINDOW - 2 * gone)


def place(state, held, sent):
    core = lax.axis_index("gz")
    low, high = slice(0, CELLS), slice(CELLS, DEPTH)
    own = span(STEPS - 1)

    @pl.when(core == 0)
    def _():
        held[...] = state[:5, own, low]
        sent[...] = state[:5, own, high]

    @pl.when(core == 1)
    def _():
        held[...] = state[:5, own, high]
        sent[...] = state[:5, own, low]


def acoustic(state, bands):
    vx, vz, pressure, one, two, light, kappa, loss_one, loss_two = state
    band_x, band_z = bands
    parts = halves(pressure)
    vx = vx - light * diff_x(band_x, parts)
    vz = vz - light * along_depth(band_z, parts)
    load = kappa * (diff_x(band_x, halves(vx)) + along_depth(band_z, halves(vz)))
    one = RELAXATION[0] * one + loss_one * load
    two = RELAXATION[1] * two + loss_two * load
    pressure = pressure - TIME_STEP * (load - one - two)
    return [vx, vz, pressure, one, two, light, kappa, loss_one, loss_two]


def constants_kernel(plane_rows, box_offset, *targets):
    band_x, band_z, pick, land = targets
    row = lax.broadcasted_iota(jnp.int32, band_x.shape, 0)
    column = lax.broadcasted_iota(jnp.int32, band_x.shape, 1)
    band_x[...] = banded(jnp.where(column < WINDOW, column, column - WINDOW) - row)
    shape = (DEPTH, DEPTH)
    distance = lax.broadcasted_iota(jnp.int32, shape, 0) - lax.broadcasted_iota(jnp.int32, shape, 1)
    band_z[:DEPTH] = banded(distance)
    band_z[DEPTH:] = band_z[:DEPTH]
    row = plane_rows[...]
    lane = lax.broadcasted_iota(jnp.int32, box_offset.shape, 1)
    offset = jnp.where(lane == lax.axis_index("sec") - 1, box_offset[...], 0)
    landing = row // 2 + jnp.sum(offset, axis=1, keepdims=True)
    depth = lax.broadcasted_iota(jnp.int32, (DEPTH, NP), 0)
    spread = lax.broadcasted_iota(jnp.int32, (NP, CELLS), 1) % NP
    spread = spread == lax.broadcasted_iota(jnp.int32, (NP, CELLS), 0)
    spread = jnp.where(spread, 1.0, 0.0).astype(jnp.bfloat16)
    hot = jnp.where(depth == row, 1.0, 0.0).astype(jnp.bfloat16)
    pick[:DEPTH] = dot(hot, spread).astype(jnp.bfloat16)
    pick[DEPTH:] = pick[:DEPTH]
    hot = jnp.where(depth == landing, 1.0, 0.0).astype(jnp.bfloat16)
    land[:, :CELLS] = dot(hot, spread).astype(jnp.bfloat16)
    land[:, CELLS:] = land[:, :CELLS]


def first_kernel(
    band_x, band_z, pick, block, behind, ahead, other, held, sent, rows, carry, picks
):
    assemble(carry, block, ahead, behind, other)
    section = lax.axis_index("sec")

    @pl.when(section == 0)
    def _():
        light, lame, shear = carry[5], carry[6], carry[7]
        carry[5] = light * (TIME_STEP / SCALE)
        carry[6] = (lame + 2.0 * shear) * (TIME_STEP / SCALE)
        carry[7] = lame * (TIME_STEP / SCALE)
        carry[8] = shear * (TIME_STEP / SCALE)

        @pl.loop(0, STEPS)
        def _(step):
            sxx, szz, sxz, light = carry[2], carry[3], carry[4], carry[5]
            parts_xx, parts_zz, parts_xz = halves(sxx), halves(szz), halves(sxz)
            vx = carry[0] + light * (diff_x(band_x, parts_xx) + along_depth(band_z, parts_xz))
            vz = carry[1] + light * (diff_x(band_x, parts_xz) + along_depth(band_z, parts_zz))
            carry[0], carry[1] = vx, vz
            parts_x, parts_z = halves(vx), halves(vz)
            strain_x, strain_z = diff_x(band_x, parts_x), along_depth(band_z, parts_z)
            both, lame, shear = carry[6], carry[7], carry[8]
            sxx = sxx + (both * strain_x + lame * strain_z)
            szz = szz + (lame * strain_x + both * strain_z)
            carry[2], carry[3] = sxx, szz
            carry[4] = sxz + shear * (along_depth(band_z, parts_x) + diff_x(band_x, parts_z))
            picks[3 * step] = COUPLING * along_depth(pick, parts_x)
            picks[3 * step + 1] = COUPLING * along_depth(pick, parts_z)
            picks[3 * step + 2] = (-0.5 * COUPLING) * along_depth(pick, halves(sxx + szz))

        for step in range(STEPS):
            for component, (group, base) in enumerate(SLOT[step]):
                picked = picks[3 * step + component, span(step)]
                spot = pl.ds(base, picked.shape[0])
                rows[spot] = jnp.where(lanes_of(picked.shape) == group, picked, rows[spot])
        place(carry, held, sent)

    @pl.when(section > 0)
    def _():
        vx, vz, pressure, one, two, light, kappa, loss = [carry[index] for index in range(8)]
        light = light * (TIME_STEP / SCALE)
        kappa = kappa * (1.0 / SCALE)
        loss_one = loss * ((1.0 - RELAXATION[0]) * MEMORY_WEIGHT[0])
        loss_two = loss * ((1.0 - RELAXATION[1]) * MEMORY_WEIGHT[1])
        state = [vx, vz, pressure, one, two, light, kappa, loss_one, loss_two]
        for index, array in enumerate(acoustic(state, (band_x, band_z))):
            carry[index] = array


def second_kernel(
    band_x, band_z, land, carry, rows, held_in, sent_in, held, sent, state, picks
):
    section = lax.axis_index("sec")

    def inject(values, group):
        added = lax.dot_general(
            jnp.concatenate(halves(picks[group]), axis=1),
            land[...],
            (((1,), (1,)), ((), ())),
            preferred_element_type=jnp.float32,
        )
        return values + added

    @pl.when(section == 0)
    def _():
        held[...] = held_in[...]
        sent[...] = sent_in[...]

    @pl.when(section > 0)
    def _():
        for step in range(STEPS):
            edge = 2 * RADIUS * (step + 1)
            for component, (group, base) in enumerate(SLOT[step]):
                taken = rows[pl.ds(base, WINDOW - 2 * edge)]
                taken = jnp.where(lanes_of(taken.shape) == group, taken, 0.0)
                index = 3 * step + component
                picks[index, span(step)] = taken
                picks[index, :edge] = jnp.zeros((edge, CELLS), jnp.float32)
                picks[index, WINDOW - edge :] = jnp.zeros((edge, CELLS), jnp.float32)
        for index in range(3):
            state[index] = inject(carry[index], index)
        state[3:] = carry[3:5]

        @pl.loop(1, STEPS)
        def _(step):
            fields = [state[index] for index in range(5)]
            media = [carry[index] for index in range(5, 9)]
            fields = acoustic(fields + media, (band_x, band_z))
            for index in range(3):
                state[index] = inject(fields[index], 3 * step + index)
            state[3], state[4] = fields[3], fields[4]

        place(state, held, sent)


def last_kernel(held, swapped, out, sems):
    core = lax.axis_index("gz")
    copies = [
        pltpu.make_async_copy(
            source, out.at[:, pl.ds(pl.multiple_of(HALF * half, HALF), HALF)], sems.at[index]
        )
        for index, (source, half) in enumerate(((held, core), (swapped, 1 - core)))
    ]
    for copy in copies:
        copy.start()
    for copy in copies:
        copy.wait()


def call(
    kernel,
    outs,
    operands,
    flops,
    place_in=pltpu.VMEM,
    place_out=pltpu.VMEM,
    scratch=(),
):
    return pl.pallas_call(
        kernel,
        out_shape=outs,
        in_specs=[pl.BlockSpec(memory_space=place_in)] * len(operands),
        out_specs=[pl.BlockSpec(memory_space=place_out)] * len(outs),
        scratch_shapes=scratch,
        compiler_params=pltpu.CompilerParams(vmem_limit_bytes=48 * 1024 * 1024),
        cost_estimate=pl.CostEstimate(
            flops=flops, bytes_accessed=2 * 1024 * 1024, transcendentals=0
        ),
    )(*operands)


def full(*shape):
    return jax.ShapeDtypeStruct(shape, jnp.float32)


def narrow(*shape):
    return jax.ShapeDtypeStruct(shape, jnp.bfloat16)


def local_window(columns, fields, media, plane_rows, box_offset):
    fields, media = fields[0], media[0]
    core = lax.axis_index("gz")
    is_first = core == 0
    block, straight, crossed, swap = call(
        pack_kernel,
        [
            full(8, CELLS, CELLS),
            full(EDGE_ROWS, CELLS),
            full(EDGE_ROWS, CELLS),
            full(8, PART, CELLS),
        ],
        [pltpu.with_memory_space_constraint(array, pltpu.HBM) for array in (fields, media)],
        1000,
        place_in=pltpu.HBM,
        scratch=[pltpu.SemaphoreType.DMA((2,))],
    )
    straight_pairs, crossed_pairs = [], []
    for column in range(columns):
        if column + 1 < columns:
            straight_pairs.append((2 * column, 2 * column + 2))
            crossed_pairs.append((2 * column + 1, 2 * column + 2))
        if column:
            straight_pairs.append((2 * column + 1, 2 * column - 1))
            crossed_pairs.append((2 * column, 2 * column - 1))
    turn = [(0, 1), (1, 0)]
    behind = lax.ppermute(crossed, ("gx", "gz"), crossed_pairs)
    ahead = lax.ppermute(straight, ("gx", "gz"), straight_pairs)
    joined = lax.all_gather(swap, "gz")
    other = jnp.where(is_first, joined[1], joined[0])
    *bands, pick, land = call(
        constants_kernel,
        [
            narrow(WINDOW, 2 * WINDOW),
            narrow(2 * DEPTH, DEPTH),
            narrow(2 * DEPTH, CELLS),
            narrow(DEPTH, 2 * CELLS),
        ],
        [plane_rows[None], box_offset[None]],
        1_000_000_000,
    )
    held, sent, rows, carry = call(
        first_kernel,
        [
            full(5, HALF, CELLS),
            full(5, HALF, CELLS),
            full(ROWS, CELLS),
            full(9, WINDOW, DEPTH),
        ],
        [*bands, pick, block, behind, ahead, other],
        4_000_000_000,
        scratch=[pltpu.VMEM((3 * STEPS, WINDOW, CELLS), jnp.float32)],
    )
    arrived = [lax.ppermute(rows, "sec", [(0, target)]) for target in (1, 2, 3)]
    rows = arrived[0] + arrived[1] + arrived[2]
    held, sent = call(
        second_kernel,
        [full(5, HALF, CELLS), full(5, HALF, CELLS)],
        [*bands, land, carry, rows, held, sent],
        4_000_000_000,
        scratch=[
            pltpu.VMEM((5, WINDOW, DEPTH), jnp.float32),
            pltpu.VMEM((3 * STEPS, WINDOW, CELLS), jnp.float32),
        ],
    )
    swapped = lax.ppermute(sent, "gz", turn)
    (out,) = call(
        last_kernel,
        [full(5, CELLS, CELLS)],
        [held, swapped],
        1000,
        place_out=pl.ANY,
        scratch=[pltpu.SemaphoreType.DMA((2,))],
    )
    return out[None]


def solution(mesh):
    in_specs = (P("sec", None, "gx", "gz"), P("sec", None, "gx", "gz"), P(), P())
    out_specs = P("sec", None, "gx", "gz")
    if mesh.shape["gz"] == 2:
        local = functools.partial(local_window, mesh.shape["gx"])
    else:
        local = local_stepwise
    return jax.shard_map(local, mesh=mesh, in_specs=in_specs, out_specs=out_specs, check_vma=False)
```

```python
import functools

import jax
import jax.numpy as jnp
from jax import lax
from jax.experimental import pallas as pl
from jax.experimental.pallas import tpu as pltpu
from jax.sharding import PartitionSpec as P

RADIUS = 4
STEPS = 5
NPD = 8

STENCIL = (0.8, -0.2, 4.0 / 105.0, -1.0 / 280.0)
TIME_STEP = 0.2
COUPLING = 0.5
RELAXATION = (0.9, 0.5)
MEMORY_WEIGHT = (0.15, 0.1)


def padded_2(block, sides, width):
    for axis, dim in sides:
        count = lax.axis_size(axis)
        forward = [(i, i + 1) for i in range(count - 1)]
        backward = [(target, source) for source, target in forward]
        low = lax.ppermute(
            lax.slice_in_dim(block, block.shape[dim] - width, None, axis=dim), axis, forward
        )
        high = lax.ppermute(lax.slice_in_dim(block, 0, width, axis=dim), axis, backward)
        block = jnp.concatenate([low, block, high], axis=dim)
    return block


def broadcast(value, axis, source):
    kept = jnp.where(lax.axis_index(axis) == source, value, 0).astype(value.dtype)
    return lax.psum(kept, axis)


def along_x(padded, anchor, count_x, count_z):
    summed = jnp.zeros(padded.shape[:-2] + (count_x, count_z), jnp.float32)
    for offset, stencil_tap in enumerate(STENCIL, 1):
        forward = padded[
            ..., anchor + offset : anchor + offset + count_x, anchor : anchor + count_z
        ]
        backward = padded[
            ..., anchor - offset : anchor - offset + count_x, anchor : anchor + count_z
        ]
        summed = summed + stencil_tap * (forward - backward)
    return summed


def along_z(padded, anchor, count_x, count_z):
    summed = jnp.zeros(padded.shape[:-2] + (count_x, count_z), jnp.float32)
    for offset, stencil_tap in enumerate(STENCIL, 1):
        forward = padded[
            ..., anchor : anchor + count_x, anchor + offset : anchor + offset + count_z
        ]
        backward = padded[
            ..., anchor : anchor + count_x, anchor - offset : anchor - offset + count_z
        ]
        summed = summed + stencil_tap * (forward - backward)
    return summed


def velocity_elastic(velocity, stresses, buoyancy, anchor, count_x, count_z):
    updated_x = velocity[0] + TIME_STEP * buoyancy * (
        along_x(stresses[0], anchor, count_x, count_z)
        + along_z(stresses[2], anchor, count_x, count_z)
    )
    updated_z = velocity[1] + TIME_STEP * buoyancy * (
        along_x(stresses[2], anchor, count_x, count_z)
        + along_z(stresses[1], anchor, count_x, count_z)
    )
    return jnp.stack([updated_x, updated_z])


def velocity_acoustic(velocity, stresses, buoyancy, anchor, count_x, count_z):
    updated_x = velocity[0] - TIME_STEP * buoyancy * along_x(stresses[0], anchor, count_x, count_z)
    updated_z = velocity[1] - TIME_STEP * buoyancy * along_z(stresses[0], anchor, count_x, count_z)
    return jnp.stack([updated_x, updated_z])


def stress_elastic(stresses, velocity_pad, material, anchor, count_x, count_z):
    strain_x = along_x(velocity_pad[0], anchor, count_x, count_z)
    strain_z = along_z(velocity_pad[1], anchor, count_x, count_z)
    strain_shear = along_z(velocity_pad[0], anchor, count_x, count_z) + along_x(
        velocity_pad[1], anchor, count_x, count_z
    )
    lame_first = material[1]
    shear_modulus = material[2]
    normal_x = stresses[0] + TIME_STEP * (
        (lame_first + 2.0 * shear_modulus) * strain_x + lame_first * strain_z
    )
    normal_z = stresses[1] + TIME_STEP * (
        lame_first * strain_x + (lame_first + 2.0 * shear_modulus) * strain_z
    )
    shear_new = stresses[2] + TIME_STEP * shear_modulus * strain_shear
    return jnp.stack([normal_x, normal_z, shear_new])


def stress_acoustic(stresses, velocity_pad, material, anchor, count_x, count_z):
    divergence = along_x(velocity_pad[0], anchor, count_x, count_z) + along_z(
        velocity_pad[1], anchor, count_x, count_z
    )
    loading = material[1] * divergence
    memory_one = (
        RELAXATION[0] * stresses[1]
        + (1.0 - RELAXATION[0]) * MEMORY_WEIGHT[0] * material[2] * loading
    )
    memory_two = (
        RELAXATION[1] * stresses[2]
        + (1.0 - RELAXATION[1]) * MEMORY_WEIGHT[1] * material[2] * loading
    )
    pressure = stresses[0] - TIME_STEP * (loading - memory_one - memory_two)
    return jnp.stack([pressure, memory_one, memory_two])


def local_stepwise(fields, media, plane_rows, box_offset):
    current = fields[0]
    material = media[0]
    count_x = current.shape[1]
    count_z = current.shape[2]
    section = lax.axis_index("sec")
    is_source = section == 0
    block_z = lax.axis_index("gz")
    local_rows = lax.dynamic_slice_in_dim(plane_rows, block_z * NPD, NPD) - block_z * count_z
    offset = lax.dynamic_slice_in_dim(box_offset, jnp.maximum(section - 1, 0), 1)[0]
    depth_ids = block_z * count_z + jnp.arange(count_z, dtype=jnp.int32)
    landing = offset + plane_rows // 2
    chosen = (landing[:, None] == depth_ids[None, :]).astype(jnp.float32)
    for step_index in range(STEPS):
        stress_pad = padded_2(current[2:5], (("gx", 1), ("gz", 2)), RADIUS)
        velocity = lax.cond(
            is_source,
            lambda: velocity_elastic(
                current[0:2], stress_pad, material[0], RADIUS, count_x, count_z
            ),
            lambda: velocity_acoustic(
                current[0:2], stress_pad, material[0], RADIUS, count_x, count_z
            ),
        )
        velocity_pad = padded_2(velocity, (("gx", 1), ("gz", 2)), RADIUS)
        stresses = lax.cond(
            is_source,
            lambda: stress_elastic(current[2:5], velocity_pad, material, RADIUS, count_x, count_z),
            lambda: stress_acoustic(current[2:5], velocity_pad, material, RADIUS, count_x, count_z),
        )
        current = jnp.concatenate([velocity, stresses], axis=0)
        picked = jnp.take(current, local_rows, axis=2)
        block_plane = jnp.transpose(
            jnp.stack([picked[0], picked[1], -0.5 * (picked[2] + picked[3])]), (0, 2, 1)
        )
        joined = lax.all_gather(block_plane, "gz", axis=1, tiled=True)
        gathered = broadcast(joined, "sec", 0)
        injected = jnp.einsum("ckx,kz->cxz", gathered, chosen, precision=lax.Precision.HIGHEST)
        far_state = jnp.concatenate([current[0:3] + COUPLING * injected, current[3:5]], axis=0)
        current = jnp.where(is_source, current, far_state)
    return current[None]


HALO = 2 * RADIUS * STEPS
CELLS = 128
HALF = CELLS // 2
WINDOW = HALF + 2 * HALO
DEPTH = 2 * CELLS
PART = HALF + HALO
NP = 2 * NPD
TRIM = (0, 8, 16, 24, 32)
WINDOWS = [WINDOW - 2 * amount for amount in TRIM]
COUNTS = len(WINDOWS)
ROWS = 192
GROUPS = CELLS // NP
SLOT = (
    ((0, 0), (1, 0), (2, 0)),
    ((3, 0), (4, 0), (5, 0)),
    ((6, 0), (7, 0), (6, 96)),
    ((3, 112), (4, 112), (5, 112)),
    ((0, 128), (1, 128), (2, 128)),
)
SCALE = 840.0
TAPS = (672.0, -168.0, 32.0, -3.0)


def banded(distance):
    values = jnp.zeros(distance.shape, jnp.float32)
    for offset, tap in enumerate(TAPS, 1):
        values = jnp.where(distance == offset, tap, values)
        values = jnp.where(distance == -offset, -tap, values)
    return values.astype(jnp.bfloat16)


def halves(values):
    high = values.astype(jnp.bfloat16)
    low = (values - high.astype(jnp.float32)).astype(jnp.bfloat16)
    return high, low


def dot(left, right):
    return jnp.dot(left, right, preferred_element_type=jnp.float32)


def diff_x(bands, parts):
    return dot(bands[parts[0].shape[0]][...], jnp.concatenate(parts, axis=0))


def along_depth(matrix, parts):
    return dot(jnp.concatenate(parts, axis=1), matrix[...])


def trimmed(arrays, amount):
    if amount == 0:
        return arrays
    return [array[amount:-amount] for array in arrays]


def lanes_of(shape):
    return lax.broadcasted_iota(jnp.int32, shape, 1) // NP


BODY = HALO - 8
WHOLE = (2, 4)
PAIRED = ((0, 1), (3, 5))
EDGE_ROWS = 8 * BODY + 8 * len(WHOLE) + 8 * len(PAIRED)


def pack_edge(block, target, at_end):
    body, rest = (CELLS - BODY, CELLS - HALO) if at_end else (0, BODY)
    near = lax.broadcasted_iota(jnp.int32, (8, CELLS), 0) // 4 == int(at_end)
    for index in range(8):
        target[BODY * index : BODY * (index + 1)] = block[index, body : body + BODY]
    row = 8 * BODY
    for index in WHOLE:
        target[row : row + 8] = block[index, rest : rest + 8]
        row += 8
    for one, two in PAIRED:
        turned = pltpu.roll(block[two, rest : rest + 8], 4, 0)
        target[row : row + 8] = jnp.where(near, block[one, rest : rest + 8], turned)
        row += 8


def unpack_edge(edge, window, lanes, before):
    body, rest = (8, 0) if before else (PART, WINDOW - 8)
    near = lax.broadcasted_iota(jnp.int32, (8, CELLS), 0) // 4 == int(before)
    for index in range(8):
        window[index, body : body + BODY, lanes] = edge[BODY * index : BODY * (index + 1)]
    row = 8 * BODY
    for index in WHOLE:
        window[index, rest : rest + 8, lanes] = edge[row : row + 8]
        row += 8
    for one, two in PAIRED:
        tile = edge[row : row + 8]
        window[one, rest : rest + 8, lanes] = jnp.where(near, tile, 0.0)
        window[two, rest : rest + 8, lanes] = jnp.where(near, pltpu.roll(tile, 4, 0), 0.0)
        row += 8
    for index in (6, 7):
        window[index, rest : rest + 8, lanes] = jnp.zeros((8, CELLS), jnp.float32)


def pack_kernel(fields, media, block, straight, crossed, swap, sems):
    core = lax.axis_index("gz")
    copies = [
        pltpu.make_async_copy(fields, block.at[:5], sems.at[0]),
        pltpu.make_async_copy(media, block.at[5:], sems.at[1]),
    ]
    for copy in copies:
        copy.start()
    for copy in copies:
        copy.wait()

    @pl.when(core == 0)
    def _():
        pack_edge(block, straight, True)
        pack_edge(block, crossed, False)
        swap[...] = block[:, CELLS - PART :]

    @pl.when(core == 1)
    def _():
        pack_edge(block, straight, False)
        pack_edge(block, crossed, True)
        swap[...] = block[:, :PART]


def assemble(window, block, ahead, behind, other):
    core = lax.axis_index("gz")
    low, high = slice(0, CELLS), slice(CELLS, DEPTH)

    @pl.when(core == 0)
    def _():
        unpack_edge(ahead, window, low, True)
        unpack_edge(behind, window, high, True)
        window[:8, HALO:, low] = block[:, :PART]
        window[:8, HALO:, high] = other[...]

    @pl.when(core == 1)
    def _():
        window[:8, :PART, high] = block[:, CELLS - PART :]
        window[:8, :PART, low] = other[...]
        unpack_edge(ahead, window, high, False)
        unpack_edge(behind, window, low, False)


def place(state, held, sent):
    start = HALO - TRIM[-1]
    core = lax.axis_index("gz")
    state = [array[start : start + HALF] for array in state]

    @pl.when(core == 0)
    def _():
        for index in range(5):
            held[index] = state[index][:, :CELLS]
            sent[index] = state[index][:, CELLS:]

    @pl.when(core == 1)
    def _():
        for index in range(5):
            held[index] = state[index][:, CELLS:]
            sent[index] = state[index][:, :CELLS]


def acoustic(state, bands):
    vx, vz, pressure, one, two, light, kappa, loss_one, loss_two = state
    band_x, band_z = bands
    parts = halves(pressure)
    vx = vx - light * diff_x(band_x, parts)
    vz = vz - light * along_depth(band_z, parts)
    load = kappa * (diff_x(band_x, halves(vx)) + along_depth(band_z, halves(vz)))
    one = RELAXATION[0] * one + loss_one * load
    two = RELAXATION[1] * two + loss_two * load
    pressure = pressure - TIME_STEP * (load - one - two)
    return [vx, vz, pressure, one, two, light, kappa, loss_one, loss_two]


def constants_kernel(plane_rows, box_offset, *targets):
    *bands_x, band_z, pick, land = targets
    for target in bands_x:
        count = target.shape[0]
        row = lax.broadcasted_iota(jnp.int32, target.shape, 0)
        column = lax.broadcasted_iota(jnp.int32, target.shape, 1)
        target[...] = banded(jnp.where(column < count, column, column - count) - row)
    shape = (DEPTH, DEPTH)
    distance = lax.broadcasted_iota(jnp.int32, shape, 0) - lax.broadcasted_iota(jnp.int32, shape, 1)
    band_z[:DEPTH] = banded(distance)
    band_z[DEPTH:] = band_z[:DEPTH]
    row = plane_rows[...]
    lane = lax.broadcasted_iota(jnp.int32, box_offset.shape, 1)
    offset = jnp.where(lane == lax.axis_index("sec") - 1, box_offset[...], 0)
    landing = row // 2 + jnp.sum(offset, axis=1, keepdims=True)
    depth = lax.broadcasted_iota(jnp.int32, (DEPTH, NP), 0)
    spread = lax.broadcasted_iota(jnp.int32, (NP, CELLS), 1) % NP
    spread = spread == lax.broadcasted_iota(jnp.int32, (NP, CELLS), 0)
    spread = jnp.where(spread, 1.0, 0.0).astype(jnp.bfloat16)
    hot = jnp.where(depth == row, 1.0, 0.0).astype(jnp.bfloat16)
    pick[:DEPTH] = dot(hot, spread).astype(jnp.bfloat16)
    pick[DEPTH:] = pick[:DEPTH]
    hot = jnp.where(depth == landing, 1.0, 0.0).astype(jnp.bfloat16)
    land[:CELLS] = dot(hot, spread).T.astype(jnp.bfloat16)
    land[CELLS:] = land[:CELLS]


def first_kernel(*refs):
    bands_x, (band_z, pick, block, behind, ahead, other) = refs[:COUNTS], refs[COUNTS:-4]
    held, sent, rows, carry = refs[-4:]
    band_x = {band.shape[0]: band for band in bands_x}
    assemble(carry, block, ahead, behind, other)
    section = lax.axis_index("sec")

    @pl.when(section == 0)
    def _():
        vx, vz, sxx, szz, sxz, light, lame, shear = [carry[index] for index in range(8)]
        light = light * (TIME_STEP / SCALE)
        both = (lame + 2.0 * shear) * (TIME_STEP / SCALE)
        lame = lame * (TIME_STEP / SCALE)
        shear = shear * (TIME_STEP / SCALE)
        at = 0
        for step in range(STEPS):
            cut = TRIM[step] - at
            at = TRIM[step]
            vx, vz, sxx, szz, sxz, light, both, lame, shear = trimmed(
                [vx, vz, sxx, szz, sxz, light, both, lame, shear], cut
            )
            parts_xx, parts_zz, parts_xz = halves(sxx), halves(szz), halves(sxz)
            vx = vx + light * (diff_x(band_x, parts_xx) + along_depth(band_z, parts_xz))
            vz = vz + light * (diff_x(band_x, parts_xz) + along_depth(band_z, parts_zz))
            parts_x, parts_z = halves(vx), halves(vz)
            strain_x, strain_z = diff_x(band_x, parts_x), along_depth(band_z, parts_z)
            sxx = sxx + (both * strain_x + lame * strain_z)
            szz = szz + (lame * strain_x + both * strain_z)
            sxz = sxz + shear * (along_depth(band_z, parts_x) + diff_x(band_x, parts_z))
            low = 2 * RADIUS * (step + 1) - at
            for component, (parts, factor) in enumerate(
                ((parts_x, COUPLING), (parts_z, COUPLING), (halves(sxx + szz), -0.5 * COUPLING))
            ):
                picked = factor * along_depth(pick, parts)
                picked = picked[low : picked.shape[0] - low]
                group, base = SLOT[step][component]
                spot = pl.ds(base, picked.shape[0])
                rows[spot] = jnp.where(lanes_of(picked.shape) == group, picked, rows[spot])
        place([vx, vz, sxx, szz, sxz], held, sent)

    @pl.when(section > 0)
    def _():
        vx, vz, pressure, one, two, light, kappa, loss = [carry[index] for index in range(8)]
        light = light * (TIME_STEP / SCALE)
        kappa = kappa * (1.0 / SCALE)
        loss_one = loss * ((1.0 - RELAXATION[0]) * MEMORY_WEIGHT[0])
        loss_two = loss * ((1.0 - RELAXATION[1]) * MEMORY_WEIGHT[1])
        state = [vx, vz, pressure, one, two, light, kappa, loss_one, loss_two]
        for index, array in enumerate(acoustic(state, (band_x, band_z))):
            carry[index] = array


def second_kernel(*refs):
    bands_x, (band_z, land, carry, rows, held_in, sent_in, held, sent) = refs[:COUNTS], refs[COUNTS:]
    band_x = {band.shape[0]: band for band in bands_x}
    section = lax.axis_index("sec")

    @pl.when(section == 0)
    def _():
        held[...] = held_in[...]
        sent[...] = sent_in[...]

    @pl.when(section > 0)
    def _():
        state = [carry[index] for index in range(9)]
        at = 0
        for step in range(STEPS):
            if step:
                state = trimmed(state, TRIM[step] - at)
                at = TRIM[step]
                state = acoustic(state, (band_x, band_z))
            low = 2 * RADIUS * (step + 1) - at
            high = WINDOW - 2 * at - low
            for component in range(3):
                group, base = SLOT[step][component]
                taken = rows[pl.ds(base, high - low)]
                taken = halves(jnp.where(lanes_of(taken.shape) == group, taken, 0.0))
                added = along_depth(land, taken)
                array = state[component]
                state[component] = jnp.concatenate(
                    [array[:low], array[low:high] + added, array[high:]], axis=0
                )
        place(state[:5], held, sent)


def last_kernel(held, swapped, out, sems):
    core = lax.axis_index("gz")
    copies = [
        pltpu.make_async_copy(
            source, out.at[:, pl.ds(pl.multiple_of(HALF * half, HALF), HALF)], sems.at[index]
        )
        for index, (source, half) in enumerate(((held, core), (swapped, 1 - core)))
    ]
    for copy in copies:
        copy.start()
    for copy in copies:
        copy.wait()


def call(
    kernel,
    outs,
    operands,
    flops,
    place_in=pltpu.VMEM,
    place_out=pltpu.VMEM,
    scratch=(),
):
    return pl.pallas_call(
        kernel,
        out_shape=outs,
        in_specs=[pl.BlockSpec(memory_space=place_in)] * len(operands),
        out_specs=[pl.BlockSpec(memory_space=place_out)] * len(outs),
        scratch_shapes=scratch,
        compiler_params=pltpu.CompilerParams(vmem_limit_bytes=48 * 1024 * 1024),
        cost_estimate=pl.CostEstimate(
            flops=flops, bytes_accessed=2 * 1024 * 1024, transcendentals=0
        ),
    )(*operands)


def full(*shape):
    return jax.ShapeDtypeStruct(shape, jnp.float32)


def narrow(*shape):
    return jax.ShapeDtypeStruct(shape, jnp.bfloat16)


def local_window(columns, fields, media, plane_rows, box_offset):
    fields, media = fields[0], media[0]
    core = lax.axis_index("gz")
    is_first = core == 0
    block, straight, crossed, swap = call(
        pack_kernel,
        [
            full(8, CELLS, CELLS),
            full(EDGE_ROWS, CELLS),
            full(EDGE_ROWS, CELLS),
            full(8, PART, CELLS),
        ],
        [pltpu.with_memory_space_constraint(array, pltpu.HBM) for array in (fields, media)],
        1000,
        place_in=pltpu.HBM,
        scratch=[pltpu.SemaphoreType.DMA((2,))],
    )
    straight_pairs, crossed_pairs = [], []
    for column in range(columns):
        if column + 1 < columns:
            straight_pairs.append((2 * column, 2 * column + 2))
            crossed_pairs.append((2 * column + 1, 2 * column + 2))
        if column:
            straight_pairs.append((2 * column + 1, 2 * column - 1))
            crossed_pairs.append((2 * column, 2 * column - 1))
    turn = [(0, 1), (1, 0)]
    behind = lax.ppermute(crossed, ("gx", "gz"), crossed_pairs)
    ahead = lax.ppermute(straight, ("gx", "gz"), straight_pairs)
    joined = lax.all_gather(swap, "gz")
    other = jnp.where(is_first, joined[1], joined[0])
    *bands, pick, land = call(
        constants_kernel,
        [narrow(count, 2 * count) for count in WINDOWS]
        + [narrow(2 * DEPTH, DEPTH), narrow(2 * DEPTH, CELLS), narrow(2 * CELLS, DEPTH)],
        [plane_rows[None], box_offset[None]],
        1_000_000_000,
    )
    held, sent, rows, carry = call(
        first_kernel,
        [
            full(5, HALF, CELLS),
            full(5, HALF, CELLS),
            full(ROWS, CELLS),
            full(9, WINDOW, DEPTH),
        ],
        [*bands, pick, block, behind, ahead, other],
        4_000_000_000,
    )
    arrived = [lax.ppermute(rows, "sec", [(0, target)]) for target in (1, 2, 3)]
    rows = arrived[0] + arrived[1] + arrived[2]
    held, sent = call(
        second_kernel,
        [full(5, HALF, CELLS), full(5, HALF, CELLS)],
        [*bands, land, carry, rows, held, sent],
        4_000_000_000,
    )
    swapped = lax.ppermute(sent, "gz", turn)
    (out,) = call(
        last_kernel,
        [full(5, CELLS, CELLS)],
        [held, swapped],
        1000,
        place_out=pl.ANY,
        scratch=[pltpu.SemaphoreType.DMA((2,))],
    )
    return out[None]


def solution(mesh):
    in_specs = (P("sec", None, "gx", "gz"), P("sec", None, "gx", "gz"), P(), P())
    out_specs = P("sec", None, "gx", "gz")
    if mesh.shape["gz"] == 2:
        local = functools.partial(local_window, mesh.shape["gx"])
    else:
        local = local_stepwise
    return jax.shard_map(local, mesh=mesh, in_specs=in_specs, out_specs=out_specs, check_vma=False)
```

```python
import functools

import jax
import jax.numpy as jnp
from jax import lax
from jax.experimental import pallas as pl
from jax.experimental.pallas import tpu as pltpu
from jax.sharding import PartitionSpec as P

RADIUS = 4
STEPS = 5
NPD = 8

STENCIL = (0.8, -0.2, 4.0 / 105.0, -1.0 / 280.0)
TIME_STEP = 0.2
COUPLING = 0.5
RELAXATION = (0.9, 0.5)
MEMORY_WEIGHT = (0.15, 0.1)


def padded_2(block, sides, width):
    for axis, dim in sides:
        count = lax.axis_size(axis)
        forward = [(i, i + 1) for i in range(count - 1)]
        backward = [(target, source) for source, target in forward]
        low = lax.ppermute(
            lax.slice_in_dim(block, block.shape[dim] - width, None, axis=dim), axis, forward
        )
        high = lax.ppermute(lax.slice_in_dim(block, 0, width, axis=dim), axis, backward)
        block = jnp.concatenate([low, block, high], axis=dim)
    return block


def broadcast(value, axis, source):
    kept = jnp.where(lax.axis_index(axis) == source, value, 0).astype(value.dtype)
    return lax.psum(kept, axis)


def along_x(padded, anchor, count_x, count_z):
    summed = jnp.zeros(padded.shape[:-2] + (count_x, count_z), jnp.float32)
    for offset, stencil_tap in enumerate(STENCIL, 1):
        forward = padded[
            ..., anchor + offset : anchor + offset + count_x, anchor : anchor + count_z
        ]
        backward = padded[
            ..., anchor - offset : anchor - offset + count_x, anchor : anchor + count_z
        ]
        summed = summed + stencil_tap * (forward - backward)
    return summed


def along_z(padded, anchor, count_x, count_z):
    summed = jnp.zeros(padded.shape[:-2] + (count_x, count_z), jnp.float32)
    for offset, stencil_tap in enumerate(STENCIL, 1):
        forward = padded[
            ..., anchor : anchor + count_x, anchor + offset : anchor + offset + count_z
        ]
        backward = padded[
            ..., anchor : anchor + count_x, anchor - offset : anchor - offset + count_z
        ]
        summed = summed + stencil_tap * (forward - backward)
    return summed


def velocity_elastic(velocity, stresses, buoyancy, anchor, count_x, count_z):
    updated_x = velocity[0] + TIME_STEP * buoyancy * (
        along_x(stresses[0], anchor, count_x, count_z)
        + along_z(stresses[2], anchor, count_x, count_z)
    )
    updated_z = velocity[1] + TIME_STEP * buoyancy * (
        along_x(stresses[2], anchor, count_x, count_z)
        + along_z(stresses[1], anchor, count_x, count_z)
    )
    return jnp.stack([updated_x, updated_z])


def velocity_acoustic(velocity, stresses, buoyancy, anchor, count_x, count_z):
    updated_x = velocity[0] - TIME_STEP * buoyancy * along_x(stresses[0], anchor, count_x, count_z)
    updated_z = velocity[1] - TIME_STEP * buoyancy * along_z(stresses[0], anchor, count_x, count_z)
    return jnp.stack([updated_x, updated_z])


def stress_elastic(stresses, velocity_pad, material, anchor, count_x, count_z):
    strain_x = along_x(velocity_pad[0], anchor, count_x, count_z)
    strain_z = along_z(velocity_pad[1], anchor, count_x, count_z)
    strain_shear = along_z(velocity_pad[0], anchor, count_x, count_z) + along_x(
        velocity_pad[1], anchor, count_x, count_z
    )
    lame_first = material[1]
    shear_modulus = material[2]
    normal_x = stresses[0] + TIME_STEP * (
        (lame_first + 2.0 * shear_modulus) * strain_x + lame_first * strain_z
    )
    normal_z = stresses[1] + TIME_STEP * (
        lame_first * strain_x + (lame_first + 2.0 * shear_modulus) * strain_z
    )
    shear_new = stresses[2] + TIME_STEP * shear_modulus * strain_shear
    return jnp.stack([normal_x, normal_z, shear_new])


def stress_acoustic(stresses, velocity_pad, material, anchor, count_x, count_z):
    divergence = along_x(velocity_pad[0], anchor, count_x, count_z) + along_z(
        velocity_pad[1], anchor, count_x, count_z
    )
    loading = material[1] * divergence
    memory_one = (
        RELAXATION[0] * stresses[1]
        + (1.0 - RELAXATION[0]) * MEMORY_WEIGHT[0] * material[2] * loading
    )
    memory_two = (
        RELAXATION[1] * stresses[2]
        + (1.0 - RELAXATION[1]) * MEMORY_WEIGHT[1] * material[2] * loading
    )
    pressure = stresses[0] - TIME_STEP * (loading - memory_one - memory_two)
    return jnp.stack([pressure, memory_one, memory_two])


def local_stepwise(fields, media, plane_rows, box_offset):
    current = fields[0]
    material = media[0]
    count_x = current.shape[1]
    count_z = current.shape[2]
    section = lax.axis_index("sec")
    is_source = section == 0
    block_z = lax.axis_index("gz")
    local_rows = lax.dynamic_slice_in_dim(plane_rows, block_z * NPD, NPD) - block_z * count_z
    offset = lax.dynamic_slice_in_dim(box_offset, jnp.maximum(section - 1, 0), 1)[0]
    depth_ids = block_z * count_z + jnp.arange(count_z, dtype=jnp.int32)
    landing = offset + plane_rows // 2
    chosen = (landing[:, None] == depth_ids[None, :]).astype(jnp.float32)
    for step_index in range(STEPS):
        stress_pad = padded_2(current[2:5], (("gx", 1), ("gz", 2)), RADIUS)
        velocity = lax.cond(
            is_source,
            lambda: velocity_elastic(
                current[0:2], stress_pad, material[0], RADIUS, count_x, count_z
            ),
            lambda: velocity_acoustic(
                current[0:2], stress_pad, material[0], RADIUS, count_x, count_z
            ),
        )
        velocity_pad = padded_2(velocity, (("gx", 1), ("gz", 2)), RADIUS)
        stresses = lax.cond(
            is_source,
            lambda: stress_elastic(current[2:5], velocity_pad, material, RADIUS, count_x, count_z),
            lambda: stress_acoustic(current[2:5], velocity_pad, material, RADIUS, count_x, count_z),
        )
        current = jnp.concatenate([velocity, stresses], axis=0)
        picked = jnp.take(current, local_rows, axis=2)
        block_plane = jnp.transpose(
            jnp.stack([picked[0], picked[1], -0.5 * (picked[2] + picked[3])]), (0, 2, 1)
        )
        joined = lax.all_gather(block_plane, "gz", axis=1, tiled=True)
        gathered = broadcast(joined, "sec", 0)
        injected = jnp.einsum("ckx,kz->cxz", gathered, chosen, precision=lax.Precision.HIGHEST)
        far_state = jnp.concatenate([current[0:3] + COUPLING * injected, current[3:5]], axis=0)
        current = jnp.where(is_source, current, far_state)
    return current[None]


HALO = 2 * RADIUS * STEPS
CELLS = 128
HALF = CELLS // 2
WINDOW = HALF + 2 * HALO
DEPTH = 2 * CELLS
PART = HALF + HALO
NP = 2 * NPD
TRIM = (0, 8, 16, 24, 32)
WINDOWS = [WINDOW - 2 * amount for amount in TRIM]
COUNTS = len(WINDOWS)
ROWS = 192
GROUPS = CELLS // NP
SLOT = (
    ((0, 0), (1, 0), (2, 0)),
    ((3, 0), (4, 0), (5, 0)),
    ((6, 0), (7, 0), (6, 96)),
    ((3, 112), (4, 112), (5, 112)),
    ((0, 128), (1, 128), (2, 128)),
)
SCALE = 840.0
TAPS = (672.0, -168.0, 32.0, -3.0)


def banded(distance):
    values = jnp.zeros(distance.shape, jnp.float32)
    for offset, tap in enumerate(TAPS, 1):
        values = jnp.where(distance == offset, tap, values)
        values = jnp.where(distance == -offset, -tap, values)
    return values.astype(jnp.bfloat16)


def halves(values):
    high = values.astype(jnp.bfloat16)
    low = (values - high.astype(jnp.float32)).astype(jnp.bfloat16)
    return high, low


def dot(left, right):
    return jnp.dot(left, right, preferred_element_type=jnp.float32)


def diff_x(bands, parts):
    return dot(bands[parts[0].shape[0]][...], jnp.concatenate(parts, axis=0))


def along_depth(matrix, parts):
    return dot(jnp.concatenate(parts, axis=1), matrix[...])


def trimmed(arrays, amount):
    if amount == 0:
        return arrays
    return [array[amount:-amount] for array in arrays]


def lanes_of(shape):
    return lax.broadcasted_iota(jnp.int32, shape, 1) // NP


BODY = HALO - 8
WHOLE = (2, 4)
PAIRED = ((0, 1), (3, 5))
EDGE_ROWS = 8 * BODY + 8 * len(WHOLE) + 8 * len(PAIRED)


def pack_edge(block, target, at_end):
    body, rest = (CELLS - BODY, CELLS - HALO) if at_end else (0, BODY)
    near = lax.broadcasted_iota(jnp.int32, (8, CELLS), 0) // 4 == int(at_end)
    for index in range(8):
        target[BODY * index : BODY * (index + 1)] = block[index, body : body + BODY]
    row = 8 * BODY
    for index in WHOLE:
        target[row : row + 8] = block[index, rest : rest + 8]
        row += 8
    for one, two in PAIRED:
        turned = pltpu.roll(block[two, rest : rest + 8], 4, 0)
        target[row : row + 8] = jnp.where(near, block[one, rest : rest + 8], turned)
        row += 8


def unpack_rest(edge, window, lanes, before):
    rest = 0 if before else WINDOW - 8
    near = lax.broadcasted_iota(jnp.int32, (8, CELLS), 0) // 4 == int(before)
    row = 8 * BODY
    for index in WHOLE:
        window[index, rest : rest + 8, lanes] = edge[row : row + 8]
        row += 8
    for one, two in PAIRED:
        tile = edge[row : row + 8]
        window[one, rest : rest + 8, lanes] = jnp.where(near, tile, 0.0)
        window[two, rest : rest + 8, lanes] = jnp.where(near, pltpu.roll(tile, 4, 0), 0.0)
        row += 8
    for index in (6, 7):
        window[index, rest : rest + 8, lanes] = jnp.zeros((8, CELLS), jnp.float32)


def pack_kernel(fields, media, block, straight, crossed, swap, sems):
    core = lax.axis_index("gz")
    copies = [
        pltpu.make_async_copy(fields, block.at[:5], sems.at[0]),
        pltpu.make_async_copy(media, block.at[5:], sems.at[1]),
    ]
    for copy in copies:
        copy.start()
    for copy in copies:
        copy.wait()

    @pl.when(core == 0)
    def _():
        pack_edge(block, straight, True)
        pack_edge(block, crossed, False)
        swap[...] = block[:, CELLS - PART :]

    @pl.when(core == 1)
    def _():
        pack_edge(block, straight, False)
        pack_edge(block, crossed, True)
        swap[...] = block[:, :PART]


def assemble(window, block, ahead, behind, other):
    core = lax.axis_index("gz")
    low, high = slice(0, CELLS), slice(CELLS, DEPTH)

    @pl.when(core == 0)
    def _():
        @pl.loop(0, 8)
        def _(index):
            body = pl.ds(pl.multiple_of(BODY * index, 8), BODY)
            window[index, 8:HALO, low] = ahead[body]
            window[index, 8:HALO, high] = behind[body]
            window[index, HALO:, low] = block[index, :PART]
            window[index, HALO:, high] = other[index]

        unpack_rest(ahead, window, low, True)
        unpack_rest(behind, window, high, True)

    @pl.when(core == 1)
    def _():
        @pl.loop(0, 8)
        def _(index):
            body = pl.ds(pl.multiple_of(BODY * index, 8), BODY)
            window[index, :PART, high] = block[index, CELLS - PART :]
            window[index, :PART, low] = other[index]
            window[index, PART : WINDOW - 8, high] = ahead[body]
            window[index, PART : WINDOW - 8, low] = behind[body]

        unpack_rest(ahead, window, high, False)
        unpack_rest(behind, window, low, False)


def place(state, held, sent):
    start = HALO - TRIM[-1]
    core = lax.axis_index("gz")
    state = [array[start : start + HALF] for array in state]

    @pl.when(core == 0)
    def _():
        for index in range(5):
            held[index] = state[index][:, :CELLS]
            sent[index] = state[index][:, CELLS:]

    @pl.when(core == 1)
    def _():
        for index in range(5):
            held[index] = state[index][:, CELLS:]
            sent[index] = state[index][:, :CELLS]


def acoustic(state, bands):
    vx, vz, pressure, one, two, light, kappa, loss_one, loss_two = state
    band_x, band_z = bands
    parts = halves(pressure)
    vx = vx - light * diff_x(band_x, parts)
    vz = vz - light * along_depth(band_z, parts)
    load = kappa * (diff_x(band_x, halves(vx)) + along_depth(band_z, halves(vz)))
    one = RELAXATION[0] * one + loss_one * load
    two = RELAXATION[1] * two + loss_two * load
    pressure = pressure - TIME_STEP * (load - one - two)
    return [vx, vz, pressure, one, two, light, kappa, loss_one, loss_two]


def constants_kernel(plane_rows, box_offset, *targets):
    *bands_x, band_z, pick, land = targets
    for target in bands_x:
        count = target.shape[0]
        row = lax.broadcasted_iota(jnp.int32, target.shape, 0)
        column = lax.broadcasted_iota(jnp.int32, target.shape, 1)
        target[...] = banded(jnp.where(column < count, column, column - count) - row)
    shape = (DEPTH, DEPTH)
    distance = lax.broadcasted_iota(jnp.int32, shape, 0) - lax.broadcasted_iota(jnp.int32, shape, 1)
    band_z[:DEPTH] = banded(distance)
    band_z[DEPTH:] = band_z[:DEPTH]
    row = plane_rows[...]
    lane = lax.broadcasted_iota(jnp.int32, box_offset.shape, 1)
    offset = jnp.where(lane == lax.axis_index("sec") - 1, box_offset[...], 0)
    landing = row // 2 + jnp.sum(offset, axis=1, keepdims=True)
    depth = lax.broadcasted_iota(jnp.int32, (DEPTH, NP), 0)
    spread = lax.broadcasted_iota(jnp.int32, (NP, CELLS), 1) % NP
    spread = spread == lax.broadcasted_iota(jnp.int32, (NP, CELLS), 0)
    spread = jnp.where(spread, 1.0, 0.0).astype(jnp.bfloat16)
    hot = jnp.where(depth == row, 1.0, 0.0).astype(jnp.bfloat16)
    pick[:DEPTH] = dot(hot, spread).astype(jnp.bfloat16)
    pick[DEPTH:] = pick[:DEPTH]
    hot = jnp.where(depth == landing, 1.0, 0.0).astype(jnp.bfloat16)
    land[:CELLS] = dot(hot, spread).T.astype(jnp.bfloat16)
    land[CELLS:] = land[:CELLS]


def first_kernel(*refs):
    bands_x, (band_z, pick, block, behind, ahead, other) = refs[:COUNTS], refs[COUNTS:-4]
    held, sent, rows, carry = refs[-4:]
    band_x = {band.shape[0]: band for band in bands_x}
    assemble(carry, block, ahead, behind, other)
    section = lax.axis_index("sec")

    @pl.when(section > 0)
    def _():
        vx, vz, pressure, one, two, light, kappa, loss = [carry[index] for index in range(8)]
        light = light * (TIME_STEP / SCALE)
        kappa = kappa * (1.0 / SCALE)
        loss_one = loss * ((1.0 - RELAXATION[0]) * MEMORY_WEIGHT[0])
        loss_two = loss * ((1.0 - RELAXATION[1]) * MEMORY_WEIGHT[1])
        state = [vx, vz, pressure, one, two, light, kappa, loss_one, loss_two]
        for index, array in enumerate(acoustic(state, (band_x, band_z))):
            carry[index] = array

    @pl.when(section == 0)
    def _():
        vx, vz, sxx, szz, sxz, light, lame, shear = [carry[index] for index in range(8)]
        light = light * (TIME_STEP / SCALE)
        both = (lame + 2.0 * shear) * (TIME_STEP / SCALE)
        lame = lame * (TIME_STEP / SCALE)
        shear = shear * (TIME_STEP / SCALE)
        at = 0
        for step in range(STEPS):
            cut = TRIM[step] - at
            at = TRIM[step]
            vx, vz, sxx, szz, sxz, light, both, lame, shear = trimmed(
                [vx, vz, sxx, szz, sxz, light, both, lame, shear], cut
            )
            parts_xx, parts_zz, parts_xz = halves(sxx), halves(szz), halves(sxz)
            vx = vx + light * (diff_x(band_x, parts_xx) + along_depth(band_z, parts_xz))
            vz = vz + light * (diff_x(band_x, parts_xz) + along_depth(band_z, parts_zz))
            parts_x, parts_z = halves(vx), halves(vz)
            strain_x, strain_z = diff_x(band_x, parts_x), along_depth(band_z, parts_z)
            sxx = sxx + (both * strain_x + lame * strain_z)
            szz = szz + (lame * strain_x + both * strain_z)
            sxz = sxz + shear * (along_depth(band_z, parts_x) + diff_x(band_x, parts_z))
            low = 2 * RADIUS * (step + 1) - at
            for component, (parts, factor) in enumerate(
                ((parts_x, COUPLING), (parts_z, COUPLING), (halves(sxx + szz), -0.5 * COUPLING))
            ):
                picked = factor * along_depth(pick, parts)
                picked = picked[low : picked.shape[0] - low]
                group, base = SLOT[step][component]
                spot = pl.ds(base, picked.shape[0])
                rows[spot] = jnp.where(lanes_of(picked.shape) == group, picked, rows[spot])
        place([vx, vz, sxx, szz, sxz], held, sent)


def second_kernel(*refs):
    bands_x, (band_z, land, carry, rows, held_in, sent_in, held, sent) = refs[:COUNTS], refs[COUNTS:]
    band_x = {band.shape[0]: band for band in bands_x}
    section = lax.axis_index("sec")

    @pl.when(section == 0)
    def _():
        held[...] = held_in[...]
        sent[...] = sent_in[...]

    @pl.when(section > 0)
    def _():
        state = [carry[index] for index in range(9)]
        at = 0
        for step in range(STEPS):
            if step:
                state = trimmed(state, TRIM[step] - at)
                at = TRIM[step]
                state = acoustic(state, (band_x, band_z))
            low = 2 * RADIUS * (step + 1) - at
            high = WINDOW - 2 * at - low
            for component in range(3):
                group, base = SLOT[step][component]
                taken = rows[pl.ds(base, high - low)]
                taken = halves(jnp.where(lanes_of(taken.shape) == group, taken, 0.0))
                added = along_depth(land, taken)
                array = state[component]
                state[component] = jnp.concatenate(
                    [array[:low], array[low:high] + added, array[high:]], axis=0
                )
        place(state[:5], held, sent)


def last_kernel(held, swapped, out, sems):
    core = lax.axis_index("gz")
    copies = [
        pltpu.make_async_copy(
            source, out.at[:, pl.ds(pl.multiple_of(HALF * half, HALF), HALF)], sems.at[index]
        )
        for index, (source, half) in enumerate(((held, core), (swapped, 1 - core)))
    ]
    for copy in copies:
        copy.start()
    for copy in copies:
        copy.wait()


def call(
    kernel,
    outs,
    operands,
    flops,
    place_in=pltpu.VMEM,
    place_out=pltpu.VMEM,
    scratch=(),
):
    return pl.pallas_call(
        kernel,
        out_shape=outs,
        in_specs=[pl.BlockSpec(memory_space=place_in)] * len(operands),
        out_specs=[pl.BlockSpec(memory_space=place_out)] * len(outs),
        scratch_shapes=scratch,
        compiler_params=pltpu.CompilerParams(vmem_limit_bytes=48 * 1024 * 1024),
        cost_estimate=pl.CostEstimate(
            flops=flops, bytes_accessed=2 * 1024 * 1024, transcendentals=0
        ),
    )(*operands)


def full(*shape):
    return jax.ShapeDtypeStruct(shape, jnp.float32)


def narrow(*shape):
    return jax.ShapeDtypeStruct(shape, jnp.bfloat16)


def local_window(columns, fields, media, plane_rows, box_offset):
    fields, media = fields[0], media[0]
    core = lax.axis_index("gz")
    is_first = core == 0
    block, straight, crossed, swap = call(
        pack_kernel,
        [
            full(8, CELLS, CELLS),
            full(EDGE_ROWS, CELLS),
            full(EDGE_ROWS, CELLS),
            full(8, PART, CELLS),
        ],
        [pltpu.with_memory_space_constraint(array, pltpu.HBM) for array in (fields, media)],
        1000,
        place_in=pltpu.HBM,
        scratch=[pltpu.SemaphoreType.DMA((2,))],
    )
    straight_pairs, crossed_pairs = [], []
    for column in range(columns):
        if column + 1 < columns:
            straight_pairs.append((2 * column, 2 * column + 2))
            crossed_pairs.append((2 * column + 1, 2 * column + 2))
        if column:
            straight_pairs.append((2 * column + 1, 2 * column - 1))
            crossed_pairs.append((2 * column, 2 * column - 1))
    turn = [(0, 1), (1, 0)]
    behind = lax.ppermute(crossed, ("gx", "gz"), crossed_pairs)
    ahead = lax.ppermute(straight, ("gx", "gz"), straight_pairs)
    joined = lax.all_gather(swap, "gz")
    other = jnp.where(is_first, joined[1], joined[0])
    *bands, pick, land = call(
        constants_kernel,
        [narrow(count, 2 * count) for count in WINDOWS]
        + [narrow(2 * DEPTH, DEPTH), narrow(2 * DEPTH, CELLS), narrow(2 * CELLS, DEPTH)],
        [plane_rows[None], box_offset[None]],
        1_000_000_000,
    )
    held, sent, rows, carry = call(
        first_kernel,
        [
            full(5, HALF, CELLS),
            full(5, HALF, CELLS),
            full(ROWS, CELLS),
            full(9, WINDOW, DEPTH),
        ],
        [*bands, pick, block, behind, ahead, other],
        4_000_000_000,
    )
    arrived = [lax.ppermute(rows, "sec", [(0, target)]) for target in (1, 2, 3)]
    rows = arrived[0] + arrived[1] + arrived[2]
    held, sent = call(
        second_kernel,
        [full(5, HALF, CELLS), full(5, HALF, CELLS)],
        [*bands, land, carry, rows, held, sent],
        4_000_000_000,
    )
    swapped = lax.ppermute(sent, "gz", turn)
    (out,) = call(
        last_kernel,
        [full(5, CELLS, CELLS)],
        [held, swapped],
        1000,
        place_out=pl.ANY,
        scratch=[pltpu.SemaphoreType.DMA((2,))],
    )
    return out[None]


def solution(mesh):
    in_specs = (P("sec", None, "gx", "gz"), P("sec", None, "gx", "gz"), P(), P())
    out_specs = P("sec", None, "gx", "gz")
    if mesh.shape["gz"] == 2:
        local = functools.partial(local_window, mesh.shape["gx"])
    else:
        local = local_stepwise
    return jax.shard_map(local, mesh=mesh, in_specs=in_specs, out_specs=out_specs, check_vma=False)
```

```python
import functools

import jax
import jax.numpy as jnp
from jax import lax
from jax.experimental import pallas as pl
from jax.experimental.pallas import tpu as pltpu
from jax.sharding import PartitionSpec as P

RADIUS = 4
STEPS = 5
NPD = 8

STENCIL = (0.8, -0.2, 4.0 / 105.0, -1.0 / 280.0)
TIME_STEP = 0.2
COUPLING = 0.5
RELAXATION = (0.9, 0.5)
MEMORY_WEIGHT = (0.15, 0.1)


def padded_2(block, sides, width):
    for axis, dim in sides:
        count = lax.axis_size(axis)
        forward = [(i, i + 1) for i in range(count - 1)]
        backward = [(target, source) for source, target in forward]
        low = lax.ppermute(
            lax.slice_in_dim(block, block.shape[dim] - width, None, axis=dim), axis, forward
        )
        high = lax.ppermute(lax.slice_in_dim(block, 0, width, axis=dim), axis, backward)
        block = jnp.concatenate([low, block, high], axis=dim)
    return block


def broadcast(value, axis, source):
    kept = jnp.where(lax.axis_index(axis) == source, value, 0).astype(value.dtype)
    return lax.psum(kept, axis)


def along_x(padded, anchor, count_x, count_z):
    summed = jnp.zeros(padded.shape[:-2] + (count_x, count_z), jnp.float32)
    for offset, stencil_tap in enumerate(STENCIL, 1):
        forward = padded[
            ..., anchor + offset : anchor + offset + count_x, anchor : anchor + count_z
        ]
        backward = padded[
            ..., anchor - offset : anchor - offset + count_x, anchor : anchor + count_z
        ]
        summed = summed + stencil_tap * (forward - backward)
    return summed


def along_z(padded, anchor, count_x, count_z):
    summed = jnp.zeros(padded.shape[:-2] + (count_x, count_z), jnp.float32)
    for offset, stencil_tap in enumerate(STENCIL, 1):
        forward = padded[
            ..., anchor : anchor + count_x, anchor + offset : anchor + offset + count_z
        ]
        backward = padded[
            ..., anchor : anchor + count_x, anchor - offset : anchor - offset + count_z
        ]
        summed = summed + stencil_tap * (forward - backward)
    return summed


def velocity_elastic(velocity, stresses, buoyancy, anchor, count_x, count_z):
    updated_x = velocity[0] + TIME_STEP * buoyancy * (
        along_x(stresses[0], anchor, count_x, count_z)
        + along_z(stresses[2], anchor, count_x, count_z)
    )
    updated_z = velocity[1] + TIME_STEP * buoyancy * (
        along_x(stresses[2], anchor, count_x, count_z)
        + along_z(stresses[1], anchor, count_x, count_z)
    )
    return jnp.stack([updated_x, updated_z])


def velocity_acoustic(velocity, stresses, buoyancy, anchor, count_x, count_z):
    updated_x = velocity[0] - TIME_STEP * buoyancy * along_x(stresses[0], anchor, count_x, count_z)
    updated_z = velocity[1] - TIME_STEP * buoyancy * along_z(stresses[0], anchor, count_x, count_z)
    return jnp.stack([updated_x, updated_z])


def stress_elastic(stresses, velocity_pad, material, anchor, count_x, count_z):
    strain_x = along_x(velocity_pad[0], anchor, count_x, count_z)
    strain_z = along_z(velocity_pad[1], anchor, count_x, count_z)
    strain_shear = along_z(velocity_pad[0], anchor, count_x, count_z) + along_x(
        velocity_pad[1], anchor, count_x, count_z
    )
    lame_first = material[1]
    shear_modulus = material[2]
    normal_x = stresses[0] + TIME_STEP * (
        (lame_first + 2.0 * shear_modulus) * strain_x + lame_first * strain_z
    )
    normal_z = stresses[1] + TIME_STEP * (
        lame_first * strain_x + (lame_first + 2.0 * shear_modulus) * strain_z
    )
    shear_new = stresses[2] + TIME_STEP * shear_modulus * strain_shear
    return jnp.stack([normal_x, normal_z, shear_new])


def stress_acoustic(stresses, velocity_pad, material, anchor, count_x, count_z):
    divergence = along_x(velocity_pad[0], anchor, count_x, count_z) + along_z(
        velocity_pad[1], anchor, count_x, count_z
    )
    loading = material[1] * divergence
    memory_one = (
        RELAXATION[0] * stresses[1]
        + (1.0 - RELAXATION[0]) * MEMORY_WEIGHT[0] * material[2] * loading
    )
    memory_two = (
        RELAXATION[1] * stresses[2]
        + (1.0 - RELAXATION[1]) * MEMORY_WEIGHT[1] * material[2] * loading
    )
    pressure = stresses[0] - TIME_STEP * (loading - memory_one - memory_two)
    return jnp.stack([pressure, memory_one, memory_two])


def local_stepwise(fields, media, plane_rows, box_offset):
    current = fields[0]
    material = media[0]
    count_x = current.shape[1]
    count_z = current.shape[2]
    section = lax.axis_index("sec")
    is_source = section == 0
    block_z = lax.axis_index("gz")
    local_rows = lax.dynamic_slice_in_dim(plane_rows, block_z * NPD, NPD) - block_z * count_z
    offset = lax.dynamic_slice_in_dim(box_offset, jnp.maximum(section - 1, 0), 1)[0]
    depth_ids = block_z * count_z + jnp.arange(count_z, dtype=jnp.int32)
    landing = offset + plane_rows // 2
    chosen = (landing[:, None] == depth_ids[None, :]).astype(jnp.float32)
    for step_index in range(STEPS):
        stress_pad = padded_2(current[2:5], (("gx", 1), ("gz", 2)), RADIUS)
        velocity = lax.cond(
            is_source,
            lambda: velocity_elastic(
                current[0:2], stress_pad, material[0], RADIUS, count_x, count_z
            ),
            lambda: velocity_acoustic(
                current[0:2], stress_pad, material[0], RADIUS, count_x, count_z
            ),
        )
        velocity_pad = padded_2(velocity, (("gx", 1), ("gz", 2)), RADIUS)
        stresses = lax.cond(
            is_source,
            lambda: stress_elastic(current[2:5], velocity_pad, material, RADIUS, count_x, count_z),
            lambda: stress_acoustic(current[2:5], velocity_pad, material, RADIUS, count_x, count_z),
        )
        current = jnp.concatenate([velocity, stresses], axis=0)
        picked = jnp.take(current, local_rows, axis=2)
        block_plane = jnp.transpose(
            jnp.stack([picked[0], picked[1], -0.5 * (picked[2] + picked[3])]), (0, 2, 1)
        )
        joined = lax.all_gather(block_plane, "gz", axis=1, tiled=True)
        gathered = broadcast(joined, "sec", 0)
        injected = jnp.einsum("ckx,kz->cxz", gathered, chosen, precision=lax.Precision.HIGHEST)
        far_state = jnp.concatenate([current[0:3] + COUPLING * injected, current[3:5]], axis=0)
        current = jnp.where(is_source, current, far_state)
    return current[None]


HALO = 2 * RADIUS * STEPS
CELLS = 128
HALF = CELLS // 2
WINDOW = HALF + 2 * HALO
DEPTH = 2 * CELLS
PART = HALF + HALO
NP = 2 * NPD
TRIM = (0, 8, 16, 24, 32)
WINDOWS = [WINDOW - 2 * amount for amount in TRIM]
COUNTS = len(WINDOWS)
ROWS = 192
GROUPS = CELLS // NP
SLOT = (
    ((0, 0), (1, 0), (2, 0)),
    ((3, 0), (4, 0), (5, 0)),
    ((6, 0), (7, 0), (6, 96)),
    ((3, 112), (4, 112), (5, 112)),
    ((0, 128), (1, 128), (2, 128)),
)
SCALE = 840.0
TAPS = (672.0, -168.0, 32.0, -3.0)


def banded(distance):
    values = jnp.zeros(distance.shape, jnp.float32)
    for offset, tap in enumerate(TAPS, 1):
        values = jnp.where(distance == offset, tap, values)
        values = jnp.where(distance == -offset, -tap, values)
    return values.astype(jnp.bfloat16)


def halves(values):
    high = values.astype(jnp.bfloat16)
    low = (values - high.astype(jnp.float32)).astype(jnp.bfloat16)
    return high, low


def dot(left, right):
    return jnp.dot(left, right, preferred_element_type=jnp.float32)


def diff_x(bands, parts):
    return dot(bands[parts[0].shape[0]][...], jnp.concatenate(parts, axis=0))


def along_depth(matrix, parts):
    return dot(jnp.concatenate(parts, axis=1), matrix[...])


def trimmed(arrays, amount):
    if amount == 0:
        return arrays
    return [array[amount:-amount] for array in arrays]


def lanes_of(shape):
    return lax.broadcasted_iota(jnp.int32, shape, 1) // NP


BODY = HALO - 8
WHOLE = (2, 4)
PAIRED = ((0, 1), (3, 5))
EDGE_ROWS = 8 * BODY + 8 * len(WHOLE) + 8 * len(PAIRED)


def pack_edge(block, target, at_end):
    body, rest = (CELLS - BODY, CELLS - HALO) if at_end else (0, BODY)
    near = lax.broadcasted_iota(jnp.int32, (8, CELLS), 0) // 4 == int(at_end)
    for index in range(8):
        target[BODY * index : BODY * (index + 1)] = block[index, body : body + BODY]
    row = 8 * BODY
    for index in WHOLE:
        target[row : row + 8] = block[index, rest : rest + 8]
        row += 8
    for one, two in PAIRED:
        turned = pltpu.roll(block[two, rest : rest + 8], 4, 0)
        target[row : row + 8] = jnp.where(near, block[one, rest : rest + 8], turned)
        row += 8


def unpack_rest(edge, window, lanes, before):
    rest = 0 if before else WINDOW - 8
    near = lax.broadcasted_iota(jnp.int32, (8, CELLS), 0) // 4 == int(before)
    row = 8 * BODY
    for index in WHOLE:
        window[index, rest : rest + 8, lanes] = edge[row : row + 8]
        row += 8
    for one, two in PAIRED:
        tile = edge[row : row + 8]
        window[one, rest : rest + 8, lanes] = jnp.where(near, tile, 0.0)
        window[two, rest : rest + 8, lanes] = jnp.where(near, pltpu.roll(tile, 4, 0), 0.0)
        row += 8
    for index in (6, 7):
        window[index, rest : rest + 8, lanes] = jnp.zeros((8, CELLS), jnp.float32)


def pack_kernel(fields, media, block, straight, crossed, swap, sems):
    core = lax.axis_index("gz")
    copies = [
        pltpu.make_async_copy(fields, block.at[:5], sems.at[0]),
        pltpu.make_async_copy(media, block.at[5:], sems.at[1]),
    ]
    for copy in copies:
        copy.start()
    for copy in copies:
        copy.wait()

    @pl.when(core == 0)
    def _():
        pack_edge(block, straight, True)
        pack_edge(block, crossed, False)
        swap[...] = block[:, CELLS - PART :]

    @pl.when(core == 1)
    def _():
        pack_edge(block, straight, False)
        pack_edge(block, crossed, True)
        swap[...] = block[:, :PART]


def assemble(window, block, ahead, behind, other):
    core = lax.axis_index("gz")
    low, high = slice(0, CELLS), slice(CELLS, DEPTH)

    @pl.when(core == 0)
    def _():
        @pl.loop(0, 8)
        def _(index):
            body = pl.ds(pl.multiple_of(BODY * index, 8), BODY)
            window[index, 8:HALO, low] = ahead[body]
            window[index, 8:HALO, high] = behind[body]
            window[index, HALO:, low] = block[index, :PART]
            window[index, HALO:, high] = other[index]

        unpack_rest(ahead, window, low, True)
        unpack_rest(behind, window, high, True)

    @pl.when(core == 1)
    def _():
        @pl.loop(0, 8)
        def _(index):
            body = pl.ds(pl.multiple_of(BODY * index, 8), BODY)
            window[index, :PART, high] = block[index, CELLS - PART :]
            window[index, :PART, low] = other[index]
            window[index, PART : WINDOW - 8, high] = ahead[body]
            window[index, PART : WINDOW - 8, low] = behind[body]

        unpack_rest(ahead, window, high, False)
        unpack_rest(behind, window, low, False)


def place(state, held, sent):
    start = HALO - TRIM[-1]
    core = lax.axis_index("gz")
    state = [array[start : start + HALF] for array in state]

    @pl.when(core == 0)
    def _():
        for index in range(5):
            held[index] = state[index][:, :CELLS]
            sent[index] = state[index][:, CELLS:]

    @pl.when(core == 1)
    def _():
        for index in range(5):
            held[index] = state[index][:, CELLS:]
            sent[index] = state[index][:, :CELLS]


def acoustic(state, bands):
    vx, vz, pressure, one, two, light, kappa, loss_one, loss_two = state
    band_x, band_z = bands
    parts = halves(pressure)
    vx = vx - light * diff_x(band_x, parts)
    vz = vz - light * along_depth(band_z, parts)
    load = kappa * (diff_x(band_x, halves(vx)) + along_depth(band_z, halves(vz)))
    one = RELAXATION[0] * one + loss_one * load
    two = RELAXATION[1] * two + loss_two * load
    pressure = pressure - TIME_STEP * (load - one - two)
    return [vx, vz, pressure, one, two, light, kappa, loss_one, loss_two]


def constants_kernel(plane_rows, box_offset, *targets):
    *bands_x, band_z, pick, land = targets
    for target in bands_x:
        count = target.shape[0]
        row = lax.broadcasted_iota(jnp.int32, target.shape, 0)
        column = lax.broadcasted_iota(jnp.int32, target.shape, 1)
        target[...] = banded(jnp.where(column < count, column, column - count) - row)
    shape = (DEPTH, DEPTH)
    distance = lax.broadcasted_iota(jnp.int32, shape, 0) - lax.broadcasted_iota(jnp.int32, shape, 1)
    band_z[:DEPTH] = banded(distance)
    band_z[DEPTH:] = band_z[:DEPTH]
    row = plane_rows[...]
    lane = lax.broadcasted_iota(jnp.int32, box_offset.shape, 1)
    offset = jnp.where(lane == lax.axis_index("sec") - 1, box_offset[...], 0)
    landing = row // 2 + jnp.sum(offset, axis=1, keepdims=True)
    depth = lax.broadcasted_iota(jnp.int32, (DEPTH, NP), 0)
    spread = lax.broadcasted_iota(jnp.int32, (NP, CELLS), 1) % NP
    spread = spread == lax.broadcasted_iota(jnp.int32, (NP, CELLS), 0)
    spread = jnp.where(spread, 1.0, 0.0).astype(jnp.bfloat16)
    hot = jnp.where(depth == row, 1.0, 0.0).astype(jnp.bfloat16)
    pick[:DEPTH] = dot(hot, spread).astype(jnp.bfloat16)
    pick[DEPTH:] = pick[:DEPTH]
    hot = jnp.where(depth == landing, 1.0, 0.0).astype(jnp.bfloat16)
    land[:CELLS] = dot(hot, spread).T.astype(jnp.bfloat16)
    land[CELLS:] = land[:CELLS]


def first_kernel(*refs):
    bands_x, (band_z, pick, block, behind, ahead, other) = refs[:COUNTS], refs[COUNTS:-4]
    held, sent, rows, carry = refs[-4:]
    band_x = {band.shape[0]: band for band in bands_x}
    assemble(carry, block, ahead, behind, other)
    section = lax.axis_index("sec")

    @pl.when(section > 0)
    def _():
        vx, vz, pressure, one, two, light, kappa, loss = [carry[index] for index in range(8)]
        light = light * (TIME_STEP / SCALE)
        kappa = kappa * (1.0 / SCALE)
        loss_one = loss * ((1.0 - RELAXATION[0]) * MEMORY_WEIGHT[0])
        loss_two = loss * ((1.0 - RELAXATION[1]) * MEMORY_WEIGHT[1])
        state = [vx, vz, pressure, one, two, light, kappa, loss_one, loss_two]
        for index, array in enumerate(acoustic(state, (band_x, band_z))):
            carry[index] = array

    @pl.when(section == 0)
    def _():
        vx, vz, sxx, szz, sxz, light, lame, shear = [carry[index] for index in range(8)]
        light = light * (TIME_STEP / SCALE)
        both = (lame + 2.0 * shear) * (TIME_STEP / SCALE)
        lame = lame * (TIME_STEP / SCALE)
        shear = shear * (TIME_STEP / SCALE)
        at = 0
        for step in range(STEPS):
            cut = TRIM[step] - at
            at = TRIM[step]
            vx, vz, sxx, szz, sxz, light, both, lame, shear = trimmed(
                [vx, vz, sxx, szz, sxz, light, both, lame, shear], cut
            )
            parts_xx, parts_zz, parts_xz = halves(sxx), halves(szz), halves(sxz)
            vx = vx + light * (diff_x(band_x, parts_xx) + along_depth(band_z, parts_xz))
            vz = vz + light * (diff_x(band_x, parts_xz) + along_depth(band_z, parts_zz))
            parts_x, parts_z = halves(vx), halves(vz)
            strain_x, strain_z = diff_x(band_x, parts_x), along_depth(band_z, parts_z)
            sxx = sxx + (both * strain_x + lame * strain_z)
            szz = szz + (lame * strain_x + both * strain_z)
            sxz = sxz + shear * (along_depth(band_z, parts_x) + diff_x(band_x, parts_z))
            low = 2 * RADIUS * (step + 1) - at
            for component, (parts, factor) in enumerate(
                ((parts_x, COUPLING), (parts_z, COUPLING), (halves(sxx + szz), -0.5 * COUPLING))
            ):
                picked = factor * along_depth(pick, parts)
                picked = picked[low : picked.shape[0] - low]
                group, base = SLOT[step][component]
                spot = pl.ds(base, picked.shape[0])
                rows[spot] = jnp.where(lanes_of(picked.shape) == group, picked, rows[spot])
        place([vx, vz, sxx, szz, sxz], held, sent)


def second_kernel(*refs):
    bands_x, (band_z, land, carry, rows, held_in, sent_in, held, sent) = refs[:COUNTS], refs[COUNTS:]
    band_x = {band.shape[0]: band for band in bands_x}
    section = lax.axis_index("sec")

    @pl.when(section == 0)
    def _():
        held[...] = held_in[...]
        sent[...] = sent_in[...]

    @pl.when(section > 0)
    def _():
        state = [carry[index] for index in range(9)]
        at = 0
        for step in range(STEPS):
            if step:
                state = trimmed(state, TRIM[step] - at)
                at = TRIM[step]
                state = acoustic(state, (band_x, band_z))
            low = 2 * RADIUS * (step + 1) - at
            high = WINDOW - 2 * at - low
            for component in range(3):
                group, base = SLOT[step][component]
                taken = rows[pl.ds(base, high - low)]
                taken = halves(jnp.where(lanes_of(taken.shape) == group, taken, 0.0))
                added = along_depth(land, taken)
                array = state[component]
                state[component] = jnp.concatenate(
                    [array[:low], array[low:high] + added, array[high:]], axis=0
                )
        place(state[:5], held, sent)


def last_kernel(held, swapped, out, sems):
    core = lax.axis_index("gz")
    copies = [
        pltpu.make_async_copy(
            source, out.at[:, pl.ds(pl.multiple_of(HALF * half, HALF), HALF)], sems.at[index]
        )
        for index, (source, half) in enumerate(((held, core), (swapped, 1 - core)))
    ]
    for copy in copies:
        copy.start()
    for copy in copies:
        copy.wait()


def call(
    kernel,
    outs,
    operands,
    flops,
    place_in=pltpu.VMEM,
    place_out=pltpu.VMEM,
    scratch=(),
):
    return pl.pallas_call(
        kernel,
        out_shape=outs,
        in_specs=[pl.BlockSpec(memory_space=place_in)] * len(operands),
        out_specs=[pl.BlockSpec(memory_space=place_out)] * len(outs),
        scratch_shapes=scratch,
        compiler_params=pltpu.CompilerParams(vmem_limit_bytes=48 * 1024 * 1024),
        cost_estimate=pl.CostEstimate(
            flops=flops, bytes_accessed=2 * 1024 * 1024, transcendentals=0
        ),
    )(*operands)


def full(*shape):
    return jax.ShapeDtypeStruct(shape, jnp.float32)


def narrow(*shape):
    return jax.ShapeDtypeStruct(shape, jnp.bfloat16)


def local_window(columns, fields, media, plane_rows, box_offset):
    fields, media = fields[0], media[0]
    core = lax.axis_index("gz")
    is_first = core == 0
    block, straight, crossed, swap = call(
        pack_kernel,
        [
            full(8, CELLS, CELLS),
            full(EDGE_ROWS, CELLS),
            full(EDGE_ROWS, CELLS),
            full(8, PART, CELLS),
        ],
        [pltpu.with_memory_space_constraint(array, pltpu.HBM) for array in (fields, media)],
        1000,
        place_in=pltpu.HBM,
        scratch=[pltpu.SemaphoreType.DMA((2,))],
    )
    straight_pairs, crossed_pairs = [], []
    for column in range(columns):
        if column + 1 < columns:
            straight_pairs.append((2 * column, 2 * column + 2))
            crossed_pairs.append((2 * column + 1, 2 * column + 2))
        if column:
            straight_pairs.append((2 * column + 1, 2 * column - 1))
            crossed_pairs.append((2 * column, 2 * column - 1))
    turn = [(0, 1), (1, 0)]
    behind = lax.ppermute(crossed, ("gx", "gz"), crossed_pairs)
    ahead = lax.ppermute(straight, ("gx", "gz"), straight_pairs)
    joined = lax.all_gather(swap, "gz")
    other = jnp.where(is_first, joined[1], joined[0])
    *bands, pick, land = call(
        constants_kernel,
        [narrow(count, 2 * count) for count in WINDOWS]
        + [narrow(2 * DEPTH, DEPTH), narrow(2 * DEPTH, CELLS), narrow(2 * CELLS, DEPTH)],
        [plane_rows[None], box_offset[None]],
        1_000_000_000,
    )
    held, sent, rows, carry = call(
        first_kernel,
        [
            full(5, HALF, CELLS),
            full(5, HALF, CELLS),
            full(ROWS, CELLS),
            full(9, WINDOW, DEPTH),
        ],
        [*bands, pick, block, behind, ahead, other],
        4_000_000_000,
    )
    routes = ([(0, 4), (1, 3)], [(0, 2), (1, 5)], [(0, 6), (1, 7)])
    arrived = [lax.ppermute(rows, ("sec", "gz"), route) for route in routes]
    rows = arrived[0] + arrived[1] + arrived[2]
    held, sent = call(
        second_kernel,
        [full(5, HALF, CELLS), full(5, HALF, CELLS)],
        [*bands, land, carry, rows, held, sent],
        4_000_000_000,
    )
    swapped = lax.ppermute(sent, "gz", turn)
    (out,) = call(
        last_kernel,
        [full(5, CELLS, CELLS)],
        [held, swapped],
        1000,
        place_out=pl.ANY,
        scratch=[pltpu.SemaphoreType.DMA((2,))],
    )
    return out[None]


def solution(mesh):
    in_specs = (P("sec", None, "gx", "gz"), P("sec", None, "gx", "gz"), P(), P())
    out_specs = P("sec", None, "gx", "gz")
    if mesh.shape["gz"] == 2:
        local = functools.partial(local_window, mesh.shape["gx"])
    else:
        local = local_stepwise
    return jax.shard_map(local, mesh=mesh, in_specs=in_specs, out_specs=out_specs, check_vma=False)
```

```python
import functools

import jax
import jax.numpy as jnp
from jax import lax
from jax.experimental import pallas as pl
from jax.experimental.pallas import tpu as pltpu
from jax.sharding import PartitionSpec as P

RADIUS = 4
STEPS = 5
NPD = 8

STENCIL = (0.8, -0.2, 4.0 / 105.0, -1.0 / 280.0)
TIME_STEP = 0.2
COUPLING = 0.5
RELAXATION = (0.9, 0.5)
MEMORY_WEIGHT = (0.15, 0.1)


def padded_2(block, sides, width):
    for axis, dim in sides:
        count = lax.axis_size(axis)
        forward = [(i, i + 1) for i in range(count - 1)]
        backward = [(target, source) for source, target in forward]
        low = lax.ppermute(
            lax.slice_in_dim(block, block.shape[dim] - width, None, axis=dim), axis, forward
        )
        high = lax.ppermute(lax.slice_in_dim(block, 0, width, axis=dim), axis, backward)
        block = jnp.concatenate([low, block, high], axis=dim)
    return block


def broadcast(value, axis, source):
    kept = jnp.where(lax.axis_index(axis) == source, value, 0).astype(value.dtype)
    return lax.psum(kept, axis)


def along_x(padded, anchor, count_x, count_z):
    summed = jnp.zeros(padded.shape[:-2] + (count_x, count_z), jnp.float32)
    for offset, stencil_tap in enumerate(STENCIL, 1):
        forward = padded[
            ..., anchor + offset : anchor + offset + count_x, anchor : anchor + count_z
        ]
        backward = padded[
            ..., anchor - offset : anchor - offset + count_x, anchor : anchor + count_z
        ]
        summed = summed + stencil_tap * (forward - backward)
    return summed


def along_z(padded, anchor, count_x, count_z):
    summed = jnp.zeros(padded.shape[:-2] + (count_x, count_z), jnp.float32)
    for offset, stencil_tap in enumerate(STENCIL, 1):
        forward = padded[
            ..., anchor : anchor + count_x, anchor + offset : anchor + offset + count_z
        ]
        backward = padded[
            ..., anchor : anchor + count_x, anchor - offset : anchor - offset + count_z
        ]
        summed = summed + stencil_tap * (forward - backward)
    return summed


def velocity_elastic(velocity, stresses, buoyancy, anchor, count_x, count_z):
    updated_x = velocity[0] + TIME_STEP * buoyancy * (
        along_x(stresses[0], anchor, count_x, count_z)
        + along_z(stresses[2], anchor, count_x, count_z)
    )
    updated_z = velocity[1] + TIME_STEP * buoyancy * (
        along_x(stresses[2], anchor, count_x, count_z)
        + along_z(stresses[1], anchor, count_x, count_z)
    )
    return jnp.stack([updated_x, updated_z])


def velocity_acoustic(velocity, stresses, buoyancy, anchor, count_x, count_z):
    updated_x = velocity[0] - TIME_STEP * buoyancy * along_x(stresses[0], anchor, count_x, count_z)
    updated_z = velocity[1] - TIME_STEP * buoyancy * along_z(stresses[0], anchor, count_x, count_z)
    return jnp.stack([updated_x, updated_z])


def stress_elastic(stresses, velocity_pad, material, anchor, count_x, count_z):
    strain_x = along_x(velocity_pad[0], anchor, count_x, count_z)
    strain_z = along_z(velocity_pad[1], anchor, count_x, count_z)
    strain_shear = along_z(velocity_pad[0], anchor, count_x, count_z) + along_x(
        velocity_pad[1], anchor, count_x, count_z
    )
    lame_first = material[1]
    shear_modulus = material[2]
    normal_x = stresses[0] + TIME_STEP * (
        (lame_first + 2.0 * shear_modulus) * strain_x + lame_first * strain_z
    )
    normal_z = stresses[1] + TIME_STEP * (
        lame_first * strain_x + (lame_first + 2.0 * shear_modulus) * strain_z
    )
    shear_new = stresses[2] + TIME_STEP * shear_modulus * strain_shear
    return jnp.stack([normal_x, normal_z, shear_new])


def stress_acoustic(stresses, velocity_pad, material, anchor, count_x, count_z):
    divergence = along_x(velocity_pad[0], anchor, count_x, count_z) + along_z(
        velocity_pad[1], anchor, count_x, count_z
    )
    loading = material[1] * divergence
    memory_one = (
        RELAXATION[0] * stresses[1]
        + (1.0 - RELAXATION[0]) * MEMORY_WEIGHT[0] * material[2] * loading
    )
    memory_two = (
        RELAXATION[1] * stresses[2]
        + (1.0 - RELAXATION[1]) * MEMORY_WEIGHT[1] * material[2] * loading
    )
    pressure = stresses[0] - TIME_STEP * (loading - memory_one - memory_two)
    return jnp.stack([pressure, memory_one, memory_two])


def local_stepwise(fields, media, plane_rows, box_offset):
    current = fields[0]
    material = media[0]
    count_x = current.shape[1]
    count_z = current.shape[2]
    section = lax.axis_index("sec")
    is_source = section == 0
    block_z = lax.axis_index("gz")
    local_rows = lax.dynamic_slice_in_dim(plane_rows, block_z * NPD, NPD) - block_z * count_z
    offset = lax.dynamic_slice_in_dim(box_offset, jnp.maximum(section - 1, 0), 1)[0]
    depth_ids = block_z * count_z + jnp.arange(count_z, dtype=jnp.int32)
    landing = offset + plane_rows // 2
    chosen = (landing[:, None] == depth_ids[None, :]).astype(jnp.float32)
    for step_index in range(STEPS):
        stress_pad = padded_2(current[2:5], (("gx", 1), ("gz", 2)), RADIUS)
        velocity = lax.cond(
            is_source,
            lambda: velocity_elastic(
                current[0:2], stress_pad, material[0], RADIUS, count_x, count_z
            ),
            lambda: velocity_acoustic(
                current[0:2], stress_pad, material[0], RADIUS, count_x, count_z
            ),
        )
        velocity_pad = padded_2(velocity, (("gx", 1), ("gz", 2)), RADIUS)
        stresses = lax.cond(
            is_source,
            lambda: stress_elastic(current[2:5], velocity_pad, material, RADIUS, count_x, count_z),
            lambda: stress_acoustic(current[2:5], velocity_pad, material, RADIUS, count_x, count_z),
        )
        current = jnp.concatenate([velocity, stresses], axis=0)
        picked = jnp.take(current, local_rows, axis=2)
        block_plane = jnp.transpose(
            jnp.stack([picked[0], picked[1], -0.5 * (picked[2] + picked[3])]), (0, 2, 1)
        )
        joined = lax.all_gather(block_plane, "gz", axis=1, tiled=True)
        gathered = broadcast(joined, "sec", 0)
        injected = jnp.einsum("ckx,kz->cxz", gathered, chosen, precision=lax.Precision.HIGHEST)
        far_state = jnp.concatenate([current[0:3] + COUPLING * injected, current[3:5]], axis=0)
        current = jnp.where(is_source, current, far_state)
    return current[None]


HALO = 2 * RADIUS * STEPS
CELLS = 128
HALF = CELLS // 2
WINDOW = HALF + 2 * HALO
DEPTH = 2 * CELLS
PART = HALF + HALO
NP = 2 * NPD
TRIM = (0, 8, 16, 24, 32)
WINDOWS = [WINDOW - 2 * amount for amount in TRIM]
COUNTS = len(WINDOWS)
ROWS = 192
GROUPS = CELLS // NP
SLOT = (
    ((0, 0), (1, 0), (2, 0)),
    ((3, 0), (4, 0), (5, 0)),
    ((6, 0), (7, 0), (6, 96)),
    ((3, 112), (4, 112), (5, 112)),
    ((0, 128), (1, 128), (2, 128)),
)
SCALE = 840.0
TAPS = (672.0, -168.0, 32.0, -3.0)


def banded(distance):
    values = jnp.zeros(distance.shape, jnp.float32)
    for offset, tap in enumerate(TAPS, 1):
        values = jnp.where(distance == offset, tap, values)
        values = jnp.where(distance == -offset, -tap, values)
    return values.astype(jnp.bfloat16)


def halves(values):
    high = values.astype(jnp.bfloat16)
    low = (values - high.astype(jnp.float32)).astype(jnp.bfloat16)
    return high, low


def dot(left, right):
    return jnp.dot(left, right, preferred_element_type=jnp.float32)


def diff_x(bands, parts):
    return dot(bands[parts[0].shape[0]][...], jnp.concatenate(parts, axis=0))


def along_depth(matrix, parts):
    return dot(jnp.concatenate(parts, axis=1), matrix[...])


def trimmed(arrays, amount):
    if amount == 0:
        return arrays
    return [array[amount:-amount] for array in arrays]


def lanes_of(shape):
    return lax.broadcasted_iota(jnp.int32, shape, 1) // NP


BODY = HALO - 8
WHOLE = (2, 4)
PAIRED = ((0, 1), (3, 5))
EDGE_ROWS = 8 * BODY + 8 * len(WHOLE) + 8 * len(PAIRED)


def pack_edge(block, target, at_end):
    body, rest = (CELLS - BODY, CELLS - HALO) if at_end else (0, BODY)
    near = lax.broadcasted_iota(jnp.int32, (8, CELLS), 0) // 4 == int(at_end)
    for index in range(8):
        target[BODY * index : BODY * (index + 1)] = block[index, body : body + BODY]
    row = 8 * BODY
    for index in WHOLE:
        target[row : row + 8] = block[index, rest : rest + 8]
        row += 8
    for one, two in PAIRED:
        turned = pltpu.roll(block[two, rest : rest + 8], 4, 0)
        target[row : row + 8] = jnp.where(near, block[one, rest : rest + 8], turned)
        row += 8


def unpack_rest(edge, window, lanes, before):
    rest = 0 if before else WINDOW - 8
    near = lax.broadcasted_iota(jnp.int32, (8, CELLS), 0) // 4 == int(before)
    row = 8 * BODY
    for index in WHOLE:
        window[index, rest : rest + 8, lanes] = edge[row : row + 8]
        row += 8
    for one, two in PAIRED:
        tile = edge[row : row + 8]
        window[one, rest : rest + 8, lanes] = jnp.where(near, tile, 0.0)
        window[two, rest : rest + 8, lanes] = jnp.where(near, pltpu.roll(tile, 4, 0), 0.0)
        row += 8
    for index in (6, 7):
        window[index, rest : rest + 8, lanes] = jnp.zeros((8, CELLS), jnp.float32)


def pack_kernel(fields, media, block, straight, crossed, swap, sems):
    core = lax.axis_index("gz")
    copies = [
        pltpu.make_async_copy(fields, block.at[:5], sems.at[0]),
        pltpu.make_async_copy(media, block.at[5:], sems.at[1]),
    ]
    for copy in copies:
        copy.start()
    for copy in copies:
        copy.wait()

    @pl.when(core == 0)
    def _():
        pack_edge(block, straight, True)
        pack_edge(block, crossed, False)
        swap[...] = block[:, CELLS - PART :]

    @pl.when(core == 1)
    def _():
        pack_edge(block, straight, False)
        pack_edge(block, crossed, True)
        swap[...] = block[:, :PART]


def assemble(window, block, ahead, behind, other):
    core = lax.axis_index("gz")
    low, high = slice(0, CELLS), slice(CELLS, DEPTH)

    @pl.when(core == 0)
    def _():
        @pl.loop(0, 8)
        def _(index):
            body = pl.ds(pl.multiple_of(BODY * index, 8), BODY)
            window[index, 8:HALO, low] = ahead[body]
            window[index, 8:HALO, high] = behind[body]
            window[index, HALO:, low] = block[index, :PART]
            window[index, HALO:, high] = other[index]

        unpack_rest(ahead, window, low, True)
        unpack_rest(behind, window, high, True)

    @pl.when(core == 1)
    def _():
        @pl.loop(0, 8)
        def _(index):
            body = pl.ds(pl.multiple_of(BODY * index, 8), BODY)
            window[index, :PART, high] = block[index, CELLS - PART :]
            window[index, :PART, low] = other[index]
            window[index, PART : WINDOW - 8, high] = ahead[body]
            window[index, PART : WINDOW - 8, low] = behind[body]

        unpack_rest(ahead, window, high, False)
        unpack_rest(behind, window, low, False)


def place(state, held, sent):
    start = HALO - TRIM[-1]
    core = lax.axis_index("gz")
    state = [array[start : start + HALF] for array in state]

    @pl.when(core == 0)
    def _():
        for index in range(5):
            held[index] = state[index][:, :CELLS]
            sent[index] = state[index][:, CELLS:]

    @pl.when(core == 1)
    def _():
        for index in range(5):
            held[index] = state[index][:, CELLS:]
            sent[index] = state[index][:, :CELLS]


def acoustic(state, bands):
    vx, vz, pressure, one, two, light, kappa, loss_one, loss_two = state
    band_x, band_z = bands
    parts = halves(pressure)
    vx = vx - light * diff_x(band_x, parts)
    vz = vz - light * along_depth(band_z, parts)
    load = kappa * (diff_x(band_x, halves(vx)) + along_depth(band_z, halves(vz)))
    one = RELAXATION[0] * one + loss_one * load
    two = RELAXATION[1] * two + loss_two * load
    pressure = pressure - TIME_STEP * (load - one - two)
    return [vx, vz, pressure, one, two, light, kappa, loss_one, loss_two]


def constants_kernel(plane_rows, box_offset, *targets):
    *bands_x, band_z, pick, land = targets
    for target in bands_x:
        count = target.shape[0]
        row = lax.broadcasted_iota(jnp.int32, target.shape, 0)
        column = lax.broadcasted_iota(jnp.int32, target.shape, 1)
        target[...] = banded(jnp.where(column < count, column, column - count) - row)
    shape = (DEPTH, DEPTH)
    distance = lax.broadcasted_iota(jnp.int32, shape, 0) - lax.broadcasted_iota(jnp.int32, shape, 1)
    band_z[:DEPTH] = banded(distance)
    band_z[DEPTH:] = band_z[:DEPTH]
    row = plane_rows[...]
    lane = lax.broadcasted_iota(jnp.int32, box_offset.shape, 1)
    offset = jnp.where(lane == lax.axis_index("sec") - 1, box_offset[...], 0)
    landing = row // 2 + jnp.sum(offset, axis=1, keepdims=True)
    depth = lax.broadcasted_iota(jnp.int32, (DEPTH, NP), 0)
    spread = lax.broadcasted_iota(jnp.int32, (NP, CELLS), 1) % NP
    spread = spread == lax.broadcasted_iota(jnp.int32, (NP, CELLS), 0)
    spread = jnp.where(spread, 1.0, 0.0).astype(jnp.bfloat16)
    hot = jnp.where(depth == row, 1.0, 0.0).astype(jnp.bfloat16)
    pick[:DEPTH] = dot(hot, spread).astype(jnp.bfloat16)
    pick[DEPTH:] = pick[:DEPTH]
    hot = jnp.where(depth == landing, 1.0, 0.0).astype(jnp.bfloat16)
    land[:CELLS] = dot(hot, spread).T.astype(jnp.bfloat16)
    land[CELLS:] = land[:CELLS]


def first_kernel(*refs):
    bands_x, (band_z, pick, block, behind, ahead, other) = refs[:COUNTS], refs[COUNTS:-4]
    held, sent, rows, carry = refs[-4:]
    band_x = {band.shape[0]: band for band in bands_x}
    assemble(carry, block, ahead, behind, other)
    section = lax.axis_index("sec")

    @pl.when(section > 0)
    def _():
        vx, vz, pressure, one, two, light, kappa, loss = [carry[index] for index in range(8)]
        light = light * (TIME_STEP / SCALE)
        kappa = kappa * (1.0 / SCALE)
        loss_one = loss * ((1.0 - RELAXATION[0]) * MEMORY_WEIGHT[0])
        loss_two = loss * ((1.0 - RELAXATION[1]) * MEMORY_WEIGHT[1])
        state = [vx, vz, pressure, one, two, light, kappa, loss_one, loss_two]
        for index, array in enumerate(acoustic(state, (band_x, band_z))):
            carry[index] = array

    @pl.when(section == 0)
    def _():
        vx, vz, sxx, szz, sxz, light, lame, shear = [carry[index] for index in range(8)]
        light = light * (TIME_STEP / SCALE)
        both = (lame + 2.0 * shear) * (TIME_STEP / SCALE)
        lame = lame * (TIME_STEP / SCALE)
        shear = shear * (TIME_STEP / SCALE)
        at = 0
        for step in range(STEPS):
            cut = TRIM[step] - at
            at = TRIM[step]
            vx, vz, sxx, szz, sxz, light, both, lame, shear = trimmed(
                [vx, vz, sxx, szz, sxz, light, both, lame, shear], cut
            )
            parts_xx, parts_zz, parts_xz = halves(sxx), halves(szz), halves(sxz)
            vx = vx + light * (diff_x(band_x, parts_xx) + along_depth(band_z, parts_xz))
            vz = vz + light * (diff_x(band_x, parts_xz) + along_depth(band_z, parts_zz))
            parts_x, parts_z = halves(vx), halves(vz)
            strain_x, strain_z = diff_x(band_x, parts_x), along_depth(band_z, parts_z)
            sxx = sxx + (both * strain_x + lame * strain_z)
            szz = szz + (lame * strain_x + both * strain_z)
            sxz = sxz + shear * (along_depth(band_z, parts_x) + diff_x(band_x, parts_z))
            low = 2 * RADIUS * (step + 1) - at
            for component, (parts, factor) in enumerate(
                ((parts_x, COUPLING), (parts_z, COUPLING), (halves(sxx + szz), -0.5 * COUPLING))
            ):
                picked = factor * along_depth(pick, parts)
                picked = picked[low : picked.shape[0] - low]
                group, base = SLOT[step][component]
                spot = pl.ds(base, picked.shape[0])
                rows[spot] = jnp.where(lanes_of(picked.shape) == group, picked, rows[spot])
        place([vx, vz, sxx, szz, sxz], held, sent)


def second_kernel(*refs):
    bands_x, (band_z, land, carry, rows, held_in, sent_in, held, sent) = refs[:COUNTS], refs[COUNTS:]
    band_x = {band.shape[0]: band for band in bands_x}
    section = lax.axis_index("sec")

    @pl.when(section == 0)
    def _():
        held[...] = held_in[...]
        sent[...] = sent_in[...]

    @pl.when(section > 0)
    def _():
        state = [carry[index] for index in range(9)]
        at = 0
        for step in range(STEPS):
            if step:
                state = trimmed(state, TRIM[step] - at)
                at = TRIM[step]
                state = acoustic(state, (band_x, band_z))
            low = 2 * RADIUS * (step + 1) - at
            high = WINDOW - 2 * at - low
            for component in range(3):
                group, base = SLOT[step][component]
                taken = rows[pl.ds(base, high - low)]
                taken = halves(jnp.where(lanes_of(taken.shape) == group, taken, 0.0))
                added = along_depth(land, taken)
                array = state[component]
                state[component] = jnp.concatenate(
                    [array[:low], array[low:high] + added, array[high:]], axis=0
                )
        place(state[:5], held, sent)


def last_kernel(held, swapped, out, sems):
    core = lax.axis_index("gz")
    copies = [
        pltpu.make_async_copy(
            source, out.at[:, pl.ds(pl.multiple_of(HALF * half, HALF), HALF)], sems.at[index]
        )
        for index, (source, half) in enumerate(((held, core), (swapped, 1 - core)))
    ]
    for copy in copies:
        copy.start()
    for copy in copies:
        copy.wait()


def call(
    kernel,
    outs,
    operands,
    flops,
    place_in=pltpu.VMEM,
    place_out=pltpu.VMEM,
    scratch=(),
):
    return pl.pallas_call(
        kernel,
        out_shape=outs,
        in_specs=[pl.BlockSpec(memory_space=place_in)] * len(operands),
        out_specs=[pl.BlockSpec(memory_space=place_out)] * len(outs),
        scratch_shapes=scratch,
        compiler_params=pltpu.CompilerParams(vmem_limit_bytes=48 * 1024 * 1024),
        cost_estimate=pl.CostEstimate(
            flops=flops, bytes_accessed=2 * 1024 * 1024, transcendentals=0
        ),
    )(*operands)


def full(*shape):
    return jax.ShapeDtypeStruct(shape, jnp.float32)


def narrow(*shape):
    return jax.ShapeDtypeStruct(shape, jnp.bfloat16)


def local_window(columns, fields, media, plane_rows, box_offset):
    fields, media = fields[0], media[0]
    core = lax.axis_index("gz")
    is_first = core == 0
    block, straight, crossed, swap = call(
        pack_kernel,
        [
            full(8, CELLS, CELLS),
            full(EDGE_ROWS, CELLS),
            full(EDGE_ROWS, CELLS),
            full(8, PART, CELLS),
        ],
        [pltpu.with_memory_space_constraint(array, pltpu.HBM) for array in (fields, media)],
        1000,
        place_in=pltpu.HBM,
        scratch=[pltpu.SemaphoreType.DMA((2,))],
    )
    straight_pairs, crossed_pairs = [], []
    for column in range(columns):
        if column + 1 < columns:
            straight_pairs.append((2 * column, 2 * column + 2))
            crossed_pairs.append((2 * column + 1, 2 * column + 2))
        if column:
            straight_pairs.append((2 * column + 1, 2 * column - 1))
            crossed_pairs.append((2 * column, 2 * column - 1))
    turn = [(0, 1), (1, 0)]
    behind = lax.ppermute(crossed, ("gx", "gz"), crossed_pairs)
    ahead = lax.ppermute(straight, ("gx", "gz"), straight_pairs)
    joined = lax.all_gather(swap, "gz")
    other = jnp.where(is_first, joined[1], joined[0])
    *bands, pick, land = call(
        constants_kernel,
        [narrow(count, 2 * count) for count in WINDOWS]
        + [narrow(2 * DEPTH, DEPTH), narrow(2 * DEPTH, CELLS), narrow(2 * CELLS, DEPTH)],
        [plane_rows[None], box_offset[None]],
        1_000_000_000,
    )
    held, sent, rows, carry = call(
        first_kernel,
        [
            full(5, HALF, CELLS),
            full(5, HALF, CELLS),
            full(ROWS, CELLS),
            full(9, WINDOW, DEPTH),
        ],
        [*bands, pick, block, behind, ahead, other],
        4_000_000_000,
    )
    routes = ([(0, 4), (1, 3)], [(0, 6), (1, 7)], [(0, 2), (1, 5)])
    arrived = [lax.ppermute(rows, ("sec", "gz"), route) for route in routes]
    rows = arrived[0] + arrived[1] + arrived[2]
    held, sent = call(
        second_kernel,
        [full(5, HALF, CELLS), full(5, HALF, CELLS)],
        [*bands, land, carry, rows, held, sent],
        4_000_000_000,
    )
    swapped = lax.ppermute(sent, "gz", turn)
    (out,) = call(
        last_kernel,
        [full(5, CELLS, CELLS)],
        [held, swapped],
        1000,
        place_out=pl.ANY,
        scratch=[pltpu.SemaphoreType.DMA((2,))],
    )
    return out[None]


def solution(mesh):
    in_specs = (P("sec", None, "gx", "gz"), P("sec", None, "gx", "gz"), P(), P())
    out_specs = P("sec", None, "gx", "gz")
    if mesh.shape["gz"] == 2:
        local = functools.partial(local_window, mesh.shape["gx"])
    else:
        local = local_stepwise
    return jax.shard_map(local, mesh=mesh, in_specs=in_specs, out_specs=out_specs, check_vma=False)
```

```python
import functools

import jax
import jax.numpy as jnp
from jax import lax
from jax.experimental import pallas as pl
from jax.experimental.pallas import tpu as pltpu
from jax.sharding import PartitionSpec as P

RADIUS = 4
STEPS = 5
NPD = 8

STENCIL = (0.8, -0.2, 4.0 / 105.0, -1.0 / 280.0)
TIME_STEP = 0.2
COUPLING = 0.5
RELAXATION = (0.9, 0.5)
MEMORY_WEIGHT = (0.15, 0.1)


def padded_2(block, sides, width):
    for axis, dim in sides:
        count = lax.axis_size(axis)
        forward = [(i, i + 1) for i in range(count - 1)]
        backward = [(target, source) for source, target in forward]
        low = lax.ppermute(
            lax.slice_in_dim(block, block.shape[dim] - width, None, axis=dim), axis, forward
        )
        high = lax.ppermute(lax.slice_in_dim(block, 0, width, axis=dim), axis, backward)
        block = jnp.concatenate([low, block, high], axis=dim)
    return block


def broadcast(value, axis, source):
    kept = jnp.where(lax.axis_index(axis) == source, value, 0).astype(value.dtype)
    return lax.psum(kept, axis)


def along_x(padded, anchor, count_x, count_z):
    summed = jnp.zeros(padded.shape[:-2] + (count_x, count_z), jnp.float32)
    for offset, stencil_tap in enumerate(STENCIL, 1):
        forward = padded[
            ..., anchor + offset : anchor + offset + count_x, anchor : anchor + count_z
        ]
        backward = padded[
            ..., anchor - offset : anchor - offset + count_x, anchor : anchor + count_z
        ]
        summed = summed + stencil_tap * (forward - backward)
    return summed


def along_z(padded, anchor, count_x, count_z):
    summed = jnp.zeros(padded.shape[:-2] + (count_x, count_z), jnp.float32)
    for offset, stencil_tap in enumerate(STENCIL, 1):
        forward = padded[
            ..., anchor : anchor + count_x, anchor + offset : anchor + offset + count_z
        ]
        backward = padded[
            ..., anchor : anchor + count_x, anchor - offset : anchor - offset + count_z
        ]
        summed = summed + stencil_tap * (forward - backward)
    return summed


def velocity_elastic(velocity, stresses, buoyancy, anchor, count_x, count_z):
    updated_x = velocity[0] + TIME_STEP * buoyancy * (
        along_x(stresses[0], anchor, count_x, count_z)
        + along_z(stresses[2], anchor, count_x, count_z)
    )
    updated_z = velocity[1] + TIME_STEP * buoyancy * (
        along_x(stresses[2], anchor, count_x, count_z)
        + along_z(stresses[1], anchor, count_x, count_z)
    )
    return jnp.stack([updated_x, updated_z])


def velocity_acoustic(velocity, stresses, buoyancy, anchor, count_x, count_z):
    updated_x = velocity[0] - TIME_STEP * buoyancy * along_x(stresses[0], anchor, count_x, count_z)
    updated_z = velocity[1] - TIME_STEP * buoyancy * along_z(stresses[0], anchor, count_x, count_z)
    return jnp.stack([updated_x, updated_z])


def stress_elastic(stresses, velocity_pad, material, anchor, count_x, count_z):
    strain_x = along_x(velocity_pad[0], anchor, count_x, count_z)
    strain_z = along_z(velocity_pad[1], anchor, count_x, count_z)
    strain_shear = along_z(velocity_pad[0], anchor, count_x, count_z) + along_x(
        velocity_pad[1], anchor, count_x, count_z
    )
    lame_first = material[1]
    shear_modulus = material[2]
    normal_x = stresses[0] + TIME_STEP * (
        (lame_first + 2.0 * shear_modulus) * strain_x + lame_first * strain_z
    )
    normal_z = stresses[1] + TIME_STEP * (
        lame_first * strain_x + (lame_first + 2.0 * shear_modulus) * strain_z
    )
    shear_new = stresses[2] + TIME_STEP * shear_modulus * strain_shear
    return jnp.stack([normal_x, normal_z, shear_new])


def stress_acoustic(stresses, velocity_pad, material, anchor, count_x, count_z):
    divergence = along_x(velocity_pad[0], anchor, count_x, count_z) + along_z(
        velocity_pad[1], anchor, count_x, count_z
    )
    loading = material[1] * divergence
    memory_one = (
        RELAXATION[0] * stresses[1]
        + (1.0 - RELAXATION[0]) * MEMORY_WEIGHT[0] * material[2] * loading
    )
    memory_two = (
        RELAXATION[1] * stresses[2]
        + (1.0 - RELAXATION[1]) * MEMORY_WEIGHT[1] * material[2] * loading
    )
    pressure = stresses[0] - TIME_STEP * (loading - memory_one - memory_two)
    return jnp.stack([pressure, memory_one, memory_two])


def local_stepwise(fields, media, plane_rows, box_offset):
    current = fields[0]
    material = media[0]
    count_x = current.shape[1]
    count_z = current.shape[2]
    section = lax.axis_index("sec")
    is_source = section == 0
    block_z = lax.axis_index("gz")
    local_rows = lax.dynamic_slice_in_dim(plane_rows, block_z * NPD, NPD) - block_z * count_z
    offset = lax.dynamic_slice_in_dim(box_offset, jnp.maximum(section - 1, 0), 1)[0]
    depth_ids = block_z * count_z + jnp.arange(count_z, dtype=jnp.int32)
    landing = offset + plane_rows // 2
    chosen = (landing[:, None] == depth_ids[None, :]).astype(jnp.float32)
    for step_index in range(STEPS):
        stress_pad = padded_2(current[2:5], (("gx", 1), ("gz", 2)), RADIUS)
        velocity = lax.cond(
            is_source,
            lambda: velocity_elastic(
                current[0:2], stress_pad, material[0], RADIUS, count_x, count_z
            ),
            lambda: velocity_acoustic(
                current[0:2], stress_pad, material[0], RADIUS, count_x, count_z
            ),
        )
        velocity_pad = padded_2(velocity, (("gx", 1), ("gz", 2)), RADIUS)
        stresses = lax.cond(
            is_source,
            lambda: stress_elastic(current[2:5], velocity_pad, material, RADIUS, count_x, count_z),
            lambda: stress_acoustic(current[2:5], velocity_pad, material, RADIUS, count_x, count_z),
        )
        current = jnp.concatenate([velocity, stresses], axis=0)
        picked = jnp.take(current, local_rows, axis=2)
        block_plane = jnp.transpose(
            jnp.stack([picked[0], picked[1], -0.5 * (picked[2] + picked[3])]), (0, 2, 1)
        )
        joined = lax.all_gather(block_plane, "gz", axis=1, tiled=True)
        gathered = broadcast(joined, "sec", 0)
        injected = jnp.einsum("ckx,kz->cxz", gathered, chosen, precision=lax.Precision.HIGHEST)
        far_state = jnp.concatenate([current[0:3] + COUPLING * injected, current[3:5]], axis=0)
        current = jnp.where(is_source, current, far_state)
    return current[None]


HALO = 2 * RADIUS * STEPS
CELLS = 128
HALF = CELLS // 2
WINDOW = HALF + 2 * HALO
DEPTH = 2 * CELLS
PART = HALF + HALO
NP = 2 * NPD
TRIM = (0, 8, 16, 24, 32)
WINDOWS = [WINDOW - 2 * amount for amount in TRIM]
COUNTS = len(WINDOWS)
ROWS = 192
GROUPS = CELLS // NP
SLOT = (
    ((0, 0), (1, 0), (2, 0)),
    ((3, 0), (4, 0), (5, 0)),
    ((6, 0), (7, 0), (6, 96)),
    ((3, 112), (4, 112), (5, 112)),
    ((0, 128), (1, 128), (2, 128)),
)
SCALE = 840.0
TAPS = (672.0, -168.0, 32.0, -3.0)


def banded(distance):
    values = jnp.zeros(distance.shape, jnp.float32)
    for offset, tap in enumerate(TAPS, 1):
        values = jnp.where(distance == offset, tap, values)
        values = jnp.where(distance == -offset, -tap, values)
    return values.astype(jnp.bfloat16)


def halves(values):
    high = values.astype(jnp.bfloat16)
    low = (values - high.astype(jnp.float32)).astype(jnp.bfloat16)
    return high, low


def dot(left, right):
    return jnp.dot(left, right, preferred_element_type=jnp.float32)


def diff_x(bands, parts):
    return dot(bands[parts[0].shape[0]][...], jnp.concatenate(parts, axis=0))


def along_depth(matrix, parts):
    return dot(jnp.concatenate(parts, axis=1), matrix[...])


def trimmed(arrays, amount):
    if amount == 0:
        return arrays
    return [array[amount:-amount] for array in arrays]


def lanes_of(shape):
    return lax.broadcasted_iota(jnp.int32, shape, 1) // NP


BODY = HALO - 8
WHOLE = (2, 4)
PAIRED = ((0, 1), (3, 5))
EDGE_ROWS = 8 * BODY + 8 * len(WHOLE) + 8 * len(PAIRED)


def pack_edge(block, target, at_end):
    body, rest = (CELLS - BODY, CELLS - HALO) if at_end else (0, BODY)
    near = lax.broadcasted_iota(jnp.int32, (8, CELLS), 0) // 4 == int(at_end)
    for index in range(8):
        target[BODY * index : BODY * (index + 1)] = block[index, body : body + BODY]
    row = 8 * BODY
    for index in WHOLE:
        target[row : row + 8] = block[index, rest : rest + 8]
        row += 8
    for one, two in PAIRED:
        turned = pltpu.roll(block[two, rest : rest + 8], 4, 0)
        target[row : row + 8] = jnp.where(near, block[one, rest : rest + 8], turned)
        row += 8


def unpack_rest(edge, window, lanes, before):
    rest = 0 if before else WINDOW - 8
    near = lax.broadcasted_iota(jnp.int32, (8, CELLS), 0) // 4 == int(before)
    row = 8 * BODY
    for index in WHOLE:
        window[index, rest : rest + 8, lanes] = edge[row : row + 8]
        row += 8
    for one, two in PAIRED:
        tile = edge[row : row + 8]
        window[one, rest : rest + 8, lanes] = jnp.where(near, tile, 0.0)
        window[two, rest : rest + 8, lanes] = jnp.where(near, pltpu.roll(tile, 4, 0), 0.0)
        row += 8
    for index in (6, 7):
        window[index, rest : rest + 8, lanes] = jnp.zeros((8, CELLS), jnp.float32)


def pack_kernel(fields, media, block, straight, crossed, swap, sems):
    core = lax.axis_index("gz")
    copies = [
        pltpu.make_async_copy(fields, block.at[:5], sems.at[0]),
        pltpu.make_async_copy(media, block.at[5:], sems.at[1]),
    ]
    for copy in copies:
        copy.start()
    for copy in copies:
        copy.wait()

    @pl.when(core == 0)
    def _():
        pack_edge(block, straight, True)
        pack_edge(block, crossed, False)
        swap[...] = block[:, CELLS - PART :]

    @pl.when(core == 1)
    def _():
        pack_edge(block, straight, False)
        pack_edge(block, crossed, True)
        swap[...] = block[:, :PART]


def assemble(window, block, ahead, behind, other):
    core = lax.axis_index("gz")
    low, high = slice(0, CELLS), slice(CELLS, DEPTH)

    @pl.when(core == 0)
    def _():
        @pl.loop(0, 8)
        def _(index):
            body = pl.ds(pl.multiple_of(BODY * index, 8), BODY)
            window[index, 8:HALO, low] = ahead[body]
            window[index, 8:HALO, high] = behind[body]
            window[index, HALO:, low] = block[index, :PART]
            window[index, HALO:, high] = other[index]

        unpack_rest(ahead, window, low, True)
        unpack_rest(behind, window, high, True)

    @pl.when(core == 1)
    def _():
        @pl.loop(0, 8)
        def _(index):
            body = pl.ds(pl.multiple_of(BODY * index, 8), BODY)
            window[index, :PART, high] = block[index, CELLS - PART :]
            window[index, :PART, low] = other[index]
            window[index, PART : WINDOW - 8, high] = ahead[body]
            window[index, PART : WINDOW - 8, low] = behind[body]

        unpack_rest(ahead, window, high, False)
        unpack_rest(behind, window, low, False)


def place(state, held, sent):
    start = HALO - TRIM[-1]
    core = lax.axis_index("gz")
    state = [array[start : start + HALF] for array in state]

    @pl.when(core == 0)
    def _():
        for index in range(5):
            held[index] = state[index][:, :CELLS]
            sent[index] = state[index][:, CELLS:]

    @pl.when(core == 1)
    def _():
        for index in range(5):
            held[index] = state[index][:, CELLS:]
            sent[index] = state[index][:, :CELLS]


def acoustic(state, bands):
    vx, vz, pressure, one, two, light, kappa, loss_one, loss_two = state
    band_x, band_z = bands
    parts = halves(pressure)
    vx = vx - light * diff_x(band_x, parts)
    vz = vz - light * along_depth(band_z, parts)
    load = kappa * (diff_x(band_x, halves(vx)) + along_depth(band_z, halves(vz)))
    one = RELAXATION[0] * one + loss_one * load
    two = RELAXATION[1] * two + loss_two * load
    pressure = pressure - TIME_STEP * (load - one - two)
    return [vx, vz, pressure, one, two, light, kappa, loss_one, loss_two]


def constants_kernel(plane_rows, box_offset, *targets):
    *bands_x, band_z, pick, land = targets
    for target in bands_x:
        count = target.shape[0]
        row = lax.broadcasted_iota(jnp.int32, target.shape, 0)
        column = lax.broadcasted_iota(jnp.int32, target.shape, 1)
        target[...] = banded(jnp.where(column < count, column, column - count) - row)
    shape = (DEPTH, DEPTH)
    distance = lax.broadcasted_iota(jnp.int32, shape, 0) - lax.broadcasted_iota(jnp.int32, shape, 1)
    band_z[:DEPTH] = banded(distance)
    band_z[DEPTH:] = band_z[:DEPTH]
    row = plane_rows[...]
    lane = lax.broadcasted_iota(jnp.int32, box_offset.shape, 1)
    offset = jnp.where(lane == lax.axis_index("sec") - 1, box_offset[...], 0)
    landing = row // 2 + jnp.sum(offset, axis=1, keepdims=True)
    depth = lax.broadcasted_iota(jnp.int32, (DEPTH, NP), 0)
    spread = lax.broadcasted_iota(jnp.int32, (NP, CELLS), 1) % NP
    spread = spread == lax.broadcasted_iota(jnp.int32, (NP, CELLS), 0)
    spread = jnp.where(spread, 1.0, 0.0).astype(jnp.bfloat16)
    hot = jnp.where(depth == row, 1.0, 0.0).astype(jnp.bfloat16)
    pick[:DEPTH] = dot(hot, spread).astype(jnp.bfloat16)
    pick[DEPTH:] = pick[:DEPTH]
    hot = jnp.where(depth == landing, 1.0, 0.0).astype(jnp.bfloat16)
    land[:CELLS] = dot(hot, spread).T.astype(jnp.bfloat16)
    land[CELLS:] = land[:CELLS]


def first_kernel(*refs):
    bands_x, (band_z, pick, block, behind, ahead, other) = refs[:COUNTS], refs[COUNTS:-4]
    held, sent, rows, carry = refs[-4:]
    band_x = {band.shape[0]: band for band in bands_x}
    assemble(carry, block, ahead, behind, other)
    section = lax.axis_index("sec")

    @pl.when(section > 0)
    def _():
        vx, vz, pressure, one, two, light, kappa, loss = [carry[index] for index in range(8)]
        light = light * (TIME_STEP / SCALE)
        kappa = kappa * (1.0 / SCALE)
        loss_one = loss * ((1.0 - RELAXATION[0]) * MEMORY_WEIGHT[0])
        loss_two = loss * ((1.0 - RELAXATION[1]) * MEMORY_WEIGHT[1])
        state = [vx, vz, pressure, one, two, light, kappa, loss_one, loss_two]
        for index, array in enumerate(acoustic(state, (band_x, band_z))):
            carry[index] = array

    @pl.when(section == 0)
    def _():
        vx, vz, sxx, szz, sxz, light, lame, shear = [carry[index] for index in range(8)]
        light = light * (TIME_STEP / SCALE)
        both = (lame + 2.0 * shear) * (TIME_STEP / SCALE)
        lame = lame * (TIME_STEP / SCALE)
        shear = shear * (TIME_STEP / SCALE)
        at = 0
        for step in range(STEPS):
            cut = TRIM[step] - at
            at = TRIM[step]
            vx, vz, sxx, szz, sxz, light, both, lame, shear = trimmed(
                [vx, vz, sxx, szz, sxz, light, both, lame, shear], cut
            )
            parts_xx, parts_zz, parts_xz = halves(sxx), halves(szz), halves(sxz)
            vx = vx + light * (diff_x(band_x, parts_xx) + along_depth(band_z, parts_xz))
            vz = vz + light * (diff_x(band_x, parts_xz) + along_depth(band_z, parts_zz))
            parts_x, parts_z = halves(vx), halves(vz)
            strain_x, strain_z = diff_x(band_x, parts_x), along_depth(band_z, parts_z)
            sxx = sxx + (both * strain_x + lame * strain_z)
            szz = szz + (lame * strain_x + both * strain_z)
            sxz = sxz + shear * (along_depth(band_z, parts_x) + diff_x(band_x, parts_z))
            low = 2 * RADIUS * (step + 1) - at
            for component, (parts, factor) in enumerate(
                ((parts_x, COUPLING), (parts_z, COUPLING), (halves(sxx + szz), -0.5 * COUPLING))
            ):
                picked = factor * along_depth(pick, parts)
                picked = picked[low : picked.shape[0] - low]
                group, base = SLOT[step][component]
                spot = pl.ds(base, picked.shape[0])
                rows[spot] = jnp.where(lanes_of(picked.shape) == group, picked, rows[spot])
        place([vx, vz, sxx, szz, sxz], held, sent)


def second_kernel(*refs):
    bands_x, (band_z, land, carry, rows, held_in, sent_in, held, sent) = refs[:COUNTS], refs[COUNTS:]
    band_x = {band.shape[0]: band for band in bands_x}
    section = lax.axis_index("sec")

    @pl.when(section == 0)
    def _():
        held[...] = held_in[...]
        sent[...] = sent_in[...]

    @pl.when(section > 0)
    def _():
        state = [carry[index] for index in range(9)]
        at = 0
        for step in range(STEPS):
            if step:
                state = trimmed(state, TRIM[step] - at)
                at = TRIM[step]
                state = acoustic(state, (band_x, band_z))
            low = 2 * RADIUS * (step + 1) - at
            high = WINDOW - 2 * at - low
            for component in range(3):
                group, base = SLOT[step][component]
                taken = rows[pl.ds(base, high - low)]
                taken = halves(jnp.where(lanes_of(taken.shape) == group, taken, 0.0))
                added = along_depth(land, taken)
                array = state[component]
                state[component] = jnp.concatenate(
                    [array[:low], array[low:high] + added, array[high:]], axis=0
                )
        place(state[:5], held, sent)


def last_kernel(held, swapped, out, sems):
    core = lax.axis_index("gz")
    copies = [
        pltpu.make_async_copy(
            source, out.at[:, pl.ds(pl.multiple_of(HALF * half, HALF), HALF)], sems.at[index]
        )
        for index, (source, half) in enumerate(((held, core), (swapped, 1 - core)))
    ]
    for copy in copies:
        copy.start()
    for copy in copies:
        copy.wait()


def call(
    kernel,
    outs,
    operands,
    flops,
    place_in=pltpu.VMEM,
    place_out=pltpu.VMEM,
    scratch=(),
):
    return pl.pallas_call(
        kernel,
        out_shape=outs,
        in_specs=[pl.BlockSpec(memory_space=place_in)] * len(operands),
        out_specs=[pl.BlockSpec(memory_space=place_out)] * len(outs),
        scratch_shapes=scratch,
        compiler_params=pltpu.CompilerParams(vmem_limit_bytes=48 * 1024 * 1024),
        cost_estimate=pl.CostEstimate(
            flops=flops, bytes_accessed=2 * 1024 * 1024, transcendentals=0
        ),
    )(*operands)


def full(*shape):
    return jax.ShapeDtypeStruct(shape, jnp.float32)


def narrow(*shape):
    return jax.ShapeDtypeStruct(shape, jnp.bfloat16)


def local_window(columns, fields, media, plane_rows, box_offset):
    fields, media = fields[0], media[0]
    core = lax.axis_index("gz")
    is_first = core == 0
    block, straight, crossed, swap = call(
        pack_kernel,
        [
            full(8, CELLS, CELLS),
            full(EDGE_ROWS, CELLS),
            full(EDGE_ROWS, CELLS),
            full(8, PART, CELLS),
        ],
        [pltpu.with_memory_space_constraint(array, pltpu.HBM) for array in (fields, media)],
        1000,
        place_in=pltpu.HBM,
        scratch=[pltpu.SemaphoreType.DMA((2,))],
    )
    straight_pairs, crossed_pairs = [], []
    for column in range(columns):
        if column + 1 < columns:
            straight_pairs.append((2 * column, 2 * column + 2))
            crossed_pairs.append((2 * column + 1, 2 * column + 2))
        if column:
            straight_pairs.append((2 * column + 1, 2 * column - 1))
            crossed_pairs.append((2 * column, 2 * column - 1))
    turn = [(0, 1), (1, 0)]
    behind = lax.ppermute(crossed, ("gx", "gz"), crossed_pairs)
    ahead = lax.ppermute(straight, ("gx", "gz"), straight_pairs)
    joined = lax.all_gather(swap, "gz")
    other = jnp.where(is_first, joined[1], joined[0])
    *bands, pick, land = call(
        constants_kernel,
        [narrow(count, 2 * count) for count in WINDOWS]
        + [narrow(2 * DEPTH, DEPTH), narrow(2 * DEPTH, CELLS), narrow(2 * CELLS, DEPTH)],
        [plane_rows[None], box_offset[None]],
        1_000_000_000,
    )
    held, sent, rows, carry = call(
        first_kernel,
        [
            full(5, HALF, CELLS),
            full(5, HALF, CELLS),
            full(ROWS, CELLS),
            full(9, WINDOW, DEPTH),
        ],
        [*bands, pick, block, behind, ahead, other],
        4_000_000_000,
    )
    routes = ([(0, 2), (1, 5)], [(0, 6), (1, 7)], [(0, 4), (1, 3)])
    arrived = [lax.ppermute(rows, ("sec", "gz"), route) for route in routes]
    rows = arrived[0] + arrived[1] + arrived[2]
    held, sent = call(
        second_kernel,
        [full(5, HALF, CELLS), full(5, HALF, CELLS)],
        [*bands, land, carry, rows, held, sent],
        4_000_000_000,
    )
    swapped = lax.ppermute(sent, "gz", turn)
    (out,) = call(
        last_kernel,
        [full(5, CELLS, CELLS)],
        [held, swapped],
        1000,
        place_out=pl.ANY,
        scratch=[pltpu.SemaphoreType.DMA((2,))],
    )
    return out[None]


def solution(mesh):
    in_specs = (P("sec", None, "gx", "gz"), P("sec", None, "gx", "gz"), P(), P())
    out_specs = P("sec", None, "gx", "gz")
    if mesh.shape["gz"] == 2:
        local = functools.partial(local_window, mesh.shape["gx"])
    else:
        local = local_stepwise
    return jax.shard_map(local, mesh=mesh, in_specs=in_specs, out_specs=out_specs, check_vma=False)
```

```python
import functools

import jax
import jax.numpy as jnp
from jax import lax
from jax.experimental import pallas as pl
from jax.experimental.pallas import tpu as pltpu
from jax.sharding import PartitionSpec as P

RADIUS = 4
STEPS = 5
NPD = 8

STENCIL = (0.8, -0.2, 4.0 / 105.0, -1.0 / 280.0)
TIME_STEP = 0.2
COUPLING = 0.5
RELAXATION = (0.9, 0.5)
MEMORY_WEIGHT = (0.15, 0.1)


def padded_2(block, sides, width):
    for axis, dim in sides:
        count = lax.axis_size(axis)
        forward = [(i, i + 1) for i in range(count - 1)]
        backward = [(target, source) for source, target in forward]
        low = lax.ppermute(
            lax.slice_in_dim(block, block.shape[dim] - width, None, axis=dim), axis, forward
        )
        high = lax.ppermute(lax.slice_in_dim(block, 0, width, axis=dim), axis, backward)
        block = jnp.concatenate([low, block, high], axis=dim)
    return block


def broadcast(value, axis, source):
    kept = jnp.where(lax.axis_index(axis) == source, value, 0).astype(value.dtype)
    return lax.psum(kept, axis)


def along_x(padded, anchor, count_x, count_z):
    summed = jnp.zeros(padded.shape[:-2] + (count_x, count_z), jnp.float32)
    for offset, stencil_tap in enumerate(STENCIL, 1):
        forward = padded[
            ..., anchor + offset : anchor + offset + count_x, anchor : anchor + count_z
        ]
        backward = padded[
            ..., anchor - offset : anchor - offset + count_x, anchor : anchor + count_z
        ]
        summed = summed + stencil_tap * (forward - backward)
    return summed


def along_z(padded, anchor, count_x, count_z):
    summed = jnp.zeros(padded.shape[:-2] + (count_x, count_z), jnp.float32)
    for offset, stencil_tap in enumerate(STENCIL, 1):
        forward = padded[
            ..., anchor : anchor + count_x, anchor + offset : anchor + offset + count_z
        ]
        backward = padded[
            ..., anchor : anchor + count_x, anchor - offset : anchor - offset + count_z
        ]
        summed = summed + stencil_tap * (forward - backward)
    return summed


def velocity_elastic(velocity, stresses, buoyancy, anchor, count_x, count_z):
    updated_x = velocity[0] + TIME_STEP * buoyancy * (
        along_x(stresses[0], anchor, count_x, count_z)
        + along_z(stresses[2], anchor, count_x, count_z)
    )
    updated_z = velocity[1] + TIME_STEP * buoyancy * (
        along_x(stresses[2], anchor, count_x, count_z)
        + along_z(stresses[1], anchor, count_x, count_z)
    )
    return jnp.stack([updated_x, updated_z])


def velocity_acoustic(velocity, stresses, buoyancy, anchor, count_x, count_z):
    updated_x = velocity[0] - TIME_STEP * buoyancy * along_x(stresses[0], anchor, count_x, count_z)
    updated_z = velocity[1] - TIME_STEP * buoyancy * along_z(stresses[0], anchor, count_x, count_z)
    return jnp.stack([updated_x, updated_z])


def stress_elastic(stresses, velocity_pad, material, anchor, count_x, count_z):
    strain_x = along_x(velocity_pad[0], anchor, count_x, count_z)
    strain_z = along_z(velocity_pad[1], anchor, count_x, count_z)
    strain_shear = along_z(velocity_pad[0], anchor, count_x, count_z) + along_x(
        velocity_pad[1], anchor, count_x, count_z
    )
    lame_first = material[1]
    shear_modulus = material[2]
    normal_x = stresses[0] + TIME_STEP * (
        (lame_first + 2.0 * shear_modulus) * strain_x + lame_first * strain_z
    )
    normal_z = stresses[1] + TIME_STEP * (
        lame_first * strain_x + (lame_first + 2.0 * shear_modulus) * strain_z
    )
    shear_new = stresses[2] + TIME_STEP * shear_modulus * strain_shear
    return jnp.stack([normal_x, normal_z, shear_new])


def stress_acoustic(stresses, velocity_pad, material, anchor, count_x, count_z):
    divergence = along_x(velocity_pad[0], anchor, count_x, count_z) + along_z(
        velocity_pad[1], anchor, count_x, count_z
    )
    loading = material[1] * divergence
    memory_one = (
        RELAXATION[0] * stresses[1]
        + (1.0 - RELAXATION[0]) * MEMORY_WEIGHT[0] * material[2] * loading
    )
    memory_two = (
        RELAXATION[1] * stresses[2]
        + (1.0 - RELAXATION[1]) * MEMORY_WEIGHT[1] * material[2] * loading
    )
    pressure = stresses[0] - TIME_STEP * (loading - memory_one - memory_two)
    return jnp.stack([pressure, memory_one, memory_two])


def local_stepwise(fields, media, plane_rows, box_offset):
    current = fields[0]
    material = media[0]
    count_x = current.shape[1]
    count_z = current.shape[2]
    section = lax.axis_index("sec")
    is_source = section == 0
    block_z = lax.axis_index("gz")
    local_rows = lax.dynamic_slice_in_dim(plane_rows, block_z * NPD, NPD) - block_z * count_z
    offset = lax.dynamic_slice_in_dim(box_offset, jnp.maximum(section - 1, 0), 1)[0]
    depth_ids = block_z * count_z + jnp.arange(count_z, dtype=jnp.int32)
    landing = offset + plane_rows // 2
    chosen = (landing[:, None] == depth_ids[None, :]).astype(jnp.float32)
    for step_index in range(STEPS):
        stress_pad = padded_2(current[2:5], (("gx", 1), ("gz", 2)), RADIUS)
        velocity = lax.cond(
            is_source,
            lambda: velocity_elastic(
                current[0:2], stress_pad, material[0], RADIUS, count_x, count_z
            ),
            lambda: velocity_acoustic(
                current[0:2], stress_pad, material[0], RADIUS, count_x, count_z
            ),
        )
        velocity_pad = padded_2(velocity, (("gx", 1), ("gz", 2)), RADIUS)
        stresses = lax.cond(
            is_source,
            lambda: stress_elastic(current[2:5], velocity_pad, material, RADIUS, count_x, count_z),
            lambda: stress_acoustic(current[2:5], velocity_pad, material, RADIUS, count_x, count_z),
        )
        current = jnp.concatenate([velocity, stresses], axis=0)
        picked = jnp.take(current, local_rows, axis=2)
        block_plane = jnp.transpose(
            jnp.stack([picked[0], picked[1], -0.5 * (picked[2] + picked[3])]), (0, 2, 1)
        )
        joined = lax.all_gather(block_plane, "gz", axis=1, tiled=True)
        gathered = broadcast(joined, "sec", 0)
        injected = jnp.einsum("ckx,kz->cxz", gathered, chosen, precision=lax.Precision.HIGHEST)
        far_state = jnp.concatenate([current[0:3] + COUPLING * injected, current[3:5]], axis=0)
        current = jnp.where(is_source, current, far_state)
    return current[None]


HALO = 2 * RADIUS * STEPS
CELLS = 128
HALF = CELLS // 2
WINDOW = HALF + 2 * HALO
DEPTH = 2 * CELLS
PART = HALF + HALO
NP = 2 * NPD
TRIM = (0, 8, 16, 24, 32)
WINDOWS = [WINDOW - 2 * amount for amount in TRIM]
COUNTS = len(WINDOWS)
ROWS = 192
GROUPS = CELLS // NP
SLOT = (
    ((0, 0), (1, 0), (2, 0)),
    ((3, 0), (4, 0), (5, 0)),
    ((6, 0), (7, 0), (6, 96)),
    ((3, 112), (4, 112), (5, 112)),
    ((0, 128), (1, 128), (2, 128)),
)
SCALE = 840.0
TAPS = (672.0, -168.0, 32.0, -3.0)


def banded(distance):
    values = jnp.zeros(distance.shape, jnp.float32)
    for offset, tap in enumerate(TAPS, 1):
        values = jnp.where(distance == offset, tap, values)
        values = jnp.where(distance == -offset, -tap, values)
    return values.astype(jnp.bfloat16)


def halves(values):
    high = values.astype(jnp.bfloat16)
    low = (values - high.astype(jnp.float32)).astype(jnp.bfloat16)
    return high, low


def dot(left, right):
    return jnp.dot(left, right, preferred_element_type=jnp.float32)


def diff_x(bands, parts):
    return dot(bands[parts[0].shape[0]][...], jnp.concatenate(parts, axis=0))


def along_depth(matrix, parts):
    return dot(jnp.concatenate(parts, axis=1), matrix[...])


def trimmed(arrays, amount):
    if amount == 0:
        return arrays
    return [array[amount:-amount] for array in arrays]


def lanes_of(shape):
    return lax.broadcasted_iota(jnp.int32, shape, 1) // NP


BODY = HALO - 8
WHOLE = (2, 4)
PAIRED = ((0, 1), (3, 5))
EDGE_ROWS = 8 * BODY + 8 * len(WHOLE) + 8 * len(PAIRED)


def pack_edge(block, target, at_end):
    body, rest = (CELLS - BODY, CELLS - HALO) if at_end else (0, BODY)
    near = lax.broadcasted_iota(jnp.int32, (8, CELLS), 0) // 4 == int(at_end)
    for index in range(8):
        target[BODY * index : BODY * (index + 1)] = block[index, body : body + BODY]
    row = 8 * BODY
    for index in WHOLE:
        target[row : row + 8] = block[index, rest : rest + 8]
        row += 8
    for one, two in PAIRED:
        turned = pltpu.roll(block[two, rest : rest + 8], 4, 0)
        target[row : row + 8] = jnp.where(near, block[one, rest : rest + 8], turned)
        row += 8


def unpack_rest(edge, window, lanes, before):
    rest = 0 if before else WINDOW - 8
    near = lax.broadcasted_iota(jnp.int32, (8, CELLS), 0) // 4 == int(before)
    row = 8 * BODY
    for index in WHOLE:
        window[index, rest : rest + 8, lanes] = edge[row : row + 8]
        row += 8
    for one, two in PAIRED:
        tile = edge[row : row + 8]
        window[one, rest : rest + 8, lanes] = jnp.where(near, tile, 0.0)
        window[two, rest : rest + 8, lanes] = jnp.where(near, pltpu.roll(tile, 4, 0), 0.0)
        row += 8
    for index in (6, 7):
        window[index, rest : rest + 8, lanes] = jnp.zeros((8, CELLS), jnp.float32)


def pack_kernel(fields, media, block, straight, crossed, swap, sems):
    core = lax.axis_index("gz")
    copies = [
        pltpu.make_async_copy(fields, block.at[:5], sems.at[0]),
        pltpu.make_async_copy(media, block.at[5:], sems.at[1]),
    ]
    for copy in copies:
        copy.start()
    for copy in copies:
        copy.wait()

    @pl.when(core == 0)
    def _():
        pack_edge(block, straight, True)
        pack_edge(block, crossed, False)
        swap[...] = block[:, CELLS - PART :]

    @pl.when(core == 1)
    def _():
        pack_edge(block, straight, False)
        pack_edge(block, crossed, True)
        swap[...] = block[:, :PART]


def assemble(window, block, ahead, behind, other):
    core = lax.axis_index("gz")
    low, high = slice(0, CELLS), slice(CELLS, DEPTH)

    @pl.when(core == 0)
    def _():
        @pl.loop(0, 8)
        def _(index):
            body = pl.ds(pl.multiple_of(BODY * index, 8), BODY)
            window[index, 8:HALO, low] = ahead[body]
            window[index, 8:HALO, high] = behind[body]
            window[index, HALO:, low] = block[index, :PART]
            window[index, HALO:, high] = other[index]

        unpack_rest(ahead, window, low, True)
        unpack_rest(behind, window, high, True)

    @pl.when(core == 1)
    def _():
        @pl.loop(0, 8)
        def _(index):
            body = pl.ds(pl.multiple_of(BODY * index, 8), BODY)
            window[index, :PART, high] = block[index, CELLS - PART :]
            window[index, :PART, low] = other[index]
            window[index, PART : WINDOW - 8, high] = ahead[body]
            window[index, PART : WINDOW - 8, low] = behind[body]

        unpack_rest(ahead, window, high, False)
        unpack_rest(behind, window, low, False)


def place(state, held, sent):
    start = HALO - TRIM[-1]
    core = lax.axis_index("gz")
    state = [array[start : start + HALF] for array in state]

    @pl.when(core == 0)
    def _():
        for index in range(5):
            held[index] = state[index][:, :CELLS]
            sent[index] = state[index][:, CELLS:]

    @pl.when(core == 1)
    def _():
        for index in range(5):
            held[index] = state[index][:, CELLS:]
            sent[index] = state[index][:, :CELLS]


def acoustic(state, bands):
    vx, vz, pressure, one, two, light, kappa, loss_one, loss_two = state
    band_x, band_z = bands
    parts = halves(pressure)
    vx = vx - light * diff_x(band_x, parts)
    vz = vz - light * along_depth(band_z, parts)
    load = kappa * (diff_x(band_x, halves(vx)) + along_depth(band_z, halves(vz)))
    one = RELAXATION[0] * one + loss_one * load
    two = RELAXATION[1] * two + loss_two * load
    pressure = pressure - TIME_STEP * (load - one - two)
    return [vx, vz, pressure, one, two, light, kappa, loss_one, loss_two]


def constants_kernel(plane_rows, box_offset, *targets):
    *bands_x, band_z, pick, land = targets
    for target in bands_x:
        count = target.shape[0]
        row = lax.broadcasted_iota(jnp.int32, target.shape, 0)
        column = lax.broadcasted_iota(jnp.int32, target.shape, 1)
        target[...] = banded(jnp.where(column < count, column, column - count) - row)
    shape = (DEPTH, DEPTH)
    distance = lax.broadcasted_iota(jnp.int32, shape, 0) - lax.broadcasted_iota(jnp.int32, shape, 1)
    band_z[:DEPTH] = banded(distance)
    band_z[DEPTH:] = band_z[:DEPTH]
    row = plane_rows[...]
    lane = lax.broadcasted_iota(jnp.int32, box_offset.shape, 1)
    offset = jnp.where(lane == lax.axis_index("sec") - 1, box_offset[...], 0)
    landing = row // 2 + jnp.sum(offset, axis=1, keepdims=True)
    depth = lax.broadcasted_iota(jnp.int32, (DEPTH, NP), 0)
    spread = lax.broadcasted_iota(jnp.int32, (NP, CELLS), 1) % NP
    spread = spread == lax.broadcasted_iota(jnp.int32, (NP, CELLS), 0)
    spread = jnp.where(spread, 1.0, 0.0).astype(jnp.bfloat16)
    hot = jnp.where(depth == row, 1.0, 0.0).astype(jnp.bfloat16)
    pick[:DEPTH] = dot(hot, spread).astype(jnp.bfloat16)
    pick[DEPTH:] = pick[:DEPTH]
    hot = jnp.where(depth == landing, 1.0, 0.0).astype(jnp.bfloat16)
    land[:CELLS] = dot(hot, spread).T.astype(jnp.bfloat16)
    land[CELLS:] = land[:CELLS]


def first_kernel(*refs):
    bands_x, (band_z, pick, block, behind, ahead, other) = refs[:COUNTS], refs[COUNTS:-2]
    rows, carry = refs[-2:]
    band_x = {band.shape[0]: band for band in bands_x}
    assemble(carry, block, ahead, behind, other)
    section = lax.axis_index("sec")

    @pl.when(section > 0)
    def _():
        vx, vz, pressure, one, two, light, kappa, loss = [carry[index] for index in range(8)]
        light = light * (TIME_STEP / SCALE)
        kappa = kappa * (1.0 / SCALE)
        loss_one = loss * ((1.0 - RELAXATION[0]) * MEMORY_WEIGHT[0])
        loss_two = loss * ((1.0 - RELAXATION[1]) * MEMORY_WEIGHT[1])
        state = [vx, vz, pressure, one, two, light, kappa, loss_one, loss_two]
        for index, array in enumerate(acoustic(state, (band_x, band_z))):
            carry[index] = array

    @pl.when(section == 0)
    def _():
        vx, vz, sxx, szz, sxz, light, lame, shear = [carry[index] for index in range(8)]
        light = light * (TIME_STEP / SCALE)
        both = (lame + 2.0 * shear) * (TIME_STEP / SCALE)
        lame = lame * (TIME_STEP / SCALE)
        shear = shear * (TIME_STEP / SCALE)
        at = 0
        for step in range(STEPS):
            cut = TRIM[step] - at
            at = TRIM[step]
            vx, vz, sxx, szz, sxz, light, both, lame, shear = trimmed(
                [vx, vz, sxx, szz, sxz, light, both, lame, shear], cut
            )
            parts_xx, parts_zz, parts_xz = halves(sxx), halves(szz), halves(sxz)
            vx = vx + light * (diff_x(band_x, parts_xx) + along_depth(band_z, parts_xz))
            vz = vz + light * (diff_x(band_x, parts_xz) + along_depth(band_z, parts_zz))
            parts_x, parts_z = halves(vx), halves(vz)
            strain_x, strain_z = diff_x(band_x, parts_x), along_depth(band_z, parts_z)
            sxx = sxx + (both * strain_x + lame * strain_z)
            szz = szz + (lame * strain_x + both * strain_z)
            if step < STEPS - 1:
                sxz = sxz + shear * (along_depth(band_z, parts_x) + diff_x(band_x, parts_z))
            low = 2 * RADIUS * (step + 1) - at
            for component, (parts, factor) in enumerate(
                ((parts_x, COUPLING), (parts_z, COUPLING), (halves(sxx + szz), -0.5 * COUPLING))
            ):
                picked = factor * along_depth(pick, parts)
                picked = picked[low : picked.shape[0] - low]
                group, base = SLOT[step][component]
                spot = pl.ds(base, picked.shape[0])
                rows[spot] = jnp.where(lanes_of(picked.shape) == group, picked, rows[spot])
        for index, array in enumerate((vx, vz, sxx, szz, sxz, shear)):
            carry[index, : array.shape[0]] = array


def second_kernel(*refs):
    bands_x, (band_z, land, carry, rows, held, sent) = refs[:COUNTS], refs[COUNTS:]
    band_x = {band.shape[0]: band for band in bands_x}
    section = lax.axis_index("sec")

    @pl.when(section == 0)
    def _():
        count = WINDOWS[-1]
        vx, vz, sxx, szz, sxz, shear = [carry[index, :count] for index in range(6)]
        slope = along_depth(band_z, halves(vx)) + diff_x(band_x, halves(vz))
        place([vx, vz, sxx, szz, sxz + shear * slope], held, sent)

    @pl.when(section > 0)
    def _():
        state = [carry[index] for index in range(9)]
        at = 0
        for step in range(STEPS):
            if step:
                state = trimmed(state, TRIM[step] - at)
                at = TRIM[step]
                state = acoustic(state, (band_x, band_z))
            low = 2 * RADIUS * (step + 1) - at
            high = WINDOW - 2 * at - low
            for component in range(3):
                group, base = SLOT[step][component]
                taken = rows[pl.ds(base, high - low)]
                taken = halves(jnp.where(lanes_of(taken.shape) == group, taken, 0.0))
                added = along_depth(land, taken)
                array = state[component]
                state[component] = jnp.concatenate(
                    [array[:low], array[low:high] + added, array[high:]], axis=0
                )
        place(state[:5], held, sent)


def last_kernel(held, swapped, out, sems):
    core = lax.axis_index("gz")
    copies = [
        pltpu.make_async_copy(
            source, out.at[:, pl.ds(pl.multiple_of(HALF * half, HALF), HALF)], sems.at[index]
        )
        for index, (source, half) in enumerate(((held, core), (swapped, 1 - core)))
    ]
    for copy in copies:
        copy.start()
    for copy in copies:
        copy.wait()


def call(
    kernel,
    outs,
    operands,
    flops,
    place_in=pltpu.VMEM,
    place_out=pltpu.VMEM,
    scratch=(),
):
    return pl.pallas_call(
        kernel,
        out_shape=outs,
        in_specs=[pl.BlockSpec(memory_space=place_in)] * len(operands),
        out_specs=[pl.BlockSpec(memory_space=place_out)] * len(outs),
        scratch_shapes=scratch,
        compiler_params=pltpu.CompilerParams(vmem_limit_bytes=48 * 1024 * 1024),
        cost_estimate=pl.CostEstimate(
            flops=flops, bytes_accessed=2 * 1024 * 1024, transcendentals=0
        ),
    )(*operands)


def full(*shape):
    return jax.ShapeDtypeStruct(shape, jnp.float32)


def narrow(*shape):
    return jax.ShapeDtypeStruct(shape, jnp.bfloat16)


def local_window(columns, fields, media, plane_rows, box_offset):
    fields, media = fields[0], media[0]
    core = lax.axis_index("gz")
    is_first = core == 0
    block, straight, crossed, swap = call(
        pack_kernel,
        [
            full(8, CELLS, CELLS),
            full(EDGE_ROWS, CELLS),
            full(EDGE_ROWS, CELLS),
            full(8, PART, CELLS),
        ],
        [pltpu.with_memory_space_constraint(array, pltpu.HBM) for array in (fields, media)],
        1000,
        place_in=pltpu.HBM,
        scratch=[pltpu.SemaphoreType.DMA((2,))],
    )
    straight_pairs, crossed_pairs = [], []
    for column in range(columns):
        if column + 1 < columns:
            straight_pairs.append((2 * column, 2 * column + 2))
            crossed_pairs.append((2 * column + 1, 2 * column + 2))
        if column:
            straight_pairs.append((2 * column + 1, 2 * column - 1))
            crossed_pairs.append((2 * column, 2 * column - 1))
    turn = [(0, 1), (1, 0)]
    behind = lax.ppermute(crossed, ("gx", "gz"), crossed_pairs)
    ahead = lax.ppermute(straight, ("gx", "gz"), straight_pairs)
    joined = lax.all_gather(swap, "gz")
    other = jnp.where(is_first, joined[1], joined[0])
    *bands, pick, land = call(
        constants_kernel,
        [narrow(count, 2 * count) for count in WINDOWS]
        + [narrow(2 * DEPTH, DEPTH), narrow(2 * DEPTH, CELLS), narrow(2 * CELLS, DEPTH)],
        [plane_rows[None], box_offset[None]],
        1_000_000_000,
    )
    rows, carry = call(
        first_kernel,
        [full(ROWS, CELLS), full(9, WINDOW, DEPTH)],
        [*bands, pick, block, behind, ahead, other],
        4_000_000_000,
    )
    routes = ([(0, 4), (1, 3)], [(0, 6), (1, 7)], [(0, 2), (1, 5)])
    arrived = [lax.ppermute(rows, ("sec", "gz"), route) for route in routes]
    rows = arrived[0] + arrived[1] + arrived[2]
    held, sent = call(
        second_kernel,
        [full(5, HALF, CELLS), full(5, HALF, CELLS)],
        [*bands, land, carry, rows],
        4_000_000_000,
    )
    swapped = lax.ppermute(sent, "gz", turn)
    (out,) = call(
        last_kernel,
        [full(5, CELLS, CELLS)],
        [held, swapped],
        1000,
        place_out=pl.ANY,
        scratch=[pltpu.SemaphoreType.DMA((2,))],
    )
    return out[None]


def solution(mesh):
    in_specs = (P("sec", None, "gx", "gz"), P("sec", None, "gx", "gz"), P(), P())
    out_specs = P("sec", None, "gx", "gz")
    if mesh.shape["gz"] == 2:
        local = functools.partial(local_window, mesh.shape["gx"])
    else:
        local = local_stepwise
    return jax.shard_map(local, mesh=mesh, in_specs=in_specs, out_specs=out_specs, check_vma=False)
```
